32 devices in a mesh: seq: 16 (over z, x, core), tp: 2 (over y).
Axes of the slice: x: 2, y: 2, z: 4, core: 2. Of those that a mesh axis runs over, the one named last changes fastest.
Arguments:
- tokens_in: bfloat16 [16384, 1024], P(('seq', 'tp')), may hold values from -6 to 6
- w_qkv: bfloat16 [1024, 3, 1024], P(None, None, 'tp'), may hold values from -0.1875 to 0.1875
- bias_qv: bfloat16 [2, 1024], P(None, 'tp'), may hold values from -4 to 4
- w_out: bfloat16 [1024, 1024], P('tp'), may hold values from -0.1875 to 0.1875
- bias_out: bfloat16 [1024], replicated, may hold values from -0.4375 to 0.4375
- w_up: bfloat16 [1024, 4096], P(None, 'tp'), may hold values from -0.1875 to 0.1875
- bias_up: bfloat16 [4096], P('tp'), may hold values from -4 to 4
- w_down: bfloat16 [4096, 1024], P('tp'), may hold values from -0.09375 to 0.09375
- bias_down: bfloat16 [1024], replicated, may hold values from -1.5 to 1.5
- norm_gains: float32 [4, 1024], replicated, may hold values from 0.5 to 1.5
- norm_shifts: float32 [4, 1024], replicated, may hold values from -1.5 to 1.5
- out_grad: float32 [16384, 1024], P(('seq', 'tp')), may hold values from -6 to 6
- lengths: int32 [12], replicated, may hold values from 1 to 4096, as said below
- prefixes: int32 [12], replicated, may hold values from 0 to 64, as said below
- placement: int32 [32], replicated, may hold values from 0 to 31, as said below
Outputs:
- result: bfloat16 [16384, 1024], P(('seq', 'tp'))
- grad_x: float32 [16384, 1024], P(('seq', 'tp'))
- grad_w_qkv: float32 [1024, 3, 1024], P(None, None, 'tp')
- grad_bias_qv: float32 [2, 1024], P(None, 'tp')
- grad_w_out: float32 [1024, 1024], P('tp')
- grad_bias_out: float32 [1024], replicated
- grad_w_up: float32 [1024, 4096], P(None, 'tp')
- grad_bias_up: float32 [4096], P('tp')
- grad_w_down: float32 [4096, 1024], P('tp')
- grad_bias_down: float32 [1024], replicated
- grad_gains: float32 [4, 1024], replicated
- grad_shifts: float32 [4, 1024], replicated
The draws below stay inside these ranges and needn't reach their ends.
Inputs may be any that keep to these rules, and one draw needn't show every extreme that they name: `lengths`: they sum to 16384; at least 7 are text-image pairs of 1088 tokens, and one is exactly 4096 long. `prefixes`: 64 for each of the 7 text-image pairs, 0 for the sequence of 4096 tokens, and for each other text document a prompt of 0 to 64 tokens. `placement`: A permutation of the block numbers; the k-th block stored on each index of seq is one of blocks k * 16 to (k + 1) * 16 - 1.
All inputs are finite; a program needn't handle non-finite values.
Results may differ from the reference program's by a relative error of at most 0.02.
Values may be sent and summed in bfloat16 or wider, within the bound.
A program may use at most 384 MiB of HBM per device.

```python
import jax
import jax.numpy as jnp
from jax import lax

D = 1024
HEADS = 16
HEAD = 64
FF = 4096
BLK = 512
B_DEV = 2
TEXT = 64
IMAGE = 1024
LONGEST = 4096
RANKS = 16
TOKENS = 16384
NPAIR = 7
SPARE = 4672
NOTHER = 4
NSEQ = 12


def doc_layout(key):
    pair_length = TEXT + IMAGE
    middle = SPARE // NOTHER
    rest = SPARE - middle * NOTHER
    swings = jax.random.randint(jax.random.fold_in(key, 1), (NOTHER // 2,), -(middle // 2), middle // 2 + 1)
    texts = jnp.concatenate([middle + swings, middle - swings]).astype(jnp.int32)
    texts = texts.at[0].add(rest)
    prompts = jax.random.randint(jax.random.fold_in(key, 3), (NOTHER,), 0, TEXT + 1).astype(jnp.int32)
    sizes_all = jnp.concatenate([jnp.full((NPAIR,), pair_length, jnp.int32), jnp.full((1,), LONGEST, jnp.int32), texts]).astype(jnp.int32)
    heads_all = jnp.concatenate([jnp.full((NPAIR,), TEXT, jnp.int32), jnp.zeros((1,), jnp.int32), prompts]).astype(jnp.int32)
    order = jax.random.permutation(jax.random.fold_in(key, 2), NSEQ)
    return (sizes_all[order].astype(jnp.int32), heads_all[order].astype(jnp.int32))


def draw_lengths(key, part):
    sizes_all, heads_all = doc_layout(key)
    return sizes_all


def draw_prefixes(key, part):
    sizes_all, heads_all = doc_layout(key)
    return heads_all


def draw_placement(key, part):
    key = jax.random.fold_in(key, 37)
    rounds_list = [index * RANKS + jax.random.permutation(jax.random.fold_in(key, index), RANKS) for index in range(B_DEV)]
    return jnp.stack(rounds_list, axis=1).reshape(-1).astype(jnp.int32)


def block_levels(own_key, extent, cuts, least, top_value):
    def one(dim, parts):
        heights = jax.random.uniform(jax.random.fold_in(jax.random.fold_in(own_key, 6), dim), (parts,), jnp.float32, least / len(cuts), top_value / len(cuts))
        return jnp.repeat(jnp.exp(heights), extent[dim] // parts).reshape((-1,) + (1,) * (len(extent) - dim - 1))

    loudness = one(*cuts[0])
    for cut in cuts[1:]:
        loudness = loudness * one(*cut)
    return loudness


def noise(rng, shape, scale, reach, pieces=(), kind=jnp.bfloat16):
    factor_of = block_levels(rng, shape, pieces, -0.22, 0.18) if pieces else 1.0
    entries = jax.random.normal(rng, shape, jnp.float32) * scale * factor_of
    return jnp.minimum(jnp.maximum(entries, -reach), reach).astype(kind)


def setup_inputs(seed: int = 0) -> dict:
    key_of = jax.random.split(jax.random.key(seed), 16)
    tokens_in = noise(key_of[0], (TOKENS, D), 1.0, 6.0, ((0, 32),))
    w_qkv = noise(key_of[1], (D, 3, D), D ** -0.5, 0.1875, ((2, 2),))
    bias_qv = noise(key_of[2], (2, D), 0.3, 4.0, ((1, 2),))
    w_out = noise(key_of[3], (D, D), D ** -0.5, 0.1875, ((0, 2),))
    bias_out = noise(key_of[4], (D,), 0.03, 0.4375)
    w_up = noise(key_of[5], (D, FF), D ** -0.5, 0.1875, ((1, 2),))
    bias_up = noise(key_of[6], (FF,), 0.3, 4.0, ((0, 2),))
    w_down = noise(key_of[7], (FF, D), FF ** -0.5, 0.09375, ((0, 2),))
    bias_down = noise(key_of[8], (D,), 0.1, 1.5)
    norm_gains = jnp.clip(1.0 + 0.1 * jax.random.normal(key_of[9], (4, D), jnp.float32), 0.5, 1.5)
    norm_shifts = noise(key_of[10], (4, D), 0.1, 1.5, (), jnp.float32)
    out_grad = noise(key_of[11], (TOKENS, D), 1.0, 6.0, ((0, 32),), jnp.float32)
    lengths = draw_lengths(jax.random.fold_in(key_of[15], 71), 0)
    prefixes = draw_prefixes(jax.random.fold_in(key_of[15], 71), 0)
    placement = draw_placement(jax.random.fold_in(key_of[15], 71), 0)
    return dict(tokens_in=tokens_in, w_qkv=w_qkv, bias_qv=bias_qv, w_out=w_out, bias_out=bias_out, w_up=w_up, bias_up=bias_up, w_down=w_down, bias_down=bias_down, norm_gains=norm_gains, norm_shifts=norm_shifts, out_grad=out_grad, lengths=lengths, prefixes=prefixes, placement=placement)


HIGH = lax.Precision.HIGHEST
EPS = 1e-05

@jax.custom_vjp
def low(v):
    return lax.optimization_barrier(v.astype(jnp.bfloat16)).astype(jnp.float32)

@jax.custom_vjp
def low_back(v):
    return v

def low_keep(v):
    return (low(v), None)

def low_pass(kept, grad):
    return (grad,)

def back_keep(v):
    return (v, None)

def back_low(kept, grad):
    return (low(grad),)
low.defvjp(low_keep, low_pass)
low_back.defvjp(back_keep, back_low)

def layer_norm(row_block, gain_row, shift_row):
    row_mean = lax.optimization_barrier(jnp.mean(row_block, axis=-1, keepdims=True))
    centred = row_block - row_mean
    spread = lax.optimization_barrier(jnp.mean(centred * centred, axis=-1, keepdims=True))
    return centred * lax.rsqrt(spread + EPS) * gain_row + shift_row

def pack_tables(lengths, prefixes, row_total):
    where_row = jnp.arange(row_total, dtype=jnp.int32)
    doc_ends = jnp.cumsum(lengths).astype(jnp.int32)
    document = lax.optimization_barrier(jnp.sum((where_row[:, None] >= doc_ends[None, :]).astype(jnp.int32), axis=1)).astype(jnp.int32)
    limits = (doc_ends - lengths + prefixes).astype(jnp.int32)
    doc_pick = document[:, None] == jnp.arange(lengths.shape[0], dtype=jnp.int32)[None, :]
    visible = lax.optimization_barrier(jnp.sum(jnp.where(doc_pick, limits[None, :], 0), axis=1)).astype(jnp.int32)
    return (document, visible)

def padded_tables(document, visible, margin):
    row_total = document.shape[0]
    border = jnp.full((margin,), -1, jnp.int32)
    doc_pad = jnp.concatenate([border, document, border])
    pos_pad = jnp.arange(-margin, row_total + margin, dtype=jnp.int32)
    blank = jnp.zeros((margin,), jnp.int32)
    seen_pad = jnp.concatenate([blank, visible, blank])
    return (doc_pad, pos_pad, seen_pad)

def allowed_pairs(query_pos, query_doc, key_pos, key_doc, key_seen):
    return (query_doc[:, None] == key_doc[None, :]) & ((key_pos[None, :] <= query_pos[:, None]) | (key_pos[None, :] < key_seen[None, :]))

def token_tables(lengths, prefixes, placement, block_size):
    row_total = placement.shape[0] * block_size
    offsets = jnp.arange(block_size, dtype=jnp.int32)
    pack_rows = (placement[:, None] * block_size + offsets[None, :]).reshape(-1).astype(jnp.int32)
    stored_rows = jnp.zeros((row_total,), jnp.int32).at[pack_rows].set(jnp.arange(row_total, dtype=jnp.int32))
    document, visible = pack_tables(lengths, prefixes, row_total)
    return (pack_rows, stored_rows, document, visible)

def attend_block(queries, key_rows, value_rows, allowed):
    score_scale = queries.shape[-1] ** (-0.5)
    scores = score_scale * jnp.einsum('qhe,khe->hqk', queries, key_rows, precision=HIGH)
    scores = low_back(scores)
    masked = jnp.where(allowed[None], scores, -jnp.inf)
    row_top = lax.optimization_barrier(jnp.max(masked, axis=2, keepdims=True))
    expo = jnp.exp(masked - row_top)
    probs = expo / lax.optimization_barrier(jnp.sum(expo, axis=2, keepdims=True))
    return jnp.einsum('hqk,khe->qhe', low(probs), value_rows, precision=HIGH)

def attention(queries, key_rows, value_rows, document, visible):
    row_total = queries.shape[0]
    margin = LONGEST + BLK
    window = LONGEST + 2 * BLK
    widths = ((margin, margin), (0, 0), (0, 0))
    keys_pad = jnp.pad(key_rows, widths)
    values_pad = jnp.pad(value_rows, widths)
    doc_pad, pos_pad, seen_pad = padded_tables(document, visible, margin)
    offsets = jnp.arange(BLK, dtype=jnp.int32)

    def one_block(block):
        first = (block * BLK).astype(jnp.int32)
        key_first = (first + margin - LONGEST).astype(jnp.int32)
        query_block = lax.dynamic_slice_in_dim(queries, first, BLK)
        key_block = lax.dynamic_slice_in_dim(keys_pad, key_first, window)
        value_block = lax.dynamic_slice_in_dim(values_pad, key_first, window)
        allowed = allowed_pairs(first + offsets, lax.dynamic_slice_in_dim(document, first, BLK), lax.dynamic_slice_in_dim(pos_pad, key_first, window), lax.dynamic_slice_in_dim(doc_pad, key_first, window), lax.dynamic_slice_in_dim(seen_pad, key_first, window))
        return attend_block(query_block, key_block, value_block, allowed)
    output = lax.map(jax.checkpoint(one_block), jnp.arange(row_total // BLK, dtype=jnp.int32))
    return output.reshape(row_total, -1)

def forward(tokens_in, w_qkv, bias_qv, w_out, bias_out, w_up, bias_up, w_down, bias_down, norm_gains, norm_shifts, tables):
    pack_rows, stored_rows, document, visible = tables
    row_total = tokens_in.shape[0]
    normed = low(layer_norm(tokens_in, norm_gains[0], norm_shifts[0]))
    mixed = jnp.einsum('td,dce->tce', normed, w_qkv, precision=HIGH)
    queries = low_back(low(mixed[:, 0] + bias_qv[0]))
    key_rows = low_back(low(mixed[:, 1]))
    value_rows = low_back(low(mixed[:, 2] + bias_qv[1]))
    shape = (row_total, HEADS, HEAD)
    attended_pack = attention(queries[stored_rows].reshape(shape), key_rows[stored_rows].reshape(shape), value_rows[stored_rows].reshape(shape), document, visible)
    attended = low_back(low(attended_pack[pack_rows]))
    branch = low_back(jnp.dot(attended, w_out, precision=HIGH)) + bias_out
    hidden = tokens_in + layer_norm(branch, norm_gains[1], norm_shifts[1])
    inner = low(layer_norm(hidden, norm_gains[2], norm_shifts[2]))
    upward = low_back(jnp.dot(inner, w_up, precision=HIGH) + bias_up)
    active = low(jax.nn.gelu(upward, approximate=True))
    down = low_back(jnp.dot(active, w_down, precision=HIGH)) + bias_down
    return hidden + layer_norm(down, norm_gains[3], norm_shifts[3])

def reference(tokens_in, w_qkv, bias_qv, w_out, bias_out, w_up, bias_up, w_down, bias_down, norm_gains, norm_shifts, out_grad, lengths, prefixes, placement):
    tables = token_tables(lengths, prefixes, placement, BLK)
    floats = [item.astype(jnp.float32) for item in (tokens_in, w_qkv, bias_qv, w_out, bias_out, w_up, bias_up, w_down, bias_down, norm_gains, norm_shifts)]

    def layer(*params):
        return forward(*params, tables)
    output, pullback = jax.vjp(layer, *floats)
    grads = pullback(out_grad.astype(jnp.float32))
    return (output.astype(jnp.bfloat16), grads[0], grads[1], grads[2], grads[3], grads[4], grads[5], grads[6], grads[7], grads[8], grads[9], grads[10])
```

```python
import functools

import jax
import jax.numpy as jnp
from jax import lax
from jax.experimental import pallas as pl
from jax.experimental.pallas import tpu as pltpu
from jax.sharding import PartitionSpec as P

HEAD = 64
BLK = 512
HALF = BLK // 2
QUART = BLK // 4
LONGEST = 4096
VMEM_LIMIT = 58 << 20

EPS = 1e-05
F32 = jnp.float32
BF16 = jnp.bfloat16
MESH = pl.DeviceIdType.MESH


def layer_norm(row_block, gain_row, shift_row):
    row_mean = jnp.mean(row_block, axis=-1, keepdims=True)
    centred = row_block - row_mean
    spread = jnp.mean(centred * centred, axis=-1, keepdims=True)
    return centred * lax.rsqrt(spread + EPS) * gain_row + shift_row


def smooth_gate(values):
    return jax.nn.gelu(values, approximate=True)


def running_ends(lengths):
    count = lengths.shape[0]
    index = jnp.arange(count, dtype=jnp.int32)
    return jnp.sum(jnp.where(index[None, :] <= index[:, None], lengths[None, :], 0), axis=1)


def inverse_order(placement):
    index = jnp.arange(placement.shape[0], dtype=jnp.int32)
    return jnp.sum(jnp.where(placement[None, :] == index[:, None], index[None, :], 0), axis=1)


def block_tables(lengths, prefixes, placement, part):
    ends = running_ends(lengths)
    starts = ends - lengths
    limits = starts + prefixes
    offset = part * HALF + jnp.arange(HALF, dtype=jnp.int32)
    pos = placement[:, None] * BLK + offset[None, :]
    inside = (pos[:, :, None] >= starts) & (pos[:, :, None] < ends)

    def pick(values):
        return jnp.sum(jnp.where(inside, values, 0), axis=2)

    low = pick(starts)
    high = jnp.minimum(pick(ends), jnp.maximum(pos + 1, pick(limits)))
    table = jnp.stack(
        [
            jnp.min(low, axis=1) // BLK,
            (jnp.max(high, axis=1) - 1) // BLK + 1,
            jnp.max(low, axis=1),
            jnp.min(high, axis=1),
            inverse_order(placement),
        ]
    )
    return low[:, None, :], high[:, None, :], table


def fill_keys(part, own_ref, sib_ref, kv, kvt):
    other = 1 - part

    def one(b, carry):
        kv[b, pl.ds(pl.multiple_of(part * HALF, HALF), HALF), :] = own_ref[b]
        kv[b, pl.ds(pl.multiple_of(other * HALF, HALF), HALF), :] = sib_ref[b]
        kvt[b] = kv[b].astype(F32).T.astype(BF16)
        return carry

    lax.fori_loop(0, kv.shape[0], one, 0)


def unpack_t(packed):
    turned = packed.astype(F32).T
    return jnp.concatenate([turned[:HEAD], turned[HEAD:]], axis=1)


def pack_t(turned):
    return jnp.concatenate([turned[:, :QUART], turned[:, QUART:]], axis=0).T


def attend_kernel(part_ref, tab, low_ref, high_ref, q_ref, own_ref, sib_ref, out_ref, ot_ref, lse_ref, kv, kvt):
    fill_keys(part_ref[0], own_ref, sib_ref, kv, kvt)
    scale = HEAD**-0.5
    depth = lax.broadcasted_iota(jnp.int32, (BLK, HALF), 0)

    def one(b, carry):
        qt = unpack_t(q_ref[b]) * scale
        rhs = jnp.concatenate([qt, jnp.zeros_like(qt)], axis=0).astype(BF16)
        low, high = low_ref[b], high_ref[b]

        def step(kb, state, masked):
            top, total, acc = state
            st = tab[4, kb]
            sc = jnp.dot(kv[st], rhs, preferred_element_type=F32)
            if masked:
                pos = depth + kb * BLK
                sc = jnp.where((pos >= low) & (pos < high), sc, -1e30)
            new = jnp.maximum(top, jnp.max(sc, axis=0, keepdims=True))
            alpha = jnp.exp(top - new)
            pr = jnp.exp(sc - new)
            total = total * alpha + jnp.sum(pr, axis=0, keepdims=True)
            acc = acc * alpha + jnp.dot(
                kvt[st, HEAD:, :], pr.astype(BF16), preferred_element_type=F32
            )
            return new, total, acc

        def visit(kb, state):
            whole = (kb * BLK >= tab[2, b]) & ((kb + 1) * BLK <= tab[3, b])
            return lax.cond(
                whole,
                lambda st: step(kb, st, False),
                lambda st: step(kb, st, True),
                state,
            )

        start = (
            jnp.full((1, HALF), -1e30, F32),
            jnp.zeros((1, HALF), F32),
            jnp.zeros((HEAD, HALF), F32),
        )
        top, total, acc = lax.fori_loop(tab[0, b], tab[1, b], visit, start)
        ot = acc / total
        ot_ref[b] = ot
        lse_ref[b] = top + jnp.log(total)
        out_ref[b] = pack_t(ot).astype(BF16)
        return carry

    lax.fori_loop(0, q_ref.shape[0], one, 0)


def attend_back_kernel(
    part_ref, tab, low_ref, high_ref, q_ref, own_ref, sib_ref, da_ref, ot_ref, lse_ref,
    dq_ref, mine_ref, theirs_ref, kv, kvt, dkv,
):
    part = part_ref[0]
    fill_keys(part, own_ref, sib_ref, kv, kvt)
    scale = HEAD**-0.5
    depth = lax.broadcasted_iota(jnp.int32, (BLK, HALF), 0)
    lane = lax.broadcasted_iota(jnp.int32, (HALF, 2 * HEAD), 1)

    def clear(b, carry):
        dkv[b] = jnp.zeros((BLK, 2 * HEAD), F32)
        return carry

    lax.fori_loop(0, dkv.shape[0], clear, 0)

    def one(b, carry):
        qt = unpack_t(q_ref[b]) * scale
        dat = unpack_t(da_ref[b])
        blank = jnp.zeros_like(qt)
        rhs_q = jnp.concatenate([qt, blank], axis=0).astype(BF16)
        rhs_d = jnp.concatenate([blank, dat], axis=0).astype(BF16)
        both = jnp.concatenate([qt, dat], axis=0).T
        rows_q = jnp.where(lane < HEAD, both, 0.0).astype(BF16)
        rows_d = jnp.where(lane < HEAD, 0.0, both).astype(BF16)
        total = jnp.sum(dat * ot_ref[b], axis=0, keepdims=True)
        lse = lse_ref[b]
        low, high = low_ref[b], high_ref[b]

        def step(kb, acc, masked):
            st = tab[4, kb]
            keys = kv[st]
            sc = jnp.dot(keys, rhs_q, preferred_element_type=F32)
            dp = jnp.dot(keys, rhs_d, preferred_element_type=F32)
            if masked:
                pos = depth + kb * BLK
                sc = jnp.where((pos >= low) & (pos < high), sc, -1e30)
            pr = jnp.exp(sc - lse)
            ds = (pr * (dp - total)).astype(BF16)
            dkv[st] += jnp.dot(ds, rows_q, preferred_element_type=F32) + jnp.dot(
                pr.astype(BF16), rows_d, preferred_element_type=F32
            )
            return acc + jnp.dot(kvt[st, :HEAD, :], ds, preferred_element_type=F32)

        def visit(kb, acc):
            whole = (kb * BLK >= tab[2, b]) & ((kb + 1) * BLK <= tab[3, b])
            return lax.cond(
                whole, lambda a: step(kb, a, False), lambda a: step(kb, a, True), acc
            )

        acc = lax.fori_loop(tab[0, b], tab[1, b], visit, jnp.zeros((HEAD, HALF), F32))
        dq_ref[b] = pack_t(acc * scale).astype(BF16)
        return carry

    lax.fori_loop(0, q_ref.shape[0], one, 0)
    other = 1 - part

    def split(b, carry):
        mine_ref[b] = dkv[b, pl.ds(pl.multiple_of(part * HALF, HALF), HALF), :]
        theirs_ref[b] = dkv[b, pl.ds(pl.multiple_of(other * HALF, HALF), HALF), :].astype(BF16)
        return carry

    lax.fori_loop(0, dkv.shape[0], split, 0)


def vmem(count):
    return [pl.BlockSpec(memory_space=pltpu.VMEM)] * count


def smem(count):
    return [pl.BlockSpec(memory_space=pltpu.SMEM)] * count


def attend(part, tables, q_chunks, kv_own, kv_sib):
    low, high, table = tables
    blocks = q_chunks.shape[0]
    return pl.pallas_call(
        attend_kernel,
        out_shape=(
            jax.ShapeDtypeStruct((blocks, QUART, 2 * HEAD), BF16),
            jax.ShapeDtypeStruct((blocks, HEAD, HALF), F32),
            jax.ShapeDtypeStruct((blocks, 1, HALF), F32),
        ),
        in_specs=smem(2) + vmem(5),
        out_specs=tuple(vmem(3)),
        scratch_shapes=[
            pltpu.VMEM((blocks, BLK, 2 * HEAD), BF16),
            pltpu.VMEM((blocks, 2 * HEAD, BLK), BF16),
        ],
        compiler_params=pltpu.CompilerParams(vmem_limit_bytes=VMEM_LIMIT),
        name="attend",
    )(part.reshape(1), table, low, high, q_chunks, kv_own, kv_sib)


def attend_back(part, tables, q_chunks, kv_own, kv_sib, da_chunks, out_t, mass):
    low, high, table = tables
    blocks = q_chunks.shape[0]
    return pl.pallas_call(
        attend_back_kernel,
        out_shape=(
            jax.ShapeDtypeStruct((blocks, QUART, 2 * HEAD), BF16),
            jax.ShapeDtypeStruct((blocks, HALF, 2 * HEAD), F32),
            jax.ShapeDtypeStruct((blocks, HALF, 2 * HEAD), BF16),
        ),
        in_specs=smem(2) + vmem(8),
        out_specs=tuple(vmem(3)),
        scratch_shapes=[
            pltpu.VMEM((blocks, BLK, 2 * HEAD), BF16),
            pltpu.VMEM((blocks, 2 * HEAD, BLK), BF16),
            pltpu.VMEM((blocks, BLK, 2 * HEAD), F32),
        ],
        compiler_params=pltpu.CompilerParams(vmem_limit_bytes=VMEM_LIMIT),
        name="attend_back",
    )(part.reshape(1), table, low, high, q_chunks, kv_own, kv_sib, da_chunks, out_t, mass)


def chunk_of(who, quarter, index, half):
    absolute = (who[0] * 2 + who[1]) ^ quarter
    tp, sub = absolute // 2, absolute % 2
    return ((sub * 4 + index) * 2 + half) * 2 + tp


def swap_lanes(values):
    return pltpu.roll(values, HEAD, 1)


def low_lanes(rows):
    return lax.broadcasted_iota(jnp.int32, (rows, 2 * HEAD), 1) < HEAD


def store_packed(who, quarter, values, out_ref):
    low = low_lanes(QUART)
    for pair in range(2):
        for half in range(2):
            top = half * HALF
            lanes = slice(pair * 128, pair * 128 + 128)
            first, second = values[top : top + QUART, lanes], values[top + QUART : top + HALF, lanes]
            even = jnp.where(low, first, swap_lanes(second))
            odd = jnp.where(low, swap_lanes(first), second)
            out_ref[chunk_of(who, quarter, 2 * pair, half)] = even.astype(BF16)
            out_ref[chunk_of(who, quarter, 2 * pair + 1, half)] = odd.astype(BF16)


def load_packed(who, quarter, ref, out_ref):
    low = low_lanes(QUART)
    for pair in range(2):
        for half in range(2):
            even = ref[chunk_of(who, quarter, 2 * pair, half)].astype(F32)
            odd = ref[chunk_of(who, quarter, 2 * pair + 1, half)].astype(F32)
            top = half * HALF
            lanes = slice(quarter * 256 + pair * 128, quarter * 256 + pair * 128 + 128)
            out_ref[top : top + QUART, lanes] = jnp.where(low, even, swap_lanes(odd)).astype(BF16)
            out_ref[top + QUART : top + HALF, lanes] = jnp.where(low, swap_lanes(even), odd).astype(BF16)


def project_kernel(who_ref, x_ref, gain_ref, shift_ref, bias_ref, w0, w1, w2, w3, normed_ref, q_ref, kv_ref):
    who = (who_ref[0], who_ref[1])
    normed = layer_norm(x_ref[...].astype(F32), gain_ref[...], shift_ref[...]).astype(BF16)
    normed_ref[...] = normed
    low = low_lanes(HALF)
    for quarter, w in enumerate((w0, w1, w2, w3)):
        def dot(col):
            return jnp.dot(normed, w[:, col : col + 256], preferred_element_type=F32)

        bias = bias_ref[quarter : quarter + 1, :].astype(F32)
        store_packed(who, quarter, dot(0) + bias[:, :256], q_ref)
        keys = dot(256)
        values = dot(512) + bias[:, 256:]
        for pair in range(2):
            lanes = slice(pair * 128, pair * 128 + 128)
            for half in range(2):
                rows = slice(half * HALF, half * HALF + HALF)
                k, v = keys[rows, lanes], values[rows, lanes]
                even = jnp.where(low, k, swap_lanes(v))
                odd = jnp.where(low, swap_lanes(k), v)
                kv_ref[chunk_of(who, quarter, 2 * pair, half)] = even.astype(BF16)
                kv_ref[chunk_of(who, quarter, 2 * pair + 1, half)] = odd.astype(BF16)


def project(who, x, gain, shift, bias, weights):
    rows, width = x.shape
    return pl.pallas_call(
        project_kernel,
        out_shape=(
            jax.ShapeDtypeStruct((rows, width), BF16),
            jax.ShapeDtypeStruct((32, QUART, 2 * HEAD), BF16),
            jax.ShapeDtypeStruct((32, HALF, 2 * HEAD), BF16),
        ),
        in_specs=smem(1) + vmem(8),
        out_specs=tuple(vmem(3)),
        compiler_params=pltpu.CompilerParams(vmem_limit_bytes=VMEM_LIMIT),
        name="project",
    )(who, x, gain, shift, bias, *weights)


def unpack_heads_kernel(who_ref, ref, out_ref):
    who = (who_ref[0], who_ref[1])
    for quarter in range(4):
        load_packed(who, quarter, ref, out_ref)


def unpack_heads(who, chunks):
    return pl.pallas_call(
        unpack_heads_kernel,
        out_shape=jax.ShapeDtypeStruct((BLK, 1024), BF16),
        in_specs=smem(1) + vmem(1),
        out_specs=vmem(1)[0],
        compiler_params=pltpu.CompilerParams(vmem_limit_bytes=VMEM_LIMIT),
        name="unpack_heads",
    )(who, chunks)


def spread_kernel(who_ref, d_ref, w0, w1, w2, w3, out_ref):
    who = (who_ref[0], who_ref[1])
    d_rows = d_ref[...]
    for quarter, w in enumerate((w0, w1, w2, w3)):
        values = lax.dot_general(
            d_rows, w[...], (((1,), (1,)), ((), ())), preferred_element_type=F32
        )
        store_packed(who, quarter, values, out_ref)


def spread(who, d_branch, weights):
    return pl.pallas_call(
        spread_kernel,
        out_shape=jax.ShapeDtypeStruct((32, QUART, 2 * HEAD), BF16),
        in_specs=smem(1) + vmem(5),
        out_specs=vmem(1)[0],
        compiler_params=pltpu.CompilerParams(vmem_limit_bytes=VMEM_LIMIT),
        name="spread",
    )(who, d_branch, *weights)


def unpack_qkv_kernel(who_ref, dq_ref, dkv_ref, q_ref, k_ref, v_ref):
    who = (who_ref[0], who_ref[1])
    low = low_lanes(HALF)
    for quarter in range(4):
        load_packed(who, quarter, dq_ref, q_ref)
        for pair in range(2):
            lanes = slice(quarter * 256 + pair * 128, quarter * 256 + pair * 128 + 128)
            for half in range(2):
                rows = slice(half * HALF, half * HALF + HALF)
                even = dkv_ref[chunk_of(who, quarter, 2 * pair, half)].astype(F32)
                odd = dkv_ref[chunk_of(who, quarter, 2 * pair + 1, half)].astype(F32)
                k_ref[rows, lanes] = jnp.where(low, even, swap_lanes(odd)).astype(BF16)
                v_ref[rows, lanes] = jnp.where(low, swap_lanes(even), odd).astype(BF16)


def unpack_qkv(who, dq_chunks, dkv_chunks):
    shape = jax.ShapeDtypeStruct((BLK, 1024), BF16)
    return pl.pallas_call(
        unpack_qkv_kernel,
        out_shape=(shape, shape, shape),
        in_specs=smem(1) + vmem(2),
        out_specs=tuple(vmem(3)),
        compiler_params=pltpu.CompilerParams(vmem_limit_bytes=VMEM_LIMIT),
        name="unpack_qkv",
    )(who, dq_chunks, dkv_chunks)


def sum_all_kernel(seq_bits, mine_ref, out_ref, slots, send, recv):
    seq, tp = lax.axis_index("seq"), lax.axis_index("tp")
    partners = [(seq ^ (1 << bit), tp) for bit in range(seq_bits)]
    partners.insert(1, (seq, tp ^ 1))
    barrier = pltpu.get_barrier_semaphore()
    for partner in partners:
        pl.semaphore_signal(barrier, inc=1, device_id=partner, device_id_type=MESH)
    pl.semaphore_wait(barrier, len(partners))
    out_ref[...] = mine_ref[...]
    for step, partner in enumerate(partners):
        slots[step] = out_ref[...]
        copy = pltpu.make_async_remote_copy(
            src_ref=slots.at[step],
            dst_ref=slots.at[len(partners) + step],
            send_sem=send.at[step],
            recv_sem=recv.at[step],
            device_id=partner,
            device_id_type=MESH,
        )
        copy.start()
        copy.wait()
        out_ref[...] += slots[len(partners) + step]


def sum_all(values, seq_count):
    seq_bits = seq_count.bit_length() - 1
    steps = seq_bits + 1
    return pl.pallas_call(
        functools.partial(sum_all_kernel, seq_bits),
        out_shape=jax.ShapeDtypeStruct(values.shape, values.dtype),
        in_specs=vmem(1),
        out_specs=vmem(1)[0],
        scratch_shapes=[
            pltpu.VMEM((2 * steps,) + values.shape, values.dtype),
            pltpu.SemaphoreType.DMA((steps,)),
            pltpu.SemaphoreType.DMA((steps,)),
        ],
        compiler_params=pltpu.CompilerParams(collective_id=7, has_side_effects=True),
        name="sum_all",
    )(values)


def norm_parts(values):
    mean = jnp.mean(values, axis=-1, keepdims=True)
    centred = values - mean
    rstd = lax.rsqrt(jnp.mean(centred * centred, axis=-1, keepdims=True) + EPS)
    return centred * rstd, rstd


def norm_back(values, gain, upstream):
    xhat, rstd = norm_parts(values)
    e = upstream * gain
    grad = rstd * (
        e
        - jnp.mean(e, axis=-1, keepdims=True)
        - xhat * jnp.mean(e * xhat, axis=-1, keepdims=True)
    )
    return grad, jnp.sum(upstream * xhat, axis=0), jnp.sum(upstream, axis=0)


def fast_local(
    tokens_in, w_qkv, bias_qv, w_out, bias_out, w_up, bias_up, w_down, bias_down,
    norm_gains, norm_shifts, out_grad, lengths, prefixes, placement,
):
    seq_count = lax.axis_size("seq")
    seq, tp = lax.axis_index("seq"), lax.axis_index("tp")
    core = seq % 2
    who = jnp.stack([tp, core]).astype(jnp.int32)
    over_tp = [(0, 1), (1, 0)]
    over_core = [(i, i ^ 1) for i in range(seq_count)]
    chips = [[c + 2 * i for i in range(seq_count // 2)] for c in range(2)]

    def to_tp(values):
        return lax.ppermute(values, "tp", over_tp)

    def to_sib(values):
        return lax.ppermute(values, "seq", over_core)

    def exchange(chunks):
        return lax.all_to_all(chunks, ("seq", "tp"), 0, 0, tiled=True)

    def quarters(values, axis):
        size = values.shape[axis] // 2
        own = lax.dynamic_slice_in_dim(values, core * size, size, axis)
        sib = lax.dynamic_slice_in_dim(values, (1 - core) * size, size, axis)
        far = to_tp(own)
        return [own, sib, far, to_sib(far)]

    width = w_qkv.shape[0]
    wq4 = [w.reshape(width, -1) for w in quarters(w_qkv, 2)]
    small = jnp.concatenate([bias_qv.reshape(2, 2, -1), bias_up.reshape(2, 2, -1).transpose(1, 0, 2)], axis=2)
    small = small.transpose(1, 0, 2)
    small4 = [s.reshape(2, -1) for s in quarters(small, 0)]
    split = bias_qv.shape[1] // 2
    bias_qv4 = jnp.stack([s[:, :split].reshape(-1) for s in small4])
    bias_up4 = [s[:, split:].reshape(-1).astype(F32) for s in small4]
    wo4 = quarters(w_out, 0)
    wu4 = quarters(w_up, 1)
    wd4 = quarters(w_down, 0)

    tables = block_tables(lengths, prefixes, placement, core)
    normed, q_chunks, kv_chunks = project(
        who, tokens_in, norm_gains[:1], norm_shifts[:1], bias_qv4, wq4
    )
    kv_own = exchange(kv_chunks)
    kv_sib = to_sib(kv_own)
    q_own = exchange(q_chunks)
    att_chunks, out_t, mass = attend(core, tables, q_own, kv_own, kv_sib)
    attended = unpack_heads(who, exchange(att_chunks))

    input_f32 = tokens_in.astype(F32)

    def cols(values, quarter, count):
        return values[:, quarter * count : (quarter + 1) * count]

    def dot(a, b):
        return jnp.dot(a, b, preferred_element_type=F32)

    def dot_t(a, b):
        return lax.dot_general(a, b, (((1,), (1,)), ((), ())), preferred_element_type=F32)

    def dot_rows(a, b):
        return lax.dot_general(a, b, (((0,), (0,)), ((), ())), preferred_element_type=F32)

    heads4 = [cols(attended, r, 256) for r in range(4)]
    branch = sum(dot(heads4[r], wo4[r]) for r in range(4)) + bias_out.astype(F32)
    hidden = input_f32 + layer_norm(branch, norm_gains[1], norm_shifts[1])
    inner = layer_norm(hidden, norm_gains[2], norm_shifts[2]).astype(BF16)
    active4, gate4 = [], []
    for r in range(4):
        act, back_gate = jax.vjp(smooth_gate, dot(inner, wu4[r]) + bias_up4[r])
        active4.append(act.astype(BF16))
        gate4.append(back_gate)
    down = sum(dot(active4[r], wd4[r]) for r in range(4)) + bias_down.astype(F32)
    result = (hidden + layer_norm(down, norm_gains[3], norm_shifts[3])).astype(BF16)
    d_down, gain_last, shift_last = norm_back(down, norm_gains[3], out_grad)
    bias_down_part = jnp.sum(d_down, axis=0)
    d_down_b = d_down.astype(BF16)
    d_up4 = [gate4[r](dot_t(d_down_b, wd4[r]))[0].astype(BF16) for r in range(4)]
    bias_up_part = [jnp.sum(d.astype(F32), axis=0) for d in d_up4]
    d_inner = sum(dot_t(d_up4[r], wu4[r]) for r in range(4))
    d_third, gain_third, shift_third = norm_back(hidden, norm_gains[2], d_inner)
    d_hidden = out_grad + d_third
    d_branch, gain_second, shift_second = norm_back(branch, norm_gains[1], d_hidden)
    bias_out_part = jnp.sum(d_branch, axis=0)
    d_branch_b = d_branch.astype(BF16)
    da_own = exchange(spread(who, d_branch_b, wo4))
    dq_chunks, dkv_mine, dkv_theirs = attend_back(
        core, tables, q_own, kv_own, kv_sib, da_own, out_t, mass
    )
    dkv_chunks = (dkv_mine + to_sib(dkv_theirs).astype(F32)).astype(BF16)
    d_q, d_k, d_v = unpack_qkv(who, exchange(dq_chunks), exchange(dkv_chunks))

    inner_sib, down_sib, branch_sib, normed_sib = (
        to_sib(inner), to_sib(d_down_b), to_sib(d_branch_b), to_sib(normed)
    )

    def paired(left4, right):
        own = [left4[r] for r in (0, 2)]
        sib = [to_sib(left4[r]) for r in (1, 3)]
        near, far = (right(o, s) for o, s in zip(own, sib))
        return near, far.astype(BF16)

    def reduced(pair):
        near, far = pair
        return (near + to_tp(far).astype(F32)).astype(BF16)

    g_down = reduced(paired(active4, lambda o, s: dot_rows(o, d_down_b) + dot_rows(s, down_sib)))
    g_up = reduced(paired(d_up4, lambda o, s: dot_rows(inner, o) + dot_rows(inner_sib, s)))
    g_out = reduced(paired(heads4, lambda o, s: dot_rows(o, d_branch_b) + dot_rows(s, branch_sib)))
    g_down, g_up, g_out = lax.psum((g_down, g_up, g_out), "seq", axis_index_groups=chips)

    mixed4 = [
        jnp.concatenate([cols(d, r, 256) for d in (d_q, d_k, d_v)], axis=1) for r in range(4)
    ]
    d_normed = sum(dot_t(mixed4[r], wq4[r]) for r in range(4))
    d_first, gain_first, shift_first = norm_back(input_f32, norm_gains[0], d_normed)
    grad_x = d_hidden + d_first
    g_qkv = reduced(paired(mixed4, lambda o, s: dot_rows(normed, o) + dot_rows(normed_sib, s)))
    g_qkv = lax.psum(g_qkv, "seq", axis_index_groups=chips).reshape(width, 3, -1)

    def joined(own, axis):
        sib = to_sib(own)
        first = jnp.concatenate([own, sib], axis=axis).astype(F32)
        second = jnp.concatenate([sib, own], axis=axis).astype(F32)
        return jnp.where(core == 0, first, second)

    def absolute(parts):
        base = tp * 2 + core
        return jnp.concatenate(
            [sum(jnp.where((base ^ r) == a, parts[r], 0.0) for r in range(4)) for a in range(4)]
        )

    bias_q_part = [jnp.sum(cols(d_q, r, 256).astype(F32), axis=0) for r in range(4)]
    bias_v_part = [jnp.sum(cols(d_v, r, 256).astype(F32), axis=0) for r in range(4)]
    vectors = jnp.stack(
        [gain_first, gain_second, gain_third, gain_last]
        + [shift_first, shift_second, shift_third, shift_last]
        + [bias_out_part, bias_down_part, absolute(bias_q_part), absolute(bias_v_part)]
    )
    vectors = jnp.concatenate([vectors, absolute(bias_up_part).reshape(4, -1)])
    vectors = sum_all(vectors, seq_count)
    own_cols = bias_qv.shape[1]
    grad_bias_qv = lax.dynamic_slice_in_dim(vectors[10:12], tp * own_cols, own_cols, 1)
    grad_bias_up = lax.dynamic_slice_in_dim(
        vectors[12:16].reshape(-1), tp * bias_up.shape[0], bias_up.shape[0]
    )
    return (
        result,
        grad_x,
        joined(g_qkv, 2),
        grad_bias_qv,
        joined(g_out, 0),
        vectors[8],
        joined(g_up, 1),
        grad_bias_up,
        joined(g_down, 0),
        vectors[9],
        vectors[0:4],
        vectors[4:8],
    )


def pack_tables(lengths, prefixes, row_total):
    where_row = jnp.arange(row_total, dtype=jnp.int32)
    doc_ends = running_ends(lengths)
    document = jnp.sum((where_row[:, None] >= doc_ends[None, :]).astype(jnp.int32), axis=1)
    limits = doc_ends - lengths + prefixes
    doc_pick = document[:, None] == jnp.arange(lengths.shape[0], dtype=jnp.int32)[None, :]
    visible = jnp.sum(jnp.where(doc_pick, limits[None, :], 0), axis=1)
    return (document, visible)


def padded_tables(document, visible, margin):
    row_total = document.shape[0]
    border = jnp.full((margin,), -1, jnp.int32)
    doc_pad = jnp.concatenate([border, document, border])
    pos_pad = jnp.arange(-margin, row_total + margin, dtype=jnp.int32)
    blank = jnp.zeros((margin,), jnp.int32)
    seen_pad = jnp.concatenate([blank, visible, blank])
    return (doc_pad, pos_pad, seen_pad)


def allowed_pairs(query_pos, query_doc, key_pos, key_doc, key_seen):
    return (query_doc[:, None] == key_doc[None, :]) & (
        (key_pos[None, :] <= query_pos[:, None]) | (key_pos[None, :] < key_seen[None, :])
    )


def pick_blocks(blocks, order):
    return lax.map(lambda i: lax.dynamic_index_in_dim(blocks, i, 0, False), order)


def to_pack(stored, pack_order, margin, block_size):
    blocks = stored.reshape((pack_order.shape[0], block_size) + stored.shape[1:])
    ordered = pick_blocks(blocks, pack_order).reshape(stored.shape)
    widths = [(margin, margin)] + [(0, 0)] * (stored.ndim - 1)
    return jnp.pad(ordered, widths)


def from_pack(padded, placement, margin, block_size, row_total):
    core = padded[margin : margin + row_total]
    blocks = core.reshape((placement.shape[0], block_size) + core.shape[1:])
    return pick_blocks(blocks, placement).reshape(core.shape)


def masked_scores(query_h, key_h, allowed):
    scores = query_h.shape[-1] ** (-0.5) * jnp.einsum(
        "qe,ke->qk", query_h, key_h, preferred_element_type=jnp.float32
    )
    return jnp.where(allowed, scores, -jnp.inf)


def forward_block(query_block, key_win, value_win, allowed):

    def forward_one_head(head):
        query_h = lax.dynamic_index_in_dim(query_block, head, 1, False)
        key_h = lax.dynamic_index_in_dim(key_win, head, 1, False)
        value_h = lax.dynamic_index_in_dim(value_win, head, 1, False)
        masked = masked_scores(query_h, key_h, allowed)
        row_top = jnp.max(masked, axis=1, keepdims=True)
        expo = jnp.exp(masked - row_top)
        row_sum = jnp.sum(expo, axis=1, keepdims=True)
        probs_b = (expo / row_sum).astype(jnp.bfloat16)
        output = jnp.dot(probs_b, value_h, preferred_element_type=jnp.float32)
        return (output, (row_top + jnp.log(row_sum))[:, 0])

    return lax.map(forward_one_head, jnp.arange(query_block.shape[1], dtype=jnp.int32))


def attention_grads(
    query_block, d_att_block, mass_block, total_block, key_block, value_block, allowed
):
    score_scale = query_block.shape[-1] ** (-0.5)

    def attention_one_head(head):
        query_h = lax.dynamic_index_in_dim(query_block, head, 1, False)
        d_att_h = lax.dynamic_index_in_dim(d_att_block, head, 1, False)
        key_h = lax.dynamic_index_in_dim(key_block, head, 1, False)
        value_h = lax.dynamic_index_in_dim(value_block, head, 1, False)
        mass_h = lax.dynamic_index_in_dim(mass_block, head, 0, False)
        total_h = lax.dynamic_index_in_dim(total_block, head, 0, False)
        masked = masked_scores(query_h, key_h, allowed)
        probs = jnp.exp(masked - mass_h[:, None])
        d_probs = jnp.einsum("qe,ke->qk", d_att_h, value_h, preferred_element_type=jnp.float32)
        d_scores = (probs * (d_probs - total_h[:, None])).astype(jnp.bfloat16)
        results = []
        results.append(
            score_scale
            * jnp.einsum("qk,ke->qe", d_scores, key_h, preferred_element_type=jnp.float32)
        )
        results.append(
            score_scale
            * jnp.einsum("qk,qe->ke", d_scores, query_h, preferred_element_type=jnp.float32)
        )
        results.append(
            jnp.einsum(
                "qk,qe->ke", probs.astype(jnp.bfloat16), d_att_h, preferred_element_type=jnp.float32
            )
        )
        return tuple(results)

    return lax.map(attention_one_head, jnp.arange(query_block.shape[1], dtype=jnp.int32))


def general_local(
    tokens_in,
    w_qkv,
    bias_qv,
    w_out,
    bias_out,
    w_up,
    bias_up,
    w_down,
    bias_down,
    norm_gains,
    norm_shifts,
    out_grad,
    lengths,
    prefixes,
    placement,
):
    seq_count = lax.axis_size("seq")
    block_total = placement.shape[0]
    blocks_here = block_total // seq_count
    total_rows = block_total * BLK
    own_rows = blocks_here * BLK
    model_width = w_qkv.shape[0]
    head_span = w_qkv.shape[2]
    heads_here = head_span // HEAD
    margin = LONGEST + BLK
    window = LONGEST + 2 * BLK
    document, visible = pack_tables(lengths, prefixes, total_rows)
    doc_pad, pos_pad, seen_pad = padded_tables(document, visible, margin)
    own_blocks = lax.dynamic_slice_in_dim(
        placement, lax.axis_index("seq") * blocks_here, blocks_here
    )
    pack_order = inverse_order(placement)
    offsets = jnp.arange(BLK, dtype=jnp.int32)

    def query_window(index):
        first = own_blocks[index] * BLK
        key_first = margin + first - LONGEST
        allowed = allowed_pairs(
            first + offsets,
            lax.dynamic_slice_in_dim(document, first, BLK),
            lax.dynamic_slice_in_dim(pos_pad, key_first, window),
            lax.dynamic_slice_in_dim(doc_pad, key_first, window),
            lax.dynamic_slice_in_dim(seen_pad, key_first, window),
        )
        return (key_first, allowed)

    input_f32 = tokens_in.astype(jnp.float32)
    normed, back_first = jax.vjp(layer_norm, input_f32, norm_gains[0], norm_shifts[0])
    rows_all = lax.all_gather(normed.astype(jnp.bfloat16), "tp", axis=0, tiled=True)
    flat_qkv = w_qkv.reshape(model_width, 3 * head_span)
    mixed = jnp.dot(rows_all, flat_qkv, preferred_element_type=jnp.float32).reshape(
        own_rows, 3, head_span
    )
    query_b = (mixed[:, 0] + bias_qv[0].astype(jnp.float32)).astype(jnp.bfloat16)
    key_b = mixed[:, 1].astype(jnp.bfloat16)
    value_b = (mixed[:, 2] + bias_qv[1].astype(jnp.float32)).astype(jnp.bfloat16)
    keys_all, values_all = (
        lax.all_gather(key_b, "seq", axis=0, tiled=True),
        lax.all_gather(value_b, "seq", axis=0, tiled=True),
    )
    keys_pad = to_pack(keys_all, pack_order, margin, BLK).reshape(-1, heads_here, HEAD)
    values_pad = to_pack(values_all, pack_order, margin, BLK).reshape(-1, heads_here, HEAD)
    head_shape = (own_rows, heads_here, HEAD)
    query3 = query_b.reshape(head_shape)
    attended_list = []
    mass_list = []
    for index in range(blocks_here):
        key_first, allowed = query_window(index)
        outputs, masses = forward_block(
            query3[index * BLK : (index + 1) * BLK],
            lax.dynamic_slice_in_dim(keys_pad, key_first, window),
            lax.dynamic_slice_in_dim(values_pad, key_first, window),
            allowed,
        )
        attended_list.append(jnp.transpose(outputs, (1, 0, 2)))
        mass_list.append(masses)
    attended32 = jnp.concatenate(attended_list, axis=0)
    log_mass = jnp.concatenate(mass_list, axis=1)
    attended_b = attended32.reshape(own_rows, head_span).astype(jnp.bfloat16)
    branch = lax.psum_scatter(
        jnp.dot(attended_b, w_out, preferred_element_type=jnp.float32).astype(jnp.bfloat16),
        "tp",
        scatter_dimension=0,
        tiled=True,
    ).astype(jnp.float32) + bias_out.astype(jnp.float32)
    post_attn, back_post = jax.vjp(layer_norm, branch, norm_gains[1], norm_shifts[1])
    hidden = input_f32 + post_attn
    inner, back_inner = jax.vjp(layer_norm, hidden, norm_gains[2], norm_shifts[2])
    inner_all = lax.all_gather(inner.astype(jnp.bfloat16), "tp", axis=0, tiled=True)
    upward = jnp.dot(inner_all, w_up, preferred_element_type=jnp.float32) + bias_up.astype(
        jnp.float32
    )
    active, back_gate = jax.vjp(smooth_gate, upward)
    active_b = active.astype(jnp.bfloat16)
    down = lax.psum_scatter(
        jnp.dot(active_b, w_down, preferred_element_type=jnp.float32).astype(jnp.bfloat16),
        "tp",
        scatter_dimension=0,
        tiled=True,
    ).astype(jnp.float32) + bias_down.astype(jnp.float32)
    final, back_final = jax.vjp(layer_norm, down, norm_gains[3], norm_shifts[3])
    result = (hidden + final).astype(jnp.bfloat16)
    d_down, gain_last, shift_last = back_final(out_grad)
    grad_bias_down = jnp.sum(d_down, axis=0)
    d_down_all = lax.all_gather(d_down.astype(jnp.bfloat16), "tp", axis=0, tiled=True)
    grad_w_down = jnp.einsum("tf,td->fd", active_b, d_down_all, preferred_element_type=jnp.float32)
    d_active = jnp.einsum("td,fd->tf", d_down_all, w_down, preferred_element_type=jnp.float32)
    (d_up,) = back_gate(d_active)
    d_up_b = d_up.astype(jnp.bfloat16)
    grad_bias_up = jnp.sum(d_up_b.astype(jnp.float32), axis=0)
    grad_w_up = jnp.einsum("td,tf->df", inner_all, d_up_b, preferred_element_type=jnp.float32)
    d_inner = lax.psum_scatter(
        jnp.einsum("tf,df->td", d_up_b, w_up, preferred_element_type=jnp.float32).astype(
            jnp.bfloat16
        ),
        "tp",
        scatter_dimension=0,
        tiled=True,
    ).astype(jnp.float32)
    d_hidden_part, gain_third, shift_third = back_inner(d_inner)
    d_hidden = out_grad + d_hidden_part
    d_branch, gain_second, shift_second = back_post(d_hidden)
    grad_bias_out = jnp.sum(d_branch, axis=0)
    d_branch_all = lax.all_gather(d_branch.astype(jnp.bfloat16), "tp", axis=0, tiled=True)
    grad_w_out = jnp.einsum(
        "te,td->ed", attended_b, d_branch_all, preferred_element_type=jnp.float32
    )
    d_att_b = jnp.einsum(
        "td,ed->te", d_branch_all, w_out, preferred_element_type=jnp.float32
    ).astype(jnp.bfloat16)
    d_att3 = d_att_b.reshape(head_shape)
    d_total = jnp.sum(d_att3.astype(jnp.float32) * attended32, axis=2).T
    d_query_list = []
    key_buffer = jnp.zeros((total_rows + 2 * margin, head_span), jnp.float32)
    value_buffer = jnp.zeros((total_rows + 2 * margin, head_span), jnp.float32)
    for index in range(blocks_here):
        key_first, allowed = query_window(index)
        rows = slice(index * BLK, (index + 1) * BLK)
        d_query_h, d_key_h, d_value_h = attention_grads(
            query3[rows],
            d_att3[rows],
            log_mass[:, rows],
            d_total[:, rows],
            lax.dynamic_slice_in_dim(keys_pad, key_first, window),
            lax.dynamic_slice_in_dim(values_pad, key_first, window),
            allowed,
        )
        d_query_list.append(jnp.transpose(d_query_h, (1, 0, 2)))
        key_piece = jnp.transpose(d_key_h, (1, 0, 2)).reshape(window, head_span)
        value_piece = jnp.transpose(d_value_h, (1, 0, 2)).reshape(window, head_span)
        key_buffer = lax.dynamic_update_slice_in_dim(
            key_buffer,
            lax.dynamic_slice_in_dim(key_buffer, key_first, window) + key_piece,
            key_first,
            0,
        )
        value_buffer = lax.dynamic_update_slice_in_dim(
            value_buffer,
            lax.dynamic_slice_in_dim(value_buffer, key_first, window) + value_piece,
            key_first,
            0,
        )
    key_terms = from_pack(key_buffer, placement, margin, BLK, total_rows)
    value_terms = from_pack(value_buffer, placement, margin, BLK, total_rows)
    d_keys, d_values = (
        lax.psum_scatter(
            key_terms.astype(jnp.bfloat16), "seq", scatter_dimension=0, tiled=True
        ).astype(jnp.float32),
        lax.psum_scatter(
            value_terms.astype(jnp.bfloat16), "seq", scatter_dimension=0, tiled=True
        ).astype(jnp.float32),
    )
    d_query = jnp.concatenate(d_query_list, axis=0)
    d_query_b = d_query.reshape(own_rows, head_span).astype(jnp.bfloat16)
    d_keys_b = d_keys.astype(jnp.bfloat16)
    d_values_b = d_values.astype(jnp.bfloat16)
    grad_bias_qv = jnp.stack(
        [
            jnp.sum(d_query_b.astype(jnp.float32), axis=0),
            jnp.sum(d_values_b.astype(jnp.float32), axis=0),
        ]
    )
    d_mixed = jnp.concatenate([d_query_b, d_keys_b, d_values_b], axis=1)
    grad_w_qkv = jnp.einsum(
        "td,tc->dc", rows_all, d_mixed, preferred_element_type=jnp.float32
    ).reshape(model_width, 3, head_span)
    d_normed = lax.psum_scatter(
        jnp.einsum("tc,dc->td", d_mixed, flat_qkv, preferred_element_type=jnp.float32).astype(
            jnp.bfloat16
        ),
        "tp",
        scatter_dimension=0,
        tiled=True,
    ).astype(jnp.float32)
    d_input_part, gain_first, shift_first = back_first(d_normed)
    grad_x = d_hidden + d_input_part
    summed = (
        lax.psum(grad_w_qkv.astype(jnp.bfloat16), "seq").astype(jnp.float32),
        lax.psum(grad_bias_qv.astype(jnp.bfloat16), "seq").astype(jnp.float32),
        lax.psum(grad_w_out.astype(jnp.bfloat16), "seq").astype(jnp.float32),
        lax.psum(grad_w_up.astype(jnp.bfloat16), "seq").astype(jnp.float32),
        lax.psum(grad_bias_up.astype(jnp.bfloat16), "seq").astype(jnp.float32),
        lax.psum(grad_w_down.astype(jnp.bfloat16), "seq").astype(jnp.float32),
    )
    gain_stack = jnp.stack([gain_first, gain_second, gain_third, gain_last])
    shift_stack = jnp.stack([shift_first, shift_second, shift_third, shift_last])
    vectors = lax.psum((gain_stack, shift_stack, grad_bias_out, grad_bias_down), ("seq", "tp"))
    return (
        result,
        grad_x,
        summed[0],
        summed[1],
        summed[2],
        vectors[2],
        summed[3],
        summed[4],
        summed[5],
        vectors[3],
        vectors[0],
        vectors[1],
    )


def solution(mesh):
    placed = (
        P(("seq", "tp"), None),
        P(None, None, "tp"),
        P(None, "tp"),
        P("tp", None),
        P(),
        P(None, "tp"),
        P("tp"),
        P("tp", None),
        P(),
        P(),
        P(),
        P(("seq", "tp"), None),
        P(),
        P(),
        P(),
    )
    seq_count, tp_count = mesh.shape["seq"], mesh.shape["tp"]

    def local(*args):
        tokens_in, w_qkv, placement = args[0], args[1], args[-1]
        heads = w_qkv.shape[2] * tp_count // HEAD
        paired = seq_count * tp_count == 2 * heads == placement.shape[0]
        sizes = (tokens_in.shape[0], w_qkv.shape[0], heads, seq_count, tp_count)
        fast = paired and sizes == (BLK, 1024, 16, 16, 2)
        return (fast_local if fast else general_local)(*args)

    return jax.shard_map(
        local,
        mesh=mesh,
        in_specs=placed,
        out_specs=(
            P(("seq", "tp"), None),
            P(("seq", "tp"), None),
            P(None, None, "tp"),
            P(None, "tp"),
            P("tp", None),
            P(),
            P(None, "tp"),
            P("tp"),
            P("tp", None),
            P(),
            P(),
            P(),
        ),
        check_vma=False,
    )
```

```python
import functools

import jax
import jax.numpy as jnp
from jax import lax
from jax.experimental import pallas as pl
from jax.experimental.pallas import tpu as pltpu
from jax.sharding import PartitionSpec as P

HEAD = 64
BLK = 512
HALF = BLK // 2
QUART = BLK // 4
LONGEST = 4096
STEP_F = 1024
STEP_B = 512
UNROLL = 4
CHUNKS = 9
CHUNKS_LAST = 8
VMEM_LIMIT = 58 << 20

EPS = 1e-05
F32 = jnp.float32
BF16 = jnp.bfloat16
MESH = pl.DeviceIdType.MESH


def layer_norm(row_block, gain_row, shift_row):
    row_mean = jnp.mean(row_block, axis=-1, keepdims=True)
    centred = row_block - row_mean
    spread = jnp.mean(centred * centred, axis=-1, keepdims=True)
    return centred * lax.rsqrt(spread + EPS) * gain_row + shift_row


def smooth_gate(values):
    return jax.nn.gelu(values, approximate=True)


def running_ends(lengths):
    count = lengths.shape[0]
    index = jnp.arange(count, dtype=jnp.int32)
    return jnp.sum(jnp.where(index[None, :] <= index[:, None], lengths[None, :], 0), axis=1)


def inverse_order(placement):
    index = jnp.arange(placement.shape[0], dtype=jnp.int32)
    return jnp.sum(jnp.where(placement[None, :] == index[:, None], index[None, :], 0), axis=1)


def block_tables(lengths, prefixes, placement, part):
    ends = running_ends(lengths)
    starts = ends - lengths
    limits = starts + prefixes
    offset = part * HALF + jnp.arange(HALF, dtype=jnp.int32)
    pos = placement[:, None] * BLK + offset[None, :]
    inside = (pos[:, :, None] >= starts) & (pos[:, :, None] < ends)

    def pick(values):
        return jnp.sum(jnp.where(inside, values, 0), axis=2)

    low = pick(starts)
    high = jnp.minimum(pick(ends), jnp.maximum(pos + 1, pick(limits)))
    table = jnp.stack(
        [
            jnp.min(low, axis=1) // HALF,
            (jnp.max(high, axis=1) - 1) // HALF + 1,
            jnp.max(low, axis=1),
            jnp.min(high, axis=1),
            placement,
        ]
    )
    return low[:, None, :], high[:, None, :], table


def unpack_t(packed):
    turned = packed.astype(F32).T
    return jnp.concatenate([turned[:HEAD], turned[HEAD:]], axis=1)


def pack_t(turned):
    return jnp.concatenate([turned[:, :QUART], turned[:, QUART:]], axis=0).T


def pieces(tab, b, keys, step, start):
    count = keys // HALF
    first = tab[0, b]

    def visit(i, state):
        at = pl.multiple_of((first + i * count) * HALF, HALF)
        whole = (at >= tab[2, b]) & (at + keys <= tab[3, b])
        return lax.cond(whole, lambda st: step(at, st, False), lambda st: step(at, st, True), state)

    return lax.fori_loop(0, (tab[1, b] - first + count - 1) // count, visit, start)


def attend_kernel(
    part_ref, tab, low_ref, high_ref, q_ref, own_ref, sib_ref,
    out_ref, ot_ref, lse_ref, kv, kvt, rhs_s,
):
    part = part_ref[0]
    scale = HEAD**-0.5
    blocks = q_ref.shape[0]
    rows = blocks * BLK
    depth = lax.broadcasted_iota(jnp.int32, (STEP_F, HALF), 0)

    def prepare(b, carry):
        for ref, which in ((own_ref, part), (sib_ref, 1 - part)):
            at = pl.multiple_of(tab[4, b] * BLK + which * HALF, HALF)
            piece = ref[b]
            kv[pl.ds(at, HALF), :] = piece
            kvt[:, pl.ds(at, HALF)] = piece.T
        qt = unpack_t(q_ref[b]) * scale
        rhs_s[b] = jnp.concatenate([qt, jnp.zeros_like(qt)], axis=0).astype(BF16)
        return carry

    lax.fori_loop(0, blocks, prepare, 0, unroll=UNROLL)
    kv[rows:, :] = jnp.zeros((kv.shape[0] - rows, 2 * HEAD), BF16)
    kvt[:, rows:] = jnp.zeros((2 * HEAD, kv.shape[0] - rows), BF16)

    def one(b, carry):
        low, high = low_ref[b], high_ref[b]

        def step(at, state, masked):
            top, total, acc = state
            sc = jnp.dot(kv[pl.ds(at, STEP_F), :], rhs_s[b], preferred_element_type=F32)
            if masked:
                sc = jnp.where((depth >= low - at) & (depth < high - at), sc, -1e30)
            new = jnp.maximum(top, jnp.max(sc, axis=0, keepdims=True))
            alpha = jnp.exp(top - new)
            pr = jnp.exp(sc - new)
            total = total * alpha + jnp.sum(pr, axis=0, keepdims=True)
            acc = acc * alpha + jnp.dot(
                kvt[HEAD:, pl.ds(at, STEP_F)], pr.astype(BF16), preferred_element_type=F32
            )
            return new, total, acc

        start = (
            jnp.full((1, HALF), -1e30, F32),
            jnp.zeros((1, HALF), F32),
            jnp.zeros((HEAD, HALF), F32),
        )
        top, total, acc = pieces(tab, b, STEP_F, step, start)
        ot_ref[b] = acc * (1.0 / total)
        lse_ref[b] = top + jnp.log(total)
        return carry

    lax.fori_loop(0, blocks, one, 0)

    def finish(b, carry):
        out_ref[b] = pack_t(ot_ref[b]).astype(BF16)
        return carry

    lax.fori_loop(0, blocks, finish, 0, unroll=UNROLL)


def attend_back_kernel(
    part_ref, tab, low_ref, high_ref, q_ref, da_ref, ot_ref, lse_ref, kv, kvt,
    dq_ref, mine_ref, theirs_ref, dkv, rhs_s, rows_s, total_s, dqt_s,
):
    part = part_ref[0]
    scale = HEAD**-0.5
    blocks = q_ref.shape[0]
    depth = lax.broadcasted_iota(jnp.int32, (STEP_B, HALF), 0)
    lane = lax.broadcasted_iota(jnp.int32, (HALF, 2 * HEAD), 1)

    def prepare(b, carry):
        dkv[pl.ds(pl.multiple_of(b * BLK, BLK), BLK), :] = jnp.zeros((BLK, 2 * HEAD), F32)
        qt = unpack_t(q_ref[b]) * scale
        dat = unpack_t(da_ref[b])
        blank = jnp.zeros_like(qt)
        rhs_s[b, :, :HALF] = jnp.concatenate([qt, blank], axis=0).astype(BF16)
        rhs_s[b, :, HALF:] = jnp.concatenate([blank, dat], axis=0).astype(BF16)
        both = jnp.concatenate([qt, dat], axis=0).T
        rows_s[b, :HALF, :] = jnp.where(lane < HEAD, both, 0.0).astype(BF16)
        rows_s[b, HALF:, :] = jnp.where(lane < HEAD, 0.0, both).astype(BF16)
        total_s[b] = jnp.sum(dat * ot_ref[b], axis=0, keepdims=True)
        return carry

    lax.fori_loop(0, blocks, prepare, 0, unroll=UNROLL)
    dkv[blocks * BLK :, :] = jnp.zeros((dkv.shape[0] - blocks * BLK, 2 * HEAD), F32)

    def one(b, carry):
        total = total_s[b]
        lse = lse_ref[b]
        low, high = low_ref[b], high_ref[b]

        def step(at, acc, masked):
            keys = kv[pl.ds(at, STEP_B), :]
            sc = jnp.dot(keys, rhs_s[b, :, :HALF], preferred_element_type=F32)
            dp = jnp.dot(keys, rhs_s[b, :, HALF:], preferred_element_type=F32)
            if masked:
                sc = jnp.where((depth >= low - at) & (depth < high - at), sc, -1e30)
            pr = jnp.exp(sc - lse)
            ds = (pr * (dp - total)).astype(BF16)
            dkv[pl.ds(at, STEP_B), :] += jnp.dot(
                ds, rows_s[b, :HALF, :], preferred_element_type=F32
            ) + jnp.dot(pr.astype(BF16), rows_s[b, HALF:, :], preferred_element_type=F32)
            return acc + jnp.dot(kvt[:HEAD, pl.ds(at, STEP_B)], ds, preferred_element_type=F32)

        dqt_s[b] = pieces(tab, b, STEP_B, step, jnp.zeros((HEAD, HALF), F32))
        return carry

    lax.fori_loop(0, blocks, one, 0)

    def finish(b, carry):
        dq_ref[b] = pack_t(dqt_s[b] * scale).astype(BF16)
        base = tab[4, b] * BLK
        mine_ref[b] = dkv[pl.ds(pl.multiple_of(base + part * HALF, HALF), HALF), :]
        theirs_ref[b] = dkv[pl.ds(pl.multiple_of(base + (1 - part) * HALF, HALF), HALF), :].astype(BF16)
        return carry

    lax.fori_loop(0, blocks, finish, 0, unroll=UNROLL)


def vmem(count):
    return [pl.BlockSpec(memory_space=pltpu.VMEM)] * count


def smem(count):
    return [pl.BlockSpec(memory_space=pltpu.SMEM)] * count


def attend(part, tables, q_chunks, kv_own, kv_sib):
    low, high, table = tables
    blocks = q_chunks.shape[0]
    rows = blocks * BLK + STEP_F
    return pl.pallas_call(
        attend_kernel,
        out_shape=(
            jax.ShapeDtypeStruct((blocks, QUART, 2 * HEAD), BF16),
            jax.ShapeDtypeStruct((blocks, HEAD, HALF), F32),
            jax.ShapeDtypeStruct((blocks, 1, HALF), F32),
            jax.ShapeDtypeStruct((rows, 2 * HEAD), BF16),
            jax.ShapeDtypeStruct((2 * HEAD, rows), BF16),
        ),
        in_specs=smem(2) + vmem(5),
        out_specs=tuple(vmem(5)),
        scratch_shapes=[pltpu.VMEM((blocks, 2 * HEAD, HALF), BF16)],
        compiler_params=pltpu.CompilerParams(vmem_limit_bytes=VMEM_LIMIT),
        cost_estimate=pl.CostEstimate(
            flops=40 * 10**9, bytes_accessed=20 << 20, transcendentals=blocks * 4 * BLK * HALF
        ),
        name="attend",
    )(part.reshape(1), table, low, high, q_chunks, kv_own, kv_sib)


def attend_back(part, tables, q_chunks, da_chunks, out_t, mass, kv, kvt):
    low, high, table = tables
    blocks = q_chunks.shape[0]
    return pl.pallas_call(
        attend_back_kernel,
        out_shape=(
            jax.ShapeDtypeStruct((blocks, QUART, 2 * HEAD), BF16),
            jax.ShapeDtypeStruct((blocks, HALF, 2 * HEAD), F32),
            jax.ShapeDtypeStruct((blocks, HALF, 2 * HEAD), BF16),
        ),
        in_specs=smem(2) + vmem(8),
        out_specs=tuple(vmem(3)),
        scratch_shapes=[
            pltpu.VMEM((blocks * BLK + STEP_F, 2 * HEAD), F32),
            pltpu.VMEM((blocks, 2 * HEAD, BLK), BF16),
            pltpu.VMEM((blocks, BLK, 2 * HEAD), BF16),
            pltpu.VMEM((blocks, 1, HALF), F32),
            pltpu.VMEM((blocks, HEAD, HALF), F32),
        ],
        compiler_params=pltpu.CompilerParams(vmem_limit_bytes=VMEM_LIMIT),
        cost_estimate=pl.CostEstimate(
            flops=60 * 10**9, bytes_accessed=30 << 20, transcendentals=blocks * 4 * BLK * HALF
        ),
        name="attend_back",
    )(part.reshape(1), table, low, high, q_chunks, da_chunks, out_t, mass, kv, kvt)


def chunk_of(who, quarter, index, half):
    absolute = (who[0] * 2 + who[1]) ^ quarter
    tp, sub = absolute // 2, absolute % 2
    return ((sub * 4 + index) * 2 + half) * 2 + tp


def swap_lanes(values):
    return pltpu.roll(values, HEAD, 1)


def low_lanes(rows):
    return lax.broadcasted_iota(jnp.int32, (rows, 2 * HEAD), 1) < HEAD


def store_packed(who, quarter, values, out_ref):
    low = low_lanes(QUART)
    for pair in range(2):
        for half in range(2):
            top = half * HALF
            lanes = slice(pair * 128, pair * 128 + 128)
            first, second = values[top : top + QUART, lanes], values[top + QUART : top + HALF, lanes]
            even = jnp.where(low, first, swap_lanes(second))
            odd = jnp.where(low, swap_lanes(first), second)
            out_ref[chunk_of(who, quarter, 2 * pair, half)] = even.astype(BF16)
            out_ref[chunk_of(who, quarter, 2 * pair + 1, half)] = odd.astype(BF16)


def load_packed(who, quarter, ref, out_ref):
    low = low_lanes(QUART)
    for pair in range(2):
        for half in range(2):
            even = ref[chunk_of(who, quarter, 2 * pair, half)].astype(F32)
            odd = ref[chunk_of(who, quarter, 2 * pair + 1, half)].astype(F32)
            top = half * HALF
            lanes = slice(quarter * 256 + pair * 128, quarter * 256 + pair * 128 + 128)
            out_ref[top : top + QUART, lanes] = jnp.where(low, even, swap_lanes(odd)).astype(BF16)
            out_ref[top + QUART : top + HALF, lanes] = jnp.where(low, swap_lanes(even), odd).astype(BF16)


def project_kernel(who_ref, x_ref, gain_ref, shift_ref, bias_ref, w0, w1, w2, w3, normed_ref, q_ref, kv_ref):
    who = (who_ref[0], who_ref[1])
    normed = layer_norm(x_ref[...].astype(F32), gain_ref[...], shift_ref[...]).astype(BF16)
    normed_ref[...] = normed
    low = low_lanes(HALF)
    for quarter, w in enumerate((w0, w1, w2, w3)):
        def dot(col):
            return jnp.dot(normed, w[:, col : col + 256], preferred_element_type=F32)

        bias = bias_ref[quarter : quarter + 1, :].astype(F32)
        store_packed(who, quarter, dot(0) + bias[:, :256], q_ref)
        keys = dot(256)
        values = dot(512) + bias[:, 256:]
        for pair in range(2):
            lanes = slice(pair * 128, pair * 128 + 128)
            for half in range(2):
                rows = slice(half * HALF, half * HALF + HALF)
                k, v = keys[rows, lanes], values[rows, lanes]
                even = jnp.where(low, k, swap_lanes(v))
                odd = jnp.where(low, swap_lanes(k), v)
                kv_ref[chunk_of(who, quarter, 2 * pair, half)] = even.astype(BF16)
                kv_ref[chunk_of(who, quarter, 2 * pair + 1, half)] = odd.astype(BF16)


def project(who, x, gain, shift, bias, weights):
    rows, width = x.shape
    return pl.pallas_call(
        project_kernel,
        out_shape=(
            jax.ShapeDtypeStruct((rows, width), BF16),
            jax.ShapeDtypeStruct((32, QUART, 2 * HEAD), BF16),
            jax.ShapeDtypeStruct((32, HALF, 2 * HEAD), BF16),
        ),
        in_specs=smem(1) + vmem(8),
        out_specs=tuple(vmem(3)),
        compiler_params=pltpu.CompilerParams(vmem_limit_bytes=VMEM_LIMIT),
        name="project",
    )(who, x, gain, shift, bias, *weights)


def unpack_heads_kernel(who_ref, ref, out_ref):
    who = (who_ref[0], who_ref[1])
    for quarter in range(4):
        load_packed(who, quarter, ref, out_ref)


def unpack_heads(who, chunks):
    return pl.pallas_call(
        unpack_heads_kernel,
        out_shape=jax.ShapeDtypeStruct((BLK, 1024), BF16),
        in_specs=smem(1) + vmem(1),
        out_specs=vmem(1)[0],
        compiler_params=pltpu.CompilerParams(vmem_limit_bytes=VMEM_LIMIT),
        name="unpack_heads",
    )(who, chunks)


def spread_kernel(who_ref, d_ref, w0, w1, w2, w3, out_ref):
    who = (who_ref[0], who_ref[1])
    d_rows = d_ref[...]
    for quarter, w in enumerate((w0, w1, w2, w3)):
        values = lax.dot_general(
            d_rows, w[...], (((1,), (1,)), ((), ())), preferred_element_type=F32
        )
        store_packed(who, quarter, values, out_ref)


def spread(who, d_branch, weights):
    return pl.pallas_call(
        spread_kernel,
        out_shape=jax.ShapeDtypeStruct((32, QUART, 2 * HEAD), BF16),
        in_specs=smem(1) + vmem(5),
        out_specs=vmem(1)[0],
        compiler_params=pltpu.CompilerParams(vmem_limit_bytes=VMEM_LIMIT),
        name="spread",
    )(who, d_branch, *weights)


def unpack_qkv_kernel(who_ref, dq_ref, dkv_ref, q_ref, k_ref, v_ref):
    who = (who_ref[0], who_ref[1])
    low = low_lanes(HALF)
    for quarter in range(4):
        load_packed(who, quarter, dq_ref, q_ref)
        for pair in range(2):
            lanes = slice(quarter * 256 + pair * 128, quarter * 256 + pair * 128 + 128)
            for half in range(2):
                rows = slice(half * HALF, half * HALF + HALF)
                even = dkv_ref[chunk_of(who, quarter, 2 * pair, half)].astype(F32)
                odd = dkv_ref[chunk_of(who, quarter, 2 * pair + 1, half)].astype(F32)
                k_ref[rows, lanes] = jnp.where(low, even, swap_lanes(odd)).astype(BF16)
                v_ref[rows, lanes] = jnp.where(low, swap_lanes(even), odd).astype(BF16)


def unpack_qkv(who, dq_chunks, dkv_chunks):
    shape = jax.ShapeDtypeStruct((BLK, 1024), BF16)
    return pl.pallas_call(
        unpack_qkv_kernel,
        out_shape=(shape, shape, shape),
        in_specs=smem(1) + vmem(2),
        out_specs=tuple(vmem(3)),
        compiler_params=pltpu.CompilerParams(vmem_limit_bytes=VMEM_LIMIT),
        name="unpack_qkv",
    )(who, dq_chunks, dkv_chunks)


def sum_all_kernel(seq_bits, mine_ref, out_ref, slots, send, recv):
    seq, tp = lax.axis_index("seq"), lax.axis_index("tp")
    partners = [(seq ^ (1 << bit), tp) for bit in range(seq_bits)]
    partners.insert(1, (seq, tp ^ 1))
    barrier = pltpu.get_barrier_semaphore()
    for partner in partners:
        pl.semaphore_signal(barrier, inc=1, device_id=partner, device_id_type=MESH)
    pl.semaphore_wait(barrier, len(partners))
    out_ref[...] = mine_ref[...]
    for step, partner in enumerate(partners):
        slots[step] = out_ref[...]
        copy = pltpu.make_async_remote_copy(
            src_ref=slots.at[step],
            dst_ref=slots.at[len(partners) + step],
            send_sem=send.at[step],
            recv_sem=recv.at[step],
            device_id=partner,
            device_id_type=MESH,
        )
        copy.start()
        copy.wait()
        out_ref[...] += slots[len(partners) + step]


def sum_all(values, seq_count):
    seq_bits = seq_count.bit_length() - 1
    steps = seq_bits + 1
    return pl.pallas_call(
        functools.partial(sum_all_kernel, seq_bits),
        out_shape=jax.ShapeDtypeStruct(values.shape, values.dtype),
        in_specs=vmem(1),
        out_specs=vmem(1)[0],
        scratch_shapes=[
            pltpu.VMEM((2 * steps,) + values.shape, values.dtype),
            pltpu.SemaphoreType.DMA((steps,)),
            pltpu.SemaphoreType.DMA((steps,)),
        ],
        compiler_params=pltpu.CompilerParams(collective_id=7, has_side_effects=True),
        name="sum_all",
    )(values)


class Place:
    def __init__(self):
        self.seq, self.tp = lax.axis_index("seq"), lax.axis_index("tp")
        self.x = lax.rem(self.seq // 2, 2)
        self.z = self.seq // 4
        self.core_partner = (self.seq ^ 1, self.tp)
        self.x_partner = (self.seq ^ 2, self.tp)
        self.z_partners = [(self.seq ^ (4 * d), self.tp) for d in (1, 2, 3)]
        self.tp_partner = (self.seq, self.tp ^ 1)


def greet_all(count, me, seq, tp):
    barrier = pltpu.get_barrier_semaphore()

    def one(k, carry):
        other = lax.rem(me + k, count)
        pl.semaphore_signal(
            barrier, inc=1, device_id=(other // 2, lax.rem(other, 2)), device_id_type=MESH
        )
        return carry

    lax.fori_loop(1, count, one, 0)
    pl.semaphore_wait(barrier, count - 1)


def greet(partners):
    barrier = pltpu.get_barrier_semaphore()
    for partner in partners:
        pl.semaphore_signal(barrier, inc=1, device_id=partner, device_id_type=MESH)
    pl.semaphore_wait(barrier, len(partners))


def remote(src, dst, send, recv, device):
    return pltpu.make_async_remote_copy(
        src_ref=src, dst_ref=dst, send_sem=send, recv_sem=recv, device_id=device, device_id_type=MESH
    )


def chunk_copy(count, me, k, src, dst, send, recv):
    other = lax.rem(me + k, count)
    return remote(src.at[other], dst.at[me], send.at[k], recv.at[k], (other // 2, lax.rem(other, 2)))


def reduce_ticks(place, chunks, near, far, out, xbuf, xsum, zbuf, ybuf, ysum, sems):
    rows = near.shape[0] // chunks
    half, piece = rows // 2, rows // 8
    x, z = place.x, place.z

    def at(start, size):
        return pl.ds(pl.multiple_of(start, size), size)

    def tp_copy(k):
        return remote(
            far.at[at(k * rows, rows)], ybuf.at[at(k * rows, rows)],
            sems["ys"].at[k], sems["yr"].at[k], place.tp_partner,
        )

    def x_copy(k):
        src = ysum if far is not None else near
        return remote(
            src.at[at(k * rows + (1 - x) * half, half)], xbuf.at[at(k * half, half)],
            sems["xs"].at[k], sems["xr"].at[k], place.x_partner,
        )

    def z_copy(k, d):
        return remote(
            xsum.at[at(k * half + (z ^ d) * piece, piece)], zbuf.at[d - 1, at(k * piece, piece)],
            sems["zs"].at[d - 1, k], sems["zr"].at[d - 1, k], place.z_partners[d - 1],
        )

    def own_piece(k):
        return at(k * rows + x * half + z * piece, piece)

    def zg_copy(k, d):
        return remote(
            out.at[0, own_piece(k)], out.at[0, own_piece(k)],
            sems["zgs"].at[d - 1, k], sems["zgr"].at[d - 1, k], place.z_partners[d - 1],
        )

    def xg_copy(k):
        span = at(k * rows + x * half, half)
        return remote(
            out.at[0, span], out.at[0, span], sems["xgs"].at[k], sems["xgr"].at[k], place.x_partner
        )

    def core_copy(k):
        span = at(k * rows, rows)
        return remote(
            out.at[0, span], out.at[1, span], sems["cs"].at[k], sems["cr"].at[k], place.core_partner
        )

    def stage_tp(k):
        tp_copy(k).start()

    def stage_x(k):
        if far is not None:
            tp_copy(k).wait_recv()
            span = at(k * rows, rows)
            ysum[span, :] = (near[span, :].astype(F32) + ybuf[span, :].astype(F32)).astype(BF16)
        x_copy(k).start()

    def stage_z(k):
        x_copy(k).wait_recv()
        src = ysum if far is not None else near
        mine = src[at(k * rows + x * half, half), :].astype(F32)
        xsum[at(k * half, half), :] = (mine + xbuf[at(k * half, half), :].astype(F32)).astype(BF16)
        for d in (3, 2, 1):
            z_copy(k, d).start()

    def stage_zg(k):
        total = xsum[at(k * half + z * piece, piece), :].astype(F32)
        for d in (1, 2, 3):
            z_copy(k, d).wait_recv()
            total = total + zbuf[d - 1, at(k * piece, piece), :].astype(F32)
        out[0, own_piece(k), :] = total.astype(BF16)
        for d in (3, 2, 1):
            zg_copy(k, d).start()

    def stage_xg(k):
        for d in (1, 2, 3):
            zg_copy(k, d).wait_recv()
        xg_copy(k).start()

    def stage_core(k):
        xg_copy(k).wait_recv()
        core_copy(k).start()

    stages = [stage_x, stage_z, stage_zg, stage_xg, stage_core]
    if far is not None:
        stages.insert(0, stage_tp)

    def tick(t, carry):
        for s, stage in reversed(list(enumerate(stages))):
            @pl.when((t >= s) & (t - s < chunks))
            def _():
                stage(t - s)
        return carry

    lax.fori_loop(0, chunks + len(stages) - 1, tick, 0)

    def drain(k, carry):
        if far is not None:
            tp_copy(k).wait_send()
        x_copy(k).wait_send()
        for d in (1, 2, 3):
            z_copy(k, d).wait_send()
            zg_copy(k, d).wait_send()
        xg_copy(k).wait_send()
        core_copy(k).wait()
        return carry

    lax.fori_loop(0, chunks, drain, 0)


SEM_NAMES = ("xs", "xr", "zs", "zr", "zgs", "zgr", "xgs", "xgr", "cs", "cr", "ys", "yr")


def reduce_scratch(rows, cols, chunks, with_tp):
    spaces = [
        pltpu.VMEM((rows // 2, cols), BF16),
        pltpu.VMEM((rows // 2, cols), BF16),
        pltpu.VMEM((3, rows // 8, cols), BF16),
    ]
    if with_tp:
        spaces += [pltpu.VMEM((rows, cols), BF16)] * 2
    names = SEM_NAMES if with_tp else SEM_NAMES[:-2]
    for name in names:
        spaces.append(pltpu.SemaphoreType.DMA((3, chunks) if name[0] == "z" else (chunks,)))
    return spaces


def send_back_kernel(chunks, dq_ref, dkv_ref, near, dq_out, dkv_out, out, xbuf, xsum, zbuf, *rest):
    place = Place()
    count = dq_ref.shape[0]
    me = place.seq * 2 + place.tp
    names = SEM_NAMES[:-2]
    sems = dict(zip(names, rest))
    qs, qr, ks, kr = rest[len(names) :]
    greet_all(count, me, place.seq, place.tp)

    def start(k, carry):
        chunk_copy(count, me, k, dkv_ref, dkv_out, ks, kr).start()
        chunk_copy(count, me, k, dq_ref, dq_out, qs, qr).start()
        return carry

    lax.fori_loop(1, count, start, 0)
    dq_out[me] = dq_ref[me]
    dkv_out[me] = dkv_ref[me]
    reduce_ticks(place, chunks, near, None, out, xbuf, xsum, zbuf, None, None, sems)

    def wait(k, carry):
        chunk_copy(count, me, k, dkv_ref, dkv_out, ks, kr).wait()
        chunk_copy(count, me, k, dq_ref, dq_out, qs, qr).wait()
        return carry

    lax.fori_loop(1, count, wait, 0)


def send_back(dq_chunks, dkv_chunks, near, chunks):
    rows, cols = near.shape
    count = dq_chunks.shape[0]
    return pl.pallas_call(
        functools.partial(send_back_kernel, chunks),
        out_shape=(
            jax.ShapeDtypeStruct(dq_chunks.shape, BF16),
            jax.ShapeDtypeStruct(dkv_chunks.shape, BF16),
            jax.ShapeDtypeStruct((2, rows, cols), BF16),
        ),
        in_specs=vmem(3),
        out_specs=tuple(vmem(3)),
        scratch_shapes=reduce_scratch(rows, cols, chunks, False)
        + [pltpu.SemaphoreType.DMA((count,))] * 4,
        compiler_params=pltpu.CompilerParams(
            collective_id=1, has_side_effects=True, vmem_limit_bytes=VMEM_LIMIT
        ),
        name="send_back",
    )(dq_chunks, dkv_chunks, near)


def reduce_last_kernel(chunks, near, far, out, xbuf, xsum, zbuf, ybuf, ysum, *rest):
    place = Place()
    greet([place.tp_partner, place.x_partner, place.core_partner] + place.z_partners)
    reduce_ticks(place, chunks, near, far, out, xbuf, xsum, zbuf, ybuf, ysum, dict(zip(SEM_NAMES, rest)))


def reduce_last(near, far, chunks):
    rows, cols = near.shape
    return pl.pallas_call(
        functools.partial(reduce_last_kernel, chunks),
        out_shape=jax.ShapeDtypeStruct((2, rows, cols), BF16),
        in_specs=vmem(2),
        out_specs=vmem(1)[0],
        scratch_shapes=reduce_scratch(rows, cols, chunks, True),
        compiler_params=pltpu.CompilerParams(
            collective_id=2, has_side_effects=True, vmem_limit_bytes=VMEM_LIMIT
        ),
        name="reduce_last",
    )(near, far)


def norm_parts(values):
    mean = jnp.mean(values, axis=-1, keepdims=True)
    centred = values - mean
    rstd = lax.rsqrt(jnp.mean(centred * centred, axis=-1, keepdims=True) + EPS)
    return centred * rstd, rstd


def norm_back(values, gain, upstream):
    xhat, rstd = norm_parts(values)
    e = upstream * gain
    grad = rstd * (
        e
        - jnp.mean(e, axis=-1, keepdims=True)
        - xhat * jnp.mean(e * xhat, axis=-1, keepdims=True)
    )
    return grad, jnp.sum(upstream * xhat, axis=0), jnp.sum(upstream, axis=0)


def fast_local(
    tokens_in, w_qkv, bias_qv, w_out, bias_out, w_up, bias_up, w_down, bias_down,
    norm_gains, norm_shifts, out_grad, lengths, prefixes, placement,
):
    seq_count = lax.axis_size("seq")
    seq, tp = lax.axis_index("seq"), lax.axis_index("tp")
    core = seq % 2
    who = jnp.stack([tp, core]).astype(jnp.int32)
    over_tp = [(0, 1), (1, 0)]
    over_core = [(i, i ^ 1) for i in range(seq_count)]

    def to_tp(values):
        return lax.ppermute(values, "tp", over_tp)

    def to_sib(values):
        return lax.ppermute(values, "seq", over_core)

    def exchange(chunks):
        return lax.all_to_all(chunks, ("seq", "tp"), 0, 0, tiled=True)

    def quarters(values, axis):
        size = values.shape[axis] // 2
        own = lax.dynamic_slice_in_dim(values, core * size, size, axis)
        sib = lax.dynamic_slice_in_dim(values, (1 - core) * size, size, axis)
        far = to_tp(own)
        return [own, sib, far, to_sib(far)]

    width = w_qkv.shape[0]
    wq4 = [w.reshape(width, -1) for w in quarters(w_qkv, 2)]
    small = jnp.concatenate([bias_qv.reshape(2, 2, -1), bias_up.reshape(2, 2, -1).transpose(1, 0, 2)], axis=2)
    small = small.transpose(1, 0, 2)
    small4 = [s.reshape(2, -1) for s in quarters(small, 0)]
    split = bias_qv.shape[1] // 2
    bias_qv4 = jnp.stack([s[:, :split].reshape(-1) for s in small4])
    bias_up4 = [s[:, split:].reshape(-1).astype(F32) for s in small4]
    wo4 = quarters(w_out, 0)
    wu4 = quarters(w_up, 1)
    wd4 = quarters(w_down, 0)

    tables = block_tables(lengths, prefixes, placement, core)
    normed, q_chunks, kv_chunks = project(
        who, tokens_in, norm_gains[:1], norm_shifts[:1], bias_qv4, wq4
    )
    kv_own = exchange(kv_chunks)
    kv_sib = to_sib(kv_own)
    q_own = exchange(q_chunks)
    att_chunks, out_t, mass, kv_pack, kv_turned = attend(core, tables, q_own, kv_own, kv_sib)
    attended = unpack_heads(who, exchange(att_chunks))

    input_f32 = tokens_in.astype(F32)

    def cols(values, quarter, count):
        return values[:, quarter * count : (quarter + 1) * count]

    def dot(a, b):
        return jnp.dot(a, b, preferred_element_type=F32)

    def dot_t(a, b):
        return lax.dot_general(a, b, (((1,), (1,)), ((), ())), preferred_element_type=F32)

    def dot_rows(a, b):
        return lax.dot_general(a, b, (((0,), (0,)), ((), ())), preferred_element_type=F32)

    heads4 = [cols(attended, r, 256) for r in range(4)]
    branch = sum(dot(heads4[r], wo4[r]) for r in range(4)) + bias_out.astype(F32)
    hidden = input_f32 + layer_norm(branch, norm_gains[1], norm_shifts[1])
    inner = layer_norm(hidden, norm_gains[2], norm_shifts[2]).astype(BF16)
    active4, gate4 = [], []
    for r in range(4):
        act, back_gate = jax.vjp(smooth_gate, dot(inner, wu4[r]) + bias_up4[r])
        active4.append(act.astype(BF16))
        gate4.append(back_gate)
    down = sum(dot(active4[r], wd4[r]) for r in range(4)) + bias_down.astype(F32)
    result = (hidden + layer_norm(down, norm_gains[3], norm_shifts[3])).astype(BF16)
    d_down, gain_last, shift_last = norm_back(down, norm_gains[3], out_grad)
    bias_down_part = jnp.sum(d_down, axis=0)
    d_down_b = d_down.astype(BF16)
    inner_sib, down_sib = to_sib(inner), to_sib(d_down_b)
    active_sib = [to_sib(active4[r]) for r in (1, 3)]

    def tie(values, *others):
        return lax.optimization_barrier((values,) + others)[0]

    def reduced(near, far):
        return (near + to_tp(far).astype(F32)).astype(BF16)

    d_up4 = [gate4[r](dot_t(d_down_b, wd4[r]))[0].astype(BF16) for r in range(4)]
    up_sib = [to_sib(d_up4[r]) for r in (1, 3)]
    near_down, far_down = (
        dot_rows(active4[r], d_down_b) + dot_rows(s, down_sib) for r, s in zip((0, 2), active_sib)
    )
    far_down = far_down.astype(BF16)
    d_up4 = tie(d_up4, far_down)
    bias_up_part = [jnp.sum(d.astype(F32), axis=0) for d in d_up4]
    d_inner = sum(dot_t(d_up4[r], wu4[r]) for r in range(4))
    d_third, gain_third, shift_third = norm_back(hidden, norm_gains[2], d_inner)
    d_hidden = out_grad + d_third
    d_branch, gain_second, shift_second = norm_back(branch, norm_gains[1], d_hidden)
    bias_out_part = jnp.sum(d_branch, axis=0)
    d_branch_b = d_branch.astype(BF16)
    branch_sib, normed_sib = to_sib(d_branch_b), to_sib(normed)
    heads_sib = [to_sib(heads4[r]) for r in (1, 3)]
    da_own = exchange(spread(who, d_branch_b, wo4))
    near_up, far_up = (
        dot_rows(inner, d_up4[r]) + dot_rows(inner_sib, s) for r, s in zip((0, 2), up_sib)
    )
    near_out, far_out = (
        dot_rows(heads4[r], d_branch_b) + dot_rows(s, branch_sib)
        for r, s in zip((0, 2), heads_sib)
    )
    far_up, far_out = far_up.astype(BF16), far_out.astype(BF16)
    g_down = reduced(near_down, far_down)
    da_own = tie(da_own, far_up, far_out, g_down)
    dq_chunks, dkv_mine, dkv_theirs = attend_back(
        core, tables, q_own, da_own, out_t, mass, kv_pack, kv_turned
    )
    dkv_chunks = (dkv_mine + to_sib(dkv_theirs).astype(F32)).astype(BF16)
    near_all = jnp.concatenate([g_down, reduced(near_up, far_up), reduced(near_out, far_out)])
    dq_home, dkv_home, sums = send_back(dq_chunks, dkv_chunks, near_all, CHUNKS)
    d_q, d_k, d_v = unpack_qkv(who, dq_home, dkv_home)

    mixed4 = [
        jnp.concatenate([cols(d, r, 256) for d in (d_q, d_k, d_v)], axis=1) for r in range(4)
    ]
    mixed_sib = [to_sib(mixed4[r]) for r in (1, 3)]
    near_qkv, far_qkv = (
        dot_rows(normed, mixed4[r]) + dot_rows(normed_sib, s) for r, s in zip((0, 2), mixed_sib)
    )
    far_qkv = far_qkv.astype(BF16)
    mixed4 = tie(mixed4, far_qkv)
    d_normed = sum(dot_t(mixed4[r], wq4[r]) for r in range(4))
    d_first, gain_first, shift_first = norm_back(input_f32, norm_gains[0], d_normed)
    grad_x = d_hidden + d_first

    def joined(pair, axis):
        own, sib = pair
        first = jnp.concatenate([own, sib], axis=axis).astype(F32)
        second = jnp.concatenate([sib, own], axis=axis).astype(F32)
        return jnp.where(core == 0, first, second)

    def absolute(parts):
        base = tp * 2 + core
        return jnp.concatenate(
            [sum(jnp.where((base ^ r) == a, parts[r], 0.0) for r in range(4)) for a in range(4)]
        )

    bias_q_part = [jnp.sum(cols(d_q, r, 256).astype(F32), axis=0) for r in range(4)]
    bias_v_part = [jnp.sum(cols(d_v, r, 256).astype(F32), axis=0) for r in range(4)]
    vectors = jnp.stack(
        [gain_first, gain_second, gain_third, gain_last]
        + [shift_first, shift_second, shift_third, shift_last]
        + [bias_out_part, bias_down_part, absolute(bias_q_part), absolute(bias_v_part)]
    )
    vectors = jnp.concatenate([vectors, absolute(bias_up_part).reshape(4, -1)])
    vectors = sum_all(vectors, seq_count)
    near_qkv, vectors = tie((near_qkv.astype(BF16), vectors), vectors)
    sums_qkv = reduce_last(near_qkv, far_qkv, CHUNKS_LAST).reshape(2, width, 3, -1)
    hidden_rows = g_down.shape[0]
    up_rows = slice(hidden_rows, hidden_rows + width)
    out_rows = slice(hidden_rows + width, None)
    own_cols = bias_qv.shape[1]
    grad_bias_qv = lax.dynamic_slice_in_dim(vectors[10:12], tp * own_cols, own_cols, 1)
    grad_bias_up = lax.dynamic_slice_in_dim(
        vectors[12:16].reshape(-1), tp * bias_up.shape[0], bias_up.shape[0]
    )
    return (
        result,
        grad_x,
        joined(sums_qkv, 2),
        grad_bias_qv,
        joined(sums[:, out_rows], 0),
        vectors[8],
        joined(sums[:, up_rows], 1),
        grad_bias_up,
        joined(sums[:, :hidden_rows], 0),
        vectors[9],
        vectors[0:4],
        vectors[4:8],
    )


def pack_tables(lengths, prefixes, row_total):
    where_row = jnp.arange(row_total, dtype=jnp.int32)
    doc_ends = running_ends(lengths)
    document = jnp.sum((where_row[:, None] >= doc_ends[None, :]).astype(jnp.int32), axis=1)
    limits = doc_ends - lengths + prefixes
    doc_pick = document[:, None] == jnp.arange(lengths.shape[0], dtype=jnp.int32)[None, :]
    visible = jnp.sum(jnp.where(doc_pick, limits[None, :], 0), axis=1)
    return (document, visible)


def padded_tables(document, visible, margin):
    row_total = document.shape[0]
    border = jnp.full((margin,), -1, jnp.int32)
    doc_pad = jnp.concatenate([border, document, border])
    pos_pad = jnp.arange(-margin, row_total + margin, dtype=jnp.int32)
    blank = jnp.zeros((margin,), jnp.int32)
    seen_pad = jnp.concatenate([blank, visible, blank])
    return (doc_pad, pos_pad, seen_pad)


def allowed_pairs(query_pos, query_doc, key_pos, key_doc, key_seen):
    return (query_doc[:, None] == key_doc[None, :]) & (
        (key_pos[None, :] <= query_pos[:, None]) | (key_pos[None, :] < key_seen[None, :])
    )


def pick_blocks(blocks, order):
    return lax.map(lambda i: lax.dynamic_index_in_dim(blocks, i, 0, False), order)


def to_pack(stored, pack_order, margin, block_size):
    blocks = stored.reshape((pack_order.shape[0], block_size) + stored.shape[1:])
    ordered = pick_blocks(blocks, pack_order).reshape(stored.shape)
    widths = [(margin, margin)] + [(0, 0)] * (stored.ndim - 1)
    return jnp.pad(ordered, widths)


def from_pack(padded, placement, margin, block_size, row_total):
    core = padded[margin : margin + row_total]
    blocks = core.reshape((placement.shape[0], block_size) + core.shape[1:])
    return pick_blocks(blocks, placement).reshape(core.shape)


def masked_scores(query_h, key_h, allowed):
    scores = query_h.shape[-1] ** (-0.5) * jnp.einsum(
        "qe,ke->qk", query_h, key_h, preferred_element_type=jnp.float32
    )
    return jnp.where(allowed, scores, -jnp.inf)


def forward_block(query_block, key_win, value_win, allowed):

    def forward_one_head(head):
        query_h = lax.dynamic_index_in_dim(query_block, head, 1, False)
        key_h = lax.dynamic_index_in_dim(key_win, head, 1, False)
        value_h = lax.dynamic_index_in_dim(value_win, head, 1, False)
        masked = masked_scores(query_h, key_h, allowed)
        row_top = jnp.max(masked, axis=1, keepdims=True)
        expo = jnp.exp(masked - row_top)
        row_sum = jnp.sum(expo, axis=1, keepdims=True)
        probs_b = (expo / row_sum).astype(jnp.bfloat16)
        output = jnp.dot(probs_b, value_h, preferred_element_type=jnp.float32)
        return (output, (row_top + jnp.log(row_sum))[:, 0])

    return lax.map(forward_one_head, jnp.arange(query_block.shape[1], dtype=jnp.int32))


def attention_grads(
    query_block, d_att_block, mass_block, total_block, key_block, value_block, allowed
):
    score_scale = query_block.shape[-1] ** (-0.5)

    def attention_one_head(head):
        query_h = lax.dynamic_index_in_dim(query_block, head, 1, False)
        d_att_h = lax.dynamic_index_in_dim(d_att_block, head, 1, False)
        key_h = lax.dynamic_index_in_dim(key_block, head, 1, False)
        value_h = lax.dynamic_index_in_dim(value_block, head, 1, False)
        mass_h = lax.dynamic_index_in_dim(mass_block, head, 0, False)
        total_h = lax.dynamic_index_in_dim(total_block, head, 0, False)
        masked = masked_scores(query_h, key_h, allowed)
        probs = jnp.exp(masked - mass_h[:, None])
        d_probs = jnp.einsum("qe,ke->qk", d_att_h, value_h, preferred_element_type=jnp.float32)
        d_scores = (probs * (d_probs - total_h[:, None])).astype(jnp.bfloat16)
        results = []
        results.append(
            score_scale
            * jnp.einsum("qk,ke->qe", d_scores, key_h, preferred_element_type=jnp.float32)
        )
        results.append(
            score_scale
            * jnp.einsum("qk,qe->ke", d_scores, query_h, preferred_element_type=jnp.float32)
        )
        results.append(
            jnp.einsum(
                "qk,qe->ke", probs.astype(jnp.bfloat16), d_att_h, preferred_element_type=jnp.float32
            )
        )
        return tuple(results)

    return lax.map(attention_one_head, jnp.arange(query_block.shape[1], dtype=jnp.int32))


def general_local(
    tokens_in,
    w_qkv,
    bias_qv,
    w_out,
    bias_out,
    w_up,
    bias_up,
    w_down,
    bias_down,
    norm_gains,
    norm_shifts,
    out_grad,
    lengths,
    prefixes,
    placement,
):
    seq_count = lax.axis_size("seq")
    block_total = placement.shape[0]
    blocks_here = block_total // seq_count
    total_rows = block_total * BLK
    own_rows = blocks_here * BLK
    model_width = w_qkv.shape[0]
    head_span = w_qkv.shape[2]
    heads_here = head_span // HEAD
    margin = LONGEST + BLK
    window = LONGEST + 2 * BLK
    document, visible = pack_tables(lengths, prefixes, total_rows)
    doc_pad, pos_pad, seen_pad = padded_tables(document, visible, margin)
    own_blocks = lax.dynamic_slice_in_dim(
        placement, lax.axis_index("seq") * blocks_here, blocks_here
    )
    pack_order = inverse_order(placement)
    offsets = jnp.arange(BLK, dtype=jnp.int32)

    def query_window(index):
        first = own_blocks[index] * BLK
        key_first = margin + first - LONGEST
        allowed = allowed_pairs(
            first + offsets,
            lax.dynamic_slice_in_dim(document, first, BLK),
            lax.dynamic_slice_in_dim(pos_pad, key_first, window),
            lax.dynamic_slice_in_dim(doc_pad, key_first, window),
            lax.dynamic_slice_in_dim(seen_pad, key_first, window),
        )
        return (key_first, allowed)

    input_f32 = tokens_in.astype(jnp.float32)
    normed, back_first = jax.vjp(layer_norm, input_f32, norm_gains[0], norm_shifts[0])
    rows_all = lax.all_gather(normed.astype(jnp.bfloat16), "tp", axis=0, tiled=True)
    flat_qkv = w_qkv.reshape(model_width, 3 * head_span)
    mixed = jnp.dot(rows_all, flat_qkv, preferred_element_type=jnp.float32).reshape(
        own_rows, 3, head_span
    )
    query_b = (mixed[:, 0] + bias_qv[0].astype(jnp.float32)).astype(jnp.bfloat16)
    key_b = mixed[:, 1].astype(jnp.bfloat16)
    value_b = (mixed[:, 2] + bias_qv[1].astype(jnp.float32)).astype(jnp.bfloat16)
    keys_all, values_all = (
        lax.all_gather(key_b, "seq", axis=0, tiled=True),
        lax.all_gather(value_b, "seq", axis=0, tiled=True),
    )
    keys_pad = to_pack(keys_all, pack_order, margin, BLK).reshape(-1, heads_here, HEAD)
    values_pad = to_pack(values_all, pack_order, margin, BLK).reshape(-1, heads_here, HEAD)
    head_shape = (own_rows, heads_here, HEAD)
    query3 = query_b.reshape(head_shape)
    attended_list = []
    mass_list = []
    for index in range(blocks_here):
        key_first, allowed = query_window(index)
        outputs, masses = forward_block(
            query3[index * BLK : (index + 1) * BLK],
            lax.dynamic_slice_in_dim(keys_pad, key_first, window),
            lax.dynamic_slice_in_dim(values_pad, key_first, window),
            allowed,
        )
        attended_list.append(jnp.transpose(outputs, (1, 0, 2)))
        mass_list.append(masses)
    attended32 = jnp.concatenate(attended_list, axis=0)
    log_mass = jnp.concatenate(mass_list, axis=1)
    attended_b = attended32.reshape(own_rows, head_span).astype(jnp.bfloat16)
    branch = lax.psum_scatter(
        jnp.dot(attended_b, w_out, preferred_element_type=jnp.float32).astype(jnp.bfloat16),
        "tp",
        scatter_dimension=0,
        tiled=True,
    ).astype(jnp.float32) + bias_out.astype(jnp.float32)
    post_attn, back_post = jax.vjp(layer_norm, branch, norm_gains[1], norm_shifts[1])
    hidden = input_f32 + post_attn
    inner, back_inner = jax.vjp(layer_norm, hidden, norm_gains[2], norm_shifts[2])
    inner_all = lax.all_gather(inner.astype(jnp.bfloat16), "tp", axis=0, tiled=True)
    upward = jnp.dot(inner_all, w_up, preferred_element_type=jnp.float32) + bias_up.astype(
        jnp.float32
    )
    active, back_gate = jax.vjp(smooth_gate, upward)
    active_b = active.astype(jnp.bfloat16)
    down = lax.psum_scatter(
        jnp.dot(active_b, w_down, preferred_element_type=jnp.float32).astype(jnp.bfloat16),
        "tp",
        scatter_dimension=0,
        tiled=True,
    ).astype(jnp.float32) + bias_down.astype(jnp.float32)
    final, back_final = jax.vjp(layer_norm, down, norm_gains[3], norm_shifts[3])
    result = (hidden + final).astype(jnp.bfloat16)
    d_down, gain_last, shift_last = back_final(out_grad)
    grad_bias_down = jnp.sum(d_down, axis=0)
    d_down_all = lax.all_gather(d_down.astype(jnp.bfloat16), "tp", axis=0, tiled=True)
    grad_w_down = jnp.einsum("tf,td->fd", active_b, d_down_all, preferred_element_type=jnp.float32)
    d_active = jnp.einsum("td,fd->tf", d_down_all, w_down, preferred_element_type=jnp.float32)
    (d_up,) = back_gate(d_active)
    d_up_b = d_up.astype(jnp.bfloat16)
    grad_bias_up = jnp.sum(d_up_b.astype(jnp.float32), axis=0)
    grad_w_up = jnp.einsum("td,tf->df", inner_all, d_up_b, preferred_element_type=jnp.float32)
    d_inner = lax.psum_scatter(
        jnp.einsum("tf,df->td", d_up_b, w_up, preferred_element_type=jnp.float32).astype(
            jnp.bfloat16
        ),
        "tp",
        scatter_dimension=0,
        tiled=True,
    ).astype(jnp.float32)
    d_hidden_part, gain_third, shift_third = back_inner(d_inner)
    d_hidden = out_grad + d_hidden_part
    d_branch, gain_second, shift_second = back_post(d_hidden)
    grad_bias_out = jnp.sum(d_branch, axis=0)
    d_branch_all = lax.all_gather(d_branch.astype(jnp.bfloat16), "tp", axis=0, tiled=True)
    grad_w_out = jnp.einsum(
        "te,td->ed", attended_b, d_branch_all, preferred_element_type=jnp.float32
    )
    d_att_b = jnp.einsum(
        "td,ed->te", d_branch_all, w_out, preferred_element_type=jnp.float32
    ).astype(jnp.bfloat16)
    d_att3 = d_att_b.reshape(head_shape)
    d_total = jnp.sum(d_att3.astype(jnp.float32) * attended32, axis=2).T
    d_query_list = []
    key_buffer = jnp.zeros((total_rows + 2 * margin, head_span), jnp.float32)
    value_buffer = jnp.zeros((total_rows + 2 * margin, head_span), jnp.float32)
    for index in range(blocks_here):
        key_first, allowed = query_window(index)
        rows = slice(index * BLK, (index + 1) * BLK)
        d_query_h, d_key_h, d_value_h = attention_grads(
            query3[rows],
            d_att3[rows],
            log_mass[:, rows],
            d_total[:, rows],
            lax.dynamic_slice_in_dim(keys_pad, key_first, window),
            lax.dynamic_slice_in_dim(values_pad, key_first, window),
            allowed,
        )
        d_query_list.append(jnp.transpose(d_query_h, (1, 0, 2)))
        key_piece = jnp.transpose(d_key_h, (1, 0, 2)).reshape(window, head_span)
        value_piece = jnp.transpose(d_value_h, (1, 0, 2)).reshape(window, head_span)
        key_buffer = lax.dynamic_update_slice_in_dim(
            key_buffer,
            lax.dynamic_slice_in_dim(key_buffer, key_first, window) + key_piece,
            key_first,
            0,
        )
        value_buffer = lax.dynamic_update_slice_in_dim(
            value_buffer,
            lax.dynamic_slice_in_dim(value_buffer, key_first, window) + value_piece,
            key_first,
            0,
        )
    key_terms = from_pack(key_buffer, placement, margin, BLK, total_rows)
    value_terms = from_pack(value_buffer, placement, margin, BLK, total_rows)
    d_keys, d_values = (
        lax.psum_scatter(
            key_terms.astype(jnp.bfloat16), "seq", scatter_dimension=0, tiled=True
        ).astype(jnp.float32),
        lax.psum_scatter(
            value_terms.astype(jnp.bfloat16), "seq", scatter_dimension=0, tiled=True
        ).astype(jnp.float32),
    )
    d_query = jnp.concatenate(d_query_list, axis=0)
    d_query_b = d_query.reshape(own_rows, head_span).astype(jnp.bfloat16)
    d_keys_b = d_keys.astype(jnp.bfloat16)
    d_values_b = d_values.astype(jnp.bfloat16)
    grad_bias_qv = jnp.stack(
        [
            jnp.sum(d_query_b.astype(jnp.float32), axis=0),
            jnp.sum(d_values_b.astype(jnp.float32), axis=0),
        ]
    )
    d_mixed = jnp.concatenate([d_query_b, d_keys_b, d_values_b], axis=1)
    grad_w_qkv = jnp.einsum(
        "td,tc->dc", rows_all, d_mixed, preferred_element_type=jnp.float32
    ).reshape(model_width, 3, head_span)
    d_normed = lax.psum_scatter(
        jnp.einsum("tc,dc->td", d_mixed, flat_qkv, preferred_element_type=jnp.float32).astype(
            jnp.bfloat16
        ),
        "tp",
        scatter_dimension=0,
        tiled=True,
    ).astype(jnp.float32)
    d_input_part, gain_first, shift_first = back_first(d_normed)
    grad_x = d_hidden + d_input_part
    summed = (
        lax.psum(grad_w_qkv.astype(jnp.bfloat16), "seq").astype(jnp.float32),
        lax.psum(grad_bias_qv.astype(jnp.bfloat16), "seq").astype(jnp.float32),
        lax.psum(grad_w_out.astype(jnp.bfloat16), "seq").astype(jnp.float32),
        lax.psum(grad_w_up.astype(jnp.bfloat16), "seq").astype(jnp.float32),
        lax.psum(grad_bias_up.astype(jnp.bfloat16), "seq").astype(jnp.float32),
        lax.psum(grad_w_down.astype(jnp.bfloat16), "seq").astype(jnp.float32),
    )
    gain_stack = jnp.stack([gain_first, gain_second, gain_third, gain_last])
    shift_stack = jnp.stack([shift_first, shift_second, shift_third, shift_last])
    vectors = lax.psum((gain_stack, shift_stack, grad_bias_out, grad_bias_down), ("seq", "tp"))
    return (
        result,
        grad_x,
        summed[0],
        summed[1],
        summed[2],
        vectors[2],
        summed[3],
        summed[4],
        summed[5],
        vectors[3],
        vectors[0],
        vectors[1],
    )


def solution(mesh):
    placed = (
        P(("seq", "tp"), None),
        P(None, None, "tp"),
        P(None, "tp"),
        P("tp", None),
        P(),
        P(None, "tp"),
        P("tp"),
        P("tp", None),
        P(),
        P(),
        P(),
        P(("seq", "tp"), None),
        P(),
        P(),
        P(),
    )
    seq_count, tp_count = mesh.shape["seq"], mesh.shape["tp"]

    def local(*args):
        tokens_in, w_qkv, placement = args[0], args[1], args[-1]
        heads = w_qkv.shape[2] * tp_count // HEAD
        paired = seq_count * tp_count == 2 * heads == placement.shape[0]
        sizes = (tokens_in.shape[0], w_qkv.shape[0], heads, seq_count, tp_count)
        fast = paired and sizes == (BLK, 1024, 16, 16, 2)
        return (fast_local if fast else general_local)(*args)

    return jax.shard_map(
        local,
        mesh=mesh,
        in_specs=placed,
        out_specs=(
            P(("seq", "tp"), None),
            P(("seq", "tp"), None),
            P(None, None, "tp"),
            P(None, "tp"),
            P("tp", None),
            P(),
            P(None, "tp"),
            P("tp"),
            P("tp", None),
            P(),
            P(),
            P(),
        ),
        check_vma=False,
    )
```

```python
import functools

import jax
import jax.numpy as jnp
from jax import lax
from jax.experimental import pallas as pl
from jax.experimental.pallas import tpu as pltpu
from jax.sharding import PartitionSpec as P

HEAD = 64
BLK = 512
HALF = BLK // 2
QUART = BLK // 4
LONGEST = 4096
STEP_F = 1024
STEP_B = 512
UNROLL = 4
CHUNK_ROWS = 256
FIRST_TICKS = 6
VMEM_LIMIT = 58 << 20

EPS = 1e-05
F32 = jnp.float32
BF16 = jnp.bfloat16
MESH = pl.DeviceIdType.MESH


def layer_norm(row_block, gain_row, shift_row):
    row_mean = jnp.mean(row_block, axis=-1, keepdims=True)
    centred = row_block - row_mean
    spread = jnp.mean(centred * centred, axis=-1, keepdims=True)
    return centred * lax.rsqrt(spread + EPS) * gain_row + shift_row


def smooth_gate(values):
    return jax.nn.gelu(values, approximate=True)


def running_ends(lengths):
    count = lengths.shape[0]
    index = jnp.arange(count, dtype=jnp.int32)
    return jnp.sum(jnp.where(index[None, :] <= index[:, None], lengths[None, :], 0), axis=1)


def inverse_order(placement):
    index = jnp.arange(placement.shape[0], dtype=jnp.int32)
    return jnp.sum(jnp.where(placement[None, :] == index[:, None], index[None, :], 0), axis=1)


def block_tables(lengths, prefixes, placement, part):
    ends = running_ends(lengths)
    starts = ends - lengths
    limits = starts + prefixes
    offset = part * HALF + jnp.arange(HALF, dtype=jnp.int32)
    pos = placement[:, None] * BLK + offset[None, :]
    inside = (pos[:, :, None] >= starts) & (pos[:, :, None] < ends)

    def pick(values):
        return jnp.sum(jnp.where(inside, values, 0), axis=2)

    low = pick(starts)
    high = jnp.minimum(pick(ends), jnp.maximum(pos + 1, pick(limits)))
    table = jnp.stack(
        [
            jnp.min(low, axis=1) // HALF,
            (jnp.max(high, axis=1) - 1) // HALF + 1,
            jnp.max(low, axis=1),
            jnp.min(high, axis=1),
            placement,
        ]
    )
    return low[:, None, :], high[:, None, :], table


def unpack_t(packed):
    turned = packed.astype(F32).T
    return jnp.concatenate([turned[:HEAD], turned[HEAD:]], axis=1)


def pack_t(turned):
    return jnp.concatenate([turned[:, :QUART], turned[:, QUART:]], axis=0).T


def pieces(tab, b, keys, step, start):
    count = keys // HALF
    first = tab[0, b]

    def visit(i, state):
        at = pl.multiple_of((first + i * count) * HALF, HALF)
        whole = (at >= tab[2, b]) & (at + keys <= tab[3, b])
        return lax.cond(whole, lambda st: step(at, st, False), lambda st: step(at, st, True), state)

    return lax.fori_loop(0, (tab[1, b] - first + count - 1) // count, visit, start)


def attend_kernel(
    part_ref, tab, low_ref, high_ref, q_ref, own_ref, sib_ref,
    out_ref, ot_ref, lse_ref, kv, kvt, rhs_s,
):
    part = part_ref[0]
    scale = HEAD**-0.5
    blocks = q_ref.shape[0]
    rows = blocks * BLK
    depth = lax.broadcasted_iota(jnp.int32, (STEP_F, HALF), 0)

    def prepare(b, carry):
        for ref, which in ((own_ref, part), (sib_ref, 1 - part)):
            at = pl.multiple_of(tab[4, b] * BLK + which * HALF, HALF)
            piece = ref[b]
            kv[pl.ds(at, HALF), :] = piece
            kvt[:, pl.ds(at, HALF)] = piece.T
        qt = unpack_t(q_ref[b]) * scale
        rhs_s[b] = jnp.concatenate([qt, jnp.zeros_like(qt)], axis=0).astype(BF16)
        return carry

    lax.fori_loop(0, blocks, prepare, 0, unroll=UNROLL)
    kv[rows:, :] = jnp.zeros((kv.shape[0] - rows, 2 * HEAD), BF16)
    kvt[:, rows:] = jnp.zeros((2 * HEAD, kv.shape[0] - rows), BF16)

    def one(b, carry):
        low, high = low_ref[b], high_ref[b]

        def step(at, state, masked):
            top, total, acc = state
            sc = jnp.dot(kv[pl.ds(at, STEP_F), :], rhs_s[b], preferred_element_type=F32)
            if masked:
                sc = jnp.where((depth >= low - at) & (depth < high - at), sc, -1e30)
            new = jnp.maximum(top, jnp.max(sc, axis=0, keepdims=True))
            alpha = jnp.exp(top - new)
            pr = jnp.exp(sc - new)
            total = total * alpha + jnp.sum(pr, axis=0, keepdims=True)
            acc = acc * alpha + jnp.dot(
                kvt[HEAD:, pl.ds(at, STEP_F)], pr.astype(BF16), preferred_element_type=F32
            )
            return new, total, acc

        start = (
            jnp.full((1, HALF), -1e30, F32),
            jnp.zeros((1, HALF), F32),
            jnp.zeros((HEAD, HALF), F32),
        )
        top, total, acc = pieces(tab, b, STEP_F, step, start)
        ot_ref[b] = acc * (1.0 / total)
        lse_ref[b] = top + jnp.log(total)
        return carry

    lax.fori_loop(0, blocks, one, 0)

    def finish(b, carry):
        out_ref[b] = pack_t(ot_ref[b]).astype(BF16)
        return carry

    lax.fori_loop(0, blocks, finish, 0, unroll=UNROLL)


def attend_back_kernel(
    part_ref, tab, low_ref, high_ref, q_ref, da_ref, ot_ref, lse_ref, kv, kvt,
    dq_ref, mine_ref, theirs_ref, dkv, rhs_s, rows_s, total_s, dqt_s,
):
    part = part_ref[0]
    scale = HEAD**-0.5
    blocks = q_ref.shape[0]
    depth = lax.broadcasted_iota(jnp.int32, (STEP_B, HALF), 0)
    lane = lax.broadcasted_iota(jnp.int32, (HALF, 2 * HEAD), 1)

    def prepare(b, carry):
        dkv[pl.ds(pl.multiple_of(b * BLK, BLK), BLK), :] = jnp.zeros((BLK, 2 * HEAD), F32)
        qt = unpack_t(q_ref[b]) * scale
        dat = unpack_t(da_ref[b])
        blank = jnp.zeros_like(qt)
        rhs_s[b, :, :HALF] = jnp.concatenate([qt, blank], axis=0).astype(BF16)
        rhs_s[b, :, HALF:] = jnp.concatenate([blank, dat], axis=0).astype(BF16)
        both = jnp.concatenate([qt, dat], axis=0).T
        rows_s[b, :HALF, :] = jnp.where(lane < HEAD, both, 0.0).astype(BF16)
        rows_s[b, HALF:, :] = jnp.where(lane < HEAD, 0.0, both).astype(BF16)
        total_s[b] = jnp.sum(dat * ot_ref[b], axis=0, keepdims=True)
        return carry

    lax.fori_loop(0, blocks, prepare, 0, unroll=UNROLL)
    dkv[blocks * BLK :, :] = jnp.zeros((dkv.shape[0] - blocks * BLK, 2 * HEAD), F32)

    def one(b, carry):
        total = total_s[b]
        lse = lse_ref[b]
        low, high = low_ref[b], high_ref[b]

        def step(at, acc, masked):
            keys = kv[pl.ds(at, STEP_B), :]
            sc = jnp.dot(keys, rhs_s[b, :, :HALF], preferred_element_type=F32)
            dp = jnp.dot(keys, rhs_s[b, :, HALF:], preferred_element_type=F32)
            if masked:
                sc = jnp.where((depth >= low - at) & (depth < high - at), sc, -1e30)
            pr = jnp.exp(sc - lse)
            ds = (pr * (dp - total)).astype(BF16)
            dkv[pl.ds(at, STEP_B), :] += jnp.dot(
                ds, rows_s[b, :HALF, :], preferred_element_type=F32
            ) + jnp.dot(pr.astype(BF16), rows_s[b, HALF:, :], preferred_element_type=F32)
            return acc + jnp.dot(kvt[:HEAD, pl.ds(at, STEP_B)], ds, preferred_element_type=F32)

        dqt_s[b] = pieces(tab, b, STEP_B, step, jnp.zeros((HEAD, HALF), F32))
        return carry

    lax.fori_loop(0, blocks, one, 0)

    def finish(b, carry):
        dq_ref[b] = pack_t(dqt_s[b] * scale).astype(BF16)
        base = tab[4, b] * BLK
        mine_ref[b] = dkv[pl.ds(pl.multiple_of(base + part * HALF, HALF), HALF), :]
        theirs_ref[b] = dkv[pl.ds(pl.multiple_of(base + (1 - part) * HALF, HALF), HALF), :].astype(BF16)
        return carry

    lax.fori_loop(0, blocks, finish, 0, unroll=UNROLL)


def vmem(count):
    return [pl.BlockSpec(memory_space=pltpu.VMEM)] * count


def smem(count):
    return [pl.BlockSpec(memory_space=pltpu.SMEM)] * count


def attend(part, tables, q_chunks, kv_own, kv_sib):
    low, high, table = tables
    blocks = q_chunks.shape[0]
    rows = blocks * BLK + STEP_F
    return pl.pallas_call(
        attend_kernel,
        out_shape=(
            jax.ShapeDtypeStruct((blocks, QUART, 2 * HEAD), BF16),
            jax.ShapeDtypeStruct((blocks, HEAD, HALF), F32),
            jax.ShapeDtypeStruct((blocks, 1, HALF), F32),
            jax.ShapeDtypeStruct((rows, 2 * HEAD), BF16),
            jax.ShapeDtypeStruct((2 * HEAD, rows), BF16),
        ),
        in_specs=smem(2) + vmem(5),
        out_specs=tuple(vmem(5)),
        scratch_shapes=[pltpu.VMEM((blocks, 2 * HEAD, HALF), BF16)],
        compiler_params=pltpu.CompilerParams(vmem_limit_bytes=VMEM_LIMIT),
        cost_estimate=pl.CostEstimate(
            flops=40 * 10**9, bytes_accessed=20 << 20, transcendentals=blocks * 4 * BLK * HALF
        ),
        name="attend",
    )(part.reshape(1), table, low, high, q_chunks, kv_own, kv_sib)


def attend_back(part, tables, q_chunks, da_chunks, out_t, mass, kv, kvt):
    low, high, table = tables
    blocks = q_chunks.shape[0]
    return pl.pallas_call(
        attend_back_kernel,
        out_shape=(
            jax.ShapeDtypeStruct((blocks, QUART, 2 * HEAD), BF16),
            jax.ShapeDtypeStruct((blocks, HALF, 2 * HEAD), F32),
            jax.ShapeDtypeStruct((blocks, HALF, 2 * HEAD), BF16),
        ),
        in_specs=smem(2) + vmem(8),
        out_specs=tuple(vmem(3)),
        scratch_shapes=[
            pltpu.VMEM((blocks * BLK + STEP_F, 2 * HEAD), F32),
            pltpu.VMEM((blocks, 2 * HEAD, BLK), BF16),
            pltpu.VMEM((blocks, BLK, 2 * HEAD), BF16),
            pltpu.VMEM((blocks, 1, HALF), F32),
            pltpu.VMEM((blocks, HEAD, HALF), F32),
        ],
        compiler_params=pltpu.CompilerParams(vmem_limit_bytes=VMEM_LIMIT),
        cost_estimate=pl.CostEstimate(
            flops=60 * 10**9, bytes_accessed=30 << 20, transcendentals=blocks * 4 * BLK * HALF
        ),
        name="attend_back",
    )(part.reshape(1), table, low, high, q_chunks, da_chunks, out_t, mass, kv, kvt)


def chunk_of(who, quarter, index, half):
    absolute = (who[0] * 2 + who[1]) ^ quarter
    tp, sub = absolute // 2, absolute % 2
    return ((sub * 4 + index) * 2 + half) * 2 + tp


def swap_lanes(values):
    return pltpu.roll(values, HEAD, 1)


def low_lanes(rows):
    return lax.broadcasted_iota(jnp.int32, (rows, 2 * HEAD), 1) < HEAD


def store_packed(who, quarter, values, out_ref):
    low = low_lanes(QUART)
    for pair in range(2):
        for half in range(2):
            top = half * HALF
            lanes = slice(pair * 128, pair * 128 + 128)
            first, second = values[top : top + QUART, lanes], values[top + QUART : top + HALF, lanes]
            even = jnp.where(low, first, swap_lanes(second))
            odd = jnp.where(low, swap_lanes(first), second)
            out_ref[chunk_of(who, quarter, 2 * pair, half)] = even.astype(BF16)
            out_ref[chunk_of(who, quarter, 2 * pair + 1, half)] = odd.astype(BF16)


def load_packed(who, quarter, ref, out_ref, base):
    low = low_lanes(QUART)
    for pair in range(2):
        for half in range(2):
            even = ref[chunk_of(who, quarter, 2 * pair, half)].astype(F32)
            odd = ref[chunk_of(who, quarter, 2 * pair + 1, half)].astype(F32)
            top = half * HALF
            lanes = slice(base + pair * 128, base + pair * 128 + 128)
            out_ref[top : top + QUART, lanes] = jnp.where(low, even, swap_lanes(odd)).astype(BF16)
            out_ref[top + QUART : top + HALF, lanes] = jnp.where(low, swap_lanes(even), odd).astype(BF16)


def project_kernel(who_ref, x_ref, gain_ref, shift_ref, bias_ref, w0, w1, w2, w3, normed_ref, q_ref, kv_ref):
    who = (who_ref[0], who_ref[1])
    normed = layer_norm(x_ref[...].astype(F32), gain_ref[...], shift_ref[...]).astype(BF16)
    normed_ref[...] = normed
    low = low_lanes(HALF)
    for quarter, w in enumerate((w0, w1, w2, w3)):
        def dot(col):
            return jnp.dot(normed, w[:, col : col + 256], preferred_element_type=F32)

        bias = bias_ref[quarter : quarter + 1, :].astype(F32)
        store_packed(who, quarter, dot(0) + bias[:, :256], q_ref)
        keys = dot(256)
        values = dot(512) + bias[:, 256:]
        for pair in range(2):
            lanes = slice(pair * 128, pair * 128 + 128)
            for half in range(2):
                rows = slice(half * HALF, half * HALF + HALF)
                k, v = keys[rows, lanes], values[rows, lanes]
                even = jnp.where(low, k, swap_lanes(v))
                odd = jnp.where(low, swap_lanes(k), v)
                kv_ref[chunk_of(who, quarter, 2 * pair, half)] = even.astype(BF16)
                kv_ref[chunk_of(who, quarter, 2 * pair + 1, half)] = odd.astype(BF16)


def project(who, x, gain, shift, bias, weights):
    rows, width = x.shape
    return pl.pallas_call(
        project_kernel,
        out_shape=(
            jax.ShapeDtypeStruct((rows, width), BF16),
            jax.ShapeDtypeStruct((32, QUART, 2 * HEAD), BF16),
            jax.ShapeDtypeStruct((32, HALF, 2 * HEAD), BF16),
        ),
        in_specs=smem(1) + vmem(8),
        out_specs=tuple(vmem(3)),
        compiler_params=pltpu.CompilerParams(vmem_limit_bytes=VMEM_LIMIT),
        name="project",
    )(who, x, gain, shift, bias, *weights)


def unpack_heads_kernel(who_ref, ref, out_ref):
    who = (who_ref[0], who_ref[1])
    for quarter in range(4):
        load_packed(who, quarter, ref, out_ref, quarter * 256)


def unpack_heads(who, chunks):
    return pl.pallas_call(
        unpack_heads_kernel,
        out_shape=jax.ShapeDtypeStruct((BLK, 1024), BF16),
        in_specs=smem(1) + vmem(1),
        out_specs=vmem(1)[0],
        compiler_params=pltpu.CompilerParams(vmem_limit_bytes=VMEM_LIMIT),
        name="unpack_heads",
    )(who, chunks)


def spread_kernel(who_ref, d_ref, w0, w1, w2, w3, out_ref):
    who = (who_ref[0], who_ref[1])
    d_rows = d_ref[...]
    for quarter, w in enumerate((w0, w1, w2, w3)):
        values = lax.dot_general(
            d_rows, w[...], (((1,), (1,)), ((), ())), preferred_element_type=F32
        )
        store_packed(who, quarter, values, out_ref)


def spread(who, d_branch, weights):
    return pl.pallas_call(
        spread_kernel,
        out_shape=jax.ShapeDtypeStruct((32, QUART, 2 * HEAD), BF16),
        in_specs=smem(1) + vmem(5),
        out_specs=vmem(1)[0],
        compiler_params=pltpu.CompilerParams(vmem_limit_bytes=VMEM_LIMIT),
        name="spread",
    )(who, d_branch, *weights)


class Place:
    def __init__(self):
        self.seq, self.tp = lax.axis_index("seq"), lax.axis_index("tp")
        self.x = lax.rem(self.seq // 2, 2)
        self.z = self.seq // 4
        self.core_partner = (self.seq ^ 1, self.tp)
        self.x_partner = (self.seq ^ 2, self.tp)
        self.z_partners = [(self.seq ^ (4 * d), self.tp) for d in (1, 2, 3)]
        self.tp_partner = (self.seq, self.tp ^ 1)


def greet_all(count, me, seq, tp):
    barrier = pltpu.get_barrier_semaphore()

    def one(k, carry):
        other = lax.rem(me + k, count)
        pl.semaphore_signal(
            barrier, inc=1, device_id=(other // 2, lax.rem(other, 2)), device_id_type=MESH
        )
        return carry

    lax.fori_loop(1, count, one, 0)
    pl.semaphore_wait(barrier, count - 1)


def greet(partners):
    barrier = pltpu.get_barrier_semaphore()
    for partner in partners:
        pl.semaphore_signal(barrier, inc=1, device_id=partner, device_id_type=MESH)
    pl.semaphore_wait(barrier, len(partners))


def remote(src, dst, send, recv, device):
    return pltpu.make_async_remote_copy(
        src_ref=src, dst_ref=dst, send_sem=send, recv_sem=recv, device_id=device, device_id_type=MESH
    )


def chunk_copy(count, me, k, src, dst, send, recv):
    other = lax.rem(me + k, count)
    return remote(src.at[other], dst.at[me], send.at[k], recv.at[k], (other // 2, lax.rem(other, 2)))


def rows_at(start, size):
    return pl.ds(pl.multiple_of(start, size), size)


def reduce_stages(place, chunks, base, out, sib, xbuf, xsum, zbuf, sems, arrived):
    rows = base.shape[0] // chunks
    half, piece = rows // 2, rows // 8
    x, z = place.x, place.z

    def x_copy(k):
        return remote(
            base.at[rows_at(k * rows + (1 - x) * half, half)], xbuf.at[rows_at(k * half, half)],
            sems["xs"].at[k], sems["xr"].at[k], place.x_partner,
        )

    def z_copy(k, d):
        return remote(
            xsum.at[rows_at(k * half + (z ^ d) * piece, piece)],
            zbuf.at[d - 1, rows_at(k * piece, piece)],
            sems["zs"].at[d - 1, k], sems["zr"].at[d - 1, k], place.z_partners[d - 1],
        )

    def own_piece(k):
        return rows_at(k * rows + x * half + z * piece, piece)

    def zg_copy(k, d):
        return remote(
            out.at[own_piece(k)], out.at[own_piece(k)],
            sems["zgs"].at[d - 1, k], sems["zgr"].at[d - 1, k], place.z_partners[d - 1],
        )

    def xg_copy(k):
        span = rows_at(k * rows + x * half, half)
        return remote(out.at[span], out.at[span], sems["xgs"].at[k], sems["xgr"].at[k], place.x_partner)

    def core_copy(k):
        span = rows_at(k * rows, rows)
        return remote(out.at[span], sib.at[span], sems["cs"].at[k], sems["cr"].at[k], place.core_partner)

    def stage_x(k):
        arrived(k)
        x_copy(k).start()

    def stage_z(k):
        x_copy(k).wait_recv()
        mine = base[rows_at(k * rows + x * half, half), :].astype(F32)
        xsum[rows_at(k * half, half), :] = (
            mine + xbuf[rows_at(k * half, half), :].astype(F32)
        ).astype(BF16)
        for d in (3, 2, 1):
            z_copy(k, d).start()

    def stage_zg(k):
        total = xsum[rows_at(k * half + z * piece, piece), :].astype(F32)
        for d in (1, 2, 3):
            z_copy(k, d).wait_recv()
            total = total + zbuf[d - 1, rows_at(k * piece, piece), :].astype(F32)
        out[own_piece(k), :] = total.astype(BF16)
        for d in (3, 2, 1):
            zg_copy(k, d).start()

    def stage_xg(k):
        for d in (1, 2, 3):
            zg_copy(k, d).wait_recv()
        xg_copy(k).start()

    def stage_core(k):
        xg_copy(k).wait_recv()
        core_copy(k).start()

    stages = [stage_x, stage_z, stage_zg, stage_xg, stage_core]

    def tick(t):
        for s, stage in reversed(list(enumerate(stages))):
            @pl.when((t >= s) & (t - s < chunks))
            def _():
                stage(t - s)

    def drain(k, carry):
        x_copy(k).wait_send()
        for d in (1, 2, 3):
            z_copy(k, d).wait_send()
            zg_copy(k, d).wait_send()
        xg_copy(k).wait_send()
        core_copy(k).wait()
        return carry

    return tick, lambda: lax.fori_loop(0, chunks, drain, 0), chunks + len(stages) - 1


SEM_NAMES = ("xs", "xr", "zs", "zr", "zgs", "zgr", "xgs", "xgr", "cs", "cr")
VECTOR_STEPS = 5


def finish_kernel(
    chunks, first_ticks, gain_ref, dq_ref, dkv_ref, near_ref, normed_ref, normed_sib_ref, x_ref, dh_ref,
    w0, w1, w2, w3, vec_ref, out, sib, gx_ref, vec_out,
    base, far, ybuf, xbuf, xsum, zbuf, dq_in, dkv_in, mixed, mixed_sib, normed, normed_sib, x_s, dh_s, w_s, slots,
    *rest,
):
    place = Place()
    count = dq_ref.shape[0]
    me = place.seq * 2 + place.tp
    who = (place.tp, lax.rem(place.seq, 2))
    sems = dict(zip(SEM_NAMES, rest))
    qs, qr, ks, kr, ys, yr, ms, mr, vs, vr, loc = rest[len(SEM_NAMES) :]
    early = near_ref.shape[0]
    rows = base.shape[0] // chunks
    settled = early // rows
    greet_all(count, me, place.seq, place.tp)

    near_copy = pltpu.make_async_copy(near_ref, base.at[pl.ds(0, early)], loc.at[0])
    near_copy.start()

    def start(k, carry):
        chunk_copy(count, me, k, dkv_ref, dkv_in, ks, kr).start()
        chunk_copy(count, me, k, dq_ref, dq_in, qs, qr).start()
        return carry

    lax.fori_loop(1, count, start, 0)
    locals_ = [
        pltpu.make_async_copy(src, dst, loc.at[1 + i])
        for i, (src, dst) in enumerate(
            [
                (dq_ref.at[me], dq_in.at[me]),
                (dkv_ref.at[me], dkv_in.at[me]),
                (normed_ref, normed),
                (normed_sib_ref, normed_sib),
                (x_ref, x_s),
                (dh_ref, dh_s),
            ]
            + [(w, w_s.at[r]) for r, w in enumerate((w0, w1, w2, w3))]
        )
    ]
    near_copy.wait()
    for copy in locals_:
        copy.start()

    def tp_copy(k):
        span = rows_at(k * rows, rows)
        return remote(far.at[span], ybuf.at[span], ys.at[k], yr.at[k], place.tp_partner)

    def arrived(k):
        @pl.when(k >= settled)
        def _():
            late = k - settled
            tp_copy(late).wait_recv()
            span = rows_at(k * rows, rows)
            base[span, :] = (
                base[span, :].astype(F32) + ybuf[rows_at(late * rows, rows), :].astype(F32)
            ).astype(BF16)

    tick, drain, ticks = reduce_stages(place, chunks, base, out, sib, xbuf, xsum, zbuf, sems, arrived)

    def plain(t, carry):
        tick(t)
        return carry

    lax.fori_loop(0, first_ticks, plain, 0)

    def wait(k, carry):
        chunk_copy(count, me, k, dkv_ref, dkv_in, ks, kr).wait()
        chunk_copy(count, me, k, dq_ref, dq_in, qs, qr).wait()
        return carry

    lax.fori_loop(1, count, wait, 0)
    for copy in locals_:
        copy.wait()
    vec_out[...] = vec_ref[...]
    low = low_lanes(HALF)
    for quarter in range(4):
        load_packed(who, quarter, dq_in, mixed.at[quarter], 0)
        for pair in range(2):
            for half in range(2):
                span = slice(half * HALF, half * HALF + HALF)
                even = dkv_in[chunk_of(who, quarter, 2 * pair, half)].astype(F32)
                odd = dkv_in[chunk_of(who, quarter, 2 * pair + 1, half)].astype(F32)
                k_at = 256 + pair * 128
                mixed[quarter, span, k_at : k_at + 128] = jnp.where(low, even, swap_lanes(odd)).astype(BF16)
                mixed[quarter, span, k_at + 256 : k_at + 384] = jnp.where(low, swap_lanes(even), odd).astype(BF16)
    mixed_copies = [
        remote(mixed.at[2 * i + 1], mixed_sib.at[i], ms.at[i], mr.at[i], place.core_partner)
        for i in range(2)
    ]
    for copy in mixed_copies:
        copy.start()
    tick(first_ticks)

    for quarter in range(4):
        absolute = (who[0] * 2 + who[1]) ^ quarter
        lanes = pl.ds(pl.multiple_of(absolute * 256, 256), 256)
        for row, col in ((10, 0), (11, 512)):
            vec_out[row : row + 1, lanes] = jnp.sum(
                mixed[quarter, :, col : col + 256].astype(F32), axis=0, keepdims=True
            )
    gains = jnp.zeros((1, base.shape[1]), F32)
    shifts = jnp.zeros((1, base.shape[1]), F32)
    for part in range(2):
        span = slice(part * HALF, part * HALF + HALF)
        d_normed = jnp.zeros((HALF, base.shape[1]), F32)
        for quarter in range(4):
            d_normed += lax.dot_general(
                mixed[quarter, span, :], w_s[quarter], (((1,), (1,)), ((), ())), preferred_element_type=F32
            )
        xhat, rstd = norm_parts(x_s[span, :].astype(F32))
        e = d_normed * gain_ref[...]
        grad = rstd * (
            e
            - jnp.mean(e, axis=-1, keepdims=True)
            - xhat * jnp.mean(e * xhat, axis=-1, keepdims=True)
        )
        gx_ref[span, :] = dh_s[span, :] + grad
        gains += jnp.sum(d_normed * xhat, axis=0, keepdims=True)
        shifts += jnp.sum(d_normed, axis=0, keepdims=True)
        tick(first_ticks + 1 + part)
    vec_out[0:1, :] = gains
    vec_out[4:5, :] = shifts

    for copy in mixed_copies:
        copy.wait()
    late = pl.ds(early, base.shape[0] - early)
    for i, target in ((1, far), (0, base.at[late])):
        for col in range(0, target.shape[0], 256):
            span = slice(col, col + 256)
            target[span, :] = (
                lax.dot_general(
                    mixed[2 * i, :, span], normed[...], (((0,), (0,)), ((), ())), preferred_element_type=F32
                )
                + lax.dot_general(
                    mixed_sib[i, :, span], normed_sib[...], (((0,), (0,)), ((), ())),
                    preferred_element_type=F32,
                )
            ).astype(BF16)
            if i == 1:
                tp_copy(col // rows).start()

    partners = [place.core_partner, place.tp_partner, place.x_partner] + [
        (place.seq ^ bit, place.tp) for bit in (4, 8)
    ]

    def vector_step(step):
        slots[step] = vec_out[...]
        copy = remote(
            slots.at[step], slots.at[VECTOR_STEPS + step], vs.at[step], vr.at[step], partners[step]
        )
        copy.start()
        copy.wait()
        vec_out[...] += slots[VECTOR_STEPS + step]

    def last(t, carry):
        tick(t)
        for step in range(VECTOR_STEPS):
            @pl.when(t == first_ticks + 3 + step)
            def _():
                vector_step(step)
        return carry

    lax.fori_loop(first_ticks + 3, ticks, last, 0)

    def sent(k, carry):
        tp_copy(k).wait_send()
        return carry

    lax.fori_loop(0, chunks - settled, sent, 0)
    drain()


def finish(gain, dq_chunks, dkv_chunks, near, normed, normed_sib, x, d_hidden, weights, vectors):
    early, cols = near.shape
    late = weights[0].shape[1]
    total = early + late
    chunks = total // CHUNK_ROWS
    late_chunks = late // CHUNK_ROWS
    count = dq_chunks.shape[0]
    rows = x.shape[0]
    dma = pltpu.SemaphoreType.DMA
    anywhere = pl.BlockSpec(memory_space=pl.ANY)
    scratch = [
        pltpu.VMEM((total, cols), BF16),
        pltpu.VMEM((late, cols), BF16),
        pltpu.VMEM((late, cols), BF16),
        pltpu.VMEM((total // 2, cols), BF16),
        pltpu.VMEM((total // 2, cols), BF16),
        pltpu.VMEM((3, total // 8, cols), BF16),
        pltpu.VMEM(dq_chunks.shape, BF16),
        pltpu.VMEM(dkv_chunks.shape, BF16),
        pltpu.VMEM((4, rows, late), BF16),
        pltpu.VMEM((2, rows, late), BF16),
        pltpu.VMEM((rows, cols), BF16),
        pltpu.VMEM((rows, cols), BF16),
        pltpu.VMEM((rows, cols), BF16),
        pltpu.VMEM((rows, cols), F32),
        pltpu.VMEM((4,) + weights[0].shape, BF16),
        pltpu.VMEM((2 * VECTOR_STEPS,) + vectors.shape, F32),
    ]
    scratch += [dma((3, chunks) if name[0] == "z" else (chunks,)) for name in SEM_NAMES]
    scratch += [dma((count,))] * 4 + [dma((late_chunks,))] * 2 + [dma((2,))] * 2
    scratch += [dma((VECTOR_STEPS,))] * 2 + [dma((11,))]
    return pl.pallas_call(
        functools.partial(finish_kernel, chunks, FIRST_TICKS),
        out_shape=(
            jax.ShapeDtypeStruct((total, cols), BF16),
            jax.ShapeDtypeStruct((total, cols), BF16),
            jax.ShapeDtypeStruct((rows, cols), F32),
            jax.ShapeDtypeStruct(vectors.shape, F32),
        ),
        in_specs=vmem(1) + [anywhere] * 11 + vmem(1),
        out_specs=(vmem(1)[0], anywhere, vmem(1)[0], vmem(1)[0]),
        scratch_shapes=scratch,
        compiler_params=pltpu.CompilerParams(
            collective_id=1, has_side_effects=True, vmem_limit_bytes=VMEM_LIMIT
        ),
        name="finish",
    )(gain, dq_chunks, dkv_chunks, near, normed, normed_sib, x, d_hidden, *weights, vectors)


def norm_parts(values):
    mean = jnp.mean(values, axis=-1, keepdims=True)
    centred = values - mean
    rstd = lax.rsqrt(jnp.mean(centred * centred, axis=-1, keepdims=True) + EPS)
    return centred * rstd, rstd


def norm_back(values, gain, upstream):
    xhat, rstd = norm_parts(values)
    e = upstream * gain
    grad = rstd * (
        e
        - jnp.mean(e, axis=-1, keepdims=True)
        - xhat * jnp.mean(e * xhat, axis=-1, keepdims=True)
    )
    return grad, jnp.sum(upstream * xhat, axis=0), jnp.sum(upstream, axis=0)


def fast_local(
    tokens_in, w_qkv, bias_qv, w_out, bias_out, w_up, bias_up, w_down, bias_down,
    norm_gains, norm_shifts, out_grad, lengths, prefixes, placement,
):
    seq_count = lax.axis_size("seq")
    seq, tp = lax.axis_index("seq"), lax.axis_index("tp")
    core = seq % 2
    who = jnp.stack([tp, core]).astype(jnp.int32)
    over_tp = [(0, 1), (1, 0)]
    over_core = [(i, i ^ 1) for i in range(seq_count)]

    def to_tp(values):
        return lax.ppermute(values, "tp", over_tp)

    def to_sib(values):
        return lax.ppermute(values, "seq", over_core)

    def exchange(chunks):
        return lax.all_to_all(chunks, ("seq", "tp"), 0, 0, tiled=True)

    def quarters(values, axis):
        size = values.shape[axis] // 2
        own = lax.dynamic_slice_in_dim(values, core * size, size, axis)
        sib = lax.dynamic_slice_in_dim(values, (1 - core) * size, size, axis)
        far = to_tp(own)
        return [own, sib, far, to_sib(far)]

    width = w_qkv.shape[0]
    wq4 = [w.reshape(width, -1) for w in quarters(w_qkv, 2)]
    small = jnp.concatenate([bias_qv.reshape(2, 2, -1), bias_up.reshape(2, 2, -1).transpose(1, 0, 2)], axis=2)
    small = small.transpose(1, 0, 2)
    small4 = [s.reshape(2, -1) for s in quarters(small, 0)]
    split = bias_qv.shape[1] // 2
    bias_qv4 = jnp.stack([s[:, :split].reshape(-1) for s in small4])
    bias_up4 = [s[:, split:].reshape(-1).astype(F32) for s in small4]
    wo4 = quarters(w_out, 0)
    wu4 = quarters(w_up, 1)
    wd4 = quarters(w_down, 0)

    tables = block_tables(lengths, prefixes, placement, core)
    normed, q_chunks, kv_chunks = project(
        who, tokens_in, norm_gains[:1], norm_shifts[:1], bias_qv4, wq4
    )
    kv_own = exchange(kv_chunks)
    kv_sib = to_sib(kv_own)
    q_own = exchange(q_chunks)
    att_chunks, out_t, mass, kv_pack, kv_turned = attend(core, tables, q_own, kv_own, kv_sib)
    attended = unpack_heads(who, exchange(att_chunks))

    input_f32 = tokens_in.astype(F32)

    def cols(values, quarter, count):
        return values[:, quarter * count : (quarter + 1) * count]

    def dot(a, b):
        return jnp.dot(a, b, preferred_element_type=F32)

    def dot_t(a, b):
        return lax.dot_general(a, b, (((1,), (1,)), ((), ())), preferred_element_type=F32)

    def dot_rows(a, b):
        return lax.dot_general(a, b, (((0,), (0,)), ((), ())), preferred_element_type=F32)

    heads4 = [cols(attended, r, 256) for r in range(4)]
    branch = sum(dot(heads4[r], wo4[r]) for r in range(4)) + bias_out.astype(F32)
    hidden = input_f32 + layer_norm(branch, norm_gains[1], norm_shifts[1])
    inner = layer_norm(hidden, norm_gains[2], norm_shifts[2]).astype(BF16)
    active4, gate4 = [], []
    for r in range(4):
        act, back_gate = jax.vjp(smooth_gate, dot(inner, wu4[r]) + bias_up4[r])
        active4.append(act.astype(BF16))
        gate4.append(back_gate)
    down = sum(dot(active4[r], wd4[r]) for r in range(4)) + bias_down.astype(F32)
    result = (hidden + layer_norm(down, norm_gains[3], norm_shifts[3])).astype(BF16)
    d_down, gain_last, shift_last = norm_back(down, norm_gains[3], out_grad)
    bias_down_part = jnp.sum(d_down, axis=0)
    d_down_b = d_down.astype(BF16)
    inner_sib, down_sib = to_sib(inner), to_sib(d_down_b)
    active_sib = [to_sib(active4[r]) for r in (1, 3)]

    def tie(values, *others):
        return lax.optimization_barrier((values,) + others)[0]

    def reduced(near, far):
        return (near + to_tp(far).astype(F32)).astype(BF16)

    d_up4 = [gate4[r](dot_t(d_down_b, wd4[r]))[0].astype(BF16) for r in range(4)]
    up_sib = [to_sib(d_up4[r]) for r in (1, 3)]
    near_down, far_down = (
        dot_rows(active4[r], d_down_b) + dot_rows(s, down_sib) for r, s in zip((0, 2), active_sib)
    )
    far_down = far_down.astype(BF16)
    d_up4 = tie(d_up4, far_down)
    bias_up_part = [jnp.sum(d.astype(F32), axis=0) for d in d_up4]
    d_inner = sum(dot_t(d_up4[r], wu4[r]) for r in range(4))
    d_third, gain_third, shift_third = norm_back(hidden, norm_gains[2], d_inner)
    d_hidden = out_grad + d_third
    d_branch, gain_second, shift_second = norm_back(branch, norm_gains[1], d_hidden)
    bias_out_part = jnp.sum(d_branch, axis=0)
    d_branch_b = d_branch.astype(BF16)
    branch_sib, normed_sib = to_sib(d_branch_b), to_sib(normed)
    heads_sib = [to_sib(heads4[r]) for r in (1, 3)]
    da_own = exchange(spread(who, d_branch_b, wo4))
    near_up, far_up = (
        dot_rows(inner, d_up4[r]) + dot_rows(inner_sib, s) for r, s in zip((0, 2), up_sib)
    )
    near_out, far_out = (
        dot_rows(heads4[r], d_branch_b) + dot_rows(s, branch_sib)
        for r, s in zip((0, 2), heads_sib)
    )
    far_up, far_out = far_up.astype(BF16), far_out.astype(BF16)
    g_down = reduced(near_down, far_down)
    da_own = tie(da_own, far_up, far_out, g_down)
    dq_chunks, dkv_mine, dkv_theirs = attend_back(
        core, tables, q_own, da_own, out_t, mass, kv_pack, kv_turned
    )
    dkv_chunks = (dkv_mine + to_sib(dkv_theirs).astype(F32)).astype(BF16)
    near_all = jnp.concatenate([g_down, reduced(near_up, far_up), reduced(near_out, far_out)])

    def joined(pair, axis):
        own, sib = pair
        first = jnp.concatenate([own, sib], axis=axis).astype(F32)
        second = jnp.concatenate([sib, own], axis=axis).astype(F32)
        return jnp.where(core == 0, first, second)

    def absolute(parts):
        base = tp * 2 + core
        return jnp.concatenate(
            [sum(jnp.where((base ^ r) == a, parts[r], 0.0) for r in range(4)) for a in range(4)]
        )

    blank = jnp.zeros_like(gain_last)
    vectors = jnp.stack(
        [blank, gain_second, gain_third, gain_last]
        + [blank, shift_second, shift_third, shift_last]
        + [bias_out_part, bias_down_part, blank, blank]
    )
    vectors = jnp.concatenate([vectors, absolute(bias_up_part).reshape(4, -1)])
    sums, sums_sib, grad_x, vectors = finish(
        norm_gains[:1], dq_chunks, dkv_chunks, near_all, normed, normed_sib, tokens_in, d_hidden, wq4, vectors
    )
    pair = (sums, sums_sib)
    hidden_rows = g_down.shape[0]
    up_end = hidden_rows + width
    out_end = near_all.shape[0]

    def rows_of(start, stop):
        return [part[start:stop] for part in pair]

    g_qkv = joined([part.reshape(3, -1, width) for part in rows_of(out_end, None)], 1)
    g_qkv = jnp.transpose(g_qkv, (2, 0, 1))
    own_cols = bias_qv.shape[1]
    grad_bias_qv = lax.dynamic_slice_in_dim(vectors[10:12], tp * own_cols, own_cols, 1)
    grad_bias_up = lax.dynamic_slice_in_dim(
        vectors[12:16].reshape(-1), tp * bias_up.shape[0], bias_up.shape[0]
    )
    return (
        result,
        grad_x,
        g_qkv,
        grad_bias_qv,
        joined(rows_of(up_end, out_end), 0),
        vectors[8],
        joined(rows_of(hidden_rows, up_end), 1),
        grad_bias_up,
        joined(rows_of(0, hidden_rows), 0),
        vectors[9],
        vectors[0:4],
        vectors[4:8],
    )


def pack_tables(lengths, prefixes, row_total):
    where_row = jnp.arange(row_total, dtype=jnp.int32)
    doc_ends = running_ends(lengths)
    document = jnp.sum((where_row[:, None] >= doc_ends[None, :]).astype(jnp.int32), axis=1)
    limits = doc_ends - lengths + prefixes
    doc_pick = document[:, None] == jnp.arange(lengths.shape[0], dtype=jnp.int32)[None, :]
    visible = jnp.sum(jnp.where(doc_pick, limits[None, :], 0), axis=1)
    return (document, visible)


def padded_tables(document, visible, margin):
    row_total = document.shape[0]
    border = jnp.full((margin,), -1, jnp.int32)
    doc_pad = jnp.concatenate([border, document, border])
    pos_pad = jnp.arange(-margin, row_total + margin, dtype=jnp.int32)
    blank = jnp.zeros((margin,), jnp.int32)
    seen_pad = jnp.concatenate([blank, visible, blank])
    return (doc_pad, pos_pad, seen_pad)


def allowed_pairs(query_pos, query_doc, key_pos, key_doc, key_seen):
    return (query_doc[:, None] == key_doc[None, :]) & (
        (key_pos[None, :] <= query_pos[:, None]) | (key_pos[None, :] < key_seen[None, :])
    )


def pick_blocks(blocks, order):
    return lax.map(lambda i: lax.dynamic_index_in_dim(blocks, i, 0, False), order)


def to_pack(stored, pack_order, margin, block_size):
    blocks = stored.reshape((pack_order.shape[0], block_size) + stored.shape[1:])
    ordered = pick_blocks(blocks, pack_order).reshape(stored.shape)
    widths = [(margin, margin)] + [(0, 0)] * (stored.ndim - 1)
    return jnp.pad(ordered, widths)


def from_pack(padded, placement, margin, block_size, row_total):
    core = padded[margin : margin + row_total]
    blocks = core.reshape((placement.shape[0], block_size) + core.shape[1:])
    return pick_blocks(blocks, placement).reshape(core.shape)


def masked_scores(query_h, key_h, allowed):
    scores = query_h.shape[-1] ** (-0.5) * jnp.einsum(
        "qe,ke->qk", query_h, key_h, preferred_element_type=jnp.float32
    )
    return jnp.where(allowed, scores, -jnp.inf)


def forward_block(query_block, key_win, value_win, allowed):

    def forward_one_head(head):
        query_h = lax.dynamic_index_in_dim(query_block, head, 1, False)
        key_h = lax.dynamic_index_in_dim(key_win, head, 1, False)
        value_h = lax.dynamic_index_in_dim(value_win, head, 1, False)
        masked = masked_scores(query_h, key_h, allowed)
        row_top = jnp.max(masked, axis=1, keepdims=True)
        expo = jnp.exp(masked - row_top)
        row_sum = jnp.sum(expo, axis=1, keepdims=True)
        probs_b = (expo / row_sum).astype(jnp.bfloat16)
        output = jnp.dot(probs_b, value_h, preferred_element_type=jnp.float32)
        return (output, (row_top + jnp.log(row_sum))[:, 0])

    return lax.map(forward_one_head, jnp.arange(query_block.shape[1], dtype=jnp.int32))


def attention_grads(
    query_block, d_att_block, mass_block, total_block, key_block, value_block, allowed
):
    score_scale = query_block.shape[-1] ** (-0.5)

    def attention_one_head(head):
        query_h = lax.dynamic_index_in_dim(query_block, head, 1, False)
        d_att_h = lax.dynamic_index_in_dim(d_att_block, head, 1, False)
        key_h = lax.dynamic_index_in_dim(key_block, head, 1, False)
        value_h = lax.dynamic_index_in_dim(value_block, head, 1, False)
        mass_h = lax.dynamic_index_in_dim(mass_block, head, 0, False)
        total_h = lax.dynamic_index_in_dim(total_block, head, 0, False)
        masked = masked_scores(query_h, key_h, allowed)
        probs = jnp.exp(masked - mass_h[:, None])
        d_probs = jnp.einsum("qe,ke->qk", d_att_h, value_h, preferred_element_type=jnp.float32)
        d_scores = (probs * (d_probs - total_h[:, None])).astype(jnp.bfloat16)
        results = []
        results.append(
            score_scale
            * jnp.einsum("qk,ke->qe", d_scores, key_h, preferred_element_type=jnp.float32)
        )
        results.append(
            score_scale
            * jnp.einsum("qk,qe->ke", d_scores, query_h, preferred_element_type=jnp.float32)
        )
        results.append(
            jnp.einsum(
                "qk,qe->ke", probs.astype(jnp.bfloat16), d_att_h, preferred_element_type=jnp.float32
            )
        )
        return tuple(results)

    return lax.map(attention_one_head, jnp.arange(query_block.shape[1], dtype=jnp.int32))


def general_local(
    tokens_in,
    w_qkv,
    bias_qv,
    w_out,
    bias_out,
    w_up,
    bias_up,
    w_down,
    bias_down,
    norm_gains,
    norm_shifts,
    out_grad,
    lengths,
    prefixes,
    placement,
):
    seq_count = lax.axis_size("seq")
    block_total = placement.shape[0]
    blocks_here = block_total // seq_count
    total_rows = block_total * BLK
    own_rows = blocks_here * BLK
    model_width = w_qkv.shape[0]
    head_span = w_qkv.shape[2]
    heads_here = head_span // HEAD
    margin = LONGEST + BLK
    window = LONGEST + 2 * BLK
    document, visible = pack_tables(lengths, prefixes, total_rows)
    doc_pad, pos_pad, seen_pad = padded_tables(document, visible, margin)
    own_blocks = lax.dynamic_slice_in_dim(
        placement, lax.axis_index("seq") * blocks_here, blocks_here
    )
    pack_order = inverse_order(placement)
    offsets = jnp.arange(BLK, dtype=jnp.int32)

    def query_window(index):
        first = own_blocks[index] * BLK
        key_first = margin + first - LONGEST
        allowed = allowed_pairs(
            first + offsets,
            lax.dynamic_slice_in_dim(document, first, BLK),
            lax.dynamic_slice_in_dim(pos_pad, key_first, window),
            lax.dynamic_slice_in_dim(doc_pad, key_first, window),
            lax.dynamic_slice_in_dim(seen_pad, key_first, window),
        )
        return (key_first, allowed)

    input_f32 = tokens_in.astype(jnp.float32)
    normed, back_first = jax.vjp(layer_norm, input_f32, norm_gains[0], norm_shifts[0])
    rows_all = lax.all_gather(normed.astype(jnp.bfloat16), "tp", axis=0, tiled=True)
    flat_qkv = w_qkv.reshape(model_width, 3 * head_span)
    mixed = jnp.dot(rows_all, flat_qkv, preferred_element_type=jnp.float32).reshape(
        own_rows, 3, head_span
    )
    query_b = (mixed[:, 0] + bias_qv[0].astype(jnp.float32)).astype(jnp.bfloat16)
    key_b = mixed[:, 1].astype(jnp.bfloat16)
    value_b = (mixed[:, 2] + bias_qv[1].astype(jnp.float32)).astype(jnp.bfloat16)
    keys_all, values_all = (
        lax.all_gather(key_b, "seq", axis=0, tiled=True),
        lax.all_gather(value_b, "seq", axis=0, tiled=True),
    )
    keys_pad = to_pack(keys_all, pack_order, margin, BLK).reshape(-1, heads_here, HEAD)
    values_pad = to_pack(values_all, pack_order, margin, BLK).reshape(-1, heads_here, HEAD)
    head_shape = (own_rows, heads_here, HEAD)
    query3 = query_b.reshape(head_shape)
    attended_list = []
    mass_list = []
    for index in range(blocks_here):
        key_first, allowed = query_window(index)
        outputs, masses = forward_block(
            query3[index * BLK : (index + 1) * BLK],
            lax.dynamic_slice_in_dim(keys_pad, key_first, window),
            lax.dynamic_slice_in_dim(values_pad, key_first, window),
            allowed,
        )
        attended_list.append(jnp.transpose(outputs, (1, 0, 2)))
        mass_list.append(masses)
    attended32 = jnp.concatenate(attended_list, axis=0)
    log_mass = jnp.concatenate(mass_list, axis=1)
    attended_b = attended32.reshape(own_rows, head_span).astype(jnp.bfloat16)
    branch = lax.psum_scatter(
        jnp.dot(attended_b, w_out, preferred_element_type=jnp.float32).astype(jnp.bfloat16),
        "tp",
        scatter_dimension=0,
        tiled=True,
    ).astype(jnp.float32) + bias_out.astype(jnp.float32)
    post_attn, back_post = jax.vjp(layer_norm, branch, norm_gains[1], norm_shifts[1])
    hidden = input_f32 + post_attn
    inner, back_inner = jax.vjp(layer_norm, hidden, norm_gains[2], norm_shifts[2])
    inner_all = lax.all_gather(inner.astype(jnp.bfloat16), "tp", axis=0, tiled=True)
    upward = jnp.dot(inner_all, w_up, preferred_element_type=jnp.float32) + bias_up.astype(
        jnp.float32
    )
    active, back_gate = jax.vjp(smooth_gate, upward)
    active_b = active.astype(jnp.bfloat16)
    down = lax.psum_scatter(
        jnp.dot(active_b, w_down, preferred_element_type=jnp.float32).astype(jnp.bfloat16),
        "tp",
        scatter_dimension=0,
        tiled=True,
    ).astype(jnp.float32) + bias_down.astype(jnp.float32)
    final, back_final = jax.vjp(layer_norm, down, norm_gains[3], norm_shifts[3])
    result = (hidden + final).astype(jnp.bfloat16)
    d_down, gain_last, shift_last = back_final(out_grad)
    grad_bias_down = jnp.sum(d_down, axis=0)
    d_down_all = lax.all_gather(d_down.astype(jnp.bfloat16), "tp", axis=0, tiled=True)
    grad_w_down = jnp.einsum("tf,td->fd", active_b, d_down_all, preferred_element_type=jnp.float32)
    d_active = jnp.einsum("td,fd->tf", d_down_all, w_down, preferred_element_type=jnp.float32)
    (d_up,) = back_gate(d_active)
    d_up_b = d_up.astype(jnp.bfloat16)
    grad_bias_up = jnp.sum(d_up_b.astype(jnp.float32), axis=0)
    grad_w_up = jnp.einsum("td,tf->df", inner_all, d_up_b, preferred_element_type=jnp.float32)
    d_inner = lax.psum_scatter(
        jnp.einsum("tf,df->td", d_up_b, w_up, preferred_element_type=jnp.float32).astype(
            jnp.bfloat16
        ),
        "tp",
        scatter_dimension=0,
        tiled=True,
    ).astype(jnp.float32)
    d_hidden_part, gain_third, shift_third = back_inner(d_inner)
    d_hidden = out_grad + d_hidden_part
    d_branch, gain_second, shift_second = back_post(d_hidden)
    grad_bias_out = jnp.sum(d_branch, axis=0)
    d_branch_all = lax.all_gather(d_branch.astype(jnp.bfloat16), "tp", axis=0, tiled=True)
    grad_w_out = jnp.einsum(
        "te,td->ed", attended_b, d_branch_all, preferred_element_type=jnp.float32
    )
    d_att_b = jnp.einsum(
        "td,ed->te", d_branch_all, w_out, preferred_element_type=jnp.float32
    ).astype(jnp.bfloat16)
    d_att3 = d_att_b.reshape(head_shape)
    d_total = jnp.sum(d_att3.astype(jnp.float32) * attended32, axis=2).T
    d_query_list = []
    key_buffer = jnp.zeros((total_rows + 2 * margin, head_span), jnp.float32)
    value_buffer = jnp.zeros((total_rows + 2 * margin, head_span), jnp.float32)
    for index in range(blocks_here):
        key_first, allowed = query_window(index)
        rows = slice(index * BLK, (index + 1) * BLK)
        d_query_h, d_key_h, d_value_h = attention_grads(
            query3[rows],
            d_att3[rows],
            log_mass[:, rows],
            d_total[:, rows],
            lax.dynamic_slice_in_dim(keys_pad, key_first, window),
            lax.dynamic_slice_in_dim(values_pad, key_first, window),
            allowed,
        )
        d_query_list.append(jnp.transpose(d_query_h, (1, 0, 2)))
        key_piece = jnp.transpose(d_key_h, (1, 0, 2)).reshape(window, head_span)
        value_piece = jnp.transpose(d_value_h, (1, 0, 2)).reshape(window, head_span)
        key_buffer = lax.dynamic_update_slice_in_dim(
            key_buffer,
            lax.dynamic_slice_in_dim(key_buffer, key_first, window) + key_piece,
            key_first,
            0,
        )
        value_buffer = lax.dynamic_update_slice_in_dim(
            value_buffer,
            lax.dynamic_slice_in_dim(value_buffer, key_first, window) + value_piece,
            key_first,
            0,
        )
    key_terms = from_pack(key_buffer, placement, margin, BLK, total_rows)
    value_terms = from_pack(value_buffer, placement, margin, BLK, total_rows)
    d_keys, d_values = (
        lax.psum_scatter(
            key_terms.astype(jnp.bfloat16), "seq", scatter_dimension=0, tiled=True
        ).astype(jnp.float32),
        lax.psum_scatter(
            value_terms.astype(jnp.bfloat16), "seq", scatter_dimension=0, tiled=True
        ).astype(jnp.float32),
    )
    d_query = jnp.concatenate(d_query_list, axis=0)
    d_query_b = d_query.reshape(own_rows, head_span).astype(jnp.bfloat16)
    d_keys_b = d_keys.astype(jnp.bfloat16)
    d_values_b = d_values.astype(jnp.bfloat16)
    grad_bias_qv = jnp.stack(
        [
            jnp.sum(d_query_b.astype(jnp.float32), axis=0),
            jnp.sum(d_values_b.astype(jnp.float32), axis=0),
        ]
    )
    d_mixed = jnp.concatenate([d_query_b, d_keys_b, d_values_b], axis=1)
    grad_w_qkv = jnp.einsum(
        "td,tc->dc", rows_all, d_mixed, preferred_element_type=jnp.float32
    ).reshape(model_width, 3, head_span)
    d_normed = lax.psum_scatter(
        jnp.einsum("tc,dc->td", d_mixed, flat_qkv, preferred_element_type=jnp.float32).astype(
            jnp.bfloat16
        ),
        "tp",
        scatter_dimension=0,
        tiled=True,
    ).astype(jnp.float32)
    d_input_part, gain_first, shift_first = back_first(d_normed)
    grad_x = d_hidden + d_input_part
    summed = (
        lax.psum(grad_w_qkv.astype(jnp.bfloat16), "seq").astype(jnp.float32),
        lax.psum(grad_bias_qv.astype(jnp.bfloat16), "seq").astype(jnp.float32),
        lax.psum(grad_w_out.astype(jnp.bfloat16), "seq").astype(jnp.float32),
        lax.psum(grad_w_up.astype(jnp.bfloat16), "seq").astype(jnp.float32),
        lax.psum(grad_bias_up.astype(jnp.bfloat16), "seq").astype(jnp.float32),
        lax.psum(grad_w_down.astype(jnp.bfloat16), "seq").astype(jnp.float32),
    )
    gain_stack = jnp.stack([gain_first, gain_second, gain_third, gain_last])
    shift_stack = jnp.stack([shift_first, shift_second, shift_third, shift_last])
    vectors = lax.psum((gain_stack, shift_stack, grad_bias_out, grad_bias_down), ("seq", "tp"))
    return (
        result,
        grad_x,
        summed[0],
        summed[1],
        summed[2],
        vectors[2],
        summed[3],
        summed[4],
        summed[5],
        vectors[3],
        vectors[0],
        vectors[1],
    )


def solution(mesh):
    placed = (
        P(("seq", "tp"), None),
        P(None, None, "tp"),
        P(None, "tp"),
        P("tp", None),
        P(),
        P(None, "tp"),
        P("tp"),
        P("tp", None),
        P(),
        P(),
        P(),
        P(("seq", "tp"), None),
        P(),
        P(),
        P(),
    )
    seq_count, tp_count = mesh.shape["seq"], mesh.shape["tp"]

    def local(*args):
        tokens_in, w_qkv, placement = args[0], args[1], args[-1]
        heads = w_qkv.shape[2] * tp_count // HEAD
        paired = seq_count * tp_count == 2 * heads == placement.shape[0]
        sizes = (tokens_in.shape[0], w_qkv.shape[0], heads, seq_count, tp_count)
        fast = paired and sizes == (BLK, 1024, 16, 16, 2)
        return (fast_local if fast else general_local)(*args)

    return jax.shard_map(
        local,
        mesh=mesh,
        in_specs=placed,
        out_specs=(
            P(("seq", "tp"), None),
            P(("seq", "tp"), None),
            P(None, None, "tp"),
            P(None, "tp"),
            P("tp", None),
            P(),
            P(None, "tp"),
            P("tp"),
            P("tp", None),
            P(),
            P(),
            P(),
        ),
        check_vma=False,
    )
```

```python
import functools

import jax
import jax.numpy as jnp
from jax import lax
from jax.experimental import pallas as pl
from jax.experimental.pallas import tpu as pltpu
from jax.sharding import PartitionSpec as P

HEAD = 64
BLK = 512
HALF = BLK // 2
QUART = BLK // 4
LONGEST = 4096
STEP_F = 1024
STEP_B = 512
UNROLL = 4
CHUNK_ROWS = 256
FIRST_TICKS = 6
VMEM_LIMIT = 58 << 20
VMEM_MIDDLE = 62 << 20

EPS = 1e-05
F32 = jnp.float32
BF16 = jnp.bfloat16
MESH = pl.DeviceIdType.MESH


def layer_norm(row_block, gain_row, shift_row):
    row_mean = jnp.mean(row_block, axis=-1, keepdims=True)
    centred = row_block - row_mean
    spread = jnp.mean(centred * centred, axis=-1, keepdims=True)
    return centred * lax.rsqrt(spread + EPS) * gain_row + shift_row


def smooth_gate(values):
    return jax.nn.gelu(values, approximate=True)


def running_ends(lengths):
    count = lengths.shape[0]
    index = jnp.arange(count, dtype=jnp.int32)
    return jnp.sum(jnp.where(index[None, :] <= index[:, None], lengths[None, :], 0), axis=1)


def inverse_order(placement):
    index = jnp.arange(placement.shape[0], dtype=jnp.int32)
    return jnp.sum(jnp.where(placement[None, :] == index[:, None], index[None, :], 0), axis=1)


def block_tables(lengths, prefixes, placement, part):
    ends = running_ends(lengths)
    starts = ends - lengths
    limits = starts + prefixes
    offset = part * HALF + jnp.arange(HALF, dtype=jnp.int32)
    pos = placement[:, None] * BLK + offset[None, :]
    inside = (pos[:, :, None] >= starts) & (pos[:, :, None] < ends)

    def pick(values):
        return jnp.sum(jnp.where(inside, values, 0), axis=2)

    low = pick(starts)
    high = jnp.minimum(pick(ends), jnp.maximum(pos + 1, pick(limits)))
    table = jnp.stack(
        [
            jnp.min(low, axis=1) // HALF,
            (jnp.max(high, axis=1) - 1) // HALF + 1,
            jnp.max(low, axis=1),
            jnp.min(high, axis=1),
            placement,
        ]
    )
    return low[:, None, :], high[:, None, :], table


def unpack_t(packed):
    turned = packed.astype(F32).T
    return jnp.concatenate([turned[:HEAD], turned[HEAD:]], axis=1)


def pack_t(turned):
    return jnp.concatenate([turned[:, :QUART], turned[:, QUART:]], axis=0).T


def pieces(tab, b, keys, step, start):
    count = keys // HALF
    first = tab[0, b]

    def visit(i, state):
        at = pl.multiple_of((first + i * count) * HALF, HALF)
        whole = (at >= tab[2, b]) & (at + keys <= tab[3, b])
        return lax.cond(whole, lambda st: step(at, st, False), lambda st: step(at, st, True), state)

    return lax.fori_loop(0, (tab[1, b] - first + count - 1) // count, visit, start)


def attend_kernel(
    part_ref, tab, low_ref, high_ref, q_ref, own_ref, sib_ref,
    out_ref, ot_ref, lse_ref, kv, kvt, rhs_s,
):
    part = part_ref[0]
    scale = HEAD**-0.5
    blocks = q_ref.shape[0]
    rows = blocks * BLK
    depth = lax.broadcasted_iota(jnp.int32, (STEP_F, HALF), 0)

    def prepare(b, carry):
        for ref, which in ((own_ref, part), (sib_ref, 1 - part)):
            at = pl.multiple_of(tab[4, b] * BLK + which * HALF, HALF)
            piece = ref[b]
            kv[pl.ds(at, HALF), :] = piece
            kvt[:, pl.ds(at, HALF)] = piece.T
        qt = unpack_t(q_ref[b]) * scale
        rhs_s[b] = jnp.concatenate([qt, jnp.zeros_like(qt)], axis=0).astype(BF16)
        return carry

    lax.fori_loop(0, blocks, prepare, 0, unroll=UNROLL)
    kv[rows:, :] = jnp.zeros((kv.shape[0] - rows, 2 * HEAD), BF16)
    kvt[:, rows:] = jnp.zeros((2 * HEAD, kv.shape[0] - rows), BF16)

    def one(b, carry):
        low, high = low_ref[b], high_ref[b]

        def step(at, state, masked):
            top, total, acc = state
            sc = jnp.dot(kv[pl.ds(at, STEP_F), :], rhs_s[b], preferred_element_type=F32)
            if masked:
                sc = jnp.where((depth >= low - at) & (depth < high - at), sc, -1e30)
            new = jnp.maximum(top, jnp.max(sc, axis=0, keepdims=True))
            alpha = jnp.exp(top - new)
            pr = jnp.exp(sc - new)
            total = total * alpha + jnp.sum(pr, axis=0, keepdims=True)
            acc = acc * alpha + jnp.dot(
                kvt[HEAD:, pl.ds(at, STEP_F)], pr.astype(BF16), preferred_element_type=F32
            )
            return new, total, acc

        start = (
            jnp.full((1, HALF), -1e30, F32),
            jnp.zeros((1, HALF), F32),
            jnp.zeros((HEAD, HALF), F32),
        )
        top, total, acc = pieces(tab, b, STEP_F, step, start)
        ot_ref[b] = acc * (1.0 / total)
        lse_ref[b] = top + jnp.log(total)
        return carry

    lax.fori_loop(0, blocks, one, 0)

    def finish(b, carry):
        out_ref[b] = pack_t(ot_ref[b]).astype(BF16)
        return carry

    lax.fori_loop(0, blocks, finish, 0, unroll=UNROLL)


def attend_back_kernel(
    part_ref, tab, low_ref, high_ref, q_ref, da_ref, ot_ref, lse_ref, kv, kvt,
    dq_ref, mine_ref, theirs_ref, dkv, rhs_s, rows_s, total_s, dqt_s,
):
    part = part_ref[0]
    scale = HEAD**-0.5
    blocks = q_ref.shape[0]
    depth = lax.broadcasted_iota(jnp.int32, (STEP_B, HALF), 0)
    lane = lax.broadcasted_iota(jnp.int32, (HALF, 2 * HEAD), 1)

    def prepare(b, carry):
        dkv[pl.ds(pl.multiple_of(b * BLK, BLK), BLK), :] = jnp.zeros((BLK, 2 * HEAD), F32)
        qt = unpack_t(q_ref[b]) * scale
        dat = unpack_t(da_ref[b])
        blank = jnp.zeros_like(qt)
        rhs_s[b, :, :HALF] = jnp.concatenate([qt, blank], axis=0).astype(BF16)
        rhs_s[b, :, HALF:] = jnp.concatenate([blank, dat], axis=0).astype(BF16)
        both = jnp.concatenate([qt, dat], axis=0).T
        rows_s[b, :HALF, :] = jnp.where(lane < HEAD, both, 0.0).astype(BF16)
        rows_s[b, HALF:, :] = jnp.where(lane < HEAD, 0.0, both).astype(BF16)
        total_s[b] = jnp.sum(dat * ot_ref[b], axis=0, keepdims=True)
        return carry

    lax.fori_loop(0, blocks, prepare, 0, unroll=UNROLL)
    dkv[blocks * BLK :, :] = jnp.zeros((dkv.shape[0] - blocks * BLK, 2 * HEAD), F32)

    def one(b, carry):
        total = total_s[b]
        lse = lse_ref[b]
        low, high = low_ref[b], high_ref[b]

        def step(at, acc, masked):
            keys = kv[pl.ds(at, STEP_B), :]
            sc = jnp.dot(keys, rhs_s[b, :, :HALF], preferred_element_type=F32)
            dp = jnp.dot(keys, rhs_s[b, :, HALF:], preferred_element_type=F32)
            if masked:
                sc = jnp.where((depth >= low - at) & (depth < high - at), sc, -1e30)
            pr = jnp.exp(sc - lse)
            ds = (pr * (dp - total)).astype(BF16)
            dkv[pl.ds(at, STEP_B), :] += jnp.dot(
                ds, rows_s[b, :HALF, :], preferred_element_type=F32
            ) + jnp.dot(pr.astype(BF16), rows_s[b, HALF:, :], preferred_element_type=F32)
            return acc + jnp.dot(kvt[:HEAD, pl.ds(at, STEP_B)], ds, preferred_element_type=F32)

        dqt_s[b] = pieces(tab, b, STEP_B, step, jnp.zeros((HEAD, HALF), F32))
        return carry

    lax.fori_loop(0, blocks, one, 0)

    def finish(b, carry):
        dq_ref[b] = pack_t(dqt_s[b] * scale).astype(BF16)
        base = tab[4, b] * BLK
        mine_ref[b] = dkv[pl.ds(pl.multiple_of(base + part * HALF, HALF), HALF), :]
        theirs_ref[b] = dkv[pl.ds(pl.multiple_of(base + (1 - part) * HALF, HALF), HALF), :].astype(BF16)
        return carry

    lax.fori_loop(0, blocks, finish, 0, unroll=UNROLL)


def vmem(count):
    return [pl.BlockSpec(memory_space=pltpu.VMEM)] * count


def smem(count):
    return [pl.BlockSpec(memory_space=pltpu.SMEM)] * count


def attend(part, tables, q_chunks, kv_own, kv_sib):
    low, high, table = tables
    blocks = q_chunks.shape[0]
    rows = blocks * BLK + STEP_F
    return pl.pallas_call(
        attend_kernel,
        out_shape=(
            jax.ShapeDtypeStruct((blocks, QUART, 2 * HEAD), BF16),
            jax.ShapeDtypeStruct((blocks, HEAD, HALF), F32),
            jax.ShapeDtypeStruct((blocks, 1, HALF), F32),
            jax.ShapeDtypeStruct((rows, 2 * HEAD), BF16),
            jax.ShapeDtypeStruct((2 * HEAD, rows), BF16),
        ),
        in_specs=smem(2) + vmem(5),
        out_specs=tuple(vmem(5)),
        scratch_shapes=[pltpu.VMEM((blocks, 2 * HEAD, HALF), BF16)],
        compiler_params=pltpu.CompilerParams(vmem_limit_bytes=VMEM_LIMIT),
        cost_estimate=pl.CostEstimate(
            flops=40 * 10**9, bytes_accessed=20 << 20, transcendentals=blocks * 4 * BLK * HALF
        ),
        name="attend",
    )(part.reshape(1), table, low, high, q_chunks, kv_own, kv_sib)


def attend_back(part, tables, q_chunks, da_chunks, out_t, mass, kv, kvt):
    low, high, table = tables
    blocks = q_chunks.shape[0]
    return pl.pallas_call(
        attend_back_kernel,
        out_shape=(
            jax.ShapeDtypeStruct((blocks, QUART, 2 * HEAD), BF16),
            jax.ShapeDtypeStruct((blocks, HALF, 2 * HEAD), F32),
            jax.ShapeDtypeStruct((blocks, HALF, 2 * HEAD), BF16),
        ),
        in_specs=smem(2) + vmem(8),
        out_specs=tuple(vmem(3)),
        scratch_shapes=[
            pltpu.VMEM((blocks * BLK + STEP_F, 2 * HEAD), F32),
            pltpu.VMEM((blocks, 2 * HEAD, BLK), BF16),
            pltpu.VMEM((blocks, BLK, 2 * HEAD), BF16),
            pltpu.VMEM((blocks, 1, HALF), F32),
            pltpu.VMEM((blocks, HEAD, HALF), F32),
        ],
        compiler_params=pltpu.CompilerParams(vmem_limit_bytes=VMEM_LIMIT),
        cost_estimate=pl.CostEstimate(
            flops=60 * 10**9, bytes_accessed=30 << 20, transcendentals=blocks * 4 * BLK * HALF
        ),
        name="attend_back",
    )(part.reshape(1), table, low, high, q_chunks, da_chunks, out_t, mass, kv, kvt)


def chunk_of(who, quarter, index, half):
    absolute = (who[0] * 2 + who[1]) ^ quarter
    tp, sub = absolute // 2, absolute % 2
    return ((sub * 4 + index) * 2 + half) * 2 + tp


def swap_lanes(values):
    return pltpu.roll(values, HEAD, 1)


def low_lanes(rows):
    return lax.broadcasted_iota(jnp.int32, (rows, 2 * HEAD), 1) < HEAD


def store_packed(who, quarter, values, out_ref):
    low = low_lanes(QUART)
    for pair in range(2):
        for half in range(2):
            top = half * HALF
            lanes = slice(pair * 128, pair * 128 + 128)
            first, second = values[top : top + QUART, lanes], values[top + QUART : top + HALF, lanes]
            even = jnp.where(low, first, swap_lanes(second))
            odd = jnp.where(low, swap_lanes(first), second)
            out_ref[chunk_of(who, quarter, 2 * pair, half)] = even.astype(BF16)
            out_ref[chunk_of(who, quarter, 2 * pair + 1, half)] = odd.astype(BF16)


def load_packed(who, quarter, ref, out_ref, base):
    low = low_lanes(QUART)
    for pair in range(2):
        for half in range(2):
            even = ref[chunk_of(who, quarter, 2 * pair, half)].astype(F32)
            odd = ref[chunk_of(who, quarter, 2 * pair + 1, half)].astype(F32)
            top = half * HALF
            lanes = slice(base + pair * 128, base + pair * 128 + 128)
            out_ref[top : top + QUART, lanes] = jnp.where(low, even, swap_lanes(odd)).astype(BF16)
            out_ref[top + QUART : top + HALF, lanes] = jnp.where(low, swap_lanes(even), odd).astype(BF16)


class Place:
    def __init__(self):
        self.seq, self.tp = lax.axis_index("seq"), lax.axis_index("tp")
        self.x = lax.rem(self.seq // 2, 2)
        self.z = self.seq // 4
        self.core_partner = (self.seq ^ 1, self.tp)
        self.x_partner = (self.seq ^ 2, self.tp)
        self.z_partners = [(self.seq ^ (4 * d), self.tp) for d in (1, 2, 3)]
        self.tp_partner = (self.seq, self.tp ^ 1)


def greet_all(count, me, seq, tp):
    barrier = pltpu.get_barrier_semaphore()

    def one(k, carry):
        other = lax.rem(me + k, count)
        pl.semaphore_signal(
            barrier, inc=1, device_id=(other // 2, lax.rem(other, 2)), device_id_type=MESH
        )
        return carry

    lax.fori_loop(1, count, one, 0)
    pl.semaphore_wait(barrier, count - 1)


def greet(partners):
    barrier = pltpu.get_barrier_semaphore()
    for partner in partners:
        pl.semaphore_signal(barrier, inc=1, device_id=partner, device_id_type=MESH)
    pl.semaphore_wait(barrier, len(partners))


def remote(src, dst, send, recv, device):
    return pltpu.make_async_remote_copy(
        src_ref=src, dst_ref=dst, send_sem=send, recv_sem=recv, device_id=device, device_id_type=MESH
    )


def chunk_copy(count, me, k, src, dst, send, recv):
    other = lax.rem(me + k, count)
    return remote(src.at[other], dst.at[me], send.at[k], recv.at[k], (other // 2, lax.rem(other, 2)))


def rows_at(start, size):
    return pl.ds(pl.multiple_of(start, size), size)


def reduce_stages(place, chunks, base, out, sib, xbuf, xsum, zbuf, sems, arrived):
    rows = base.shape[0] // chunks
    half, piece = rows // 2, rows // 8
    x, z = place.x, place.z

    def x_copy(k):
        return remote(
            base.at[rows_at(k * rows + (1 - x) * half, half)], xbuf.at[rows_at(k * half, half)],
            sems["xs"].at[k], sems["xr"].at[k], place.x_partner,
        )

    def z_copy(k, d):
        return remote(
            xsum.at[rows_at(k * half + (z ^ d) * piece, piece)],
            zbuf.at[d - 1, rows_at(k * piece, piece)],
            sems["zs"].at[d - 1, k], sems["zr"].at[d - 1, k], place.z_partners[d - 1],
        )

    def own_piece(k):
        return rows_at(k * rows + x * half + z * piece, piece)

    def zg_copy(k, d):
        return remote(
            out.at[own_piece(k)], out.at[own_piece(k)],
            sems["zgs"].at[d - 1, k], sems["zgr"].at[d - 1, k], place.z_partners[d - 1],
        )

    def xg_copy(k):
        span = rows_at(k * rows + x * half, half)
        return remote(out.at[span], out.at[span], sems["xgs"].at[k], sems["xgr"].at[k], place.x_partner)

    def core_copy(k):
        span = rows_at(k * rows, rows)
        return remote(out.at[span], sib.at[span], sems["cs"].at[k], sems["cr"].at[k], place.core_partner)

    def stage_x(k):
        arrived(k)
        x_copy(k).start()

    def stage_z(k):
        x_copy(k).wait_recv()
        mine = base[rows_at(k * rows + x * half, half), :].astype(F32)
        xsum[rows_at(k * half, half), :] = (
            mine + xbuf[rows_at(k * half, half), :].astype(F32)
        ).astype(BF16)
        for d in (3, 2, 1):
            z_copy(k, d).start()

    def stage_zg(k):
        total = xsum[rows_at(k * half + z * piece, piece), :].astype(F32)
        for d in (1, 2, 3):
            z_copy(k, d).wait_recv()
            total = total + zbuf[d - 1, rows_at(k * piece, piece), :].astype(F32)
        out[own_piece(k), :] = total.astype(BF16)
        for d in (3, 2, 1):
            zg_copy(k, d).start()

    def stage_xg(k):
        for d in (1, 2, 3):
            zg_copy(k, d).wait_recv()
        xg_copy(k).start()

    def stage_core(k):
        xg_copy(k).wait_recv()
        core_copy(k).start()

    stages = [stage_x, stage_z, stage_zg, stage_xg, stage_core]

    def tick(t):
        for s, stage in reversed(list(enumerate(stages))):
            @pl.when((t >= s) & (t - s < chunks))
            def _():
                stage(t - s)

    def drain(k, carry):
        x_copy(k).wait_send()
        for d in (1, 2, 3):
            z_copy(k, d).wait_send()
            zg_copy(k, d).wait_send()
        xg_copy(k).wait_send()
        core_copy(k).wait()
        return carry

    return tick, lambda: lax.fori_loop(0, chunks, drain, 0), chunks + len(stages) - 1


SEM_NAMES = ("xs", "xr", "zs", "zr", "zgs", "zgr", "xgs", "xgr", "cs", "cr")
VECTOR_STEPS = 5


def finish_kernel(
    chunks, first_ticks, gain_ref, dq_ref, dkv_ref, near_ref, far_ref, normed_ref, normed_sib_ref, x_ref, dh_ref,
    w0, w1, w2, w3, vec_ref, out, sib, gx_ref, vec_out,
    base, far, ybuf, xbuf, xsum, zbuf, dq_in, dkv_in, mixed, mixed_sib, normed, normed_sib, x_s, dh_s, w_s, slots,
    *rest,
):
    place = Place()
    count = dq_ref.shape[0]
    me = place.seq * 2 + place.tp
    who = (place.tp, lax.rem(place.seq, 2))
    sems = dict(zip(SEM_NAMES, rest))
    qs, qr, ks, kr, ys, yr, ms, mr, vs, vr, loc = rest[len(SEM_NAMES) :]
    early = near_ref.shape[0]
    rows = base.shape[0] // chunks
    settled = early // rows
    crossed = far_ref.shape[0]
    summed = (early - crossed) // rows
    greet_all(count, me, place.seq, place.tp)

    near_copy = pltpu.make_async_copy(near_ref, base.at[pl.ds(0, early)], loc.at[0])
    near_copy.start()
    far_copy = pltpu.make_async_copy(far_ref, ybuf.at[pl.ds(0, crossed)], loc.at[11])
    far_copy.start()

    def start(k, carry):
        chunk_copy(count, me, k, dkv_ref, dkv_in, ks, kr).start()
        chunk_copy(count, me, k, dq_ref, dq_in, qs, qr).start()
        return carry

    lax.fori_loop(1, count, start, 0)
    locals_ = [
        pltpu.make_async_copy(src, dst, loc.at[1 + i])
        for i, (src, dst) in enumerate(
            [
                (dq_ref.at[me], dq_in.at[me]),
                (dkv_ref.at[me], dkv_in.at[me]),
                (normed_ref, normed),
                (normed_sib_ref, normed_sib),
                (x_ref, x_s),
                (dh_ref, dh_s),
            ]
            + [(w.at[pl.ds(0, w_s.shape[1])], w_s.at[r]) for r, w in enumerate((w0, w1, w2, w3))]
        )
    ]
    near_copy.wait()
    far_copy.wait()
    for copy in locals_:
        copy.start()

    def tp_copy(k):
        return remote(
            far.at[rows_at(k * rows, rows)], ybuf.at[rows_at(crossed + k * rows, rows)],
            ys.at[k], yr.at[k], place.tp_partner,
        )

    def arrived(k):
        @pl.when(k >= settled)
        def _():
            tp_copy(k - settled).wait_recv()

        @pl.when(k >= summed)
        def _():
            span = rows_at(k * rows, rows)
            base[span, :] = (
                base[span, :].astype(F32) + ybuf[rows_at((k - summed) * rows, rows), :].astype(F32)
            ).astype(BF16)

    tick, drain, ticks = reduce_stages(place, chunks, base, out, sib, xbuf, xsum, zbuf, sems, arrived)

    def plain(t, carry):
        tick(t)
        return carry

    lax.fori_loop(0, first_ticks, plain, 0)

    def wait(k, carry):
        chunk_copy(count, me, k, dkv_ref, dkv_in, ks, kr).wait()
        chunk_copy(count, me, k, dq_ref, dq_in, qs, qr).wait()
        return carry

    lax.fori_loop(1, count, wait, 0)
    for copy in locals_:
        copy.wait()
    vec_out[...] = vec_ref[...]
    low = low_lanes(HALF)
    for quarter in range(4):
        load_packed(who, quarter, dq_in, mixed.at[quarter], 0)
        for pair in range(2):
            for half in range(2):
                span = slice(half * HALF, half * HALF + HALF)
                even = dkv_in[chunk_of(who, quarter, 2 * pair, half)].astype(F32)
                odd = dkv_in[chunk_of(who, quarter, 2 * pair + 1, half)].astype(F32)
                k_at = 256 + pair * 128
                mixed[quarter, span, k_at : k_at + 128] = jnp.where(low, even, swap_lanes(odd)).astype(BF16)
                mixed[quarter, span, k_at + 256 : k_at + 384] = jnp.where(low, swap_lanes(even), odd).astype(BF16)
    mixed_copies = [
        remote(mixed.at[2 * i + 1], mixed_sib.at[i], ms.at[i], mr.at[i], place.core_partner)
        for i in range(2)
    ]
    for copy in mixed_copies:
        copy.start()
    tick(first_ticks)

    for quarter in range(4):
        absolute = (who[0] * 2 + who[1]) ^ quarter
        lanes = pl.ds(pl.multiple_of(absolute * 256, 256), 256)
        for row, col in ((10, 0), (11, 512)):
            vec_out[row : row + 1, lanes] = jnp.sum(
                mixed[quarter, :, col : col + 256].astype(F32), axis=0, keepdims=True
            )
    gains = jnp.zeros((1, base.shape[1]), F32)
    shifts = jnp.zeros((1, base.shape[1]), F32)
    for part in range(2):
        span = slice(part * HALF, part * HALF + HALF)
        d_normed = jnp.zeros((HALF, base.shape[1]), F32)
        for quarter in range(4):
            d_normed += lax.dot_general(
                mixed[quarter, span, :], w_s[quarter], (((1,), (1,)), ((), ())), preferred_element_type=F32
            )
        xhat, rstd = norm_parts(x_s[span, :].astype(F32))
        e = d_normed * gain_ref[...]
        grad = rstd * (
            e
            - jnp.mean(e, axis=-1, keepdims=True)
            - xhat * jnp.mean(e * xhat, axis=-1, keepdims=True)
        )
        gx_ref[span, :] = dh_s[span, :] + grad
        gains += jnp.sum(d_normed * xhat, axis=0, keepdims=True)
        shifts += jnp.sum(d_normed, axis=0, keepdims=True)
        tick(first_ticks + 1 + part)
    vec_out[0:1, :] = gains
    vec_out[4:5, :] = shifts

    for copy in mixed_copies:
        copy.wait()
    late = pl.ds(early, base.shape[0] - early)
    for i, target in ((1, far), (0, base.at[late])):
        for col in range(0, target.shape[0], 256):
            span = slice(col, col + 256)
            target[span, :] = (
                lax.dot_general(
                    mixed[2 * i, :, span], normed[...], (((0,), (0,)), ((), ())), preferred_element_type=F32
                )
                + lax.dot_general(
                    mixed_sib[i, :, span], normed_sib[...], (((0,), (0,)), ((), ())),
                    preferred_element_type=F32,
                )
            ).astype(BF16)
            if i == 1:
                tp_copy(col // rows).start()

    partners = [place.core_partner, place.tp_partner, place.x_partner] + [
        (place.seq ^ bit, place.tp) for bit in (4, 8)
    ]

    def vector_step(step):
        slots[step] = vec_out[...]
        copy = remote(
            slots.at[step], slots.at[VECTOR_STEPS + step], vs.at[step], vr.at[step], partners[step]
        )
        copy.start()
        copy.wait()
        vec_out[...] += slots[VECTOR_STEPS + step]

    def last(t, carry):
        tick(t)
        for step in range(VECTOR_STEPS):
            @pl.when(t == first_ticks + 3 + step)
            def _():
                vector_step(step)
        return carry

    lax.fori_loop(first_ticks + 3, ticks, last, 0)

    def sent(k, carry):
        tp_copy(k).wait_send()
        return carry

    lax.fori_loop(0, chunks - settled, sent, 0)
    drain()


def finish(gain, dq_chunks, dkv_chunks, near, far, normed, normed_sib, x, d_hidden, weights, vectors):
    early, cols = near.shape
    late = weights[0].shape[1]
    total = early + late
    chunks = total // CHUNK_ROWS
    late_chunks = late // CHUNK_ROWS
    count = dq_chunks.shape[0]
    rows = x.shape[0]
    dma = pltpu.SemaphoreType.DMA
    anywhere = pl.BlockSpec(memory_space=pl.ANY)
    scratch = [
        pltpu.VMEM((total, cols), BF16),
        pltpu.VMEM((late, cols), BF16),
        pltpu.VMEM((far.shape[0] + late, cols), BF16),
        pltpu.VMEM((total // 2, cols), BF16),
        pltpu.VMEM((total // 2, cols), BF16),
        pltpu.VMEM((3, total // 8, cols), BF16),
        pltpu.VMEM(dq_chunks.shape, BF16),
        pltpu.VMEM(dkv_chunks.shape, BF16),
        pltpu.VMEM((4, rows, late), BF16),
        pltpu.VMEM((2, rows, late), BF16),
        pltpu.VMEM((rows, cols), BF16),
        pltpu.VMEM((rows, cols), BF16),
        pltpu.VMEM((rows, cols), BF16),
        pltpu.VMEM((rows, cols), F32),
        pltpu.VMEM((4, cols, late), BF16),
        pltpu.VMEM((2 * VECTOR_STEPS,) + vectors.shape, F32),
    ]
    scratch += [dma((3, chunks) if name[0] == "z" else (chunks,)) for name in SEM_NAMES]
    scratch += [dma((count,))] * 4 + [dma((late_chunks,))] * 2 + [dma((2,))] * 2
    scratch += [dma((VECTOR_STEPS,))] * 2 + [dma((12,))]
    return pl.pallas_call(
        functools.partial(finish_kernel, chunks, FIRST_TICKS),
        out_shape=(
            jax.ShapeDtypeStruct((total, cols), BF16),
            jax.ShapeDtypeStruct((total, cols), BF16),
            jax.ShapeDtypeStruct((rows, cols), F32),
            jax.ShapeDtypeStruct(vectors.shape, F32),
        ),
        in_specs=vmem(1) + [anywhere] * 12 + vmem(1),
        out_specs=(vmem(1)[0], anywhere, vmem(1)[0], vmem(1)[0]),
        scratch_shapes=scratch,
        compiler_params=pltpu.CompilerParams(
            collective_id=1, has_side_effects=True, vmem_limit_bytes=VMEM_LIMIT
        ),
        name="finish",
    )(gain, dq_chunks, dkv_chunks, near, far, normed, normed_sib, x, d_hidden, *weights, vectors)


def begin_kernel(
    x_ref, gain_ref, shift_ref, w0, w1, wo_ref,
    normed_ref, q_in, kv_own, kv_sib, w2, w3, wo2, wo3,
    q_st, kv_st, *sems,
):
    place = Place()
    count = q_in.shape[0]
    width = x_ref.shape[1]
    me = place.seq * 2 + place.tp
    who = (place.tp, lax.rem(place.seq, 2))
    ks, kr, qs, qr, fs, fr, ws, wr = sems
    greet_all(count, me, place.seq, place.tp)
    w_far = remote(w0, w2, ws.at[0], wr.at[0], place.tp_partner)
    w_far.start()
    wo_far = remote(wo_ref, wo2, ws.at[1], wr.at[1], place.tp_partner)
    wo_far.start()
    w_last = remote(w2, w3, ws.at[2], wr.at[2], place.core_partner)
    wo_last = remote(wo2, wo3, ws.at[3], wr.at[3], place.core_partner)

    def norm(part, carry):
        span = rows_at(part * 64, 64)
        normed_ref[span, :] = layer_norm(
            x_ref[span, :].astype(F32), gain_ref[...], shift_ref[...]
        ).astype(BF16)
        return carry

    lax.fori_loop(0, x_ref.shape[0] // 64, norm, 0)

    def kv_copy(other):
        return remote(kv_st.at[other], kv_own.at[me], ks.at[other], kr.at[me], (other // 2, lax.rem(other, 2)))

    def q_copy(other):
        return remote(q_st.at[other], q_in.at[me], qs.at[other], qr.at[me], (other // 2, lax.rem(other, 2)))

    def kv_came(other):
        return remote(kv_st.at[other], kv_own.at[other], ks.at[other], kr.at[other], (other // 2, lax.rem(other, 2)))

    def q_came(other):
        return remote(q_st.at[other], q_in.at[other], qs.at[other], qr.at[other], (other // 2, lax.rem(other, 2)))

    def forward(other):
        return remote(kv_own.at[other], kv_sib.at[other], fs.at[other], fr.at[other], place.core_partner)

    low = low_lanes(HALF)

    def project(quarter, w):
        def dot(col):
            return (
                jnp.dot(normed_ref[...], w[:width, col : col + 256], preferred_element_type=F32)
                + w[width : width + 1, col : col + 256].astype(F32)
            )

        keys, values = dot(256), dot(512)
        for pair in range(2):
            lanes = slice(pair * 128, pair * 128 + 128)
            for half in range(2):
                rows = slice(half * HALF, half * HALF + HALF)
                k, v = keys[rows, lanes], values[rows, lanes]
                kv_st[chunk_of(who, quarter, 2 * pair, half)] = jnp.where(low, k, swap_lanes(v)).astype(BF16)
                kv_st[chunk_of(who, quarter, 2 * pair + 1, half)] = jnp.where(low, swap_lanes(k), v).astype(BF16)
        store_packed(who, quarter, dot(0), q_st)

        def send(i, carry):
            other = chunk_of(who, quarter, i // 2, lax.rem(i, 2))

            @pl.when(other != me)
            def _():
                kv_copy(other).start()
                q_copy(other).start()

            @pl.when(other == me)
            def _():
                kv_own[me] = kv_st[me]
                q_in[me] = q_st[me]

            return carry

        lax.fori_loop(0, 8, send, 0)

    project(0, w0)
    project(1, w1)
    w_far.wait()
    w_last.start()
    project(2, w2)
    w_last.wait()
    project(3, w3)
    wo_far.wait()
    wo_last.start()
    forward(me).start()

    def receive(i, carry):
        other = lax.rem(place.seq + lax.rem(i, count // 2), count // 2) * 2 + lax.rem(
            place.tp + i // (count // 2), 2
        )
        kv_came(other).wait_recv()
        forward(other).start()
        return carry

    lax.fori_loop(1, count, receive, 0)

    def rest(k, carry):
        other = lax.rem(me + k, count)
        q_came(other).wait_recv()
        kv_copy(other).wait_send()
        q_copy(other).wait_send()
        return carry

    lax.fori_loop(1, count, rest, 0)

    def forwarded(k, carry):
        forward(k).wait()
        return carry

    lax.fori_loop(0, count, forwarded, 0)
    wo_last.wait()


def begin(x, gain, shift, w0, w1, wo0):
    rows, width = x.shape
    count = 32
    dma = pltpu.SemaphoreType.DMA
    anywhere = pl.BlockSpec(memory_space=pl.ANY)
    q_shape, kv_shape = (count, QUART, 2 * HEAD), (count, HALF, 2 * HEAD)
    return pl.pallas_call(
        begin_kernel,
        out_shape=(
            jax.ShapeDtypeStruct((rows, width), BF16),
            jax.ShapeDtypeStruct(q_shape, BF16),
            jax.ShapeDtypeStruct(kv_shape, BF16),
            jax.ShapeDtypeStruct(kv_shape, BF16),
            jax.ShapeDtypeStruct(w0.shape, BF16),
            jax.ShapeDtypeStruct(w0.shape, BF16),
            jax.ShapeDtypeStruct(wo0.shape, BF16),
            jax.ShapeDtypeStruct(wo0.shape, BF16),
        ),
        in_specs=vmem(5) + [anywhere],
        out_specs=tuple(vmem(6) + [anywhere] * 2),
        scratch_shapes=[pltpu.VMEM(q_shape, BF16), pltpu.VMEM(kv_shape, BF16)]
        + [dma((count,))] * 6
        + [dma((4,))] * 2,
        compiler_params=pltpu.CompilerParams(
            collective_id=3, has_side_effects=True, vmem_limit_bytes=VMEM_LIMIT
        ),
        name="begin",
    )(x, gain, shift, w0, w1, wo0)


def norm_parts(values):
    mean = jnp.mean(values, axis=-1, keepdims=True)
    centred = values - mean
    rstd = lax.rsqrt(jnp.mean(centred * centred, axis=-1, keepdims=True) + EPS)
    return centred * rstd, rstd


GELU_A = 0.7978845608028654
GELU_B = 0.044715


def gelu_parts(u):
    square = u * u
    t = jnp.tanh(GELU_A * u * (1.0 + GELU_B * square))
    rise = 0.5 * (1.0 + t)
    return u * rise, rise + 0.5 * u * (1.0 - t * t) * (GELU_A * (1.0 + 3.0 * GELU_B * square))


def col_sum(values):
    return jnp.sum(values, axis=0, keepdims=True)


def back_rows(xhat, rstd, gain, upstream):
    e = upstream * gain
    return rstd * (
        e - jnp.mean(e, axis=-1, keepdims=True) - xhat * jnp.mean(e * xhat, axis=-1, keepdims=True)
    )


def dot_nn(a, b):
    return jnp.dot(a, b, preferred_element_type=F32)


def dot_nt(a, b):
    return lax.dot_general(a, b, (((1,), (1,)), ((), ())), preferred_element_type=F32)


def dot_tn(a, b):
    return lax.dot_general(a, b, (((0,), (0,)), ((), ())), preferred_element_type=F32)


def middle_kernel(
    gains, shifts, bias_out, bias_down, bias_up, att_ref, x_ref, og_ref,
    wo0, wo1, wo2, wo3, wu0, wu1, wu2, wd0, wd1,
    result, da_in, dh, vec, near_ref, far_ref,
    att_in, att_s, att_sib, wo_s, wu_s, wd_s, x_s, branch_s, hidden_s, inner_s, inner_sib, act_s, act_sib,
    dg_s, dup_sib, down_s, dd_s, dd_sib, db_s, db_sib, da_st, fd_s, fd_in,
    ats, atr, das, dar, ws, wr, cs, cr, fs, fr, loc,
):
    place = Place()
    count = att_in.shape[0]
    me = place.seq * 2 + place.tp
    who = (place.tp, lax.rem(place.seq, 2))
    rows, width = x_s.shape
    hid = wd_s.shape[1]
    greet_all(count, me, place.seq, place.tp)

    def start(k, carry):
        chunk_copy(count, me, k, att_ref, att_in, ats, atr).start()
        return carry

    lax.fori_loop(1, count, start, 0)
    wd_far = remote(wd0, wd_s.at[2], ws.at[0], wr.at[0], place.tp_partner)
    wd_far.start()
    wu_last = remote(wu2, wu_s.at[3], ws.at[1], wr.at[1], place.core_partner)
    wu_last.start()
    wd_last = remote(wd_s.at[2], wd_s.at[3], ws.at[2], wr.at[2], place.core_partner)
    loads = [(att_ref.at[me], att_in.at[me]), (x_ref, x_s), (og_ref, dh)]
    loads += [(w, wo_s.at[r]) for r, w in enumerate((wo0, wo1, wo2, wo3))]
    loads += [(w, wu_s.at[r]) for r, w in enumerate((wu0, wu1, wu2))]
    loads += [(w, wd_s.at[r]) for r, w in enumerate((wd0, wd1))]
    loads = [pltpu.make_async_copy(src, dst, loc.at[i]) for i, (src, dst) in enumerate(loads)]
    for copy in loads:
        copy.start()

    def to_core(i, src, dst):
        return remote(src, dst, cs.at[i], cr.at[i], place.core_partner)

    att_pair = [to_core(i, att_s.at[2 * i + 1], att_sib.at[i]) for i in range(2)]
    act_pair = [to_core(2 + i, act_s.at[2 * i + 1], act_sib.at[i]) for i in range(2)]
    dup_pair = [to_core(4 + i, dg_s.at[2 * i + 1], dup_sib.at[i]) for i in range(2)]
    inner_pair = to_core(6, inner_s, inner_sib)
    dd_pair = to_core(7, dd_s, dd_sib)
    db_pair = to_core(8, db_s, db_sib)

    def came(k, carry):
        chunk_copy(count, me, k, att_ref, att_in, ats, atr).wait()
        return carry

    lax.fori_loop(1, count, came, 0)
    for copy in loads:
        copy.wait()
    for quarter in range(4):
        load_packed(who, quarter, att_in, att_s.at[quarter], 0)
    for copy in att_pair:
        copy.start()

    def cols(i):
        return rows_at(i * 256, 256)

    def project(i, carry):
        span = cols(i)
        branch_s[:, span] = (
            dot_nn(att_s[0], wo_s[0, :, span])
            + dot_nn(att_s[1], wo_s[1, :, span])
            + dot_nn(att_s[2], wo_s[2, :, span])
            + dot_nn(att_s[3], wo_s[3, :, span])
            + bias_out[:, span]
        )
        return carry

    lax.fori_loop(0, width // 256, project, 0)

    def into(i, carry):
        span = rows_at(i * 64, 64)
        hidden = x_s[span, :].astype(F32) + layer_norm(branch_s[span, :], gains[1:2, :], shifts[1:2, :])
        hidden_s[span, :] = hidden
        inner_s[span, :] = layer_norm(hidden, gains[2:3, :], shifts[2:3, :]).astype(BF16)
        return carry

    lax.fori_loop(0, rows // 64, into, 0)
    inner_pair.start()
    for quarter in range(4):
        if quarter == 3:
            wu_last.wait()

        def up(i, carry, quarter=quarter):
            span = cols(i)
            act, slope = gelu_parts(
                dot_nn(inner_s[...], wu_s[quarter, :, span]) + bias_up[quarter : quarter + 1, span]
            )
            act_s[quarter, :, span] = act.astype(BF16)
            dg_s[quarter, :, span] = slope.astype(BF16)
            return carry

        lax.fori_loop(0, hid // 256, up, 0)
        if quarter % 2 == 1:
            act_pair[quarter // 2].start()

    def down_own(i, carry):
        span = cols(i)
        down_s[:, span] = (
            dot_nn(act_s[0], wd_s[0, :, span]) + dot_nn(act_s[1], wd_s[1, :, span]) + bias_down[:, span]
        )
        return carry

    lax.fori_loop(0, width // 256, down_own, 0)
    wd_far.wait()
    wd_last.start()
    for quarter in (2, 3):
        if quarter == 3:
            wd_last.wait()

        def down_far(i, carry, quarter=quarter):
            span = cols(i)
            down_s[:, span] += dot_nn(act_s[quarter], wd_s[quarter, :, span])
            return carry

        lax.fori_loop(0, width // 256, down_far, 0)

    none = jnp.zeros((1, width), F32)

    def turn(i, carry):
        gain, shift, bias = carry
        span = rows_at(i * 64, 64)
        xhat, rstd = norm_parts(down_s[span, :])
        result[span, :] = (hidden_s[span, :] + xhat * gains[3:4, :] + shifts[3:4, :]).astype(BF16)
        upstream = dh[span, :]
        d_down = back_rows(xhat, rstd, gains[3:4, :], upstream)
        dd_s[span, :] = d_down.astype(BF16)
        return gain + col_sum(upstream * xhat), shift + col_sum(upstream), bias + col_sum(d_down)

    gain, shift, bias = lax.fori_loop(0, rows // 64, turn, (none,) * 3)
    vec[...] = jnp.zeros_like(vec)
    vec[3:4, :] = gain
    vec[7:8, :] = shift
    vec[9:10, :] = bias
    dd_pair.start()
    act_pair[1].wait_recv()
    dd_pair.wait_recv()

    def far_copy(i):
        return remote(fd_s.at[cols(i)], fd_in.at[cols(i)], fs.at[i], fr.at[i], place.tp_partner)

    def far_down(i, carry):
        span = cols(i)
        fd_s[span, :] = (
            dot_tn(act_s[2, :, span], dd_s[...]) + dot_tn(act_sib[1, :, span], dd_sib[...])
        ).astype(BF16)
        far_copy(i).start()
        return carry

    lax.fori_loop(0, hid // 256, far_down, 0)
    for quarter in range(4):
        absolute = (who[0] * 2 + who[1]) ^ quarter

        def back_up(i, carry, quarter=quarter, absolute=absolute):
            span = cols(i)
            d_up = dot_nt(dd_s[...], wd_s[quarter, span, :]) * dg_s[quarter, :, span].astype(F32)
            d_up = d_up.astype(BF16)
            dg_s[quarter, :, span] = d_up
            vec[pl.ds(12 + absolute, 1), span] = col_sum(d_up.astype(F32))
            return carry

        lax.fori_loop(0, hid // 256, back_up, 0)
        if quarter % 2 == 1:
            dup_pair[quarter // 2].start()

    def back_inner(i, carry):
        span = cols(i)
        down_s[:, span] = (
            dot_nt(dg_s[0], wu_s[0, span, :])
            + dot_nt(dg_s[1], wu_s[1, span, :])
            + dot_nt(dg_s[2], wu_s[2, span, :])
            + dot_nt(dg_s[3], wu_s[3, span, :])
        )
        return carry

    lax.fori_loop(0, width // 256, back_inner, 0)

    def out_of(i, carry):
        gain3, shift3, gain2, shift2, bias = carry
        span = rows_at(i * 64, 64)
        d_inner = down_s[span, :]
        xhat, rstd = norm_parts(hidden_s[span, :])
        gain3 = gain3 + col_sum(d_inner * xhat)
        shift3 = shift3 + col_sum(d_inner)
        d_hidden = dh[span, :] + back_rows(xhat, rstd, gains[2:3, :], d_inner)
        dh[span, :] = d_hidden
        xhat, rstd = norm_parts(branch_s[span, :])
        d_branch = back_rows(xhat, rstd, gains[1:2, :], d_hidden)
        db_s[span, :] = d_branch.astype(BF16)
        return (
            gain3, shift3, gain2 + col_sum(d_hidden * xhat), shift2 + col_sum(d_hidden),
            bias + col_sum(d_branch),
        )

    sums = lax.fori_loop(0, rows // 64, out_of, (none,) * 5)
    for row, value in zip((2, 6, 1, 5, 8), sums):
        vec[row : row + 1, :] = value
    db_pair.start()

    def da_copy(other):
        return remote(
            da_st.at[other], da_in.at[me], das.at[other], dar.at[me], (other // 2, lax.rem(other, 2))
        )

    def da_came(other):
        return remote(
            da_st.at[other], da_in.at[other], das.at[other], dar.at[other], (other // 2, lax.rem(other, 2))
        )

    for quarter in range(4):
        store_packed(who, quarter, dot_nt(db_s[...], wo_s[quarter]), da_st)

        def send(i, carry, quarter=quarter):
            other = chunk_of(who, quarter, i // 2, lax.rem(i, 2))

            @pl.when(other != me)
            def _():
                da_copy(other).start()

            @pl.when(other == me)
            def _():
                da_in[me] = da_st[me]

            return carry

        lax.fori_loop(0, 8, send, 0)

    for copy in dup_pair + [inner_pair]:
        copy.wait()

    def grad_up(i, carry):
        span = cols(i)
        for near, slot in ((0, 0), (2, 1)):
            wu_s[near, :, span] = (
                dot_tn(inner_s[...], dg_s[near, :, span]) + dot_tn(inner_sib[...], dup_sib[slot, :, span])
            ).astype(BF16)
        return carry

    lax.fori_loop(0, hid // 256, grad_up, 0)
    for copy in att_pair + [db_pair]:
        copy.wait()
    for near, slot in ((0, 0), (2, 1)):
        wo_s[near] = (dot_tn(att_s[near], db_s[...]) + dot_tn(att_sib[slot], db_sib[...])).astype(BF16)
    up_rows, out_rows = wu_s.shape[1], wo_s.shape[1]
    stores = [
        (wu_s.at[0], near_ref.at[pl.ds(hid, up_rows)]),
        (wo_s.at[0], near_ref.at[pl.ds(hid + up_rows, out_rows)]),
        (wu_s.at[2], far_ref.at[pl.ds(0, up_rows)]),
        (wo_s.at[2], far_ref.at[pl.ds(up_rows, out_rows)]),
    ]
    stores = [pltpu.make_async_copy(src, dst, loc.at[i]) for i, (src, dst) in enumerate(stores)]
    for copy in stores:
        copy.start()
    act_pair[0].wait()
    act_pair[1].wait_send()
    dd_pair.wait_send()

    def near_down(i, carry):
        span = cols(i)
        far_copy(i).wait()
        wd_s[0, span, :] = (
            dot_tn(act_s[0, :, span], dd_s[...])
            + dot_tn(act_sib[0, :, span], dd_sib[...])
            + fd_in[span, :].astype(F32)
        ).astype(BF16)
        return carry

    lax.fori_loop(0, hid // 256, near_down, 0)
    last = pltpu.make_async_copy(wd_s.at[0], near_ref.at[pl.ds(0, hid)], loc.at[4])
    last.start()

    def da_wait(k, carry):
        other = lax.rem(me + k, count)
        da_came(other).wait_recv()
        da_copy(other).wait_send()
        return carry

    lax.fori_loop(1, count, da_wait, 0)
    for copy in stores + [last]:
        copy.wait()


def middle(gains, shifts, bias_out, bias_down, bias_up, att, x, out_grad, wo4, wu3, wd2):
    rows, width = x.shape
    count = att.shape[0]
    hid = wd2[0].shape[0]
    out_rows = wo4[0].shape[0]
    dma = pltpu.SemaphoreType.DMA
    anywhere = pl.BlockSpec(memory_space=pl.ANY)

    def held(*shape, dtype=BF16):
        return pltpu.VMEM(shape, dtype)

    scratch = [
        held(*att.shape),
        held(4, rows, out_rows),
        held(2, rows, out_rows),
        held(4, out_rows, width),
        held(4, width, hid),
        held(4, hid, width),
        held(rows, width),
        held(rows, width, dtype=F32),
        held(rows, width, dtype=F32),
        held(rows, width),
        held(rows, width),
        held(4, rows, hid),
        held(2, rows, hid),
        held(4, rows, hid),
        held(2, rows, hid),
        held(rows, width, dtype=F32),
        held(rows, width),
        held(rows, width),
        held(rows, width),
        held(rows, width),
        held(*att.shape),
        held(hid, width),
        held(hid, width),
    ]
    scratch += [dma((count,))] * 4 + [dma((3,))] * 2 + [dma((9,))] * 2 + [dma((4,))] * 2 + [dma((12,))]
    return pl.pallas_call(
        middle_kernel,
        out_shape=(
            jax.ShapeDtypeStruct((rows, width), BF16),
            jax.ShapeDtypeStruct(att.shape, BF16),
            jax.ShapeDtypeStruct((rows, width), F32),
            jax.ShapeDtypeStruct((16, width), F32),
            jax.ShapeDtypeStruct((hid + width + out_rows, width), BF16),
            jax.ShapeDtypeStruct((width + out_rows, width), BF16),
        ),
        in_specs=vmem(5) + [anywhere] * 12,
        out_specs=tuple(vmem(4) + [anywhere] * 2),
        scratch_shapes=scratch,
        compiler_params=pltpu.CompilerParams(
            collective_id=4, has_side_effects=True, vmem_limit_bytes=VMEM_MIDDLE
        ),
        name="middle",
    )(gains, shifts, bias_out, bias_down, bias_up, att, x, out_grad, *wo4, *wu3, *wd2)


def fast_local(
    tokens_in, w_qkv, bias_qv, w_out, bias_out, w_up, bias_up, w_down, bias_down,
    norm_gains, norm_shifts, out_grad, lengths, prefixes, placement,
):
    seq_count = lax.axis_size("seq")
    seq, tp = lax.axis_index("seq"), lax.axis_index("tp")
    core = seq % 2
    who = jnp.stack([tp, core]).astype(jnp.int32)
    over_tp = [(0, 1), (1, 0)]
    over_core = [(i, i ^ 1) for i in range(seq_count)]

    def to_tp(values):
        return lax.ppermute(values, "tp", over_tp)

    def to_sib(values):
        return lax.ppermute(values, "seq", over_core)

    def exchange(chunks):
        return lax.all_to_all(chunks, ("seq", "tp"), 0, 0, tiled=True)

    def quarters(values, axis):
        size = values.shape[axis] // 2
        own = lax.dynamic_slice_in_dim(values, core * size, size, axis)
        sib = lax.dynamic_slice_in_dim(values, (1 - core) * size, size, axis)
        far = to_tp(own)
        return [own, sib, far, to_sib(far)]

    width = w_qkv.shape[0]

    def halves(values, axis):
        size = values.shape[axis] // 2
        return [
            lax.dynamic_slice_in_dim(values, which * size, size, axis) for which in (core, 1 - core)
        ]

    bias3 = jnp.stack([bias_qv[0], jnp.zeros_like(bias_qv[0]), bias_qv[1]])
    bias3 = jnp.broadcast_to(bias3[None], (16,) + bias3.shape)
    w_ext = jnp.concatenate([w_qkv, bias3])
    wq0, wq1 = [w.reshape(w.shape[0], -1) for w in halves(w_ext, 2)]
    wo0, wo1 = halves(w_out, 0)
    bias_up4 = jnp.concatenate([b.astype(F32).reshape(1, -1) for b in quarters(bias_up.reshape(2, 1, -1), 0)])

    tables = block_tables(lengths, prefixes, placement, core)
    normed, q_own, kv_own, kv_sib, wq2, wq3, wo2, wo3 = begin(
        tokens_in, norm_gains[:1], norm_shifts[:1], wq0, wq1, wo0
    )
    wq4 = [wq0, wq1, wq2, wq3]
    wo4 = [wo0, wo1, wo2, wo3]
    w_up, w_down, normed = lax.optimization_barrier((w_up, w_down, normed))
    wu0, wu1 = halves(w_up, 1)
    wd0, wd1 = halves(w_down, 0)
    wu2 = to_tp(wu0)
    att_chunks, out_t, mass, kv_pack, kv_turned = attend(core, tables, q_own, kv_own, kv_sib)
    normed_sib = to_sib(normed)
    result, da_own, d_hidden, vectors, near, far = middle(
        norm_gains, norm_shifts, bias_out.astype(F32)[None], bias_down.astype(F32)[None], bias_up4,
        att_chunks, tokens_in, out_grad, wo4, [wu0, wu1, wu2], [wd0, wd1],
    )
    far = to_tp(far)
    dq_chunks, dkv_mine, dkv_theirs = attend_back(
        core, tables, q_own, da_own, out_t, mass, kv_pack, kv_turned
    )
    dkv_chunks = (dkv_mine + to_sib(dkv_theirs).astype(F32)).astype(BF16)
    sums, sums_sib, grad_x, vectors = finish(
        norm_gains[:1], dq_chunks, dkv_chunks, near, far, normed, normed_sib, tokens_in, d_hidden, wq4, vectors
    )

    def joined(pair, axis):
        own, sib = pair
        first = jnp.concatenate([own, sib], axis=axis).astype(F32)
        second = jnp.concatenate([sib, own], axis=axis).astype(F32)
        return jnp.where(core == 0, first, second)

    pair = (sums, sums_sib)
    hidden_rows = wd0.shape[0]
    up_end = hidden_rows + width
    out_end = near.shape[0]

    def rows_of(start, stop):
        return [part[start:stop] for part in pair]

    g_qkv = joined([part.reshape(3, -1, width) for part in rows_of(out_end, None)], 1)
    g_qkv = jnp.transpose(g_qkv, (2, 0, 1))
    own_cols = bias_qv.shape[1]
    grad_bias_qv = lax.dynamic_slice_in_dim(vectors[10:12], tp * own_cols, own_cols, 1)
    grad_bias_up = lax.dynamic_slice_in_dim(
        vectors[12:16].reshape(-1), tp * bias_up.shape[0], bias_up.shape[0]
    )
    return (
        result,
        grad_x,
        g_qkv,
        grad_bias_qv,
        joined(rows_of(up_end, out_end), 0),
        vectors[8],
        joined(rows_of(hidden_rows, up_end), 1),
        grad_bias_up,
        joined(rows_of(0, hidden_rows), 0),
        vectors[9],
        vectors[0:4],
        vectors[4:8],
    )


def pack_tables(lengths, prefixes, row_total):
    where_row = jnp.arange(row_total, dtype=jnp.int32)
    doc_ends = running_ends(lengths)
    document = jnp.sum((where_row[:, None] >= doc_ends[None, :]).astype(jnp.int32), axis=1)
    limits = doc_ends - lengths + prefixes
    doc_pick = document[:, None] == jnp.arange(lengths.shape[0], dtype=jnp.int32)[None, :]
    visible = jnp.sum(jnp.where(doc_pick, limits[None, :], 0), axis=1)
    return (document, visible)


def padded_tables(document, visible, margin):
    row_total = document.shape[0]
    border = jnp.full((margin,), -1, jnp.int32)
    doc_pad = jnp.concatenate([border, document, border])
    pos_pad = jnp.arange(-margin, row_total + margin, dtype=jnp.int32)
    blank = jnp.zeros((margin,), jnp.int32)
    seen_pad = jnp.concatenate([blank, visible, blank])
    return (doc_pad, pos_pad, seen_pad)


def allowed_pairs(query_pos, query_doc, key_pos, key_doc, key_seen):
    return (query_doc[:, None] == key_doc[None, :]) & (
        (key_pos[None, :] <= query_pos[:, None]) | (key_pos[None, :] < key_seen[None, :])
    )


def pick_blocks(blocks, order):
    return lax.map(lambda i: lax.dynamic_index_in_dim(blocks, i, 0, False), order)


def to_pack(stored, pack_order, margin, block_size):
    blocks = stored.reshape((pack_order.shape[0], block_size) + stored.shape[1:])
    ordered = pick_blocks(blocks, pack_order).reshape(stored.shape)
    widths = [(margin, margin)] + [(0, 0)] * (stored.ndim - 1)
    return jnp.pad(ordered, widths)


def from_pack(padded, placement, margin, block_size, row_total):
    core = padded[margin : margin + row_total]
    blocks = core.reshape((placement.shape[0], block_size) + core.shape[1:])
    return pick_blocks(blocks, placement).reshape(core.shape)


def masked_scores(query_h, key_h, allowed):
    scores = query_h.shape[-1] ** (-0.5) * jnp.einsum(
        "qe,ke->qk", query_h, key_h, preferred_element_type=jnp.float32
    )
    return jnp.where(allowed, scores, -jnp.inf)


def forward_block(query_block, key_win, value_win, allowed):

    def forward_one_head(head):
        query_h = lax.dynamic_index_in_dim(query_block, head, 1, False)
        key_h = lax.dynamic_index_in_dim(key_win, head, 1, False)
        value_h = lax.dynamic_index_in_dim(value_win, head, 1, False)
        masked = masked_scores(query_h, key_h, allowed)
        row_top = jnp.max(masked, axis=1, keepdims=True)
        expo = jnp.exp(masked - row_top)
        row_sum = jnp.sum(expo, axis=1, keepdims=True)
        probs_b = (expo / row_sum).astype(jnp.bfloat16)
        output = jnp.dot(probs_b, value_h, preferred_element_type=jnp.float32)
        return (output, (row_top + jnp.log(row_sum))[:, 0])

    return lax.map(forward_one_head, jnp.arange(query_block.shape[1], dtype=jnp.int32))


def attention_grads(
    query_block, d_att_block, mass_block, total_block, key_block, value_block, allowed
):
    score_scale = query_block.shape[-1] ** (-0.5)

    def attention_one_head(head):
        query_h = lax.dynamic_index_in_dim(query_block, head, 1, False)
        d_att_h = lax.dynamic_index_in_dim(d_att_block, head, 1, False)
        key_h = lax.dynamic_index_in_dim(key_block, head, 1, False)
        value_h = lax.dynamic_index_in_dim(value_block, head, 1, False)
        mass_h = lax.dynamic_index_in_dim(mass_block, head, 0, False)
        total_h = lax.dynamic_index_in_dim(total_block, head, 0, False)
        masked = masked_scores(query_h, key_h, allowed)
        probs = jnp.exp(masked - mass_h[:, None])
        d_probs = jnp.einsum("qe,ke->qk", d_att_h, value_h, preferred_element_type=jnp.float32)
        d_scores = (probs * (d_probs - total_h[:, None])).astype(jnp.bfloat16)
        results = []
        results.append(
            score_scale
            * jnp.einsum("qk,ke->qe", d_scores, key_h, preferred_element_type=jnp.float32)
        )
        results.append(
            score_scale
            * jnp.einsum("qk,qe->ke", d_scores, query_h, preferred_element_type=jnp.float32)
        )
        results.append(
            jnp.einsum(
                "qk,qe->ke", probs.astype(jnp.bfloat16), d_att_h, preferred_element_type=jnp.float32
            )
        )
        return tuple(results)

    return lax.map(attention_one_head, jnp.arange(query_block.shape[1], dtype=jnp.int32))


def general_local(
    tokens_in,
    w_qkv,
    bias_qv,
    w_out,
    bias_out,
    w_up,
    bias_up,
    w_down,
    bias_down,
    norm_gains,
    norm_shifts,
    out_grad,
    lengths,
    prefixes,
    placement,
):
    seq_count = lax.axis_size("seq")
    block_total = placement.shape[0]
    blocks_here = block_total // seq_count
    total_rows = block_total * BLK
    own_rows = blocks_here * BLK
    model_width = w_qkv.shape[0]
    head_span = w_qkv.shape[2]
    heads_here = head_span // HEAD
    margin = LONGEST + BLK
    window = LONGEST + 2 * BLK
    document, visible = pack_tables(lengths, prefixes, total_rows)
    doc_pad, pos_pad, seen_pad = padded_tables(document, visible, margin)
    own_blocks = lax.dynamic_slice_in_dim(
        placement, lax.axis_index("seq") * blocks_here, blocks_here
    )
    pack_order = inverse_order(placement)
    offsets = jnp.arange(BLK, dtype=jnp.int32)

    def query_window(index):
        first = own_blocks[index] * BLK
        key_first = margin + first - LONGEST
        allowed = allowed_pairs(
            first + offsets,
            lax.dynamic_slice_in_dim(document, first, BLK),
            lax.dynamic_slice_in_dim(pos_pad, key_first, window),
            lax.dynamic_slice_in_dim(doc_pad, key_first, window),
            lax.dynamic_slice_in_dim(seen_pad, key_first, window),
        )
        return (key_first, allowed)

    input_f32 = tokens_in.astype(jnp.float32)
    normed, back_first = jax.vjp(layer_norm, input_f32, norm_gains[0], norm_shifts[0])
    rows_all = lax.all_gather(normed.astype(jnp.bfloat16), "tp", axis=0, tiled=True)
    flat_qkv = w_qkv.reshape(model_width, 3 * head_span)
    mixed = jnp.dot(rows_all, flat_qkv, preferred_element_type=jnp.float32).reshape(
        own_rows, 3, head_span
    )
    query_b = (mixed[:, 0] + bias_qv[0].astype(jnp.float32)).astype(jnp.bfloat16)
    key_b = mixed[:, 1].astype(jnp.bfloat16)
    value_b = (mixed[:, 2] + bias_qv[1].astype(jnp.float32)).astype(jnp.bfloat16)
    keys_all, values_all = (
        lax.all_gather(key_b, "seq", axis=0, tiled=True),
        lax.all_gather(value_b, "seq", axis=0, tiled=True),
    )
    keys_pad = to_pack(keys_all, pack_order, margin, BLK).reshape(-1, heads_here, HEAD)
    values_pad = to_pack(values_all, pack_order, margin, BLK).reshape(-1, heads_here, HEAD)
    head_shape = (own_rows, heads_here, HEAD)
    query3 = query_b.reshape(head_shape)
    attended_list = []
    mass_list = []
    for index in range(blocks_here):
        key_first, allowed = query_window(index)
        outputs, masses = forward_block(
            query3[index * BLK : (index + 1) * BLK],
            lax.dynamic_slice_in_dim(keys_pad, key_first, window),
            lax.dynamic_slice_in_dim(values_pad, key_first, window),
            allowed,
        )
        attended_list.append(jnp.transpose(outputs, (1, 0, 2)))
        mass_list.append(masses)
    attended32 = jnp.concatenate(attended_list, axis=0)
    log_mass = jnp.concatenate(mass_list, axis=1)
    attended_b = attended32.reshape(own_rows, head_span).astype(jnp.bfloat16)
    branch = lax.psum_scatter(
        jnp.dot(attended_b, w_out, preferred_element_type=jnp.float32).astype(jnp.bfloat16),
        "tp",
        scatter_dimension=0,
        tiled=True,
    ).astype(jnp.float32) + bias_out.astype(jnp.float32)
    post_attn, back_post = jax.vjp(layer_norm, branch, norm_gains[1], norm_shifts[1])
    hidden = input_f32 + post_attn
    inner, back_inner = jax.vjp(layer_norm, hidden, norm_gains[2], norm_shifts[2])
    inner_all = lax.all_gather(inner.astype(jnp.bfloat16), "tp", axis=0, tiled=True)
    upward = jnp.dot(inner_all, w_up, preferred_element_type=jnp.float32) + bias_up.astype(
        jnp.float32
    )
    active, back_gate = jax.vjp(smooth_gate, upward)
    active_b = active.astype(jnp.bfloat16)
    down = lax.psum_scatter(
        jnp.dot(active_b, w_down, preferred_element_type=jnp.float32).astype(jnp.bfloat16),
        "tp",
        scatter_dimension=0,
        tiled=True,
    ).astype(jnp.float32) + bias_down.astype(jnp.float32)
    final, back_final = jax.vjp(layer_norm, down, norm_gains[3], norm_shifts[3])
    result = (hidden + final).astype(jnp.bfloat16)
    d_down, gain_last, shift_last = back_final(out_grad)
    grad_bias_down = jnp.sum(d_down, axis=0)
    d_down_all = lax.all_gather(d_down.astype(jnp.bfloat16), "tp", axis=0, tiled=True)
    grad_w_down = jnp.einsum("tf,td->fd", active_b, d_down_all, preferred_element_type=jnp.float32)
    d_active = jnp.einsum("td,fd->tf", d_down_all, w_down, preferred_element_type=jnp.float32)
    (d_up,) = back_gate(d_active)
    d_up_b = d_up.astype(jnp.bfloat16)
    grad_bias_up = jnp.sum(d_up_b.astype(jnp.float32), axis=0)
    grad_w_up = jnp.einsum("td,tf->df", inner_all, d_up_b, preferred_element_type=jnp.float32)
    d_inner = lax.psum_scatter(
        jnp.einsum("tf,df->td", d_up_b, w_up, preferred_element_type=jnp.float32).astype(
            jnp.bfloat16
        ),
        "tp",
        scatter_dimension=0,
        tiled=True,
    ).astype(jnp.float32)
    d_hidden_part, gain_third, shift_third = back_inner(d_inner)
    d_hidden = out_grad + d_hidden_part
    d_branch, gain_second, shift_second = back_post(d_hidden)
    grad_bias_out = jnp.sum(d_branch, axis=0)
    d_branch_all = lax.all_gather(d_branch.astype(jnp.bfloat16), "tp", axis=0, tiled=True)
    grad_w_out = jnp.einsum(
        "te,td->ed", attended_b, d_branch_all, preferred_element_type=jnp.float32
    )
    d_att_b = jnp.einsum(
        "td,ed->te", d_branch_all, w_out, preferred_element_type=jnp.float32
    ).astype(jnp.bfloat16)
    d_att3 = d_att_b.reshape(head_shape)
    d_total = jnp.sum(d_att3.astype(jnp.float32) * attended32, axis=2).T
    d_query_list = []
    key_buffer = jnp.zeros((total_rows + 2 * margin, head_span), jnp.float32)
    value_buffer = jnp.zeros((total_rows + 2 * margin, head_span), jnp.float32)
    for index in range(blocks_here):
        key_first, allowed = query_window(index)
        rows = slice(index * BLK, (index + 1) * BLK)
        d_query_h, d_key_h, d_value_h = attention_grads(
            query3[rows],
            d_att3[rows],
            log_mass[:, rows],
            d_total[:, rows],
            lax.dynamic_slice_in_dim(keys_pad, key_first, window),
            lax.dynamic_slice_in_dim(values_pad, key_first, window),
            allowed,
        )
        d_query_list.append(jnp.transpose(d_query_h, (1, 0, 2)))
        key_piece = jnp.transpose(d_key_h, (1, 0, 2)).reshape(window, head_span)
        value_piece = jnp.transpose(d_value_h, (1, 0, 2)).reshape(window, head_span)
        key_buffer = lax.dynamic_update_slice_in_dim(
            key_buffer,
            lax.dynamic_slice_in_dim(key_buffer, key_first, window) + key_piece,
            key_first,
            0,
        )
        value_buffer = lax.dynamic_update_slice_in_dim(
            value_buffer,
            lax.dynamic_slice_in_dim(value_buffer, key_first, window) + value_piece,
            key_first,
            0,
        )
    key_terms = from_pack(key_buffer, placement, margin, BLK, total_rows)
    value_terms = from_pack(value_buffer, placement, margin, BLK, total_rows)
    d_keys, d_values = (
        lax.psum_scatter(
            key_terms.astype(jnp.bfloat16), "seq", scatter_dimension=0, tiled=True
        ).astype(jnp.float32),
        lax.psum_scatter(
            value_terms.astype(jnp.bfloat16), "seq", scatter_dimension=0, tiled=True
        ).astype(jnp.float32),
    )
    d_query = jnp.concatenate(d_query_list, axis=0)
    d_query_b = d_query.reshape(own_rows, head_span).astype(jnp.bfloat16)
    d_keys_b = d_keys.astype(jnp.bfloat16)
    d_values_b = d_values.astype(jnp.bfloat16)
    grad_bias_qv = jnp.stack(
        [
            jnp.sum(d_query_b.astype(jnp.float32), axis=0),
            jnp.sum(d_values_b.astype(jnp.float32), axis=0),
        ]
    )
    d_mixed = jnp.concatenate([d_query_b, d_keys_b, d_values_b], axis=1)
    grad_w_qkv = jnp.einsum(
        "td,tc->dc", rows_all, d_mixed, preferred_element_type=jnp.float32
    ).reshape(model_width, 3, head_span)
    d_normed = lax.psum_scatter(
        jnp.einsum("tc,dc->td", d_mixed, flat_qkv, preferred_element_type=jnp.float32).astype(
            jnp.bfloat16
        ),
        "tp",
        scatter_dimension=0,
        tiled=True,
    ).astype(jnp.float32)
    d_input_part, gain_first, shift_first = back_first(d_normed)
    grad_x = d_hidden + d_input_part
    summed = (
        lax.psum(grad_w_qkv.astype(jnp.bfloat16), "seq").astype(jnp.float32),
        lax.psum(grad_bias_qv.astype(jnp.bfloat16), "seq").astype(jnp.float32),
        lax.psum(grad_w_out.astype(jnp.bfloat16), "seq").astype(jnp.float32),
        lax.psum(grad_w_up.astype(jnp.bfloat16), "seq").astype(jnp.float32),
        lax.psum(grad_bias_up.astype(jnp.bfloat16), "seq").astype(jnp.float32),
        lax.psum(grad_w_down.astype(jnp.bfloat16), "seq").astype(jnp.float32),
    )
    gain_stack = jnp.stack([gain_first, gain_second, gain_third, gain_last])
    shift_stack = jnp.stack([shift_first, shift_second, shift_third, shift_last])
    vectors = lax.psum((gain_stack, shift_stack, grad_bias_out, grad_bias_down), ("seq", "tp"))
    return (
        result,
        grad_x,
        summed[0],
        summed[1],
        summed[2],
        vectors[2],
        summed[3],
        summed[4],
        summed[5],
        vectors[3],
        vectors[0],
        vectors[1],
    )


def solution(mesh):
    placed = (
        P(("seq", "tp"), None),
        P(None, None, "tp"),
        P(None, "tp"),
        P("tp", None),
        P(),
        P(None, "tp"),
        P("tp"),
        P("tp", None),
        P(),
        P(),
        P(),
        P(("seq", "tp"), None),
        P(),
        P(),
        P(),
    )
    seq_count, tp_count = mesh.shape["seq"], mesh.shape["tp"]

    def local(*args):
        tokens_in, w_qkv, placement = args[0], args[1], args[-1]
        heads = w_qkv.shape[2] * tp_count // HEAD
        paired = seq_count * tp_count == 2 * heads == placement.shape[0]
        sizes = (tokens_in.shape[0], w_qkv.shape[0], heads, seq_count, tp_count)
        fast = paired and sizes == (BLK, 1024, 16, 16, 2)
        return (fast_local if fast else general_local)(*args)

    return jax.shard_map(
        local,
        mesh=mesh,
        in_specs=placed,
        out_specs=(
            P(("seq", "tp"), None),
            P(("seq", "tp"), None),
            P(None, None, "tp"),
            P(None, "tp"),
            P("tp", None),
            P(),
            P(None, "tp"),
            P("tp"),
            P("tp", None),
            P(),
            P(),
            P(),
        ),
        check_vma=False,
    )
```

```python
import functools

import jax
import jax.numpy as jnp
from jax import lax
from jax.experimental import pallas as pl
from jax.experimental.pallas import tpu as pltpu
from jax.sharding import PartitionSpec as P

HEAD = 64
BLK = 512
HALF = BLK // 2
QUART = BLK // 4
LONGEST = 4096
STEP_F = 1024
STEP_B = 512
UNROLL = 4
CHUNK_ROWS = 256
FIRST_TICKS = 6
SLACK = 1
VMEM_LIMIT = 58 << 20
VMEM_MIDDLE = 62 << 20

EPS = 1e-05
F32 = jnp.float32
BF16 = jnp.bfloat16
MESH = pl.DeviceIdType.MESH


def layer_norm(row_block, gain_row, shift_row):
    row_mean = jnp.mean(row_block, axis=-1, keepdims=True)
    centred = row_block - row_mean
    spread = jnp.mean(centred * centred, axis=-1, keepdims=True)
    return centred * lax.rsqrt(spread + EPS) * gain_row + shift_row


def smooth_gate(values):
    return jax.nn.gelu(values, approximate=True)


def running_ends(lengths):
    count = lengths.shape[0]
    index = jnp.arange(count, dtype=jnp.int32)
    return jnp.sum(jnp.where(index[None, :] <= index[:, None], lengths[None, :], 0), axis=1)


def inverse_order(placement):
    index = jnp.arange(placement.shape[0], dtype=jnp.int32)
    return jnp.sum(jnp.where(placement[None, :] == index[:, None], index[None, :], 0), axis=1)


def block_tables(lengths, prefixes, placement, part):
    ends = running_ends(lengths)
    starts = ends - lengths
    limits = starts + prefixes
    offset = part * HALF + jnp.arange(HALF, dtype=jnp.int32)
    pos = placement[:, None] * BLK + offset[None, :]
    inside = (pos[:, :, None] >= starts) & (pos[:, :, None] < ends)

    def pick(values):
        return jnp.sum(jnp.where(inside, values, 0), axis=2)

    low = pick(starts)
    high = jnp.minimum(pick(ends), jnp.maximum(pos + 1, pick(limits)))
    table = jnp.stack(
        [
            jnp.min(low, axis=1) // HALF,
            (jnp.max(high, axis=1) - 1) // HALF + 1,
            jnp.max(low, axis=1),
            jnp.min(high, axis=1),
            placement,
        ]
    )
    return low[:, None, :], high[:, None, :], table


def unpack_t(packed):
    turned = packed.astype(F32).T
    return jnp.concatenate([turned[:HEAD], turned[HEAD:]], axis=1)


def pack_t(turned):
    return jnp.concatenate([turned[:, :QUART], turned[:, QUART:]], axis=0).T


def pieces(tab, b, keys, step, start):
    count = keys // HALF
    first = tab[0, b]

    def visit(i, state):
        at = pl.multiple_of((first + i * count) * HALF, HALF)
        whole = (at >= tab[2, b]) & (at + keys <= tab[3, b])
        return lax.cond(whole, lambda st: step(at, st, False), lambda st: step(at, st, True), state)

    return lax.fori_loop(0, (tab[1, b] - first + count - 1) // count, visit, start)


def attend_kernel(
    part_ref, tab, low_ref, high_ref, q_ref, own_ref, sib_ref,
    out_ref, ot_ref, lse_ref, kv, kvt, rhs_s,
):
    part = part_ref[0]
    scale = HEAD**-0.5
    blocks = q_ref.shape[0]
    rows = blocks * BLK
    depth = lax.broadcasted_iota(jnp.int32, (STEP_F, HALF), 0)

    def prepare(b, carry):
        for ref, which in ((own_ref, part), (sib_ref, 1 - part)):
            at = pl.multiple_of(tab[4, b] * BLK + which * HALF, HALF)
            piece = ref[b]
            kv[pl.ds(at, HALF), :] = piece
            kvt[:, pl.ds(at, HALF)] = piece.T
        qt = unpack_t(q_ref[b]) * scale
        rhs_s[b] = jnp.concatenate([qt, jnp.zeros_like(qt)], axis=0).astype(BF16)
        return carry

    lax.fori_loop(0, blocks, prepare, 0, unroll=UNROLL)
    kv[rows:, :] = jnp.zeros((kv.shape[0] - rows, 2 * HEAD), BF16)
    kvt[:, rows:] = jnp.zeros((2 * HEAD, kv.shape[0] - rows), BF16)

    def one(b, carry):
        low, high = low_ref[b], high_ref[b]

        def step(at, state, masked):
            top, total, acc = state
            sc = jnp.dot(kv[pl.ds(at, STEP_F), :], rhs_s[b], preferred_element_type=F32)
            if masked:
                sc = jnp.where((depth >= low - at) & (depth < high - at), sc, -1e30)
            new = jnp.maximum(top, jnp.max(sc, axis=0, keepdims=True))
            alpha = jnp.exp(top - new)
            pr = jnp.exp(sc - new)
            total = total * alpha + jnp.sum(pr, axis=0, keepdims=True)
            acc = acc * alpha + jnp.dot(
                kvt[HEAD:, pl.ds(at, STEP_F)], pr.astype(BF16), preferred_element_type=F32
            )
            return new, total, acc

        start = (
            jnp.full((1, HALF), -1e30, F32),
            jnp.zeros((1, HALF), F32),
            jnp.zeros((HEAD, HALF), F32),
        )
        top, total, acc = pieces(tab, b, STEP_F, step, start)
        ot_ref[b] = acc * (1.0 / total)
        lse_ref[b] = top + jnp.log(total)
        return carry

    lax.fori_loop(0, blocks, one, 0)

    def finish(b, carry):
        out_ref[b] = pack_t(ot_ref[b]).astype(BF16)
        return carry

    lax.fori_loop(0, blocks, finish, 0, unroll=UNROLL)


def attend_back_kernel(
    part_ref, tab, low_ref, high_ref, q_ref, da_ref, ot_ref, lse_ref, kv, kvt,
    dq_ref, mine_ref, theirs_ref, dkv, rhs_s, rows_s, total_s, dqt_s,
):
    part = part_ref[0]
    scale = HEAD**-0.5
    blocks = q_ref.shape[0]
    depth = lax.broadcasted_iota(jnp.int32, (STEP_B, HALF), 0)
    lane = lax.broadcasted_iota(jnp.int32, (HALF, 2 * HEAD), 1)

    def prepare(b, carry):
        dkv[pl.ds(pl.multiple_of(b * BLK, BLK), BLK), :] = jnp.zeros((BLK, 2 * HEAD), F32)
        qt = unpack_t(q_ref[b]) * scale
        dat = unpack_t(da_ref[b])
        blank = jnp.zeros_like(qt)
        rhs_s[b, :, :HALF] = jnp.concatenate([qt, blank], axis=0).astype(BF16)
        rhs_s[b, :, HALF:] = jnp.concatenate([blank, dat], axis=0).astype(BF16)
        both = jnp.concatenate([qt, dat], axis=0).T
        rows_s[b, :HALF, :] = jnp.where(lane < HEAD, both, 0.0).astype(BF16)
        rows_s[b, HALF:, :] = jnp.where(lane < HEAD, 0.0, both).astype(BF16)
        total_s[b] = jnp.sum(dat * ot_ref[b], axis=0, keepdims=True)
        return carry

    lax.fori_loop(0, blocks, prepare, 0, unroll=UNROLL)
    dkv[blocks * BLK :, :] = jnp.zeros((dkv.shape[0] - blocks * BLK, 2 * HEAD), F32)

    def one(b, carry):
        total = total_s[b]
        lse = lse_ref[b]
        low, high = low_ref[b], high_ref[b]

        def step(at, acc, masked):
            keys = kv[pl.ds(at, STEP_B), :]
            sc = jnp.dot(keys, rhs_s[b, :, :HALF], preferred_element_type=F32)
            dp = jnp.dot(keys, rhs_s[b, :, HALF:], preferred_element_type=F32)
            if masked:
                sc = jnp.where((depth >= low - at) & (depth < high - at), sc, -1e30)
            pr = jnp.exp(sc - lse)
            ds = (pr * (dp - total)).astype(BF16)
            dkv[pl.ds(at, STEP_B), :] += jnp.dot(
                ds, rows_s[b, :HALF, :], preferred_element_type=F32
            ) + jnp.dot(pr.astype(BF16), rows_s[b, HALF:, :], preferred_element_type=F32)
            return acc + jnp.dot(kvt[:HEAD, pl.ds(at, STEP_B)], ds, preferred_element_type=F32)

        dqt_s[b] = pieces(tab, b, STEP_B, step, jnp.zeros((HEAD, HALF), F32))
        return carry

    lax.fori_loop(0, blocks, one, 0)

    def finish(b, carry):
        dq_ref[b] = pack_t(dqt_s[b] * scale).astype(BF16)
        base = tab[4, b] * BLK
        mine_ref[b] = dkv[pl.ds(pl.multiple_of(base + part * HALF, HALF), HALF), :].astype(BF16)
        theirs_ref[b] = dkv[pl.ds(pl.multiple_of(base + (1 - part) * HALF, HALF), HALF), :].astype(BF16)
        return carry

    lax.fori_loop(0, blocks, finish, 0, unroll=UNROLL)


def vmem(count):
    return [pl.BlockSpec(memory_space=pltpu.VMEM)] * count


def smem(count):
    return [pl.BlockSpec(memory_space=pltpu.SMEM)] * count


def attend(part, tables, q_chunks, kv_own, kv_sib):
    low, high, table = tables
    blocks = q_chunks.shape[0]
    rows = blocks * BLK + STEP_F
    return pl.pallas_call(
        attend_kernel,
        out_shape=(
            jax.ShapeDtypeStruct((blocks, QUART, 2 * HEAD), BF16),
            jax.ShapeDtypeStruct((blocks, HEAD, HALF), F32),
            jax.ShapeDtypeStruct((blocks, 1, HALF), F32),
            jax.ShapeDtypeStruct((rows, 2 * HEAD), BF16),
            jax.ShapeDtypeStruct((2 * HEAD, rows), BF16),
        ),
        in_specs=smem(2) + vmem(5),
        out_specs=tuple(vmem(5)),
        scratch_shapes=[pltpu.VMEM((blocks, 2 * HEAD, HALF), BF16)],
        compiler_params=pltpu.CompilerParams(vmem_limit_bytes=VMEM_LIMIT),
        cost_estimate=pl.CostEstimate(
            flops=40 * 10**9, bytes_accessed=20 << 20, transcendentals=blocks * 4 * BLK * HALF
        ),
        name="attend",
    )(part.reshape(1), table, low, high, q_chunks, kv_own, kv_sib)


def attend_back(part, tables, q_chunks, da_chunks, out_t, mass, kv, kvt):
    low, high, table = tables
    blocks = q_chunks.shape[0]
    return pl.pallas_call(
        attend_back_kernel,
        out_shape=(
            jax.ShapeDtypeStruct((blocks, QUART, 2 * HEAD), BF16),
            jax.ShapeDtypeStruct((blocks, HALF, 2 * HEAD), BF16),
            jax.ShapeDtypeStruct((blocks, HALF, 2 * HEAD), BF16),
        ),
        in_specs=smem(2) + vmem(8),
        out_specs=tuple(vmem(3)),
        scratch_shapes=[
            pltpu.VMEM((blocks * BLK + STEP_F, 2 * HEAD), F32),
            pltpu.VMEM((blocks, 2 * HEAD, BLK), BF16),
            pltpu.VMEM((blocks, BLK, 2 * HEAD), BF16),
            pltpu.VMEM((blocks, 1, HALF), F32),
            pltpu.VMEM((blocks, HEAD, HALF), F32),
        ],
        compiler_params=pltpu.CompilerParams(vmem_limit_bytes=VMEM_LIMIT),
        cost_estimate=pl.CostEstimate(
            flops=60 * 10**9, bytes_accessed=30 << 20, transcendentals=blocks * 4 * BLK * HALF
        ),
        name="attend_back",
    )(part.reshape(1), table, low, high, q_chunks, da_chunks, out_t, mass, kv, kvt)


def chunk_of(who, quarter, index, half):
    absolute = (who[0] * 2 + who[1]) ^ quarter
    tp, sub = absolute // 2, absolute % 2
    return ((sub * 4 + index) * 2 + half) * 2 + tp


def swap_lanes(values):
    return pltpu.roll(values, HEAD, 1)


def low_lanes(rows):
    return lax.broadcasted_iota(jnp.int32, (rows, 2 * HEAD), 1) < HEAD


def store_packed(who, quarter, values, out_ref):
    low = low_lanes(QUART)
    for pair in range(2):
        for half in range(2):
            top = half * HALF
            lanes = slice(pair * 128, pair * 128 + 128)
            first, second = values[top : top + QUART, lanes], values[top + QUART : top + HALF, lanes]
            even = jnp.where(low, first, swap_lanes(second))
            odd = jnp.where(low, swap_lanes(first), second)
            out_ref[chunk_of(who, quarter, 2 * pair, half)] = even.astype(BF16)
            out_ref[chunk_of(who, quarter, 2 * pair + 1, half)] = odd.astype(BF16)


def load_packed(who, quarter, ref, out_ref, base):
    low = low_lanes(QUART)
    for pair in range(2):
        for half in range(2):
            even = ref[chunk_of(who, quarter, 2 * pair, half)].astype(F32)
            odd = ref[chunk_of(who, quarter, 2 * pair + 1, half)].astype(F32)
            top = half * HALF
            lanes = slice(base + pair * 128, base + pair * 128 + 128)
            out_ref[top : top + QUART, lanes] = jnp.where(low, even, swap_lanes(odd)).astype(BF16)
            out_ref[top + QUART : top + HALF, lanes] = jnp.where(low, swap_lanes(even), odd).astype(BF16)


class Place:
    def __init__(self):
        self.seq, self.tp = lax.axis_index("seq"), lax.axis_index("tp")
        self.x = lax.rem(self.seq // 2, 2)
        self.z = self.seq // 4
        self.core_partner = (self.seq ^ 1, self.tp)
        self.x_partner = (self.seq ^ 2, self.tp)
        self.z_partners = [(self.seq ^ (4 * d), self.tp) for d in (1, 2)]
        self.tp_partner = (self.seq, self.tp ^ 1)


def greet_all(count, me, seq, tp):
    barrier = pltpu.get_barrier_semaphore()

    def one(k, carry):
        other = lax.rem(me + k, count)
        pl.semaphore_signal(
            barrier, inc=1, device_id=(other // 2, lax.rem(other, 2)), device_id_type=MESH
        )
        return carry

    lax.fori_loop(1, count, one, 0)
    pl.semaphore_wait(barrier, count - 1)


def greet(partners):
    barrier = pltpu.get_barrier_semaphore()
    for partner in partners:
        pl.semaphore_signal(barrier, inc=1, device_id=partner, device_id_type=MESH)
    pl.semaphore_wait(barrier, len(partners))


def remote(src, dst, send, recv, device):
    return pltpu.make_async_remote_copy(
        src_ref=src, dst_ref=dst, send_sem=send, recv_sem=recv, device_id=device, device_id_type=MESH
    )


def chunk_copy(count, me, k, src, dst, send, recv):
    other = lax.rem(me + k, count)
    return remote(src.at[other], dst.at[me], send.at[k], recv.at[k], (other // 2, lax.rem(other, 2)))


def rows_at(start, size):
    return pl.ds(pl.multiple_of(start, size), size)


def reduce_stages(place, chunks, base, out, both, kept, xbuf, xsum, zbuf, zsum, fbuf, sems, arrived):
    rows = base.shape[0] // chunks
    half, piece = rows // 2, rows // 8
    x, odd, upper = place.x, lax.rem(place.z, 2), place.z // 2
    pair = half // 2

    def x_copy(k):
        return remote(
            base.at[rows_at(k * rows + (1 - x) * half, half)], xbuf.at[rows_at(k * half, half)],
            sems["xs"].at[k], sems["xr"].at[k], place.x_partner,
        )

    def z_copy(k):
        return remote(
            xsum.at[rows_at(k * half + (1 - odd) * pair, pair)], zbuf.at[rows_at(k * pair, pair)],
            sems["zs"].at[0, k], sems["zr"].at[0, k], place.z_partners[0],
        )

    def far_z_copy(k):
        return remote(
            zsum.at[rows_at(k * pair + (1 - upper) * piece, piece)], fbuf.at[rows_at(k * piece, piece)],
            sems["zs"].at[1, k], sems["zr"].at[1, k], place.z_partners[1],
        )

    def own_pair(k):
        return rows_at(k * rows + x * half + odd * pair, pair)

    def own_piece(k):
        return rows_at(k * rows + x * half + odd * pair + upper * piece, piece)

    def far_zg_copy(k):
        return remote(
            out.at[own_piece(k)], out.at[own_piece(k)],
            sems["zgs"].at[1, k], sems["zgr"].at[1, k], place.z_partners[1],
        )

    def zg_copy(k):
        return remote(
            out.at[own_pair(k)], out.at[own_pair(k)],
            sems["zgs"].at[0, k], sems["zgr"].at[0, k], place.z_partners[0],
        )

    def xg_copy(k):
        span = rows_at(k * rows + x * half, half)
        return remote(out.at[span], out.at[span], sems["xgs"].at[k], sems["xgr"].at[k], place.x_partner)

    def core_copy(k):
        span = rows_at(k * rows, rows)
        return remote(out.at[span], both.at[1, span], sems["cs"].at[k], sems["cr"].at[k], place.core_partner)

    def stage_x(k):
        arrived(k)
        x_copy(k).start()

    def stage_z(k):
        x_copy(k).wait_recv()
        mine = base[rows_at(k * rows + x * half, half), :].astype(F32)
        xsum[rows_at(k * half, half), :] = (
            mine + xbuf[rows_at(k * half, half), :].astype(F32)
        ).astype(BF16)
        z_copy(k).start()

    def stage_far_z(k):
        z_copy(k).wait_recv()
        span = rows_at(k * pair, pair)
        zsum[span, :] = (
            xsum[rows_at(k * half + odd * pair, pair), :].astype(F32) + zbuf[span, :].astype(F32)
        ).astype(BF16)
        far_z_copy(k).start()

    def stage_far_zg(k):
        far_z_copy(k).wait_recv()
        out[own_piece(k), :] = (
            zsum[rows_at(k * pair + upper * piece, piece), :].astype(F32)
            + fbuf[rows_at(k * piece, piece), :].astype(F32)
        ).astype(BF16)
        far_zg_copy(k).start()

    def stage_zg(k):
        far_zg_copy(k).wait_recv()
        zg_copy(k).start()

    def stage_xg(k):
        zg_copy(k).wait_recv()
        xg_copy(k).start()

    def stage_core(k):
        xg_copy(k).wait_recv()
        core_copy(k).start()

    stages = [stage_x, stage_z, stage_far_z, stage_far_zg, stage_zg, stage_xg, stage_core]

    def tick(t):
        for s, stage in reversed(list(enumerate(stages))):
            k = t - SLACK * s

            @pl.when((k >= 0) & (k < chunks))
            def _():
                stage(k)

    def drain(k, carry):
        for copy in (x_copy, z_copy, far_z_copy, far_zg_copy, zg_copy, xg_copy):
            copy(k).wait_send()
        core_copy(k).wait()
        return carry

    def finale():
        keep = pltpu.make_async_copy(out, both.at[0], kept)
        keep.start()
        lax.fori_loop(0, chunks, drain, 0)
        keep.wait()

    return tick, finale, chunks + SLACK * (len(stages) - 1)


SEM_NAMES = ("xs", "xr", "zs", "zr", "zgs", "zgr", "xgs", "xgr", "cs", "cr")
VECTOR_STEPS = 5


def finish_kernel(
    chunks, first_ticks, gain_ref, dq_ref, mine_ref, theirs_ref, near_ref, far_up_ref, far_ref,
    normed_ref, normed_sib_ref, x_ref, dh_ref, w_ref, w2, w3, vec_ref,
    both, gx_ref, vec_out,
    out, base, far, ybuf, xbuf, xsum, zbuf, zsum, fbuf, dq_in, dkv_in, dkv_st, dkv_sib, mixed, mixed_sib,
    normed, normed_sib, x_s, w_s, slots, *rest,
):
    place = Place()
    count = dq_ref.shape[0]
    me = place.seq * 2 + place.tp
    who = (place.tp, lax.rem(place.seq, 2))
    sems = dict(zip(SEM_NAMES, rest))
    qs, qr, ks, kr, ys, yr, ms, mr, vs, vr, loc = rest[len(SEM_NAMES) :]
    rows = base.shape[0] // chunks
    early = near_ref.shape[0]
    crossed = far_up_ref.shape[0] // rows
    greet_all(count, me, place.seq, place.tp)
    dkv_pair = remote(theirs_ref, dkv_sib, ms.at[2], mr.at[2], place.core_partner)
    dkv_pair.start()
    mine_copy = pltpu.make_async_copy(mine_ref, dkv_st, loc.at[0])
    mine_copy.start()

    def dq_copy(k):
        return chunk_copy(count, me, k, dq_ref, dq_in, qs, qr)

    def dkv_copy(k):
        return chunk_copy(count, me, k, dkv_st, dkv_in, ks, kr)

    def start_q(k, carry):
        dq_copy(k).start()
        return carry

    lax.fori_loop(1, count, start_q, 0)
    near_copy = pltpu.make_async_copy(near_ref, base.at[pl.ds(0, early)], loc.at[1])
    near_copy.start()
    far_copy = pltpu.make_async_copy(far_up_ref, ybuf.at[pl.ds(0, far_up_ref.shape[0])], loc.at[2])
    far_copy.start()
    locals_ = [(dq_ref.at[me], dq_in.at[me]), (normed_ref, normed), (normed_sib_ref, normed_sib)]
    locals_ += [(x_ref, x_s), (dh_ref, gx_ref)]
    col = w_s.shape[3]
    halves = [w_ref.at[:, :, rows_at(c * col, col)] for c in (who[1], 1 - who[1])]
    locals_ += [(w, w_s.at[r]) for r, w in enumerate(halves + [w2, w3])]
    locals_ = [pltpu.make_async_copy(src, dst, loc.at[3 + i]) for i, (src, dst) in enumerate(locals_)]

    def tp_copy(k, src, first):
        return remote(
            src.at[rows_at((k - first) * rows, rows)], ybuf.at[rows_at(k * rows, rows)],
            ys.at[k], yr.at[k], place.tp_partner,
        )

    def cross(k, carry):
        tp_copy(k, far_ref, crossed).start()
        return carry

    settled = early // rows
    lax.fori_loop(crossed, settled, cross, 0)
    mine_copy.wait()
    dkv_pair.wait()

    def add(b, carry):
        dkv_st[b] = (dkv_st[b].astype(F32) + dkv_sib[b].astype(F32)).astype(BF16)
        return carry

    lax.fori_loop(0, count, add, 0)

    def start_kv(k, carry):
        dkv_copy(k).start()
        return carry

    lax.fori_loop(1, count, start_kv, 0)
    dkv_in[me] = dkv_st[me]
    near_copy.wait()
    far_copy.wait()
    for copy in locals_:
        copy.start()

    def arrived(k):
        @pl.when(k >= crossed)
        def _():
            tp_copy(k, base, 0).wait_recv()

        span = rows_at(k * rows, rows)
        base[span, :] = (base[span, :].astype(F32) + ybuf[span, :].astype(F32)).astype(BF16)

    tick, drain, ticks = reduce_stages(
        place, chunks, base, out, both, loc.at[12], xbuf, xsum, zbuf, zsum, fbuf, sems, arrived
    )

    def plain(t, carry):
        tick(t)
        return carry

    lax.fori_loop(0, first_ticks, plain, 0)

    def wait(k, carry):
        dq_copy(k).wait()
        dkv_copy(k).wait()
        return carry

    lax.fori_loop(1, count, wait, 0)
    for copy in locals_:
        copy.wait()
    vec_out[...] = vec_ref[...]
    low = low_lanes(HALF)
    for quarter in range(4):
        load_packed(who, quarter, dq_in, mixed.at[quarter], 0)
        for pair in range(2):
            for half in range(2):
                span = slice(half * HALF, half * HALF + HALF)
                even = dkv_in[chunk_of(who, quarter, 2 * pair, half)].astype(F32)
                odd = dkv_in[chunk_of(who, quarter, 2 * pair + 1, half)].astype(F32)
                k_at = 256 + pair * 128
                mixed[quarter, span, k_at : k_at + 128] = jnp.where(low, even, swap_lanes(odd)).astype(BF16)
                mixed[quarter, span, k_at + 256 : k_at + 384] = jnp.where(low, swap_lanes(even), odd).astype(BF16)
    mixed_copies = [
        remote(mixed.at[2 * i + 1], mixed_sib.at[i], ms.at[i], mr.at[i], place.core_partner)
        for i in range(2)
    ]
    for copy in mixed_copies:
        copy.start()
    tick(first_ticks)

    for quarter in range(4):
        absolute = (who[0] * 2 + who[1]) ^ quarter
        lanes = pl.ds(pl.multiple_of(absolute * 256, 256), 256)
        for row, left in ((10, 0), (11, 512)):
            vec_out[row : row + 1, lanes] = jnp.sum(
                mixed[quarter, :, left : left + 256].astype(F32), axis=0, keepdims=True
            )
    gains = jnp.zeros((1, base.shape[1]), F32)
    shifts = jnp.zeros((1, base.shape[1]), F32)
    for part in range(2):
        span = slice(part * HALF, part * HALF + HALF)
        d_normed = jnp.zeros((HALF, base.shape[1]), F32)
        for quarter in range(4):
            for which in range(3):
                lanes = slice(which * col, which * col + col)
                d_normed += dot_nt(mixed[quarter, span, lanes], w_s[quarter, which])
        xhat, rstd = norm_parts(x_s[span, :].astype(F32))
        e = d_normed * gain_ref[0:1, :]
        grad = rstd * (
            e
            - jnp.mean(e, axis=-1, keepdims=True)
            - xhat * jnp.mean(e * xhat, axis=-1, keepdims=True)
        )
        gx_ref[span, :] += grad
        gains += jnp.sum(d_normed * xhat, axis=0, keepdims=True)
        shifts += jnp.sum(d_normed, axis=0, keepdims=True)
        tick(first_ticks + 1 + part)
    vec_out[0:1, :] = gains
    vec_out[4:5, :] = shifts

    for copy in mixed_copies:
        copy.wait()
    late = pl.ds(early, base.shape[0] - early)
    for i, target in ((1, far), (0, base.at[late])):
        for row in range(0, target.shape[0], 256):
            span = slice(row, row + 256)
            target[span, :] = (
                lax.dot_general(
                    mixed[2 * i, :, span], normed[...], (((0,), (0,)), ((), ())), preferred_element_type=F32
                )
                + lax.dot_general(
                    mixed_sib[i, :, span], normed_sib[...], (((0,), (0,)), ((), ())),
                    preferred_element_type=F32,
                )
            ).astype(BF16)
            if i == 1:
                for k in range(settled + row // rows, settled + (row + 256) // rows):
                    tp_copy(k, far, settled).start()

    partners = [place.core_partner, place.tp_partner, place.x_partner] + [
        (place.seq ^ bit, place.tp) for bit in (4, 8)
    ]

    def vector_step(step):
        slots[step] = vec_out[...]
        copy = remote(
            slots.at[step], slots.at[VECTOR_STEPS + step], vs.at[step], vr.at[step], partners[step]
        )
        copy.start()
        copy.wait()
        vec_out[...] += slots[VECTOR_STEPS + step]

    def last(t, carry):
        tick(t)
        for step in range(VECTOR_STEPS):
            @pl.when(t == first_ticks + 3 + step)
            def _():
                vector_step(step)
        return carry

    lax.fori_loop(first_ticks + 3, ticks, last, 0)

    def sent(k, carry):
        tp_copy(k, base, 0).wait_send()
        return carry

    lax.fori_loop(crossed, chunks, sent, 0)
    drain()


def finish(gain, dq_chunks, mine, theirs, near, far_up, far, normed, normed_sib, x, d_hidden, weights, vectors):
    early, cols = near.shape
    late = 3 * weights[1].shape[2]
    total = early + late
    chunks = total // CHUNK_ROWS
    count = dq_chunks.shape[0]
    rows = x.shape[0]
    dma = pltpu.SemaphoreType.DMA
    anywhere = pl.BlockSpec(memory_space=pl.ANY)
    scratch = [
        pltpu.VMEM((total, cols), BF16),
        pltpu.VMEM((total, cols), BF16),
        pltpu.VMEM((late, cols), BF16),
        pltpu.VMEM((total, cols), BF16),
        pltpu.VMEM((total // 2, cols), BF16),
        pltpu.VMEM((total // 2, cols), BF16),
        pltpu.VMEM((total // 4, cols), BF16),
        pltpu.VMEM((total // 4, cols), BF16),
        pltpu.VMEM((total // 8, cols), BF16),
        pltpu.VMEM(dq_chunks.shape, BF16),
        pltpu.VMEM(mine.shape, BF16),
        pltpu.VMEM(mine.shape, BF16),
        pltpu.VMEM(mine.shape, BF16),
        pltpu.VMEM((4, rows, late), BF16),
        pltpu.VMEM((2, rows, late), BF16),
        pltpu.VMEM((rows, cols), BF16),
        pltpu.VMEM((rows, cols), BF16),
        pltpu.VMEM((rows, cols), BF16),
        pltpu.VMEM((4,) + weights[1].shape, BF16),
        pltpu.VMEM((2 * VECTOR_STEPS,) + vectors.shape, F32),
    ]
    scratch += [dma((2, chunks) if name[0] == "z" else (chunks,)) for name in SEM_NAMES]
    scratch += [dma((count,))] * 4 + [dma((chunks,))] * 2 + [dma((3,))] * 2
    scratch += [dma((VECTOR_STEPS,))] * 2 + [dma((13,))]
    return pl.pallas_call(
        functools.partial(finish_kernel, chunks, FIRST_TICKS),
        out_shape=(
            jax.ShapeDtypeStruct((2, total, cols), BF16),
            jax.ShapeDtypeStruct((rows, cols), F32),
            jax.ShapeDtypeStruct(vectors.shape, F32),
        ),
        in_specs=vmem(1) + [anywhere] * 13 + vmem(1),
        out_specs=(anywhere, vmem(1)[0], vmem(1)[0]),
        scratch_shapes=scratch,
        compiler_params=pltpu.CompilerParams(
            collective_id=1, has_side_effects=True, vmem_limit_bytes=VMEM_MIDDLE
        ),
        name="finish",
    )(
        gain, dq_chunks, mine, theirs, near, far_up, far, normed, normed_sib, x, d_hidden, *weights, vectors
    )


def join_kernel(core_ref, in_ref, out_ref):
    out_ref[...] = in_ref[0].astype(F32)


def join_turned_kernel(core_ref, in_ref, out_ref):
    out_ref[0] = in_ref[0].astype(F32).T


def join(core, both, size, first, count, shape, place, turned=False):
    cols = both.shape[2]
    block = (1, cols, size) if turned else (size, cols)
    return pl.pallas_call(
        join_turned_kernel if turned else join_kernel,
        grid_spec=pltpu.PrefetchScalarGridSpec(
            num_scalar_prefetch=1,
            grid=(2, count),
            in_specs=[pl.BlockSpec((1, size, cols), lambda p, i, c: ((p + c[0]) % 2, first + i, 0))],
            out_specs=pl.BlockSpec(block, lambda p, i, c: place(p, i)),
        ),
        out_shape=jax.ShapeDtypeStruct(shape, F32),
        compiler_params=pltpu.CompilerParams(vmem_limit_bytes=VMEM_LIMIT),
        name="join",
    )(core.reshape(1).astype(jnp.int32), both)


def begin_kernel(
    x_ref, gain_ref, shift_ref, bias_ref, w_ref, wo_ref,
    normed_ref, normed_sib, q_in, kv_own, kv_sib, bias_far, w2, w3, wo2, wo3,
    w0, w1, q_st, kv_st, *sems,
):
    place = Place()
    count = q_in.shape[0]
    width = x_ref.shape[1]
    me = place.seq * 2 + place.tp
    who = (place.tp, lax.rem(place.seq, 2))
    ks, kr, qs, qr, fs, fr, ws, wr, ls = sems
    greet_all(count, me, place.seq, place.tp)
    core = who[1]
    col, wo_rows = w0.shape[2], wo2.shape[0]
    w_own = w_ref.at[:, :, rows_at(core * col, col)]
    w_far = remote(w_own, w2, ws.at[0], wr.at[0], place.tp_partner)
    w_far.start()
    bias_pair = remote(bias_ref, bias_far, ws.at[5], wr.at[5], place.tp_partner)
    bias_pair.start()
    w_loads = [
        pltpu.make_async_copy(w_own, w0, ls.at[0]),
        pltpu.make_async_copy(w_ref.at[:, :, rows_at((1 - core) * col, col)], w1, ls.at[1]),
    ]
    for copy in w_loads:
        copy.start()
    wo_far = remote(wo_ref.at[rows_at(core * wo_rows, wo_rows)], wo2, ws.at[1], wr.at[1], place.tp_partner)
    wo_far.start()
    w_last = remote(w2, w3, ws.at[2], wr.at[2], place.core_partner)
    wo_last = remote(wo2, wo3, ws.at[3], wr.at[3], place.core_partner)

    def norm(part, carry):
        span = rows_at(part * 64, 64)
        normed_ref[span, :] = layer_norm(
            x_ref[span, :].astype(F32), gain_ref[0:1, :], shift_ref[0:1, :]
        ).astype(BF16)
        return carry

    lax.fori_loop(0, x_ref.shape[0] // 64, norm, 0)

    normed_pair = remote(normed_ref, normed_sib, ws.at[4], wr.at[4], place.core_partner)
    normed_pair.start()

    def kv_copy(other):
        return remote(kv_st.at[other], kv_own.at[me], ks.at[other], kr.at[me], (other // 2, lax.rem(other, 2)))

    def q_copy(other):
        return remote(q_st.at[other], q_in.at[me], qs.at[other], qr.at[me], (other // 2, lax.rem(other, 2)))

    def kv_came(other):
        return remote(kv_st.at[other], kv_own.at[other], ks.at[other], kr.at[other], (other // 2, lax.rem(other, 2)))

    def q_came(other):
        return remote(q_st.at[other], q_in.at[other], qs.at[other], qr.at[other], (other // 2, lax.rem(other, 2)))

    def forward(other):
        return remote(kv_own.at[other], kv_sib.at[other], fs.at[other], fr.at[other], place.core_partner)

    low = low_lanes(HALF)

    def project(quarter, w):
        bias = bias_ref if quarter < 2 else bias_far
        side = core if quarter % 2 == 0 else 1 - core

        def bias_at(which):
            return bias[2:3, rows_at(which * 2 * col + side * col, col)]

        def dot(which):
            return dot_nn(normed_ref[...], w[which])

        keys, values = dot(1), dot(2) + bias_at(1)
        for pair in range(2):
            lanes = slice(pair * 128, pair * 128 + 128)
            for half in range(2):
                rows = slice(half * HALF, half * HALF + HALF)
                k, v = keys[rows, lanes], values[rows, lanes]
                kv_st[chunk_of(who, quarter, 2 * pair, half)] = jnp.where(low, k, swap_lanes(v)).astype(BF16)
                kv_st[chunk_of(who, quarter, 2 * pair + 1, half)] = jnp.where(low, swap_lanes(k), v).astype(BF16)
        store_packed(who, quarter, dot(0) + bias_at(0), q_st)

        def send(i, carry):
            other = chunk_of(who, quarter, i // 2, lax.rem(i, 2))

            @pl.when(other != me)
            def _():
                kv_copy(other).start()
                q_copy(other).start()

            @pl.when(other == me)
            def _():
                kv_own[me] = kv_st[me]
                q_in[me] = q_st[me]

            return carry

        lax.fori_loop(0, 8, send, 0)

    for copy in w_loads:
        copy.wait()
    project(0, w0)
    project(1, w1)
    w_far.wait()
    bias_pair.wait()
    w_last.start()
    project(2, w2)
    w_last.wait()
    project(3, w3)
    wo_far.wait()
    wo_last.start()
    forward(me).start()

    def receive(i, carry):
        other = lax.rem(place.seq + lax.rem(i, count // 2), count // 2) * 2 + lax.rem(
            place.tp + i // (count // 2), 2
        )
        kv_came(other).wait_recv()
        forward(other).start()
        return carry

    lax.fori_loop(1, count, receive, 0)

    def rest(k, carry):
        other = lax.rem(me + k, count)
        q_came(other).wait_recv()
        kv_copy(other).wait_send()
        q_copy(other).wait_send()
        return carry

    lax.fori_loop(1, count, rest, 0)

    def forwarded(k, carry):
        forward(k).wait()
        return carry

    lax.fori_loop(0, count, forwarded, 0)
    wo_last.wait()
    normed_pair.wait()


def begin(x, gains, shifts, bias, w, wo):
    rows, width = x.shape
    count = 32
    dma = pltpu.SemaphoreType.DMA
    anywhere = pl.BlockSpec(memory_space=pl.ANY)
    q_shape, kv_shape = (count, QUART, 2 * HEAD), (count, HALF, 2 * HEAD)
    w_quarter = (3, width, w.shape[2] // 2)
    wo_quarter = (wo.shape[0] // 2, wo.shape[1])
    return pl.pallas_call(
        begin_kernel,
        out_shape=(
            jax.ShapeDtypeStruct((rows, width), BF16),
            jax.ShapeDtypeStruct((rows, width), BF16),
            jax.ShapeDtypeStruct(q_shape, BF16),
            jax.ShapeDtypeStruct(kv_shape, BF16),
            jax.ShapeDtypeStruct(kv_shape, BF16),
            jax.ShapeDtypeStruct(bias.shape, F32),
            jax.ShapeDtypeStruct(w_quarter, BF16),
            jax.ShapeDtypeStruct(w_quarter, BF16),
            jax.ShapeDtypeStruct(wo_quarter, BF16),
            jax.ShapeDtypeStruct(wo_quarter, BF16),
        ),
        in_specs=vmem(4) + [anywhere] * 2,
        out_specs=tuple(vmem(1) + [anywhere] + vmem(6) + [anywhere] * 2),
        scratch_shapes=[pltpu.VMEM(w_quarter, BF16)] * 2
        + [pltpu.VMEM(q_shape, BF16), pltpu.VMEM(kv_shape, BF16)]
        + [dma((count,))] * 6
        + [dma((6,))] * 2
        + [dma((2,))],
        compiler_params=pltpu.CompilerParams(
            collective_id=3, has_side_effects=True, vmem_limit_bytes=VMEM_LIMIT
        ),
        name="begin",
    )(x, gains, shifts, bias, w, wo)


def norm_parts(values):
    mean = jnp.mean(values, axis=-1, keepdims=True)
    centred = values - mean
    rstd = lax.rsqrt(jnp.mean(centred * centred, axis=-1, keepdims=True) + EPS)
    return centred * rstd, rstd


GELU_A = 0.7978845608028654
GELU_B = 0.044715


def gelu_parts(u):
    square = u * u
    t = jnp.tanh(GELU_A * u * (1.0 + GELU_B * square))
    rise = 0.5 * (1.0 + t)
    return u * rise, rise + 0.5 * u * (1.0 - t * t) * (GELU_A * (1.0 + 3.0 * GELU_B * square))


def col_sum(values):
    return jnp.sum(values, axis=0, keepdims=True)


def back_rows(xhat, rstd, gain, upstream):
    e = upstream * gain
    return rstd * (
        e - jnp.mean(e, axis=-1, keepdims=True) - xhat * jnp.mean(e * xhat, axis=-1, keepdims=True)
    )


def dot_nn(a, b):
    return jnp.dot(a, b, preferred_element_type=F32)


def dot_nt(a, b):
    return lax.dot_general(a, b, (((1,), (1,)), ((), ())), preferred_element_type=F32)


def dot_tn(a, b):
    return lax.dot_general(a, b, (((0,), (0,)), ((), ())), preferred_element_type=F32)


def middle_kernel(
    gains, shifts, bias_out, bias_down, bias_own, bias_far, att_ref, x_ref, og_ref,
    wo_ref, wo2, wo3, wu_ref, wu2, wd_ref,
    result, da_in, dh, vec, near_ref, far_up_ref, far_ref,
    att_in, att_s, att_sib, wo_s, wu_s, wd_s, x_s, branch_s, hidden_s, inner_s, inner_sib, act_s, act_sib,
    dg_s, dup_sib, down_s, dd_s, dd_sib, db_s, db_sib, da_st,
    ats, atr, das, dar, ws, wr, cs, cr, loc,
):
    place = Place()
    count = att_in.shape[0]
    me = place.seq * 2 + place.tp
    who = (place.tp, lax.rem(place.seq, 2))
    rows, width = x_s.shape
    hid = wd_s.shape[1]
    wu0, wu1 = (wu_ref.at[:, rows_at(c * hid, hid)] for c in (who[1], 1 - who[1]))
    wo0, wo1 = (wo_ref.at[rows_at(c * wo2.shape[0], wo2.shape[0])] for c in (who[1], 1 - who[1]))
    wd0, wd1 = (wd_ref.at[rows_at(c * hid, hid)] for c in (who[1], 1 - who[1]))
    greet_all(count, me, place.seq, place.tp)

    def start(k, carry):
        chunk_copy(count, me, k, att_ref, att_in, ats, atr).start()
        return carry

    lax.fori_loop(1, count, start, 0)
    wd_far = remote(wd0, wd_s.at[2], ws.at[0], wr.at[0], place.tp_partner)
    wd_far.start()
    wu_last = remote(wu2, wu_s.at[3], ws.at[1], wr.at[1], place.core_partner)
    wu_last.start()
    wd_last = remote(wd_s.at[2], wd_s.at[3], ws.at[2], wr.at[2], place.core_partner)
    loads = [(att_ref.at[me], att_in.at[me]), (x_ref, x_s), (og_ref, dh)]
    loads += [(w, wo_s.at[r]) for r, w in enumerate((wo0, wo1, wo2, wo3))]
    loads += [(w, wu_s.at[r]) for r, w in enumerate((wu0, wu1, wu2))]
    loads += [(w, wd_s.at[r]) for r, w in enumerate((wd0, wd1))]
    loads = [pltpu.make_async_copy(src, dst, loc.at[i]) for i, (src, dst) in enumerate(loads)]
    for copy in loads:
        copy.start()

    def to_core(i, src, dst):
        return remote(src, dst, cs.at[i], cr.at[i], place.core_partner)

    att_pair = [to_core(i, att_s.at[2 * i + 1], att_sib.at[i]) for i in range(2)]
    act_pair = [to_core(2 + i, act_s.at[2 * i + 1], act_sib.at[i]) for i in range(2)]
    dup_pair = [to_core(4 + i, dg_s.at[2 * i + 1], dup_sib.at[i]) for i in range(2)]
    inner_pair = to_core(6, inner_s, inner_sib)
    dd_pair = to_core(7, dd_s, dd_sib)
    db_pair = to_core(8, db_s, db_sib)

    def came(k, carry):
        chunk_copy(count, me, k, att_ref, att_in, ats, atr).wait()
        return carry

    lax.fori_loop(1, count, came, 0)
    for copy in loads:
        copy.wait()
    for quarter in range(4):
        load_packed(who, quarter, att_in, att_s.at[quarter], 0)
    for copy in att_pair:
        copy.start()

    def cols(i):
        return rows_at(i * 256, 256)

    def project(i, carry):
        span = cols(i)
        branch_s[:, span] = (
            dot_nn(att_s[0], wo_s[0, :, span])
            + dot_nn(att_s[1], wo_s[1, :, span])
            + dot_nn(att_s[2], wo_s[2, :, span])
            + dot_nn(att_s[3], wo_s[3, :, span])
            + bias_out[:, span]
        )
        return carry

    lax.fori_loop(0, width // 256, project, 0)

    def into(i, carry):
        span = rows_at(i * 64, 64)
        hidden = x_s[span, :].astype(F32) + layer_norm(branch_s[span, :], gains[1:2, :], shifts[1:2, :])
        hidden_s[span, :] = hidden
        inner_s[span, :] = layer_norm(hidden, gains[2:3, :], shifts[2:3, :]).astype(BF16)
        return carry

    lax.fori_loop(0, rows // 64, into, 0)
    inner_pair.start()
    for quarter in range(4):
        if quarter == 3:
            wu_last.wait()

        bias = bias_own if quarter < 2 else bias_far
        side = who[1] if quarter % 2 == 0 else 1 - who[1]

        def up(i, carry, quarter=quarter, bias=bias, side=side):
            span = cols(i)
            act, slope = gelu_parts(
                dot_nn(inner_s[...], wu_s[quarter, :, span]) + bias[pl.ds(side, 1), span]
            )
            act_s[quarter, :, span] = act.astype(BF16)
            dg_s[quarter, :, span] = slope.astype(BF16)
            return carry

        lax.fori_loop(0, hid // 256, up, 0)
        if quarter % 2 == 1:
            act_pair[quarter // 2].start()

    def down_own(i, carry):
        span = cols(i)
        down_s[:, span] = (
            dot_nn(act_s[0], wd_s[0, :, span]) + dot_nn(act_s[1], wd_s[1, :, span]) + bias_down[:, span]
        )
        return carry

    lax.fori_loop(0, width // 256, down_own, 0)
    wd_far.wait()
    wd_last.start()
    for quarter in (2, 3):
        if quarter == 3:
            wd_last.wait()

        def down_far(i, carry, quarter=quarter):
            span = cols(i)
            down_s[:, span] += dot_nn(act_s[quarter], wd_s[quarter, :, span])
            return carry

        lax.fori_loop(0, width // 256, down_far, 0)

    none = jnp.zeros((1, width), F32)

    def turn(i, carry):
        gain, shift, bias = carry
        span = rows_at(i * 64, 64)
        xhat, rstd = norm_parts(down_s[span, :])
        result[span, :] = (hidden_s[span, :] + xhat * gains[3:4, :] + shifts[3:4, :]).astype(BF16)
        upstream = dh[span, :]
        d_down = back_rows(xhat, rstd, gains[3:4, :], upstream)
        dd_s[span, :] = d_down.astype(BF16)
        return gain + col_sum(upstream * xhat), shift + col_sum(upstream), bias + col_sum(d_down)

    gain, shift, bias = lax.fori_loop(0, rows // 64, turn, (none,) * 3)
    vec[...] = jnp.zeros_like(vec)
    vec[3:4, :] = gain
    vec[7:8, :] = shift
    vec[9:10, :] = bias
    dd_pair.start()
    for quarter in range(4):
        absolute = (who[0] * 2 + who[1]) ^ quarter

        def back_up(i, carry, quarter=quarter, absolute=absolute):
            span = cols(i)
            d_up = dot_nt(dd_s[...], wd_s[quarter, span, :]) * dg_s[quarter, :, span].astype(F32)
            d_up = d_up.astype(BF16)
            dg_s[quarter, :, span] = d_up
            vec[pl.ds(12 + absolute, 1), span] = col_sum(d_up.astype(F32))
            return carry

        lax.fori_loop(0, hid // 256, back_up, 0)
        if quarter % 2 == 1:
            dup_pair[quarter // 2].start()

    def back_inner(i, carry):
        span = cols(i)
        down_s[:, span] = (
            dot_nt(dg_s[0], wu_s[0, span, :])
            + dot_nt(dg_s[1], wu_s[1, span, :])
            + dot_nt(dg_s[2], wu_s[2, span, :])
            + dot_nt(dg_s[3], wu_s[3, span, :])
        )
        return carry

    lax.fori_loop(0, width // 256, back_inner, 0)

    def out_of(i, carry):
        gain3, shift3, gain2, shift2, bias = carry
        span = rows_at(i * 64, 64)
        d_inner = down_s[span, :]
        xhat, rstd = norm_parts(hidden_s[span, :])
        gain3 = gain3 + col_sum(d_inner * xhat)
        shift3 = shift3 + col_sum(d_inner)
        d_hidden = dh[span, :] + back_rows(xhat, rstd, gains[2:3, :], d_inner)
        dh[span, :] = d_hidden
        xhat, rstd = norm_parts(branch_s[span, :])
        d_branch = back_rows(xhat, rstd, gains[1:2, :], d_hidden)
        db_s[span, :] = d_branch.astype(BF16)
        return (
            gain3, shift3, gain2 + col_sum(d_hidden * xhat), shift2 + col_sum(d_hidden),
            bias + col_sum(d_branch),
        )

    sums = lax.fori_loop(0, rows // 64, out_of, (none,) * 5)
    for row, value in zip((2, 6, 1, 5, 8), sums):
        vec[row : row + 1, :] = value
    db_pair.start()

    def da_copy(other):
        return remote(
            da_st.at[other], da_in.at[me], das.at[other], dar.at[me], (other // 2, lax.rem(other, 2))
        )

    def da_came(other):
        return remote(
            da_st.at[other], da_in.at[other], das.at[other], dar.at[other], (other // 2, lax.rem(other, 2))
        )

    for quarter in range(4):
        store_packed(who, quarter, dot_nt(db_s[...], wo_s[quarter]), da_st)

        def send(i, carry, quarter=quarter):
            other = chunk_of(who, quarter, i // 2, lax.rem(i, 2))

            @pl.when(other != me)
            def _():
                da_copy(other).start()

            @pl.when(other == me)
            def _():
                da_in[me] = da_st[me]

            return carry

        lax.fori_loop(0, 8, send, 0)

    for copy in dup_pair + [inner_pair]:
        copy.wait()

    def grad_up(i, carry):
        span = cols(i)
        for near, slot in ((0, 0), (2, 1)):
            wu_s[near, :, span] = (
                dot_tn(inner_s[...], dg_s[near, :, span]) + dot_tn(inner_sib[...], dup_sib[slot, :, span])
            ).astype(BF16)
        return carry

    lax.fori_loop(0, hid // 256, grad_up, 0)
    for copy in att_pair + [db_pair]:
        copy.wait()
    for near, slot in ((0, 0), (2, 1)):
        wo_s[near] = (dot_tn(att_s[near], db_s[...]) + dot_tn(att_sib[slot], db_sib[...])).astype(BF16)
    up_rows, out_rows = wu_s.shape[1], wo_s.shape[1]
    stores = [
        (wu_s.at[0], near_ref.at[pl.ds(0, up_rows)]),
        (wo_s.at[0], near_ref.at[pl.ds(up_rows + hid, out_rows)]),
        (wu_s.at[2], far_up_ref),
        (wo_s.at[2], far_ref.at[pl.ds(hid, out_rows)]),
        (wd_s.at[0], near_ref.at[pl.ds(up_rows, hid)]),
        (wd_s.at[2], far_ref.at[pl.ds(0, hid)]),
    ]
    stores = [pltpu.make_async_copy(src, dst, loc.at[i]) for i, (src, dst) in enumerate(stores)]
    for copy in stores[:4]:
        copy.start()
    for copy in act_pair + [dd_pair]:
        copy.wait()

    def grad_down(i, carry):
        span = cols(i)
        for near, slot in ((0, 0), (2, 1)):
            wd_s[near, span, :] = (
                dot_tn(act_s[near, :, span], dd_s[...]) + dot_tn(act_sib[slot, :, span], dd_sib[...])
            ).astype(BF16)
        return carry

    lax.fori_loop(0, hid // 256, grad_down, 0)
    for copy in stores[4:]:
        copy.start()

    def da_wait(k, carry):
        other = lax.rem(me + k, count)
        da_came(other).wait_recv()
        da_copy(other).wait_send()
        return carry

    lax.fori_loop(1, count, da_wait, 0)
    for copy in stores:
        copy.wait()


def middle(gains, shifts, bias_out, bias_down, bias, bias_far, att, x, out_grad, wo3, w_up, wu2, w_down):
    rows, width = x.shape
    count = att.shape[0]
    hid = wu2.shape[1]
    out_rows = wo3[1].shape[0]
    dma = pltpu.SemaphoreType.DMA
    anywhere = pl.BlockSpec(memory_space=pl.ANY)

    def held(*shape, dtype=BF16):
        return pltpu.VMEM(shape, dtype)

    scratch = [
        held(*att.shape),
        held(4, rows, out_rows),
        held(2, rows, out_rows),
        held(4, out_rows, width),
        held(4, width, hid),
        held(4, hid, width),
        held(rows, width),
        held(rows, width, dtype=F32),
        held(rows, width, dtype=F32),
        held(rows, width),
        held(rows, width),
        held(4, rows, hid),
        held(2, rows, hid),
        held(4, rows, hid),
        held(2, rows, hid),
        held(rows, width, dtype=F32),
        held(rows, width),
        held(rows, width),
        held(rows, width),
        held(rows, width),
        held(*att.shape),
    ]
    scratch += [dma((count,))] * 4 + [dma((3,))] * 2 + [dma((9,))] * 2 + [dma((12,))]
    return pl.pallas_call(
        middle_kernel,
        out_shape=(
            jax.ShapeDtypeStruct((rows, width), BF16),
            jax.ShapeDtypeStruct(att.shape, BF16),
            jax.ShapeDtypeStruct((rows, width), F32),
            jax.ShapeDtypeStruct((16, width), F32),
            jax.ShapeDtypeStruct((hid + width + out_rows, width), BF16),
            jax.ShapeDtypeStruct((width, hid), BF16),
            jax.ShapeDtypeStruct((hid + out_rows, width), BF16),
        ),
        in_specs=vmem(6) + [anywhere] * 9,
        out_specs=tuple(vmem(4) + [anywhere] * 3),
        scratch_shapes=scratch,
        compiler_params=pltpu.CompilerParams(
            collective_id=4, has_side_effects=True, vmem_limit_bytes=VMEM_MIDDLE
        ),
        name="middle",
    )(
        gains, shifts, bias_out, bias_down, bias, bias_far, att, x, out_grad, *wo3, w_up, wu2, w_down
    )


def fast_local(
    tokens_in, w_qkv, bias_qv, w_out, bias_out, w_up, bias_up, w_down, bias_down,
    norm_gains, norm_shifts, out_grad, lengths, prefixes, placement,
):
    seq_count = lax.axis_size("seq")
    seq, tp = lax.axis_index("seq"), lax.axis_index("tp")
    core = seq % 2
    over_tp = [(0, 1), (1, 0)]

    def to_tp(values):
        return lax.ppermute(values, "tp", over_tp)

    width = w_qkv.shape[0]
    w3 = jnp.transpose(w_qkv, (1, 0, 2))
    bias = jnp.concatenate([bias_up.reshape(2, width), bias_qv.reshape(1, width)]).astype(F32)
    bias = jnp.pad(bias, ((0, 5), (0, 0)))
    tables = block_tables(lengths, prefixes, placement, core)
    normed, normed_sib, q_own, kv_own, kv_sib, bias_far, wq2, wq3, wo2, wo3 = begin(
        tokens_in, norm_gains, norm_shifts, bias, w3, w_out
    )
    w_up, normed = lax.optimization_barrier((w_up, normed))
    half = w_up.shape[1] // 2
    wu2 = to_tp(lax.dynamic_slice_in_dim(w_up, core * half, half, 1))
    att_chunks, out_t, mass, kv_pack, kv_turned = attend(core, tables, q_own, kv_own, kv_sib)
    result, da_own, d_hidden, vectors, near, far_up, far = middle(
        norm_gains, norm_shifts, bias_out.astype(F32)[None], bias_down.astype(F32)[None], bias, bias_far,
        att_chunks, tokens_in, out_grad, [w_out, wo2, wo3], w_up, wu2, w_down,
    )
    far_up = to_tp(far_up)
    dq_chunks, mine, theirs = attend_back(core, tables, q_own, da_own, out_t, mass, kv_pack, kv_turned)
    both, grad_x, vectors = finish(
        norm_gains, dq_chunks, mine, theirs, near, far_up, far, normed, normed_sib, tokens_in, d_hidden,
        [w3, wq2, wq3], vectors,
    )
    up, down, out = (n // 256 for n in (width, wu2.shape[1], wo2.shape[0]))
    g_up = join(core, both, 512, 0, up // 2, w_up.shape, lambda p, i: (i, p))
    g_down = join(core, both, 512, up // 2, down // 2, w_down.shape, lambda p, i: (p * (down // 2) + i, 0))
    g_out = join(core, both, 256, up + down, out, w_out.shape, lambda p, i: (p * out + i, 0))
    g_qkv = join(
        core, both, 256, up + down + out, 3, (3, width, w_qkv.shape[2]), lambda p, i: (i, 0, p), turned=True
    )
    g_qkv = jnp.transpose(g_qkv, (1, 0, 2))
    own_cols = bias_qv.shape[1]
    grad_bias_qv = lax.dynamic_slice_in_dim(vectors[10:12], tp * own_cols, own_cols, 1)
    grad_bias_up = lax.dynamic_slice_in_dim(
        vectors[12:16].reshape(-1), tp * bias_up.shape[0], bias_up.shape[0]
    )
    return (
        result,
        grad_x,
        g_qkv,
        grad_bias_qv,
        g_out,
        vectors[8],
        g_up,
        grad_bias_up,
        g_down,
        vectors[9],
        vectors[0:4],
        vectors[4:8],
    )


def pack_tables(lengths, prefixes, row_total):
    where_row = jnp.arange(row_total, dtype=jnp.int32)
    doc_ends = running_ends(lengths)
    document = jnp.sum((where_row[:, None] >= doc_ends[None, :]).astype(jnp.int32), axis=1)
    limits = doc_ends - lengths + prefixes
    doc_pick = document[:, None] == jnp.arange(lengths.shape[0], dtype=jnp.int32)[None, :]
    visible = jnp.sum(jnp.where(doc_pick, limits[None, :], 0), axis=1)
    return (document, visible)


def padded_tables(document, visible, margin):
    row_total = document.shape[0]
    border = jnp.full((margin,), -1, jnp.int32)
    doc_pad = jnp.concatenate([border, document, border])
    pos_pad = jnp.arange(-margin, row_total + margin, dtype=jnp.int32)
    blank = jnp.zeros((margin,), jnp.int32)
    seen_pad = jnp.concatenate([blank, visible, blank])
    return (doc_pad, pos_pad, seen_pad)


def allowed_pairs(query_pos, query_doc, key_pos, key_doc, key_seen):
    return (query_doc[:, None] == key_doc[None, :]) & (
        (key_pos[None, :] <= query_pos[:, None]) | (key_pos[None, :] < key_seen[None, :])
    )


def pick_blocks(blocks, order):
    return lax.map(lambda i: lax.dynamic_index_in_dim(blocks, i, 0, False), order)


def to_pack(stored, pack_order, margin, block_size):
    blocks = stored.reshape((pack_order.shape[0], block_size) + stored.shape[1:])
    ordered = pick_blocks(blocks, pack_order).reshape(stored.shape)
    widths = [(margin, margin)] + [(0, 0)] * (stored.ndim - 1)
    return jnp.pad(ordered, widths)


def from_pack(padded, placement, margin, block_size, row_total):
    core = padded[margin : margin + row_total]
    blocks = core.reshape((placement.shape[0], block_size) + core.shape[1:])
    return pick_blocks(blocks, placement).reshape(core.shape)


def masked_scores(query_h, key_h, allowed):
    scores = query_h.shape[-1] ** (-0.5) * jnp.einsum(
        "qe,ke->qk", query_h, key_h, preferred_element_type=jnp.float32
    )
    return jnp.where(allowed, scores, -jnp.inf)


def forward_block(query_block, key_win, value_win, allowed):

    def forward_one_head(head):
        query_h = lax.dynamic_index_in_dim(query_block, head, 1, False)
        key_h = lax.dynamic_index_in_dim(key_win, head, 1, False)
        value_h = lax.dynamic_index_in_dim(value_win, head, 1, False)
        masked = masked_scores(query_h, key_h, allowed)
        row_top = jnp.max(masked, axis=1, keepdims=True)
        expo = jnp.exp(masked - row_top)
        row_sum = jnp.sum(expo, axis=1, keepdims=True)
        probs_b = (expo / row_sum).astype(jnp.bfloat16)
        output = jnp.dot(probs_b, value_h, preferred_element_type=jnp.float32)
        return (output, (row_top + jnp.log(row_sum))[:, 0])

    return lax.map(forward_one_head, jnp.arange(query_block.shape[1], dtype=jnp.int32))


def attention_grads(
    query_block, d_att_block, mass_block, total_block, key_block, value_block, allowed
):
    score_scale = query_block.shape[-1] ** (-0.5)

    def attention_one_head(head):
        query_h = lax.dynamic_index_in_dim(query_block, head, 1, False)
        d_att_h = lax.dynamic_index_in_dim(d_att_block, head, 1, False)
        key_h = lax.dynamic_index_in_dim(key_block, head, 1, False)
        value_h = lax.dynamic_index_in_dim(value_block, head, 1, False)
        mass_h = lax.dynamic_index_in_dim(mass_block, head, 0, False)
        total_h = lax.dynamic_index_in_dim(total_block, head, 0, False)
        masked = masked_scores(query_h, key_h, allowed)
        probs = jnp.exp(masked - mass_h[:, None])
        d_probs = jnp.einsum("qe,ke->qk", d_att_h, value_h, preferred_element_type=jnp.float32)
        d_scores = (probs * (d_probs - total_h[:, None])).astype(jnp.bfloat16)
        results = []
        results.append(
            score_scale
            * jnp.einsum("qk,ke->qe", d_scores, key_h, preferred_element_type=jnp.float32)
        )
        results.append(
            score_scale
            * jnp.einsum("qk,qe->ke", d_scores, query_h, preferred_element_type=jnp.float32)
        )
        results.append(
            jnp.einsum(
                "qk,qe->ke", probs.astype(jnp.bfloat16), d_att_h, preferred_element_type=jnp.float32
            )
        )
        return tuple(results)

    return lax.map(attention_one_head, jnp.arange(query_block.shape[1], dtype=jnp.int32))


def general_local(
    tokens_in,
    w_qkv,
    bias_qv,
    w_out,
    bias_out,
    w_up,
    bias_up,
    w_down,
    bias_down,
    norm_gains,
    norm_shifts,
    out_grad,
    lengths,
    prefixes,
    placement,
):
    seq_count = lax.axis_size("seq")
    block_total = placement.shape[0]
    blocks_here = block_total // seq_count
    total_rows = block_total * BLK
    own_rows = blocks_here * BLK
    model_width = w_qkv.shape[0]
    head_span = w_qkv.shape[2]
    heads_here = head_span // HEAD
    margin = LONGEST + BLK
    window = LONGEST + 2 * BLK
    document, visible = pack_tables(lengths, prefixes, total_rows)
    doc_pad, pos_pad, seen_pad = padded_tables(document, visible, margin)
    own_blocks = lax.dynamic_slice_in_dim(
        placement, lax.axis_index("seq") * blocks_here, blocks_here
    )
    pack_order = inverse_order(placement)
    offsets = jnp.arange(BLK, dtype=jnp.int32)

    def query_window(index):
        first = own_blocks[index] * BLK
        key_first = margin + first - LONGEST
        allowed = allowed_pairs(
            first + offsets,
            lax.dynamic_slice_in_dim(document, first, BLK),
            lax.dynamic_slice_in_dim(pos_pad, key_first, window),
            lax.dynamic_slice_in_dim(doc_pad, key_first, window),
            lax.dynamic_slice_in_dim(seen_pad, key_first, window),
        )
        return (key_first, allowed)

    input_f32 = tokens_in.astype(jnp.float32)
    normed, back_first = jax.vjp(layer_norm, input_f32, norm_gains[0], norm_shifts[0])
    rows_all = lax.all_gather(normed.astype(jnp.bfloat16), "tp", axis=0, tiled=True)
    flat_qkv = w_qkv.reshape(model_width, 3 * head_span)
    mixed = jnp.dot(rows_all, flat_qkv, preferred_element_type=jnp.float32).reshape(
        own_rows, 3, head_span
    )
    query_b = (mixed[:, 0] + bias_qv[0].astype(jnp.float32)).astype(jnp.bfloat16)
    key_b = mixed[:, 1].astype(jnp.bfloat16)
    value_b = (mixed[:, 2] + bias_qv[1].astype(jnp.float32)).astype(jnp.bfloat16)
    keys_all, values_all = (
        lax.all_gather(key_b, "seq", axis=0, tiled=True),
        lax.all_gather(value_b, "seq", axis=0, tiled=True),
    )
    keys_pad = to_pack(keys_all, pack_order, margin, BLK).reshape(-1, heads_here, HEAD)
    values_pad = to_pack(values_all, pack_order, margin, BLK).reshape(-1, heads_here, HEAD)
    head_shape = (own_rows, heads_here, HEAD)
    query3 = query_b.reshape(head_shape)
    attended_list = []
    mass_list = []
    for index in range(blocks_here):
        key_first, allowed = query_window(index)
        outputs, masses = forward_block(
            query3[index * BLK : (index + 1) * BLK],
            lax.dynamic_slice_in_dim(keys_pad, key_first, window),
            lax.dynamic_slice_in_dim(values_pad, key_first, window),
            allowed,
        )
        attended_list.append(jnp.transpose(outputs, (1, 0, 2)))
        mass_list.append(masses)
    attended32 = jnp.concatenate(attended_list, axis=0)
    log_mass = jnp.concatenate(mass_list, axis=1)
    attended_b = attended32.reshape(own_rows, head_span).astype(jnp.bfloat16)
    branch = lax.psum_scatter(
        jnp.dot(attended_b, w_out, preferred_element_type=jnp.float32).astype(jnp.bfloat16),
        "tp",
        scatter_dimension=0,
        tiled=True,
    ).astype(jnp.float32) + bias_out.astype(jnp.float32)
    post_attn, back_post = jax.vjp(layer_norm, branch, norm_gains[1], norm_shifts[1])
    hidden = input_f32 + post_attn
    inner, back_inner = jax.vjp(layer_norm, hidden, norm_gains[2], norm_shifts[2])
    inner_all = lax.all_gather(inner.astype(jnp.bfloat16), "tp", axis=0, tiled=True)
    upward = jnp.dot(inner_all, w_up, preferred_element_type=jnp.float32) + bias_up.astype(
        jnp.float32
    )
    active, back_gate = jax.vjp(smooth_gate, upward)
    active_b = active.astype(jnp.bfloat16)
    down = lax.psum_scatter(
        jnp.dot(active_b, w_down, preferred_element_type=jnp.float32).astype(jnp.bfloat16),
        "tp",
        scatter_dimension=0,
        tiled=True,
    ).astype(jnp.float32) + bias_down.astype(jnp.float32)
    final, back_final = jax.vjp(layer_norm, down, norm_gains[3], norm_shifts[3])
    result = (hidden + final).astype(jnp.bfloat16)
    d_down, gain_last, shift_last = back_final(out_grad)
    grad_bias_down = jnp.sum(d_down, axis=0)
    d_down_all = lax.all_gather(d_down.astype(jnp.bfloat16), "tp", axis=0, tiled=True)
    grad_w_down = jnp.einsum("tf,td->fd", active_b, d_down_all, preferred_element_type=jnp.float32)
    d_active = jnp.einsum("td,fd->tf", d_down_all, w_down, preferred_element_type=jnp.float32)
    (d_up,) = back_gate(d_active)
    d_up_b = d_up.astype(jnp.bfloat16)
    grad_bias_up = jnp.sum(d_up_b.astype(jnp.float32), axis=0)
    grad_w_up = jnp.einsum("td,tf->df", inner_all, d_up_b, preferred_element_type=jnp.float32)
    d_inner = lax.psum_scatter(
        jnp.einsum("tf,df->td", d_up_b, w_up, preferred_element_type=jnp.float32).astype(
            jnp.bfloat16
        ),
        "tp",
        scatter_dimension=0,
        tiled=True,
    ).astype(jnp.float32)
    d_hidden_part, gain_third, shift_third = back_inner(d_inner)
    d_hidden = out_grad + d_hidden_part
    d_branch, gain_second, shift_second = back_post(d_hidden)
    grad_bias_out = jnp.sum(d_branch, axis=0)
    d_branch_all = lax.all_gather(d_branch.astype(jnp.bfloat16), "tp", axis=0, tiled=True)
    grad_w_out = jnp.einsum(
        "te,td->ed", attended_b, d_branch_all, preferred_element_type=jnp.float32
    )
    d_att_b = jnp.einsum(
        "td,ed->te", d_branch_all, w_out, preferred_element_type=jnp.float32
    ).astype(jnp.bfloat16)
    d_att3 = d_att_b.reshape(head_shape)
    d_total = jnp.sum(d_att3.astype(jnp.float32) * attended32, axis=2).T
    d_query_list = []
    key_buffer = jnp.zeros((total_rows + 2 * margin, head_span), jnp.float32)
    value_buffer = jnp.zeros((total_rows + 2 * margin, head_span), jnp.float32)
    for index in range(blocks_here):
        key_first, allowed = query_window(index)
        rows = slice(index * BLK, (index + 1) * BLK)
        d_query_h, d_key_h, d_value_h = attention_grads(
            query3[rows],
            d_att3[rows],
            log_mass[:, rows],
            d_total[:, rows],
            lax.dynamic_slice_in_dim(keys_pad, key_first, window),
            lax.dynamic_slice_in_dim(values_pad, key_first, window),
            allowed,
        )
        d_query_list.append(jnp.transpose(d_query_h, (1, 0, 2)))
        key_piece = jnp.transpose(d_key_h, (1, 0, 2)).reshape(window, head_span)
        value_piece = jnp.transpose(d_value_h, (1, 0, 2)).reshape(window, head_span)
        key_buffer = lax.dynamic_update_slice_in_dim(
            key_buffer,
            lax.dynamic_slice_in_dim(key_buffer, key_first, window) + key_piece,
            key_first,
            0,
        )
        value_buffer = lax.dynamic_update_slice_in_dim(
            value_buffer,
            lax.dynamic_slice_in_dim(value_buffer, key_first, window) + value_piece,
            key_first,
            0,
        )
    key_terms = from_pack(key_buffer, placement, margin, BLK, total_rows)
    value_terms = from_pack(value_buffer, placement, margin, BLK, total_rows)
    d_keys, d_values = (
        lax.psum_scatter(
            key_terms.astype(jnp.bfloat16), "seq", scatter_dimension=0, tiled=True
        ).astype(jnp.float32),
        lax.psum_scatter(
            value_terms.astype(jnp.bfloat16), "seq", scatter_dimension=0, tiled=True
        ).astype(jnp.float32),
    )
    d_query = jnp.concatenate(d_query_list, axis=0)
    d_query_b = d_query.reshape(own_rows, head_span).astype(jnp.bfloat16)
    d_keys_b = d_keys.astype(jnp.bfloat16)
    d_values_b = d_values.astype(jnp.bfloat16)
    grad_bias_qv = jnp.stack(
        [
            jnp.sum(d_query_b.astype(jnp.float32), axis=0),
            jnp.sum(d_values_b.astype(jnp.float32), axis=0),
        ]
    )
    d_mixed = jnp.concatenate([d_query_b, d_keys_b, d_values_b], axis=1)
    grad_w_qkv = jnp.einsum(
        "td,tc->dc", rows_all, d_mixed, preferred_element_type=jnp.float32
    ).reshape(model_width, 3, head_span)
    d_normed = lax.psum_scatter(
        jnp.einsum("tc,dc->td", d_mixed, flat_qkv, preferred_element_type=jnp.float32).astype(
            jnp.bfloat16
        ),
        "tp",
        scatter_dimension=0,
        tiled=True,
    ).astype(jnp.float32)
    d_input_part, gain_first, shift_first = back_first(d_normed)
    grad_x = d_hidden + d_input_part
    summed = (
        lax.psum(grad_w_qkv.astype(jnp.bfloat16), "seq").astype(jnp.float32),
        lax.psum(grad_bias_qv.astype(jnp.bfloat16), "seq").astype(jnp.float32),
        lax.psum(grad_w_out.astype(jnp.bfloat16), "seq").astype(jnp.float32),
        lax.psum(grad_w_up.astype(jnp.bfloat16), "seq").astype(jnp.float32),
        lax.psum(grad_bias_up.astype(jnp.bfloat16), "seq").astype(jnp.float32),
        lax.psum(grad_w_down.astype(jnp.bfloat16), "seq").astype(jnp.float32),
    )
    gain_stack = jnp.stack([gain_first, gain_second, gain_third, gain_last])
    shift_stack = jnp.stack([shift_first, shift_second, shift_third, shift_last])
    vectors = lax.psum((gain_stack, shift_stack, grad_bias_out, grad_bias_down), ("seq", "tp"))
    return (
        result,
        grad_x,
        summed[0],
        summed[1],
        summed[2],
        vectors[2],
        summed[3],
        summed[4],
        summed[5],
        vectors[3],
        vectors[0],
        vectors[1],
    )


def solution(mesh):
    placed = (
        P(("seq", "tp"), None),
        P(None, None, "tp"),
        P(None, "tp"),
        P("tp", None),
        P(),
        P(None, "tp"),
        P("tp"),
        P("tp", None),
        P(),
        P(),
        P(),
        P(("seq", "tp"), None),
        P(),
        P(),
        P(),
    )
    seq_count, tp_count = mesh.shape["seq"], mesh.shape["tp"]

    def local(*args):
        tokens_in, w_qkv, placement = args[0], args[1], args[-1]
        heads = w_qkv.shape[2] * tp_count // HEAD
        paired = seq_count * tp_count == 2 * heads == placement.shape[0]
        sizes = (tokens_in.shape[0], w_qkv.shape[0], heads, seq_count, tp_count)
        fast = paired and sizes == (BLK, 1024, 16, 16, 2)
        return (fast_local if fast else general_local)(*args)

    return jax.shard_map(
        local,
        mesh=mesh,
        in_specs=placed,
        out_specs=(
            P(("seq", "tp"), None),
            P(("seq", "tp"), None),
            P(None, None, "tp"),
            P(None, "tp"),
            P("tp", None),
            P(),
            P(None, "tp"),
            P("tp"),
            P("tp", None),
            P(),
            P(),
            P(),
        ),
        check_vma=False,
    )
```

```python
import functools

import jax
import jax.numpy as jnp
from jax import lax
from jax.experimental import pallas as pl
from jax.experimental.pallas import tpu as pltpu
from jax.sharding import PartitionSpec as P

HEAD = 64
BLK = 512
HALF = BLK // 2
QUART = BLK // 4
LONGEST = 4096
STEP_F = 1024
STEP_B = 512
UNROLL = 8
CHUNK_ROWS = 256
FIRST_TICKS = 6
VMEM_LIMIT = 58 << 20
VMEM_MIDDLE = 62 << 20

EPS = 1e-05
F32 = jnp.float32
BF16 = jnp.bfloat16
MESH = pl.DeviceIdType.MESH


def layer_norm(row_block, gain_row, shift_row):
    row_mean = jnp.mean(row_block, axis=-1, keepdims=True)
    centred = row_block - row_mean
    spread = jnp.mean(centred * centred, axis=-1, keepdims=True)
    return centred * lax.rsqrt(spread + EPS) * gain_row + shift_row


def smooth_gate(values):
    return jax.nn.gelu(values, approximate=True)


def running_ends(lengths):
    count = lengths.shape[0]
    index = jnp.arange(count, dtype=jnp.int32)
    return jnp.sum(jnp.where(index[None, :] <= index[:, None], lengths[None, :], 0), axis=1)


def inverse_order(placement):
    index = jnp.arange(placement.shape[0], dtype=jnp.int32)
    return jnp.sum(jnp.where(placement[None, :] == index[:, None], index[None, :], 0), axis=1)


def block_tables(lengths, prefixes, placement, part):
    ends = running_ends(lengths)
    starts = ends - lengths
    limits = starts + prefixes
    offset = part * HALF + jnp.arange(HALF, dtype=jnp.int32)
    pos = placement[:, None] * BLK + offset[None, :]
    inside = (pos[:, :, None] >= starts) & (pos[:, :, None] < ends)

    def pick(values):
        return jnp.sum(jnp.where(inside, values, 0), axis=2)

    low = pick(starts)
    high = jnp.minimum(pick(ends), jnp.maximum(pos + 1, pick(limits)))
    table = jnp.stack(
        [
            jnp.min(low, axis=1) // HALF,
            (jnp.max(high, axis=1) - 1) // HALF + 1,
            jnp.max(low, axis=1),
            jnp.min(high, axis=1),
            placement,
        ]
    )
    return low[:, None, :], high[:, None, :], table


def unpack_t(packed):
    turned = packed.astype(F32).T
    return jnp.concatenate([turned[:HEAD], turned[HEAD:]], axis=1)


def pack_t(turned):
    return jnp.concatenate([turned[:, :QUART], turned[:, QUART:]], axis=0).T


def pieces_two(tab, b, keys, step, start):
    count = keys // HALF
    first, last = tab[0, b], tab[1, b]
    total = last - first
    short = lax.rem(total, count)
    many = total // count + (short > count // 2).astype(jnp.int32)

    def visit(size):
        def at_piece(i, state):
            at = pl.multiple_of((first + i * count) * HALF, HALF)
            whole = (at >= tab[2, b]) & (at + size <= tab[3, b])
            return lax.cond(
                whole, lambda st: step(at, st, False, size), lambda st: step(at, st, True, size), state
            )

        return at_piece

    state = lax.fori_loop(0, many, visit(keys), start)
    half_step = ((short > 0) & (short <= count // 2)).astype(jnp.int32)
    return lax.fori_loop(many, many + half_step, visit(keys // 2), state)


def pieces(tab, b, keys, step, start):
    count = keys // HALF
    first = tab[0, b]

    def visit(i, state):
        at = pl.multiple_of((first + i * count) * HALF, HALF)
        whole = (at >= tab[2, b]) & (at + keys <= tab[3, b])
        return lax.cond(whole, lambda st: step(at, st, False), lambda st: step(at, st, True), state)

    return lax.fori_loop(0, (tab[1, b] - first + count - 1) // count, visit, start)


def attend_kernel(
    part_ref, tab, low_ref, high_ref, q_ref, own_ref, sib_ref,
    out_ref, ot_ref, lse_ref, kv, kvt, rhs_s,
):
    part = part_ref[0]
    scale = HEAD**-0.5
    blocks = q_ref.shape[0]
    rows = blocks * BLK
    depth = lax.broadcasted_iota(jnp.int32, (STEP_F, HALF), 0)

    def prepare(b, carry):
        for ref, which in ((own_ref, part), (sib_ref, 1 - part)):
            at = pl.multiple_of(tab[4, b] * BLK + which * HALF, HALF)
            piece = ref[b]
            kv[pl.ds(at, HALF), :] = piece
            kvt[:, pl.ds(at, HALF)] = piece.T
        qt = unpack_t(q_ref[b]) * scale
        rhs_s[b] = jnp.concatenate([qt, jnp.zeros_like(qt)], axis=0).astype(BF16)
        return carry

    lax.fori_loop(0, blocks, prepare, 0, unroll=UNROLL)
    kv[rows:, :] = jnp.zeros((kv.shape[0] - rows, 2 * HEAD), BF16)
    kvt[:, rows:] = jnp.zeros((2 * HEAD, kv.shape[0] - rows), BF16)

    def one(b, carry):
        low, high = low_ref[b], high_ref[b]

        def step(at, state, masked, size):
            top, total, acc = state
            sc = jnp.dot(kv[pl.ds(at, size), :], rhs_s[b], preferred_element_type=F32)
            if masked:
                rows_of = depth[:size]
                sc = jnp.where((rows_of >= low - at) & (rows_of < high - at), sc, -1e30)
            new = jnp.maximum(top, jnp.max(sc, axis=0, keepdims=True))
            alpha = jnp.exp(top - new)
            pr = jnp.exp(sc - new)
            total = total * alpha + jnp.sum(pr, axis=0, keepdims=True)
            acc = acc * alpha + jnp.dot(
                kvt[HEAD:, pl.ds(at, size)], pr.astype(BF16), preferred_element_type=F32
            )
            return new, total, acc

        start = (
            jnp.full((1, HALF), -1e30, F32),
            jnp.zeros((1, HALF), F32),
            jnp.zeros((HEAD, HALF), F32),
        )
        top, total, acc = pieces_two(tab, b, STEP_F, step, start)
        ot_ref[b] = acc * (1.0 / total)
        lse_ref[b] = top + jnp.log(total)
        return carry

    lax.fori_loop(0, blocks, one, 0)

    def finish(b, carry):
        out_ref[b] = pack_t(ot_ref[b]).astype(BF16)
        return carry

    lax.fori_loop(0, blocks, finish, 0, unroll=UNROLL)


def attend_back_kernel(
    part_ref, tab, low_ref, high_ref, q_ref, da_ref, ot_ref, lse_ref, kv, kvt,
    dq_ref, mine_ref, theirs_ref, dkv, rhs_s, rows_s, total_s, dqt_s,
):
    part = part_ref[0]
    scale = HEAD**-0.5
    blocks = q_ref.shape[0]
    depth = lax.broadcasted_iota(jnp.int32, (STEP_B, HALF), 0)
    lane = lax.broadcasted_iota(jnp.int32, (HALF, 2 * HEAD), 1)

    def prepare(b, carry):
        dkv[pl.ds(pl.multiple_of(b * BLK, BLK), BLK), :] = jnp.zeros((BLK, 2 * HEAD), F32)
        qt = unpack_t(q_ref[b]) * scale
        dat = unpack_t(da_ref[b])
        blank = jnp.zeros_like(qt)
        rhs_s[b, :, :HALF] = jnp.concatenate([qt, blank], axis=0).astype(BF16)
        rhs_s[b, :, HALF:] = jnp.concatenate([blank, dat], axis=0).astype(BF16)
        both = jnp.concatenate([qt, dat], axis=0).T
        rows_s[b, :HALF, :] = jnp.where(lane < HEAD, both, 0.0).astype(BF16)
        rows_s[b, HALF:, :] = jnp.where(lane < HEAD, 0.0, both).astype(BF16)
        total_s[b] = jnp.sum(dat * ot_ref[b], axis=0, keepdims=True)
        return carry

    lax.fori_loop(0, blocks, prepare, 0, unroll=UNROLL)
    dkv[blocks * BLK :, :] = jnp.zeros((dkv.shape[0] - blocks * BLK, 2 * HEAD), F32)

    def one(b, carry):
        total = total_s[b]
        lse = lse_ref[b]
        low, high = low_ref[b], high_ref[b]

        def step(at, acc, masked):
            keys = kv[pl.ds(at, STEP_B), :]
            sc = jnp.dot(keys, rhs_s[b, :, :HALF], preferred_element_type=F32)
            dp = jnp.dot(keys, rhs_s[b, :, HALF:], preferred_element_type=F32)
            if masked:
                sc = jnp.where((depth >= low - at) & (depth < high - at), sc, -1e30)
            pr = jnp.exp(sc - lse)
            ds = (pr * (dp - total)).astype(BF16)
            dkv[pl.ds(at, STEP_B), :] += jnp.dot(
                ds, rows_s[b, :HALF, :], preferred_element_type=F32
            ) + jnp.dot(pr.astype(BF16), rows_s[b, HALF:, :], preferred_element_type=F32)
            return acc + jnp.dot(kvt[:HEAD, pl.ds(at, STEP_B)], ds, preferred_element_type=F32)

        dqt_s[b] = pieces(tab, b, STEP_B, step, jnp.zeros((HEAD, HALF), F32))
        return carry

    lax.fori_loop(0, blocks, one, 0)

    def finish(b, carry):
        dq_ref[b] = pack_t(dqt_s[b] * scale).astype(BF16)
        base = tab[4, b] * BLK
        mine_ref[b] = dkv[pl.ds(pl.multiple_of(base + part * HALF, HALF), HALF), :].astype(BF16)
        theirs_ref[b] = dkv[pl.ds(pl.multiple_of(base + (1 - part) * HALF, HALF), HALF), :].astype(BF16)
        return carry

    lax.fori_loop(0, blocks, finish, 0, unroll=UNROLL)


def vmem(count):
    return [pl.BlockSpec(memory_space=pltpu.VMEM)] * count


def smem(count):
    return [pl.BlockSpec(memory_space=pltpu.SMEM)] * count


def attend(part, tables, q_chunks, kv_own, kv_sib):
    low, high, table = tables
    blocks = q_chunks.shape[0]
    rows = blocks * BLK + STEP_F
    return pl.pallas_call(
        attend_kernel,
        out_shape=(
            jax.ShapeDtypeStruct((blocks, QUART, 2 * HEAD), BF16),
            jax.ShapeDtypeStruct((blocks, HEAD, HALF), F32),
            jax.ShapeDtypeStruct((blocks, 1, HALF), F32),
            jax.ShapeDtypeStruct((rows, 2 * HEAD), BF16),
            jax.ShapeDtypeStruct((2 * HEAD, rows), BF16),
        ),
        in_specs=smem(2) + vmem(5),
        out_specs=tuple(vmem(5)),
        scratch_shapes=[pltpu.VMEM((blocks, 2 * HEAD, HALF), BF16)],
        compiler_params=pltpu.CompilerParams(vmem_limit_bytes=VMEM_LIMIT),
        cost_estimate=pl.CostEstimate(
            flops=40 * 10**9, bytes_accessed=20 << 20, transcendentals=blocks * 4 * BLK * HALF
        ),
        name="attend",
    )(part.reshape(1), table, low, high, q_chunks, kv_own, kv_sib)


def attend_back(part, tables, q_chunks, da_chunks, out_t, mass, kv, kvt):
    low, high, table = tables
    blocks = q_chunks.shape[0]
    return pl.pallas_call(
        attend_back_kernel,
        out_shape=(
            jax.ShapeDtypeStruct((blocks, QUART, 2 * HEAD), BF16),
            jax.ShapeDtypeStruct((blocks, HALF, 2 * HEAD), BF16),
            jax.ShapeDtypeStruct((blocks, HALF, 2 * HEAD), BF16),
        ),
        in_specs=smem(2) + vmem(8),
        out_specs=tuple(vmem(3)),
        scratch_shapes=[
            pltpu.VMEM((blocks * BLK + STEP_F, 2 * HEAD), F32),
            pltpu.VMEM((blocks, 2 * HEAD, BLK), BF16),
            pltpu.VMEM((blocks, BLK, 2 * HEAD), BF16),
            pltpu.VMEM((blocks, 1, HALF), F32),
            pltpu.VMEM((blocks, HEAD, HALF), F32),
        ],
        compiler_params=pltpu.CompilerParams(vmem_limit_bytes=VMEM_LIMIT),
        cost_estimate=pl.CostEstimate(
            flops=60 * 10**9, bytes_accessed=30 << 20, transcendentals=blocks * 4 * BLK * HALF
        ),
        name="attend_back",
    )(part.reshape(1), table, low, high, q_chunks, da_chunks, out_t, mass, kv, kvt)


def chunk_of(who, quarter, index, half):
    absolute = (who[0] * 2 + who[1]) ^ quarter
    tp, sub = absolute // 2, absolute % 2
    return ((sub * 4 + index) * 2 + half) * 2 + tp


def swap_lanes(values):
    return pltpu.roll(values, HEAD, 1)


def low_lanes(rows):
    return lax.broadcasted_iota(jnp.int32, (rows, 2 * HEAD), 1) < HEAD


def store_packed(who, quarter, values, out_ref):
    low = low_lanes(QUART)
    for pair in range(2):
        for half in range(2):
            top = half * HALF
            lanes = slice(pair * 128, pair * 128 + 128)
            first, second = values[top : top + QUART, lanes], values[top + QUART : top + HALF, lanes]
            even = jnp.where(low, first, swap_lanes(second))
            odd = jnp.where(low, swap_lanes(first), second)
            out_ref[chunk_of(who, quarter, 2 * pair, half)] = even.astype(BF16)
            out_ref[chunk_of(who, quarter, 2 * pair + 1, half)] = odd.astype(BF16)


def load_packed(who, quarter, ref, out_ref, base):
    low = low_lanes(QUART)
    for pair in range(2):
        for half in range(2):
            even = ref[chunk_of(who, quarter, 2 * pair, half)].astype(F32)
            odd = ref[chunk_of(who, quarter, 2 * pair + 1, half)].astype(F32)
            top = half * HALF
            lanes = slice(base + pair * 128, base + pair * 128 + 128)
            out_ref[top : top + QUART, lanes] = jnp.where(low, even, swap_lanes(odd)).astype(BF16)
            out_ref[top + QUART : top + HALF, lanes] = jnp.where(low, swap_lanes(even), odd).astype(BF16)


class Place:
    def __init__(self):
        self.seq, self.tp = lax.axis_index("seq"), lax.axis_index("tp")
        self.x = lax.rem(self.seq // 2, 2)
        self.z = self.seq // 4
        self.core_partner = (self.seq ^ 1, self.tp)
        self.x_partner = (self.seq ^ 2, self.tp)
        self.z_partners = [(self.seq ^ (4 * d), self.tp) for d in (1, 2)]
        self.tp_partner = (self.seq, self.tp ^ 1)


def greet_all(count, me, seq, tp):
    barrier = pltpu.get_barrier_semaphore()

    def one(k, carry):
        other = lax.rem(me + k, count)
        pl.semaphore_signal(
            barrier, inc=1, device_id=(other // 2, lax.rem(other, 2)), device_id_type=MESH
        )
        return carry

    lax.fori_loop(1, count, one, 0)
    pl.semaphore_wait(barrier, count - 1)


def greet(partners):
    barrier = pltpu.get_barrier_semaphore()
    for partner in partners:
        pl.semaphore_signal(barrier, inc=1, device_id=partner, device_id_type=MESH)
    pl.semaphore_wait(barrier, len(partners))


def remote(src, dst, send, recv, device):
    return pltpu.make_async_remote_copy(
        src_ref=src, dst_ref=dst, send_sem=send, recv_sem=recv, device_id=device, device_id_type=MESH
    )


def chunk_copy(count, me, k, src, dst, send, recv):
    other = lax.rem(me + k, count)
    return remote(src.at[other], dst.at[me], send.at[k], recv.at[k], (other // 2, lax.rem(other, 2)))


def rows_at(start, size):
    return pl.ds(pl.multiple_of(start, size), size)


def reduce_stages(place, chunks, halved, base, out, both, kept, xbuf, xsum, zbuf, zsum, fbuf, sems, arrived):
    rows = base.shape[0] // chunks
    half, piece = rows // 2, rows // 8
    x, odd, upper = place.x, lax.rem(place.z, 2), place.z // 2
    pair = half // 2

    def x_copy(k):
        seq, tp = place.x_partner
        over_tp = (k >= halved[0]) & (k < halved[1])
        return remote(
            base.at[rows_at(k * rows + (1 - x) * half, half)], xbuf.at[rows_at(k * half, half)],
            sems["xs"].at[k], sems["xr"].at[k],
            (jnp.where(over_tp, place.seq, seq), jnp.where(over_tp, place.tp_partner[1], tp)),
        )

    def z_copy(k):
        return remote(
            xsum.at[rows_at(k * half + (1 - odd) * pair, pair)], zbuf.at[rows_at(k * pair, pair)],
            sems["zs"].at[0, k], sems["zr"].at[0, k], place.z_partners[0],
        )

    def far_z_copy(k):
        return remote(
            zsum.at[rows_at(k * pair + (1 - upper) * piece, piece)], fbuf.at[rows_at(k * piece, piece)],
            sems["zs"].at[1, k], sems["zr"].at[1, k], place.z_partners[1],
        )

    def own_pair(k):
        return rows_at(k * rows + x * half + odd * pair, pair)

    def own_piece(k):
        return rows_at(k * rows + x * half + odd * pair + upper * piece, piece)

    def far_zg_copy(k):
        return remote(
            out.at[own_piece(k)], out.at[own_piece(k)],
            sems["zgs"].at[1, k], sems["zgr"].at[1, k], place.z_partners[1],
        )

    def zg_copy(k):
        return remote(
            out.at[own_pair(k)], out.at[own_pair(k)],
            sems["zgs"].at[0, k], sems["zgr"].at[0, k], place.z_partners[0],
        )

    def xg_copy(k):
        span = rows_at(k * rows + x * half, half)
        return remote(out.at[span], out.at[span], sems["xgs"].at[k], sems["xgr"].at[k], place.x_partner)

    def core_copy(k):
        span = rows_at(k * rows, rows)
        return remote(out.at[span], both.at[1, span], sems["cs"].at[k], sems["cr"].at[k], place.core_partner)

    def stage_x(k):
        arrived(k)
        x_copy(k).start()

    def stage_z(k):
        x_copy(k).wait_recv()
        mine = base[rows_at(k * rows + x * half, half), :].astype(F32)
        xsum[rows_at(k * half, half), :] = (
            mine + xbuf[rows_at(k * half, half), :].astype(F32)
        ).astype(BF16)
        z_copy(k).start()

    def stage_far_z(k):
        z_copy(k).wait_recv()
        span = rows_at(k * pair, pair)
        zsum[span, :] = (
            xsum[rows_at(k * half + odd * pair, pair), :].astype(F32) + zbuf[span, :].astype(F32)
        ).astype(BF16)
        far_z_copy(k).start()

    def stage_far_zg(k):
        far_z_copy(k).wait_recv()
        out[own_piece(k), :] = (
            zsum[rows_at(k * pair + upper * piece, piece), :].astype(F32)
            + fbuf[rows_at(k * piece, piece), :].astype(F32)
        ).astype(BF16)
        far_zg_copy(k).start()

    def stage_zg(k):
        far_zg_copy(k).wait_recv()
        zg_copy(k).start()

    def stage_xg(k):
        zg_copy(k).wait_recv()
        xg_copy(k).start()

    def stage_core(k):
        xg_copy(k).wait_recv()
        core_copy(k).start()

    stages = [stage_x, stage_z, stage_far_z, stage_far_zg, stage_zg, stage_xg, stage_core]

    def tick(t):
        for s, stage in reversed(list(enumerate(stages))):
            @pl.when((t >= s) & (t - s < chunks))
            def _():
                stage(t - s)

    def drain(k, carry):
        for copy in (x_copy, z_copy, far_z_copy, far_zg_copy, zg_copy, xg_copy):
            copy(k).wait_send()
        core_copy(k).wait()
        return carry

    def finale():
        keep = pltpu.make_async_copy(out, both.at[0], kept)
        keep.start()
        lax.fori_loop(0, chunks, drain, 0)
        keep.wait()

    return tick, finale, chunks + len(stages) - 1


SEM_NAMES = ("xs", "xr", "zs", "zr", "zgs", "zgr", "xgs", "xgr", "cs", "cr")
VECTOR_STEPS = 5


def finish_kernel(
    chunks, first_ticks, gain_ref, dq_ref, mine_ref, theirs_ref, near_ref, far_up_ref, far_ref, over_x_ref,
    normed_ref, normed_sib_ref, x_ref, dh_ref, w_ref, w2, w3, vec_ref,
    both, gx_ref, vec_out,
    out, base, far, ybuf, xbuf, xsum, zbuf, zsum, fbuf, dq_in, dkv_in, dkv_st, dkv_sib, mixed, mixed_sib,
    normed, normed_sib, x_s, w_s, slots, *rest,
):
    place = Place()
    count = dq_ref.shape[0]
    me = place.seq * 2 + place.tp
    who = (place.tp, lax.rem(place.seq, 2))
    sems = dict(zip(SEM_NAMES, rest))
    qs, qr, ks, kr, ys, yr, ms, mr, vs, vr, loc = rest[len(SEM_NAMES) :]
    rows = base.shape[0] // chunks
    early = near_ref.shape[0]
    crossed = far_up_ref.shape[0] // rows
    met = crossed + over_x_ref.shape[0] // rows
    strip = rows // 2
    greet_all(count, me, place.seq, place.tp)
    dkv_pair = remote(theirs_ref, dkv_sib, ms.at[2], mr.at[2], place.core_partner)
    dkv_pair.start()
    mine_copy = pltpu.make_async_copy(mine_ref, dkv_st, loc.at[0])
    mine_copy.start()

    def dq_copy(k):
        return chunk_copy(count, me, k, dq_ref, dq_in, qs, qr)

    def dkv_copy(k):
        return chunk_copy(count, me, k, dkv_st, dkv_in, ks, kr)

    def start_q(k, carry):
        dq_copy(k).start()
        return carry

    lax.fori_loop(1, count, start_q, 0)
    near_copy = pltpu.make_async_copy(near_ref, base.at[pl.ds(0, early)], loc.at[1])
    near_copy.start()
    far_copy = pltpu.make_async_copy(far_up_ref, ybuf.at[pl.ds(0, far_up_ref.shape[0])], loc.at[2])
    far_copy.start()
    over_copy = pltpu.make_async_copy(
        over_x_ref, ybuf.at[pl.ds(crossed * rows, over_x_ref.shape[0])], loc.at[13]
    )
    over_copy.start()
    strips = [
        pltpu.make_async_copy(
            far_ref.at[rows_at(j * rows + place.x * strip, strip)],
            base.at[rows_at((crossed + j) * rows + (1 - place.x) * strip, strip)],
            loc.at[14 + j],
        )
        for j in range(met - crossed)
    ]
    locals_ = [(dq_ref.at[me], dq_in.at[me]), (normed_ref, normed), (normed_sib_ref, normed_sib)]
    locals_ += [(x_ref, x_s), (dh_ref, gx_ref)]
    col = w_s.shape[3]
    halves = [w_ref.at[:, :, rows_at(c * col, col)] for c in (who[1], 1 - who[1])]
    locals_ += [(w, w_s.at[r]) for r, w in enumerate(halves + [w2, w3])]
    locals_ = [pltpu.make_async_copy(src, dst, loc.at[3 + i]) for i, (src, dst) in enumerate(locals_)]

    def tp_copy(k, src, first):
        return remote(
            src.at[rows_at((k - first) * rows, rows)], ybuf.at[rows_at(k * rows, rows)],
            ys.at[k], yr.at[k], place.tp_partner,
        )

    def cross(k, carry):
        tp_copy(k, far_ref, crossed).start()
        return carry

    settled = early // rows
    lax.fori_loop(met, settled, cross, 0)
    mine_copy.wait()
    dkv_pair.wait()

    def add(b, carry):
        dkv_st[b] = (dkv_st[b].astype(F32) + dkv_sib[b].astype(F32)).astype(BF16)
        return carry

    lax.fori_loop(0, count, add, 0)

    def start_kv(k, carry):
        dkv_copy(k).start()
        return carry

    lax.fori_loop(1, count, start_kv, 0)
    dkv_in[me] = dkv_st[me]
    near_copy.wait()
    for copy in strips + locals_:
        copy.start()
    for copy in [far_copy, over_copy] + strips:
        copy.wait()

    def add_in(into, other):
        base[into, :] = (base[into, :].astype(F32) + ybuf[other, :].astype(F32)).astype(BF16)

    def arrived(k):
        x_met = (k >= crossed) & (k < met)

        @pl.when(k >= met)
        def _():
            tp_copy(k, base, 0).wait_recv()

        @pl.when(jnp.logical_not(x_met))
        def _():
            span = rows_at(k * rows, rows)
            add_in(span, span)

        @pl.when(x_met)
        def _():
            add_in(rows_at(k * rows + place.x * strip, strip), rows_at(k * rows, strip))
            add_in(
                rows_at(k * rows + (1 - place.x) * strip, strip), rows_at(k * rows + strip, strip)
            )

    tick, drain, ticks = reduce_stages(
        place, chunks, (crossed, met), base, out, both, loc.at[12], xbuf, xsum, zbuf, zsum, fbuf, sems, arrived
    )

    def plain(t, carry):
        tick(t)
        return carry

    lax.fori_loop(0, first_ticks, plain, 0)

    def wait(k, carry):
        dq_copy(k).wait()
        dkv_copy(k).wait()
        return carry

    lax.fori_loop(1, count, wait, 0)
    for copy in locals_:
        copy.wait()
    vec_out[...] = vec_ref[...]
    low = low_lanes(HALF)
    for quarter in range(4):
        load_packed(who, quarter, dq_in, mixed.at[quarter], 0)
        for pair in range(2):
            for half in range(2):
                span = slice(half * HALF, half * HALF + HALF)
                even = dkv_in[chunk_of(who, quarter, 2 * pair, half)].astype(F32)
                odd = dkv_in[chunk_of(who, quarter, 2 * pair + 1, half)].astype(F32)
                k_at = 256 + pair * 128
                mixed[quarter, span, k_at : k_at + 128] = jnp.where(low, even, swap_lanes(odd)).astype(BF16)
                mixed[quarter, span, k_at + 256 : k_at + 384] = jnp.where(low, swap_lanes(even), odd).astype(BF16)
    mixed_copies = [
        remote(mixed.at[2 * i + 1], mixed_sib.at[i], ms.at[i], mr.at[i], place.core_partner)
        for i in range(2)
    ]
    for copy in mixed_copies:
        copy.start()
    tick(first_ticks)

    for quarter in range(4):
        absolute = (who[0] * 2 + who[1]) ^ quarter
        lanes = pl.ds(pl.multiple_of(absolute * 256, 256), 256)
        for row, left in ((10, 0), (11, 512)):
            vec_out[row : row + 1, lanes] = jnp.sum(
                mixed[quarter, :, left : left + 256].astype(F32), axis=0, keepdims=True
            )
    gains = jnp.zeros((1, base.shape[1]), F32)
    shifts = jnp.zeros((1, base.shape[1]), F32)
    for part in range(2):
        span = slice(part * HALF, part * HALF + HALF)
        d_normed = jnp.zeros((HALF, base.shape[1]), F32)
        for quarter in range(4):
            for which in range(3):
                lanes = slice(which * col, which * col + col)
                d_normed += dot_nt(mixed[quarter, span, lanes], w_s[quarter, which])
        xhat, rstd = norm_parts(x_s[span, :].astype(F32))
        e = d_normed * gain_ref[0:1, :]
        grad = rstd * (
            e
            - jnp.mean(e, axis=-1, keepdims=True)
            - xhat * jnp.mean(e * xhat, axis=-1, keepdims=True)
        )
        gx_ref[span, :] += grad
        gains += jnp.sum(d_normed * xhat, axis=0, keepdims=True)
        shifts += jnp.sum(d_normed, axis=0, keepdims=True)
        tick(first_ticks + 1 + part)
    vec_out[0:1, :] = gains
    vec_out[4:5, :] = shifts

    for copy in mixed_copies:
        copy.wait()
    late = pl.ds(early, base.shape[0] - early)
    for i, target in ((1, far), (0, base.at[late])):
        for row in range(0, target.shape[0], 256):
            span = slice(row, row + 256)
            target[span, :] = (
                lax.dot_general(
                    mixed[2 * i, :, span], normed[...], (((0,), (0,)), ((), ())), preferred_element_type=F32
                )
                + lax.dot_general(
                    mixed_sib[i, :, span], normed_sib[...], (((0,), (0,)), ((), ())),
                    preferred_element_type=F32,
                )
            ).astype(BF16)
            if i == 1:
                for k in range(settled + row // rows, settled + (row + 256) // rows):
                    tp_copy(k, far, settled).start()

    partners = [place.core_partner, place.tp_partner, place.x_partner] + [
        (place.seq ^ bit, place.tp) for bit in (4, 8)
    ]

    def vector_step(step):
        slots[step] = vec_out[...]
        copy = remote(
            slots.at[step], slots.at[VECTOR_STEPS + step], vs.at[step], vr.at[step], partners[step]
        )
        copy.start()
        copy.wait()
        vec_out[...] += slots[VECTOR_STEPS + step]

    def last(t, carry):
        tick(t)
        for step in range(VECTOR_STEPS):
            @pl.when(t == first_ticks + 3 + step)
            def _():
                vector_step(step)
        return carry

    lax.fori_loop(first_ticks + 3, ticks, last, 0)

    def sent(k, carry):
        tp_copy(k, base, 0).wait_send()
        return carry

    lax.fori_loop(met, chunks, sent, 0)
    drain()


def finish(gain, dq_chunks, mine, theirs, near, far_up, far, over_x, normed, normed_sib, x, d_hidden, weights, vectors):
    early, cols = near.shape
    late = 3 * weights[1].shape[2]
    total = early + late
    chunks = total // CHUNK_ROWS
    count = dq_chunks.shape[0]
    rows = x.shape[0]
    dma = pltpu.SemaphoreType.DMA
    anywhere = pl.BlockSpec(memory_space=pl.ANY)
    scratch = [
        pltpu.VMEM((total, cols), BF16),
        pltpu.VMEM((total, cols), BF16),
        pltpu.VMEM((late, cols), BF16),
        pltpu.VMEM((total, cols), BF16),
        pltpu.VMEM((total // 2, cols), BF16),
        pltpu.VMEM((total // 2, cols), BF16),
        pltpu.VMEM((total // 4, cols), BF16),
        pltpu.VMEM((total // 4, cols), BF16),
        pltpu.VMEM((total // 8, cols), BF16),
        pltpu.VMEM(dq_chunks.shape, BF16),
        pltpu.VMEM(mine.shape, BF16),
        pltpu.VMEM(mine.shape, BF16),
        pltpu.VMEM(mine.shape, BF16),
        pltpu.VMEM((4, rows, late), BF16),
        pltpu.VMEM((2, rows, late), BF16),
        pltpu.VMEM((rows, cols), BF16),
        pltpu.VMEM((rows, cols), BF16),
        pltpu.VMEM((rows, cols), BF16),
        pltpu.VMEM((4,) + weights[1].shape, BF16),
        pltpu.VMEM((2 * VECTOR_STEPS,) + vectors.shape, F32),
    ]
    scratch += [dma((2, chunks) if name[0] == "z" else (chunks,)) for name in SEM_NAMES]
    scratch += [dma((count,))] * 4 + [dma((chunks,))] * 2 + [dma((3,))] * 2
    scratch += [dma((VECTOR_STEPS,))] * 2 + [dma((14 + over_x.shape[0] // CHUNK_ROWS,))]
    return pl.pallas_call(
        functools.partial(finish_kernel, chunks, FIRST_TICKS),
        out_shape=(
            jax.ShapeDtypeStruct((2, total, cols), BF16),
            jax.ShapeDtypeStruct((rows, cols), F32),
            jax.ShapeDtypeStruct(vectors.shape, F32),
        ),
        in_specs=vmem(1) + [anywhere] * 14 + vmem(1),
        out_specs=(anywhere, vmem(1)[0], vmem(1)[0]),
        scratch_shapes=scratch,
        compiler_params=pltpu.CompilerParams(
            collective_id=1, has_side_effects=True, vmem_limit_bytes=VMEM_MIDDLE
        ),
        name="finish",
    )(
        gain, dq_chunks, mine, theirs, near, far_up, far, over_x, normed, normed_sib, x, d_hidden, *weights,
        vectors,
    )


def join_kernel(core_ref, in_ref, out_ref):
    out_ref[...] = in_ref[0].astype(F32)


def join_turned_kernel(core_ref, in_ref, out_ref):
    out_ref[0] = in_ref[0].astype(F32).T


def join(core, both, size, first, count, shape, place, turned=False):
    cols = both.shape[2]
    block = (1, cols, size) if turned else (size, cols)
    return pl.pallas_call(
        join_turned_kernel if turned else join_kernel,
        grid_spec=pltpu.PrefetchScalarGridSpec(
            num_scalar_prefetch=1,
            grid=(2, count),
            in_specs=[pl.BlockSpec((1, size, cols), lambda p, i, c: ((p + c[0]) % 2, first + i, 0))],
            out_specs=pl.BlockSpec(block, lambda p, i, c: place(p, i)),
        ),
        out_shape=jax.ShapeDtypeStruct(shape, F32),
        compiler_params=pltpu.CompilerParams(vmem_limit_bytes=VMEM_LIMIT),
        name="join",
    )(core.reshape(1).astype(jnp.int32), both)


def begin_kernel(
    x_ref, gain_ref, shift_ref, bias_ref, w_ref, wo_ref, wu_ref,
    normed_ref, normed_sib, q_in, kv_own, kv_sib, bias_far, w2, w3, wo2, wo3, wu0,
    w0, w1, q_st, kv_st, *sems,
):
    place = Place()
    count = q_in.shape[0]
    width = x_ref.shape[1]
    me = place.seq * 2 + place.tp
    who = (place.tp, lax.rem(place.seq, 2))
    ks, kr, qs, qr, fs, fr, ws, wr, ls = sems
    greet_all(count, me, place.seq, place.tp)
    core = who[1]
    col, wo_rows = w0.shape[2], wo2.shape[0]
    w_own = w_ref.at[:, :, rows_at(core * col, col)]
    w_far = remote(w_own, w2, ws.at[0], wr.at[0], place.tp_partner)
    w_far.start()
    bias_pair = remote(bias_ref, bias_far, ws.at[5], wr.at[5], place.tp_partner)
    bias_pair.start()
    w_loads = [
        pltpu.make_async_copy(w_own, w0, ls.at[0]),
        pltpu.make_async_copy(w_ref.at[:, :, rows_at((1 - core) * col, col)], w1, ls.at[1]),
    ]
    wu_copy = pltpu.make_async_copy(wu_ref.at[:, rows_at(core * wu0.shape[1], wu0.shape[1])], wu0, ls.at[2])
    wu_copy.start()
    for copy in w_loads:
        copy.start()
    wo_far = remote(wo_ref.at[rows_at(core * wo_rows, wo_rows)], wo2, ws.at[1], wr.at[1], place.tp_partner)
    wo_far.start()
    w_last = remote(w2, w3, ws.at[2], wr.at[2], place.core_partner)
    wo_last = remote(wo2, wo3, ws.at[3], wr.at[3], place.core_partner)

    def norm(part, carry):
        span = rows_at(part * 64, 64)
        normed_ref[span, :] = layer_norm(
            x_ref[span, :].astype(F32), gain_ref[0:1, :], shift_ref[0:1, :]
        ).astype(BF16)
        return carry

    lax.fori_loop(0, x_ref.shape[0] // 64, norm, 0)

    normed_pair = remote(normed_ref, normed_sib, ws.at[4], wr.at[4], place.core_partner)
    normed_pair.start()

    def kv_copy(other):
        return remote(kv_st.at[other], kv_own.at[me], ks.at[other], kr.at[me], (other // 2, lax.rem(other, 2)))

    def q_copy(other):
        return remote(q_st.at[other], q_in.at[me], qs.at[other], qr.at[me], (other // 2, lax.rem(other, 2)))

    def kv_came(other):
        return remote(kv_st.at[other], kv_own.at[other], ks.at[other], kr.at[other], (other // 2, lax.rem(other, 2)))

    def q_came(other):
        return remote(q_st.at[other], q_in.at[other], qs.at[other], qr.at[other], (other // 2, lax.rem(other, 2)))

    def forward(other):
        return remote(kv_own.at[other], kv_sib.at[other], fs.at[other], fr.at[other], place.core_partner)

    low = low_lanes(HALF)

    def project(quarter, w):
        bias = bias_ref if quarter < 2 else bias_far
        side = core if quarter % 2 == 0 else 1 - core

        def bias_at(which):
            return bias[2:3, rows_at(which * 2 * col + side * col, col)]

        def dot(which):
            return dot_nn(normed_ref[...], w[which])

        keys, values = dot(1), dot(2) + bias_at(1)
        for pair in range(2):
            lanes = slice(pair * 128, pair * 128 + 128)
            for half in range(2):
                rows = slice(half * HALF, half * HALF + HALF)
                k, v = keys[rows, lanes], values[rows, lanes]
                kv_st[chunk_of(who, quarter, 2 * pair, half)] = jnp.where(low, k, swap_lanes(v)).astype(BF16)
                kv_st[chunk_of(who, quarter, 2 * pair + 1, half)] = jnp.where(low, swap_lanes(k), v).astype(BF16)
        store_packed(who, quarter, dot(0) + bias_at(0), q_st)

        def send(i, carry):
            turned = lax.rem(i + 2 * (place.seq // 2) + 2, 8)
            other = chunk_of(who, quarter, turned // 2, lax.rem(turned, 2))

            @pl.when(other != me)
            def _():
                kv_copy(other).start()
                q_copy(other).start()

            @pl.when(other == me)
            def _():
                kv_own[me] = kv_st[me]
                q_in[me] = q_st[me]

            return carry

        lax.fori_loop(0, 8, send, 0)

    for copy in w_loads:
        copy.wait()
    project(0, w0)
    project(1, w1)
    w_far.wait()
    bias_pair.wait()
    w_last.start()
    project(2, w2)
    w_last.wait()
    project(3, w3)
    wo_far.wait()
    wo_last.start()
    forward(me).start()

    def receive(i, carry):
        other = lax.rem(place.seq + lax.rem(i, count // 2), count // 2) * 2 + lax.rem(
            place.tp + i // (count // 2), 2
        )
        kv_came(other).wait_recv()
        forward(other).start()
        return carry

    lax.fori_loop(1, count, receive, 0)

    def rest(k, carry):
        other = lax.rem(me + k, count)
        q_came(other).wait_recv()
        kv_copy(other).wait_send()
        q_copy(other).wait_send()
        return carry

    lax.fori_loop(1, count, rest, 0)

    def forwarded(k, carry):
        forward(k).wait()
        return carry

    lax.fori_loop(0, count, forwarded, 0)
    wo_last.wait()
    normed_pair.wait()
    wu_copy.wait()


def begin(x, gains, shifts, bias, w, wo, wu):
    rows, width = x.shape
    count = 32
    dma = pltpu.SemaphoreType.DMA
    anywhere = pl.BlockSpec(memory_space=pl.ANY)
    q_shape, kv_shape = (count, QUART, 2 * HEAD), (count, HALF, 2 * HEAD)
    w_quarter = (3, width, w.shape[2] // 2)
    wo_quarter = (wo.shape[0] // 2, wo.shape[1])
    return pl.pallas_call(
        begin_kernel,
        out_shape=(
            jax.ShapeDtypeStruct((rows, width), BF16),
            jax.ShapeDtypeStruct((rows, width), BF16),
            jax.ShapeDtypeStruct(q_shape, BF16),
            jax.ShapeDtypeStruct(kv_shape, BF16),
            jax.ShapeDtypeStruct(kv_shape, BF16),
            jax.ShapeDtypeStruct(bias.shape, F32),
            jax.ShapeDtypeStruct(w_quarter, BF16),
            jax.ShapeDtypeStruct(w_quarter, BF16),
            jax.ShapeDtypeStruct(wo_quarter, BF16),
            jax.ShapeDtypeStruct(wo_quarter, BF16),
            jax.ShapeDtypeStruct((wu.shape[0], wu.shape[1] // 2), BF16),
        ),
        in_specs=vmem(4) + [anywhere] * 3,
        out_specs=tuple(vmem(1) + [anywhere] + vmem(6) + [anywhere] * 3),
        scratch_shapes=[pltpu.VMEM(w_quarter, BF16)] * 2
        + [pltpu.VMEM(q_shape, BF16), pltpu.VMEM(kv_shape, BF16)]
        + [dma((count,))] * 6
        + [dma((6,))] * 2
        + [dma((3,))],
        compiler_params=pltpu.CompilerParams(
            collective_id=3, has_side_effects=True, vmem_limit_bytes=VMEM_LIMIT
        ),
        name="begin",
    )(x, gains, shifts, bias, w, wo, wu)


def norm_parts(values):
    mean = jnp.mean(values, axis=-1, keepdims=True)
    centred = values - mean
    rstd = lax.rsqrt(jnp.mean(centred * centred, axis=-1, keepdims=True) + EPS)
    return centred * rstd, rstd


GELU_A = 0.7978845608028654
GELU_B = 0.044715


def gelu_parts(u):
    square = u * u
    t = jnp.tanh(GELU_A * u * (1.0 + GELU_B * square))
    rise = 0.5 * (1.0 + t)
    return u * rise, rise + 0.5 * u * (1.0 - t * t) * (GELU_A * (1.0 + 3.0 * GELU_B * square))


def col_sum(values):
    return jnp.sum(values, axis=0, keepdims=True)


def back_rows(xhat, rstd, gain, upstream):
    e = upstream * gain
    return rstd * (
        e - jnp.mean(e, axis=-1, keepdims=True) - xhat * jnp.mean(e * xhat, axis=-1, keepdims=True)
    )


def dot_nn(a, b):
    return jnp.dot(a, b, preferred_element_type=F32)


def dot_nt(a, b):
    return lax.dot_general(a, b, (((1,), (1,)), ((), ())), preferred_element_type=F32)


def dot_tn(a, b):
    return lax.dot_general(a, b, (((0,), (0,)), ((), ())), preferred_element_type=F32)


def middle_kernel(
    gains, shifts, bias_out, bias_down, bias_own, bias_far, att_ref, x_ref, og_ref,
    wo_ref, wo2, wo3, wu_ref, wu2, wd_ref,
    result, da_in, dh, vec, near_ref, far_up_ref, far_ref, over_x_ref,
    att_in, att_s, att_sib, wo_s, wu_s, wd_s, x_s, branch_s, hidden_s, inner_s, inner_sib, act_s, act_sib,
    dg_s, dup_sib, down_s, dd_s, dd_sib, db_s, db_sib, da_st,
    ats, atr, das, dar, ws, wr, cs, cr, loc,
):
    place = Place()
    count = att_in.shape[0]
    me = place.seq * 2 + place.tp
    who = (place.tp, lax.rem(place.seq, 2))
    rows, width = x_s.shape
    hid = wd_s.shape[1]
    wu0, wu1 = (wu_ref.at[:, rows_at(c * hid, hid)] for c in (who[1], 1 - who[1]))
    wo0, wo1 = (wo_ref.at[rows_at(c * wo2.shape[0], wo2.shape[0])] for c in (who[1], 1 - who[1]))
    wd0, wd1 = (wd_ref.at[rows_at(c * hid, hid)] for c in (who[1], 1 - who[1]))
    greet_all(count, me, place.seq, place.tp)

    def start(k, carry):
        chunk_copy(count, me, k, att_ref, att_in, ats, atr).start()
        return carry

    lax.fori_loop(1, count, start, 0)
    wd_far = remote(wd0, wd_s.at[2], ws.at[0], wr.at[0], place.tp_partner)
    wd_far.start()
    wu_last = remote(wu2, wu_s.at[3], ws.at[1], wr.at[1], place.core_partner)
    wu_last.start()
    wd_last = remote(wd_s.at[2], wd_s.at[3], ws.at[2], wr.at[2], place.core_partner)
    loads = [(att_ref.at[me], att_in.at[me]), (x_ref, x_s), (og_ref, dh)]
    loads += [(w, wo_s.at[r]) for r, w in enumerate((wo0, wo1, wo2, wo3))]
    loads += [(w, wu_s.at[r]) for r, w in enumerate((wu0, wu1, wu2))]
    loads += [(w, wd_s.at[r]) for r, w in enumerate((wd0, wd1))]
    loads = [pltpu.make_async_copy(src, dst, loc.at[i]) for i, (src, dst) in enumerate(loads)]
    for copy in loads:
        copy.start()

    def to_core(i, src, dst):
        return remote(src, dst, cs.at[i], cr.at[i], place.core_partner)

    att_pair = [to_core(i, att_s.at[2 * i + 1], att_sib.at[i]) for i in range(2)]
    act_pair = [to_core(2 + i, act_s.at[2 * i + 1], act_sib.at[i]) for i in range(2)]
    dup_pair = [to_core(4 + i, dg_s.at[2 * i + 1], dup_sib.at[i]) for i in range(2)]
    inner_pair = to_core(6, inner_s, inner_sib)
    dd_pair = to_core(7, dd_s, dd_sib)
    db_pair = to_core(8, db_s, db_sib)

    def came(k, carry):
        chunk_copy(count, me, k, att_ref, att_in, ats, atr).wait()
        return carry

    lax.fori_loop(1, count, came, 0)
    for copy in loads:
        copy.wait()
    for quarter in range(4):
        load_packed(who, quarter, att_in, att_s.at[quarter], 0)
    for copy in att_pair:
        copy.start()

    def cols(i):
        return rows_at(i * 256, 256)

    def project(i, carry):
        span = cols(i)
        branch_s[:, span] = (
            dot_nn(att_s[0], wo_s[0, :, span])
            + dot_nn(att_s[1], wo_s[1, :, span])
            + dot_nn(att_s[2], wo_s[2, :, span])
            + dot_nn(att_s[3], wo_s[3, :, span])
            + bias_out[:, span]
        )
        return carry

    lax.fori_loop(0, width // 256, project, 0)

    def into(i, carry):
        span = rows_at(i * 64, 64)
        hidden = x_s[span, :].astype(F32) + layer_norm(branch_s[span, :], gains[1:2, :], shifts[1:2, :])
        hidden_s[span, :] = hidden
        inner_s[span, :] = layer_norm(hidden, gains[2:3, :], shifts[2:3, :]).astype(BF16)
        return carry

    lax.fori_loop(0, rows // 64, into, 0)
    inner_pair.start()
    for quarter in range(4):
        if quarter == 3:
            wu_last.wait()

        bias = bias_own if quarter < 2 else bias_far
        side = who[1] if quarter % 2 == 0 else 1 - who[1]

        def up(i, carry, quarter=quarter, bias=bias, side=side):
            span = cols(i)
            act, slope = gelu_parts(
                dot_nn(inner_s[...], wu_s[quarter, :, span]) + bias[pl.ds(side, 1), span]
            )
            act_s[quarter, :, span] = act.astype(BF16)
            dg_s[quarter, :, span] = slope.astype(BF16)
            return carry

        lax.fori_loop(0, hid // 256, up, 0)
        if quarter % 2 == 1:
            act_pair[quarter // 2].start()

    def down_own(i, carry):
        span = cols(i)
        down_s[:, span] = (
            dot_nn(act_s[0], wd_s[0, :, span]) + dot_nn(act_s[1], wd_s[1, :, span]) + bias_down[:, span]
        )
        return carry

    lax.fori_loop(0, width // 256, down_own, 0)
    wd_far.wait()
    wd_last.start()
    for quarter in (2, 3):
        if quarter == 3:
            wd_last.wait()

        def down_far(i, carry, quarter=quarter):
            span = cols(i)
            down_s[:, span] += dot_nn(act_s[quarter], wd_s[quarter, :, span])
            return carry

        lax.fori_loop(0, width // 256, down_far, 0)

    none = jnp.zeros((1, width), F32)

    def turn(i, carry):
        gain, shift, bias = carry
        span = rows_at(i * 64, 64)
        xhat, rstd = norm_parts(down_s[span, :])
        result[span, :] = (hidden_s[span, :] + xhat * gains[3:4, :] + shifts[3:4, :]).astype(BF16)
        upstream = dh[span, :]
        d_down = back_rows(xhat, rstd, gains[3:4, :], upstream)
        dd_s[span, :] = d_down.astype(BF16)
        return gain + col_sum(upstream * xhat), shift + col_sum(upstream), bias + col_sum(d_down)

    gain, shift, bias = lax.fori_loop(0, rows // 64, turn, (none,) * 3)
    vec[...] = jnp.zeros_like(vec)
    vec[3:4, :] = gain
    vec[7:8, :] = shift
    vec[9:10, :] = bias
    dd_pair.start()
    for quarter in range(4):
        absolute = (who[0] * 2 + who[1]) ^ quarter

        def back_up(i, carry, quarter=quarter, absolute=absolute):
            span = cols(i)
            d_up = dot_nt(dd_s[...], wd_s[quarter, span, :]) * dg_s[quarter, :, span].astype(F32)
            d_up = d_up.astype(BF16)
            dg_s[quarter, :, span] = d_up
            vec[pl.ds(12 + absolute, 1), span] = col_sum(d_up.astype(F32))
            return carry

        lax.fori_loop(0, hid // 256, back_up, 0)
        if quarter % 2 == 1:
            dup_pair[quarter // 2].start()

    def back_inner(i, carry):
        span = cols(i)
        down_s[:, span] = (
            dot_nt(dg_s[0], wu_s[0, span, :])
            + dot_nt(dg_s[1], wu_s[1, span, :])
            + dot_nt(dg_s[2], wu_s[2, span, :])
            + dot_nt(dg_s[3], wu_s[3, span, :])
        )
        return carry

    lax.fori_loop(0, width // 256, back_inner, 0)

    def out_of(i, carry):
        gain3, shift3, gain2, shift2, bias = carry
        span = rows_at(i * 64, 64)
        d_inner = down_s[span, :]
        xhat, rstd = norm_parts(hidden_s[span, :])
        gain3 = gain3 + col_sum(d_inner * xhat)
        shift3 = shift3 + col_sum(d_inner)
        d_hidden = dh[span, :] + back_rows(xhat, rstd, gains[2:3, :], d_inner)
        dh[span, :] = d_hidden
        xhat, rstd = norm_parts(branch_s[span, :])
        d_branch = back_rows(xhat, rstd, gains[1:2, :], d_hidden)
        db_s[span, :] = d_branch.astype(BF16)
        return (
            gain3, shift3, gain2 + col_sum(d_hidden * xhat), shift2 + col_sum(d_hidden),
            bias + col_sum(d_branch),
        )

    sums = lax.fori_loop(0, rows // 64, out_of, (none,) * 5)
    for row, value in zip((2, 6, 1, 5, 8), sums):
        vec[row : row + 1, :] = value
    db_pair.start()

    def da_copy(other):
        return remote(
            da_st.at[other], da_in.at[me], das.at[other], dar.at[me], (other // 2, lax.rem(other, 2))
        )

    def da_came(other):
        return remote(
            da_st.at[other], da_in.at[other], das.at[other], dar.at[other], (other // 2, lax.rem(other, 2))
        )

    for quarter in range(4):
        store_packed(who, quarter, dot_nt(db_s[...], wo_s[quarter]), da_st)

        def send(i, carry, quarter=quarter):
            turned = lax.rem(i + 2 * (place.seq // 2) + 2, 8)
            other = chunk_of(who, quarter, turned // 2, lax.rem(turned, 2))

            @pl.when(other != me)
            def _():
                da_copy(other).start()

            @pl.when(other == me)
            def _():
                da_in[me] = da_st[me]

            return carry

        lax.fori_loop(0, 8, send, 0)

    for copy in dup_pair + [inner_pair]:
        copy.wait()

    def grad_up(i, carry):
        span = cols(i)
        for near, slot in ((0, 0), (2, 1)):
            wu_s[near, :, span] = (
                dot_tn(inner_s[...], dg_s[near, :, span]) + dot_tn(inner_sib[...], dup_sib[slot, :, span])
            ).astype(BF16)
        return carry

    lax.fori_loop(0, hid // 256, grad_up, 0)
    for copy in att_pair + [db_pair]:
        copy.wait()
    for near, slot in ((0, 0), (2, 1)):
        wo_s[near] = (dot_tn(att_s[near], db_s[...]) + dot_tn(att_sib[slot], db_sib[...])).astype(BF16)
    up_rows, out_rows = wu_s.shape[1], wo_s.shape[1]
    stores = [
        (wu_s.at[0], near_ref.at[pl.ds(0, up_rows)]),
        (wo_s.at[0], near_ref.at[pl.ds(up_rows + hid, out_rows)]),
        (wu_s.at[2], far_up_ref),
        (wo_s.at[2], far_ref.at[pl.ds(hid, out_rows)]),
        (wd_s.at[0], near_ref.at[pl.ds(up_rows, hid)]),
        (wd_s.at[2], far_ref.at[pl.ds(0, hid)]),
    ]
    strip = CHUNK_ROWS // 2
    for j in range(hid // CHUNK_ROWS):
        span = rows_at(j * CHUNK_ROWS + (1 - place.x) * strip, strip)
        for i, slot in enumerate((0, 2)):
            stores.append((wd_s.at[slot, span], over_x_ref.at[pl.ds(j * CHUNK_ROWS + i * strip, strip)]))
    stores = [pltpu.make_async_copy(src, dst, loc.at[i]) for i, (src, dst) in enumerate(stores)]
    for copy in stores[:4]:
        copy.start()
    for copy in act_pair + [dd_pair]:
        copy.wait()

    def grad_down(i, carry):
        span = cols(i)
        for near, slot in ((0, 0), (2, 1)):
            wd_s[near, span, :] = (
                dot_tn(act_s[near, :, span], dd_s[...]) + dot_tn(act_sib[slot, :, span], dd_sib[...])
            ).astype(BF16)
        return carry

    lax.fori_loop(0, hid // 256, grad_down, 0)
    for copy in stores[4:]:
        copy.start()

    def da_wait(k, carry):
        other = lax.rem(me + k, count)
        da_came(other).wait_recv()
        da_copy(other).wait_send()
        return carry

    lax.fori_loop(1, count, da_wait, 0)
    for copy in stores:
        copy.wait()


def middle(gains, shifts, bias_out, bias_down, bias, bias_far, att, x, out_grad, wo3, w_up, wu2, w_down):
    rows, width = x.shape
    count = att.shape[0]
    hid = wu2.shape[1]
    out_rows = wo3[1].shape[0]
    dma = pltpu.SemaphoreType.DMA
    anywhere = pl.BlockSpec(memory_space=pl.ANY)

    def held(*shape, dtype=BF16):
        return pltpu.VMEM(shape, dtype)

    scratch = [
        held(*att.shape),
        held(4, rows, out_rows),
        held(2, rows, out_rows),
        held(4, out_rows, width),
        held(4, width, hid),
        held(4, hid, width),
        held(rows, width),
        held(rows, width, dtype=F32),
        held(rows, width, dtype=F32),
        held(rows, width),
        held(rows, width),
        held(4, rows, hid),
        held(2, rows, hid),
        held(4, rows, hid),
        held(2, rows, hid),
        held(rows, width, dtype=F32),
        held(rows, width),
        held(rows, width),
        held(rows, width),
        held(rows, width),
        held(*att.shape),
    ]
    scratch += [dma((count,))] * 4 + [dma((3,))] * 2 + [dma((9,))] * 2 + [dma((6 + 2 * hid // CHUNK_ROWS,))]
    return pl.pallas_call(
        middle_kernel,
        out_shape=(
            jax.ShapeDtypeStruct((rows, width), BF16),
            jax.ShapeDtypeStruct(att.shape, BF16),
            jax.ShapeDtypeStruct((rows, width), F32),
            jax.ShapeDtypeStruct((16, width), F32),
            jax.ShapeDtypeStruct((hid + width + out_rows, width), BF16),
            jax.ShapeDtypeStruct((width, hid), BF16),
            jax.ShapeDtypeStruct((hid + out_rows, width), BF16),
            jax.ShapeDtypeStruct((hid, width), BF16),
        ),
        in_specs=vmem(6) + [anywhere] * 9,
        out_specs=tuple(vmem(4) + [anywhere] * 4),
        scratch_shapes=scratch,
        compiler_params=pltpu.CompilerParams(
            collective_id=4, has_side_effects=True, vmem_limit_bytes=VMEM_MIDDLE
        ),
        name="middle",
    )(
        gains, shifts, bias_out, bias_down, bias, bias_far, att, x, out_grad, *wo3, w_up, wu2, w_down
    )


def fast_local(
    tokens_in, w_qkv, bias_qv, w_out, bias_out, w_up, bias_up, w_down, bias_down,
    norm_gains, norm_shifts, out_grad, lengths, prefixes, placement,
):
    seq_count = lax.axis_size("seq")
    seq, tp = lax.axis_index("seq"), lax.axis_index("tp")
    core = seq % 2
    over_tp = [(0, 1), (1, 0)]

    def to_tp(values):
        return lax.ppermute(values, "tp", over_tp)

    width = w_qkv.shape[0]
    w3 = jnp.transpose(w_qkv, (1, 0, 2))
    bias = jnp.concatenate([bias_up.reshape(2, width), bias_qv.reshape(1, width)]).astype(F32)
    bias = jnp.pad(bias, ((0, 5), (0, 0)))
    tables = block_tables(lengths, prefixes, placement, core)
    normed, normed_sib, q_own, kv_own, kv_sib, bias_far, wq2, wq3, wo2, wo3, wu0 = begin(
        tokens_in, norm_gains, norm_shifts, bias, w3, w_out, w_up
    )
    wu2 = to_tp(wu0)
    att_chunks, out_t, mass, kv_pack, kv_turned = attend(core, tables, q_own, kv_own, kv_sib)
    result, da_own, d_hidden, vectors, near, far_up, far, over_x = middle(
        norm_gains, norm_shifts, bias_out.astype(F32)[None], bias_down.astype(F32)[None], bias, bias_far,
        att_chunks, tokens_in, out_grad, [w_out, wo2, wo3], w_up, wu2, w_down,
    )
    far_up = to_tp(far_up)
    over_x = lax.ppermute(over_x, "seq", [(i, i ^ 2) for i in range(lax.axis_size("seq"))])
    dq_chunks, mine, theirs = attend_back(core, tables, q_own, da_own, out_t, mass, kv_pack, kv_turned)
    both, grad_x, vectors = finish(
        norm_gains, dq_chunks, mine, theirs, near, far_up, far, over_x, normed, normed_sib, tokens_in, d_hidden,
        [w3, wq2, wq3], vectors,
    )
    up, down, out = (n // 256 for n in (width, wu2.shape[1], wo2.shape[0]))
    g_up = join(core, both, 512, 0, up // 2, w_up.shape, lambda p, i: (i, p))
    g_down = join(core, both, 512, up // 2, down // 2, w_down.shape, lambda p, i: (p * (down // 2) + i, 0))
    g_out = join(core, both, 256, up + down, out, w_out.shape, lambda p, i: (p * out + i, 0))
    g_qkv = join(
        core, both, 256, up + down + out, 3, (3, width, w_qkv.shape[2]), lambda p, i: (i, 0, p), turned=True
    )
    g_qkv = jnp.transpose(g_qkv, (1, 0, 2))
    own_cols = bias_qv.shape[1]
    grad_bias_qv = lax.dynamic_slice_in_dim(vectors[10:12], tp * own_cols, own_cols, 1)
    grad_bias_up = lax.dynamic_slice_in_dim(
        vectors[12:16].reshape(-1), tp * bias_up.shape[0], bias_up.shape[0]
    )
    return (
        result,
        grad_x,
        g_qkv,
        grad_bias_qv,
        g_out,
        vectors[8],
        g_up,
        grad_bias_up,
        g_down,
        vectors[9],
        vectors[0:4],
        vectors[4:8],
    )


def pack_tables(lengths, prefixes, row_total):
    where_row = jnp.arange(row_total, dtype=jnp.int32)
    doc_ends = running_ends(lengths)
    document = jnp.sum((where_row[:, None] >= doc_ends[None, :]).astype(jnp.int32), axis=1)
    limits = doc_ends - lengths + prefixes
    doc_pick = document[:, None] == jnp.arange(lengths.shape[0], dtype=jnp.int32)[None, :]
    visible = jnp.sum(jnp.where(doc_pick, limits[None, :], 0), axis=1)
    return (document, visible)


def padded_tables(document, visible, margin):
    row_total = document.shape[0]
    border = jnp.full((margin,), -1, jnp.int32)
    doc_pad = jnp.concatenate([border, document, border])
    pos_pad = jnp.arange(-margin, row_total + margin, dtype=jnp.int32)
    blank = jnp.zeros((margin,), jnp.int32)
    seen_pad = jnp.concatenate([blank, visible, blank])
    return (doc_pad, pos_pad, seen_pad)


def allowed_pairs(query_pos, query_doc, key_pos, key_doc, key_seen):
    return (query_doc[:, None] == key_doc[None, :]) & (
        (key_pos[None, :] <= query_pos[:, None]) | (key_pos[None, :] < key_seen[None, :])
    )


def pick_blocks(blocks, order):
    return lax.map(lambda i: lax.dynamic_index_in_dim(blocks, i, 0, False), order)


def to_pack(stored, pack_order, margin, block_size):
    blocks = stored.reshape((pack_order.shape[0], block_size) + stored.shape[1:])
    ordered = pick_blocks(blocks, pack_order).reshape(stored.shape)
    widths = [(margin, margin)] + [(0, 0)] * (stored.ndim - 1)
    return jnp.pad(ordered, widths)


def from_pack(padded, placement, margin, block_size, row_total):
    core = padded[margin : margin + row_total]
    blocks = core.reshape((placement.shape[0], block_size) + core.shape[1:])
    return pick_blocks(blocks, placement).reshape(core.shape)


def masked_scores(query_h, key_h, allowed):
    scores = query_h.shape[-1] ** (-0.5) * jnp.einsum(
        "qe,ke->qk", query_h, key_h, preferred_element_type=jnp.float32
    )
    return jnp.where(allowed, scores, -jnp.inf)


def forward_block(query_block, key_win, value_win, allowed):

    def forward_one_head(head):
        query_h = lax.dynamic_index_in_dim(query_block, head, 1, False)
        key_h = lax.dynamic_index_in_dim(key_win, head, 1, False)
        value_h = lax.dynamic_index_in_dim(value_win, head, 1, False)
        masked = masked_scores(query_h, key_h, allowed)
        row_top = jnp.max(masked, axis=1, keepdims=True)
        expo = jnp.exp(masked - row_top)
        row_sum = jnp.sum(expo, axis=1, keepdims=True)
        probs_b = (expo / row_sum).astype(jnp.bfloat16)
        output = jnp.dot(probs_b, value_h, preferred_element_type=jnp.float32)
        return (output, (row_top + jnp.log(row_sum))[:, 0])

    return lax.map(forward_one_head, jnp.arange(query_block.shape[1], dtype=jnp.int32))


def attention_grads(
    query_block, d_att_block, mass_block, total_block, key_block, value_block, allowed
):
    score_scale = query_block.shape[-1] ** (-0.5)

    def attention_one_head(head):
        query_h = lax.dynamic_index_in_dim(query_block, head, 1, False)
        d_att_h = lax.dynamic_index_in_dim(d_att_block, head, 1, False)
        key_h = lax.dynamic_index_in_dim(key_block, head, 1, False)
        value_h = lax.dynamic_index_in_dim(value_block, head, 1, False)
        mass_h = lax.dynamic_index_in_dim(mass_block, head, 0, False)
        total_h = lax.dynamic_index_in_dim(total_block, head, 0, False)
        masked = masked_scores(query_h, key_h, allowed)
        probs = jnp.exp(masked - mass_h[:, None])
        d_probs = jnp.einsum("qe,ke->qk", d_att_h, value_h, preferred_element_type=jnp.float32)
        d_scores = (probs * (d_probs - total_h[:, None])).astype(jnp.bfloat16)
        results = []
        results.append(
            score_scale
            * jnp.einsum("qk,ke->qe", d_scores, key_h, preferred_element_type=jnp.float32)
        )
        results.append(
            score_scale
            * jnp.einsum("qk,qe->ke", d_scores, query_h, preferred_element_type=jnp.float32)
        )
        results.append(
            jnp.einsum(
                "qk,qe->ke", probs.astype(jnp.bfloat16), d_att_h, preferred_element_type=jnp.float32
            )
        )
        return tuple(results)

    return lax.map(attention_one_head, jnp.arange(query_block.shape[1], dtype=jnp.int32))


def general_local(
    tokens_in,
    w_qkv,
    bias_qv,
    w_out,
    bias_out,
    w_up,
    bias_up,
    w_down,
    bias_down,
    norm_gains,
    norm_shifts,
    out_grad,
    lengths,
    prefixes,
    placement,
):
    seq_count = lax.axis_size("seq")
    block_total = placement.shape[0]
    blocks_here = block_total // seq_count
    total_rows = block_total * BLK
    own_rows = blocks_here * BLK
    model_width = w_qkv.shape[0]
    head_span = w_qkv.shape[2]
    heads_here = head_span // HEAD
    margin = LONGEST + BLK
    window = LONGEST + 2 * BLK
    document, visible = pack_tables(lengths, prefixes, total_rows)
    doc_pad, pos_pad, seen_pad = padded_tables(document, visible, margin)
    own_blocks = lax.dynamic_slice_in_dim(
        placement, lax.axis_index("seq") * blocks_here, blocks_here
    )
    pack_order = inverse_order(placement)
    offsets = jnp.arange(BLK, dtype=jnp.int32)

    def query_window(index):
        first = own_blocks[index] * BLK
        key_first = margin + first - LONGEST
        allowed = allowed_pairs(
            first + offsets,
            lax.dynamic_slice_in_dim(document, first, BLK),
            lax.dynamic_slice_in_dim(pos_pad, key_first, window),
            lax.dynamic_slice_in_dim(doc_pad, key_first, window),
            lax.dynamic_slice_in_dim(seen_pad, key_first, window),
        )
        return (key_first, allowed)

    input_f32 = tokens_in.astype(jnp.float32)
    normed, back_first = jax.vjp(layer_norm, input_f32, norm_gains[0], norm_shifts[0])
    rows_all = lax.all_gather(normed.astype(jnp.bfloat16), "tp", axis=0, tiled=True)
    flat_qkv = w_qkv.reshape(model_width, 3 * head_span)
    mixed = jnp.dot(rows_all, flat_qkv, preferred_element_type=jnp.float32).reshape(
        own_rows, 3, head_span
    )
    query_b = (mixed[:, 0] + bias_qv[0].astype(jnp.float32)).astype(jnp.bfloat16)
    key_b = mixed[:, 1].astype(jnp.bfloat16)
    value_b = (mixed[:, 2] + bias_qv[1].astype(jnp.float32)).astype(jnp.bfloat16)
    keys_all, values_all = (
        lax.all_gather(key_b, "seq", axis=0, tiled=True),
        lax.all_gather(value_b, "seq", axis=0, tiled=True),
    )
    keys_pad = to_pack(keys_all, pack_order, margin, BLK).reshape(-1, heads_here, HEAD)
    values_pad = to_pack(values_all, pack_order, margin, BLK).reshape(-1, heads_here, HEAD)
    head_shape = (own_rows, heads_here, HEAD)
    query3 = query_b.reshape(head_shape)
    attended_list = []
    mass_list = []
    for index in range(blocks_here):
        key_first, allowed = query_window(index)
        outputs, masses = forward_block(
            query3[index * BLK : (index + 1) * BLK],
            lax.dynamic_slice_in_dim(keys_pad, key_first, window),
            lax.dynamic_slice_in_dim(values_pad, key_first, window),
            allowed,
        )
        attended_list.append(jnp.transpose(outputs, (1, 0, 2)))
        mass_list.append(masses)
    attended32 = jnp.concatenate(attended_list, axis=0)
    log_mass = jnp.concatenate(mass_list, axis=1)
    attended_b = attended32.reshape(own_rows, head_span).astype(jnp.bfloat16)
    branch = lax.psum_scatter(
        jnp.dot(attended_b, w_out, preferred_element_type=jnp.float32).astype(jnp.bfloat16),
        "tp",
        scatter_dimension=0,
        tiled=True,
    ).astype(jnp.float32) + bias_out.astype(jnp.float32)
    post_attn, back_post = jax.vjp(layer_norm, branch, norm_gains[1], norm_shifts[1])
    hidden = input_f32 + post_attn
    inner, back_inner = jax.vjp(layer_norm, hidden, norm_gains[2], norm_shifts[2])
    inner_all = lax.all_gather(inner.astype(jnp.bfloat16), "tp", axis=0, tiled=True)
    upward = jnp.dot(inner_all, w_up, preferred_element_type=jnp.float32) + bias_up.astype(
        jnp.float32
    )
    active, back_gate = jax.vjp(smooth_gate, upward)
    active_b = active.astype(jnp.bfloat16)
    down = lax.psum_scatter(
        jnp.dot(active_b, w_down, preferred_element_type=jnp.float32).astype(jnp.bfloat16),
        "tp",
        scatter_dimension=0,
        tiled=True,
    ).astype(jnp.float32) + bias_down.astype(jnp.float32)
    final, back_final = jax.vjp(layer_norm, down, norm_gains[3], norm_shifts[3])
    result = (hidden + final).astype(jnp.bfloat16)
    d_down, gain_last, shift_last = back_final(out_grad)
    grad_bias_down = jnp.sum(d_down, axis=0)
    d_down_all = lax.all_gather(d_down.astype(jnp.bfloat16), "tp", axis=0, tiled=True)
    grad_w_down = jnp.einsum("tf,td->fd", active_b, d_down_all, preferred_element_type=jnp.float32)
    d_active = jnp.einsum("td,fd->tf", d_down_all, w_down, preferred_element_type=jnp.float32)
    (d_up,) = back_gate(d_active)
    d_up_b = d_up.astype(jnp.bfloat16)
    grad_bias_up = jnp.sum(d_up_b.astype(jnp.float32), axis=0)
    grad_w_up = jnp.einsum("td,tf->df", inner_all, d_up_b, preferred_element_type=jnp.float32)
    d_inner = lax.psum_scatter(
        jnp.einsum("tf,df->td", d_up_b, w_up, preferred_element_type=jnp.float32).astype(
            jnp.bfloat16
        ),
        "tp",
        scatter_dimension=0,
        tiled=True,
    ).astype(jnp.float32)
    d_hidden_part, gain_third, shift_third = back_inner(d_inner)
    d_hidden = out_grad + d_hidden_part
    d_branch, gain_second, shift_second = back_post(d_hidden)
    grad_bias_out = jnp.sum(d_branch, axis=0)
    d_branch_all = lax.all_gather(d_branch.astype(jnp.bfloat16), "tp", axis=0, tiled=True)
    grad_w_out = jnp.einsum(
        "te,td->ed", attended_b, d_branch_all, preferred_element_type=jnp.float32
    )
    d_att_b = jnp.einsum(
        "td,ed->te", d_branch_all, w_out, preferred_element_type=jnp.float32
    ).astype(jnp.bfloat16)
    d_att3 = d_att_b.reshape(head_shape)
    d_total = jnp.sum(d_att3.astype(jnp.float32) * attended32, axis=2).T
    d_query_list = []
    key_buffer = jnp.zeros((total_rows + 2 * margin, head_span), jnp.float32)
    value_buffer = jnp.zeros((total_rows + 2 * margin, head_span), jnp.float32)
    for index in range(blocks_here):
        key_first, allowed = query_window(index)
        rows = slice(index * BLK, (index + 1) * BLK)
        d_query_h, d_key_h, d_value_h = attention_grads(
            query3[rows],
            d_att3[rows],
            log_mass[:, rows],
            d_total[:, rows],
            lax.dynamic_slice_in_dim(keys_pad, key_first, window),
            lax.dynamic_slice_in_dim(values_pad, key_first, window),
            allowed,
        )
        d_query_list.append(jnp.transpose(d_query_h, (1, 0, 2)))
        key_piece = jnp.transpose(d_key_h, (1, 0, 2)).reshape(window, head_span)
        value_piece = jnp.transpose(d_value_h, (1, 0, 2)).reshape(window, head_span)
        key_buffer = lax.dynamic_update_slice_in_dim(
            key_buffer,
            lax.dynamic_slice_in_dim(key_buffer, key_first, window) + key_piece,
            key_first,
            0,
        )
        value_buffer = lax.dynamic_update_slice_in_dim(
            value_buffer,
            lax.dynamic_slice_in_dim(value_buffer, key_first, window) + value_piece,
            key_first,
            0,
        )
    key_terms = from_pack(key_buffer, placement, margin, BLK, total_rows)
    value_terms = from_pack(value_buffer, placement, margin, BLK, total_rows)
    d_keys, d_values = (
        lax.psum_scatter(
            key_terms.astype(jnp.bfloat16), "seq", scatter_dimension=0, tiled=True
        ).astype(jnp.float32),
        lax.psum_scatter(
            value_terms.astype(jnp.bfloat16), "seq", scatter_dimension=0, tiled=True
        ).astype(jnp.float32),
    )
    d_query = jnp.concatenate(d_query_list, axis=0)
    d_query_b = d_query.reshape(own_rows, head_span).astype(jnp.bfloat16)
    d_keys_b = d_keys.astype(jnp.bfloat16)
    d_values_b = d_values.astype(jnp.bfloat16)
    grad_bias_qv = jnp.stack(
        [
            jnp.sum(d_query_b.astype(jnp.float32), axis=0),
            jnp.sum(d_values_b.astype(jnp.float32), axis=0),
        ]
    )
    d_mixed = jnp.concatenate([d_query_b, d_keys_b, d_values_b], axis=1)
    grad_w_qkv = jnp.einsum(
        "td,tc->dc", rows_all, d_mixed, preferred_element_type=jnp.float32
    ).reshape(model_width, 3, head_span)
    d_normed = lax.psum_scatter(
        jnp.einsum("tc,dc->td", d_mixed, flat_qkv, preferred_element_type=jnp.float32).astype(
            jnp.bfloat16
        ),
        "tp",
        scatter_dimension=0,
        tiled=True,
    ).astype(jnp.float32)
    d_input_part, gain_first, shift_first = back_first(d_normed)
    grad_x = d_hidden + d_input_part
    summed = (
        lax.psum(grad_w_qkv.astype(jnp.bfloat16), "seq").astype(jnp.float32),
        lax.psum(grad_bias_qv.astype(jnp.bfloat16), "seq").astype(jnp.float32),
        lax.psum(grad_w_out.astype(jnp.bfloat16), "seq").astype(jnp.float32),
        lax.psum(grad_w_up.astype(jnp.bfloat16), "seq").astype(jnp.float32),
        lax.psum(grad_bias_up.astype(jnp.bfloat16), "seq").astype(jnp.float32),
        lax.psum(grad_w_down.astype(jnp.bfloat16), "seq").astype(jnp.float32),
    )
    gain_stack = jnp.stack([gain_first, gain_second, gain_third, gain_last])
    shift_stack = jnp.stack([shift_first, shift_second, shift_third, shift_last])
    vectors = lax.psum((gain_stack, shift_stack, grad_bias_out, grad_bias_down), ("seq", "tp"))
    return (
        result,
        grad_x,
        summed[0],
        summed[1],
        summed[2],
        vectors[2],
        summed[3],
        summed[4],
        summed[5],
        vectors[3],
        vectors[0],
        vectors[1],
    )


def solution(mesh):
    placed = (
        P(("seq", "tp"), None),
        P(None, None, "tp"),
        P(None, "tp"),
        P("tp", None),
        P(),
        P(None, "tp"),
        P("tp"),
        P("tp", None),
        P(),
        P(),
        P(),
        P(("seq", "tp"), None),
        P(),
        P(),
        P(),
    )
    seq_count, tp_count = mesh.shape["seq"], mesh.shape["tp"]

    def local(*args):
        tokens_in, w_qkv, placement = args[0], args[1], args[-1]
        heads = w_qkv.shape[2] * tp_count // HEAD
        paired = seq_count * tp_count == 2 * heads == placement.shape[0]
        sizes = (tokens_in.shape[0], w_qkv.shape[0], heads, seq_count, tp_count)
        fast = paired and sizes == (BLK, 1024, 16, 16, 2)
        return (fast_local if fast else general_local)(*args)

    return jax.shard_map(
        local,
        mesh=mesh,
        in_specs=placed,
        out_specs=(
            P(("seq", "tp"), None),
            P(("seq", "tp"), None),
            P(None, None, "tp"),
            P(None, "tp"),
            P("tp", None),
            P(),
            P(None, "tp"),
            P("tp"),
            P("tp", None),
            P(),
            P(),
            P(),
        ),
        check_vma=False,
    )
```

```python
import functools

import jax
import jax.numpy as jnp
from jax import lax
from jax.experimental import pallas as pl
from jax.experimental.pallas import tpu as pltpu
from jax.sharding import PartitionSpec as P

HEAD = 64
BLK = 512
HALF = BLK // 2
QUART = BLK // 4
LONGEST = 4096
STEP_F = 1024
STEP_B = 512
UNROLL = 8
CHUNK_ROWS = 256
FIRST_TICKS = 6
VMEM_LIMIT = 58 << 20
VMEM_MIDDLE = 62 << 20

EPS = 1e-05
F32 = jnp.float32
BF16 = jnp.bfloat16
MESH = pl.DeviceIdType.MESH


def layer_norm(row_block, gain_row, shift_row):
    row_mean = jnp.mean(row_block, axis=-1, keepdims=True)
    centred = row_block - row_mean
    spread = jnp.mean(centred * centred, axis=-1, keepdims=True)
    return centred * lax.rsqrt(spread + EPS) * gain_row + shift_row


def smooth_gate(values):
    return jax.nn.gelu(values, approximate=True)


def running_ends(lengths):
    count = lengths.shape[0]
    index = jnp.arange(count, dtype=jnp.int32)
    return jnp.sum(jnp.where(index[None, :] <= index[:, None], lengths[None, :], 0), axis=1)


def inverse_order(placement):
    index = jnp.arange(placement.shape[0], dtype=jnp.int32)
    return jnp.sum(jnp.where(placement[None, :] == index[:, None], index[None, :], 0), axis=1)


def block_tables(lengths, prefixes, placement, part):
    ends = running_ends(lengths)
    starts = ends - lengths
    limits = starts + prefixes
    offset = part * HALF + jnp.arange(HALF, dtype=jnp.int32)
    pos = placement[:, None] * BLK + offset[None, :]
    inside = (pos[:, :, None] >= starts) & (pos[:, :, None] < ends)

    def pick(values):
        return jnp.sum(jnp.where(inside, values, 0), axis=2)

    low = pick(starts)
    high = jnp.minimum(pick(ends), jnp.maximum(pos + 1, pick(limits)))
    table = jnp.stack(
        [
            jnp.min(low, axis=1) // HALF,
            (jnp.max(high, axis=1) - 1) // HALF + 1,
            jnp.max(low, axis=1),
            jnp.min(high, axis=1),
            placement,
        ]
    )
    return low[:, None, :], high[:, None, :], table


def unpack_t(packed):
    turned = packed.astype(F32).T
    return jnp.concatenate([turned[:HEAD], turned[HEAD:]], axis=1)


def pack_t(turned):
    return jnp.concatenate([turned[:, :QUART], turned[:, QUART:]], axis=0).T


def pieces_two(tab, b, keys, step, start):
    count = keys // HALF
    first, last = tab[0, b], tab[1, b]
    total = last - first
    short = lax.rem(total, count)
    many = total // count + (short > count // 2).astype(jnp.int32)

    def visit(size):
        def at_piece(i, state):
            at = pl.multiple_of((first + i * count) * HALF, HALF)
            whole = (at >= tab[2, b]) & (at + size <= tab[3, b])
            return lax.cond(
                whole, lambda st: step(at, st, False, size), lambda st: step(at, st, True, size), state
            )

        return at_piece

    state = lax.fori_loop(0, many, visit(keys), start)
    half_step = ((short > 0) & (short <= count // 2)).astype(jnp.int32)
    return lax.fori_loop(many, many + half_step, visit(keys // 2), state)


def pieces(tab, b, keys, step, start):
    count = keys // HALF
    first = tab[0, b]

    def visit(i, state):
        at = pl.multiple_of((first + i * count) * HALF, HALF)
        whole = (at >= tab[2, b]) & (at + keys <= tab[3, b])
        return lax.cond(whole, lambda st: step(at, st, False), lambda st: step(at, st, True), state)

    return lax.fori_loop(0, (tab[1, b] - first + count - 1) // count, visit, start)


def attend_kernel(
    part_ref, tab, low_ref, high_ref, q_ref, own_ref, sib_ref,
    out_ref, ot_ref, lse_ref, kv, kvt, rhs_s,
):
    part = part_ref[0]
    scale = HEAD**-0.5
    blocks = q_ref.shape[0]
    rows = blocks * BLK
    depth = lax.broadcasted_iota(jnp.int32, (STEP_F, HALF), 0)

    def prepare(b, carry):
        for ref, which in ((own_ref, part), (sib_ref, 1 - part)):
            at = pl.multiple_of(tab[4, b] * BLK + which * HALF, HALF)
            piece = ref[b]
            kv[pl.ds(at, HALF), :] = piece
            kvt[:, pl.ds(at, HALF)] = piece.T
        qt = unpack_t(q_ref[b]) * scale
        rhs_s[b] = jnp.concatenate([qt, jnp.zeros_like(qt)], axis=0).astype(BF16)
        return carry

    lax.fori_loop(0, blocks, prepare, 0, unroll=UNROLL)
    kv[rows:, :] = jnp.zeros((kv.shape[0] - rows, 2 * HEAD), BF16)
    kvt[:, rows:] = jnp.zeros((2 * HEAD, kv.shape[0] - rows), BF16)

    def one(b, carry):
        low, high = low_ref[b], high_ref[b]

        def step(at, state, masked, size):
            top, total, acc = state
            sc = jnp.dot(kv[pl.ds(at, size), :], rhs_s[b], preferred_element_type=F32)
            if masked:
                rows_of = depth[:size]
                sc = jnp.where((rows_of >= low - at) & (rows_of < high - at), sc, -1e30)
            new = jnp.maximum(top, jnp.max(sc, axis=0, keepdims=True))
            alpha = jnp.exp(top - new)
            pr = jnp.exp(sc - new)
            total = total * alpha + jnp.sum(pr, axis=0, keepdims=True)
            acc = acc * alpha + jnp.dot(
                kvt[HEAD:, pl.ds(at, size)], pr.astype(BF16), preferred_element_type=F32
            )
            return new, total, acc

        start = (
            jnp.full((1, HALF), -1e30, F32),
            jnp.zeros((1, HALF), F32),
            jnp.zeros((HEAD, HALF), F32),
        )
        top, total, acc = pieces_two(tab, b, STEP_F, step, start)
        ot_ref[b] = acc * (1.0 / total)
        lse_ref[b] = top + jnp.log(total)
        return carry

    lax.fori_loop(0, blocks, one, 0)

    def finish(b, carry):
        out_ref[b] = pack_t(ot_ref[b]).astype(BF16)
        return carry

    lax.fori_loop(0, blocks, finish, 0, unroll=UNROLL)


def attend_back_kernel(
    part_ref, tab, low_ref, high_ref, q_ref, da_ref, ot_ref, lse_ref, kv, kvt,
    dq_ref, mine_ref, theirs_ref, dkv, rhs_s, rows_s, total_s, dqt_s,
):
    part = part_ref[0]
    scale = HEAD**-0.5
    blocks = q_ref.shape[0]
    depth = lax.broadcasted_iota(jnp.int32, (STEP_B, HALF), 0)
    lane = lax.broadcasted_iota(jnp.int32, (HALF, 2 * HEAD), 1)

    def prepare(b, carry):
        dkv[pl.ds(pl.multiple_of(b * BLK, BLK), BLK), :] = jnp.zeros((BLK, 2 * HEAD), F32)
        qt = unpack_t(q_ref[b]) * scale
        dat = unpack_t(da_ref[b])
        blank = jnp.zeros_like(qt)
        rhs_s[b, :, :HALF] = jnp.concatenate([qt, blank], axis=0).astype(BF16)
        rhs_s[b, :, HALF:] = jnp.concatenate([blank, dat], axis=0).astype(BF16)
        both = jnp.concatenate([qt, dat], axis=0).T
        rows_s[b, :HALF, :] = jnp.where(lane < HEAD, both, 0.0).astype(BF16)
        rows_s[b, HALF:, :] = jnp.where(lane < HEAD, 0.0, both).astype(BF16)
        total_s[b] = jnp.sum(dat * ot_ref[b], axis=0, keepdims=True)
        return carry

    lax.fori_loop(0, blocks, prepare, 0, unroll=UNROLL)
    dkv[blocks * BLK :, :] = jnp.zeros((dkv.shape[0] - blocks * BLK, 2 * HEAD), F32)

    def one(b, carry):
        total = total_s[b]
        lse = lse_ref[b]
        low, high = low_ref[b], high_ref[b]

        def step(at, acc, masked):
            keys = kv[pl.ds(at, STEP_B), :]
            sc = jnp.dot(keys, rhs_s[b, :, :HALF], preferred_element_type=F32)
            dp = jnp.dot(keys, rhs_s[b, :, HALF:], preferred_element_type=F32)
            if masked:
                sc = jnp.where((depth >= low - at) & (depth < high - at), sc, -1e30)
            pr = jnp.exp(sc - lse)
            ds = (pr * (dp - total)).astype(BF16)
            dkv[pl.ds(at, STEP_B), :] += jnp.dot(
                ds, rows_s[b, :HALF, :], preferred_element_type=F32
            ) + jnp.dot(pr.astype(BF16), rows_s[b, HALF:, :], preferred_element_type=F32)
            return acc + jnp.dot(kvt[:HEAD, pl.ds(at, STEP_B)], ds, preferred_element_type=F32)

        dqt_s[b] = pieces(tab, b, STEP_B, step, jnp.zeros((HEAD, HALF), F32))
        return carry

    lax.fori_loop(0, blocks, one, 0)

    def finish(b, carry):
        dq_ref[b] = pack_t(dqt_s[b] * scale).astype(BF16)
        base = tab[4, b] * BLK
        mine_ref[b] = dkv[pl.ds(pl.multiple_of(base + part * HALF, HALF), HALF), :].astype(BF16)
        theirs_ref[b] = dkv[pl.ds(pl.multiple_of(base + (1 - part) * HALF, HALF), HALF), :].astype(BF16)
        return carry

    lax.fori_loop(0, blocks, finish, 0, unroll=UNROLL)


def vmem(count):
    return [pl.BlockSpec(memory_space=pltpu.VMEM)] * count


def smem(count):
    return [pl.BlockSpec(memory_space=pltpu.SMEM)] * count


def attend(part, tables, q_chunks, kv_own, kv_sib):
    low, high, table = tables
    blocks = q_chunks.shape[0]
    rows = blocks * BLK + STEP_F
    return pl.pallas_call(
        attend_kernel,
        out_shape=(
            jax.ShapeDtypeStruct((blocks, QUART, 2 * HEAD), BF16),
            jax.ShapeDtypeStruct((blocks, HEAD, HALF), F32),
            jax.ShapeDtypeStruct((blocks, 1, HALF), F32),
            jax.ShapeDtypeStruct((rows, 2 * HEAD), BF16),
            jax.ShapeDtypeStruct((2 * HEAD, rows), BF16),
        ),
        in_specs=smem(2) + vmem(5),
        out_specs=tuple(vmem(5)),
        scratch_shapes=[pltpu.VMEM((blocks, 2 * HEAD, HALF), BF16)],
        compiler_params=pltpu.CompilerParams(vmem_limit_bytes=VMEM_LIMIT),
        cost_estimate=pl.CostEstimate(
            flops=40 * 10**9, bytes_accessed=20 << 20, transcendentals=blocks * 4 * BLK * HALF
        ),
        name="attend",
    )(part.reshape(1), table, low, high, q_chunks, kv_own, kv_sib)


def attend_back(part, tables, q_chunks, da_chunks, out_t, mass, kv, kvt):
    low, high, table = tables
    blocks = q_chunks.shape[0]
    return pl.pallas_call(
        attend_back_kernel,
        out_shape=(
            jax.ShapeDtypeStruct((blocks, QUART, 2 * HEAD), BF16),
            jax.ShapeDtypeStruct((blocks, HALF, 2 * HEAD), BF16),
            jax.ShapeDtypeStruct((blocks, HALF, 2 * HEAD), BF16),
        ),
        in_specs=smem(2) + vmem(8),
        out_specs=tuple(vmem(3)),
        scratch_shapes=[
            pltpu.VMEM((blocks * BLK + STEP_F, 2 * HEAD), F32),
            pltpu.VMEM((blocks, 2 * HEAD, BLK), BF16),
            pltpu.VMEM((blocks, BLK, 2 * HEAD), BF16),
            pltpu.VMEM((blocks, 1, HALF), F32),
            pltpu.VMEM((blocks, HEAD, HALF), F32),
        ],
        compiler_params=pltpu.CompilerParams(vmem_limit_bytes=VMEM_LIMIT),
        cost_estimate=pl.CostEstimate(
            flops=60 * 10**9, bytes_accessed=30 << 20, transcendentals=blocks * 4 * BLK * HALF
        ),
        name="attend_back",
    )(part.reshape(1), table, low, high, q_chunks, da_chunks, out_t, mass, kv, kvt)


def chunk_of(who, quarter, index, half):
    absolute = (who[0] * 2 + who[1]) ^ quarter
    tp, sub = absolute // 2, absolute % 2
    return ((sub * 4 + index) * 2 + half) * 2 + tp


def swap_lanes(values):
    return pltpu.roll(values, HEAD, 1)


def low_lanes(rows):
    return lax.broadcasted_iota(jnp.int32, (rows, 2 * HEAD), 1) < HEAD


def store_packed(who, quarter, values, out_ref):
    low = low_lanes(QUART)
    for pair in range(2):
        for half in range(2):
            top = half * HALF
            lanes = slice(pair * 128, pair * 128 + 128)
            first, second = values[top : top + QUART, lanes], values[top + QUART : top + HALF, lanes]
            even = jnp.where(low, first, swap_lanes(second))
            odd = jnp.where(low, swap_lanes(first), second)
            out_ref[chunk_of(who, quarter, 2 * pair, half)] = even.astype(BF16)
            out_ref[chunk_of(who, quarter, 2 * pair + 1, half)] = odd.astype(BF16)


def load_packed(who, quarter, ref, out_ref, base):
    low = low_lanes(QUART)
    for pair in range(2):
        for half in range(2):
            even = ref[chunk_of(who, quarter, 2 * pair, half)].astype(F32)
            odd = ref[chunk_of(who, quarter, 2 * pair + 1, half)].astype(F32)
            top = half * HALF
            lanes = slice(base + pair * 128, base + pair * 128 + 128)
            out_ref[top : top + QUART, lanes] = jnp.where(low, even, swap_lanes(odd)).astype(BF16)
            out_ref[top + QUART : top + HALF, lanes] = jnp.where(low, swap_lanes(even), odd).astype(BF16)


class Place:
    def __init__(self):
        self.seq, self.tp = lax.axis_index("seq"), lax.axis_index("tp")
        self.x = lax.rem(self.seq // 2, 2)
        self.z = self.seq // 4
        self.core_partner = (self.seq ^ 1, self.tp)
        self.x_partner = (self.seq ^ 2, self.tp)
        self.z_partners = [(self.seq ^ (4 * d), self.tp) for d in (1, 2)]
        self.tp_partner = (self.seq, self.tp ^ 1)


def greet_all(count, me, seq, tp):
    barrier = pltpu.get_barrier_semaphore()

    def one(k, carry):
        other = lax.rem(me + k, count)
        pl.semaphore_signal(
            barrier, inc=1, device_id=(other // 2, lax.rem(other, 2)), device_id_type=MESH
        )
        return carry

    lax.fori_loop(1, count, one, 0)
    pl.semaphore_wait(barrier, count - 1)


def greet(partners):
    barrier = pltpu.get_barrier_semaphore()
    for partner in partners:
        pl.semaphore_signal(barrier, inc=1, device_id=partner, device_id_type=MESH)
    pl.semaphore_wait(barrier, len(partners))


def remote(src, dst, send, recv, device):
    return pltpu.make_async_remote_copy(
        src_ref=src, dst_ref=dst, send_sem=send, recv_sem=recv, device_id=device, device_id_type=MESH
    )


def chunk_copy(count, me, k, src, dst, send, recv):
    other = lax.rem(me + k, count)
    return remote(src.at[other], dst.at[me], send.at[k], recv.at[k], (other // 2, lax.rem(other, 2)))


def rows_at(start, size):
    return pl.ds(pl.multiple_of(start, size), size)


def reduce_stages(place, chunks, halved, base, out, both, kept, xbuf, xsum, zbuf, zsum, fbuf, sems, arrived):
    rows = base.shape[0] // chunks
    half, piece = rows // 2, rows // 8
    x, odd, upper = place.x, lax.rem(place.z, 2), place.z // 2
    pair = half // 2

    def x_copy(k):
        seq, tp = place.x_partner
        over_tp = (k >= halved[0]) & (k < halved[1])
        return remote(
            base.at[rows_at(k * rows + (1 - x) * half, half)], xbuf.at[rows_at(k * half, half)],
            sems["xs"].at[k], sems["xr"].at[k],
            (jnp.where(over_tp, place.seq, seq), jnp.where(over_tp, place.tp_partner[1], tp)),
        )

    def z_copy(k):
        return remote(
            xsum.at[rows_at(k * half + (1 - odd) * pair, pair)], zbuf.at[rows_at(k * pair, pair)],
            sems["zs"].at[0, k], sems["zr"].at[0, k], place.z_partners[0],
        )

    def far_z_copy(k):
        return remote(
            zsum.at[rows_at(k * pair + (1 - upper) * piece, piece)], fbuf.at[rows_at(k * piece, piece)],
            sems["zs"].at[1, k], sems["zr"].at[1, k], place.z_partners[1],
        )

    def own_pair(k):
        return rows_at(k * rows + x * half + odd * pair, pair)

    def own_piece(k):
        return rows_at(k * rows + x * half + odd * pair + upper * piece, piece)

    def far_zg_copy(k):
        return remote(
            out.at[own_piece(k)], out.at[own_piece(k)],
            sems["zgs"].at[1, k], sems["zgr"].at[1, k], place.z_partners[1],
        )

    def zg_copy(k):
        return remote(
            out.at[own_pair(k)], out.at[own_pair(k)],
            sems["zgs"].at[0, k], sems["zgr"].at[0, k], place.z_partners[0],
        )

    def xg_copy(k):
        span = rows_at(k * rows + x * half, half)
        return remote(out.at[span], out.at[span], sems["xgs"].at[k], sems["xgr"].at[k], place.x_partner)

    def core_copy(k):
        span = rows_at(k * rows, rows)
        return remote(out.at[span], both.at[1, span], sems["cs"].at[k], sems["cr"].at[k], place.core_partner)

    def stage_x(k):
        arrived(k)
        x_copy(k).start()

    def stage_z(k):
        x_copy(k).wait_recv()
        mine = base[rows_at(k * rows + x * half, half), :].astype(F32)
        xsum[rows_at(k * half, half), :] = (
            mine + xbuf[rows_at(k * half, half), :].astype(F32)
        ).astype(BF16)
        z_copy(k).start()

    def stage_far_z(k):
        z_copy(k).wait_recv()
        span = rows_at(k * pair, pair)
        zsum[span, :] = (
            xsum[rows_at(k * half + odd * pair, pair), :].astype(F32) + zbuf[span, :].astype(F32)
        ).astype(BF16)
        far_z_copy(k).start()

    def stage_far_zg(k):
        far_z_copy(k).wait_recv()
        out[own_piece(k), :] = (
            zsum[rows_at(k * pair + upper * piece, piece), :].astype(F32)
            + fbuf[rows_at(k * piece, piece), :].astype(F32)
        ).astype(BF16)
        far_zg_copy(k).start()

    def stage_zg(k):
        far_zg_copy(k).wait_recv()
        zg_copy(k).start()

    def stage_xg(k):
        zg_copy(k).wait_recv()
        xg_copy(k).start()

    def stage_core(k):
        xg_copy(k).wait_recv()
        core_copy(k).start()

    stages = [stage_x, stage_z, stage_far_z, stage_far_zg, stage_zg, stage_xg, stage_core]

    def tick(t):
        for s, stage in reversed(list(enumerate(stages))):
            @pl.when((t >= s) & (t - s < chunks))
            def _():
                stage(t - s)

    def drain(k, carry):
        for copy in (x_copy, z_copy, far_z_copy, far_zg_copy, zg_copy, xg_copy):
            copy(k).wait_send()
        core_copy(k).wait()
        return carry

    def finale():
        keep = pltpu.make_async_copy(out, both.at[0], kept)
        keep.start()
        lax.fori_loop(0, chunks, drain, 0)
        keep.wait()

    return tick, finale, chunks + len(stages) - 1


SEM_NAMES = ("xs", "xr", "zs", "zr", "zgs", "zgr", "xgs", "xgr", "cs", "cr")
VECTOR_STEPS = 5


def finish_kernel(
    chunks, first_ticks, gain_ref, dq_ref, mine_ref, theirs_ref, near_ref, far_up_ref, far_ref, over_x_ref,
    normed_ref, normed_sib_ref, x_ref, dh_ref, w_ref, w2, w3, vec_ref,
    both, gx_ref, vec_out,
    out, base, far, ybuf, xbuf, xsum, zbuf, zsum, fbuf, dq_in, dkv_in, dkv_st, dkv_sib, mixed, mixed_sib,
    normed, normed_sib, x_s, w_s, slots, *rest,
):
    place = Place()
    count = dq_ref.shape[0]
    me = place.seq * 2 + place.tp
    who = (place.tp, lax.rem(place.seq, 2))
    sems = dict(zip(SEM_NAMES, rest))
    qs, qr, ks, kr, ys, yr, ms, mr, vs, vr, loc = rest[len(SEM_NAMES) :]
    rows = base.shape[0] // chunks
    early = near_ref.shape[0]
    crossed = far_up_ref.shape[0] // rows
    met = crossed + over_x_ref.shape[0] // rows
    strip = rows // 2
    greet_all(count, me, place.seq, place.tp)
    dkv_pair = remote(theirs_ref, dkv_sib, ms.at[2], mr.at[2], place.core_partner)
    dkv_pair.start()
    mine_copy = pltpu.make_async_copy(mine_ref, dkv_st, loc.at[0])
    mine_copy.start()

    def dq_copy(k):
        return chunk_copy(count, me, k, dq_ref, dq_in, qs, qr)

    def dkv_copy(k):
        return chunk_copy(count, me, k, dkv_st, dkv_in, ks, kr)

    def start_q(k, carry):
        dq_copy(k).start()
        return carry

    lax.fori_loop(1, count, start_q, 0)
    near_copy = pltpu.make_async_copy(near_ref, base.at[pl.ds(0, early)], loc.at[1])
    near_copy.start()
    far_copy = pltpu.make_async_copy(far_up_ref, ybuf.at[pl.ds(0, far_up_ref.shape[0])], loc.at[2])
    far_copy.start()
    over_copy = pltpu.make_async_copy(
        over_x_ref, ybuf.at[pl.ds(crossed * rows, over_x_ref.shape[0])], loc.at[13]
    )
    over_copy.start()
    strips = [
        pltpu.make_async_copy(
            far_ref.at[rows_at(j * rows + place.x * strip, strip)],
            base.at[rows_at((crossed + j) * rows + (1 - place.x) * strip, strip)],
            loc.at[14 + j],
        )
        for j in range(met - crossed)
    ]
    locals_ = [(dq_ref.at[me], dq_in.at[me]), (normed_ref, normed), (normed_sib_ref, normed_sib)]
    locals_ += [(x_ref, x_s), (dh_ref, gx_ref)]
    col = w_s.shape[3]
    halves = [w_ref.at[:, :, rows_at(c * col, col)] for c in (who[1], 1 - who[1])]
    locals_ += [(w, w_s.at[r]) for r, w in enumerate(halves + [w2, w3])]
    locals_ = [pltpu.make_async_copy(src, dst, loc.at[3 + i]) for i, (src, dst) in enumerate(locals_)]

    def tp_copy(k, src, first):
        return remote(
            src.at[rows_at((k - first) * rows, rows)], ybuf.at[rows_at(k * rows, rows)],
            ys.at[k], yr.at[k], place.tp_partner,
        )

    def cross(k, carry):
        tp_copy(k, far_ref, crossed).start()
        return carry

    settled = early // rows
    lax.fori_loop(met, settled, cross, 0)
    mine_copy.wait()
    dkv_pair.wait()

    def add(b, carry):
        dkv_st[b] = (dkv_st[b].astype(F32) + dkv_sib[b].astype(F32)).astype(BF16)
        return carry

    lax.fori_loop(0, count, add, 0)

    def start_kv(k, carry):
        dkv_copy(k).start()
        return carry

    lax.fori_loop(1, count, start_kv, 0)
    dkv_in[me] = dkv_st[me]
    near_copy.wait()
    for copy in strips + locals_:
        copy.start()
    for copy in [far_copy, over_copy] + strips:
        copy.wait()

    def add_in(into, other):
        base[into, :] = (base[into, :].astype(F32) + ybuf[other, :].astype(F32)).astype(BF16)

    def arrived(k):
        x_met = (k >= crossed) & (k < met)

        @pl.when(k >= met)
        def _():
            tp_copy(k, base, 0).wait_recv()

        @pl.when(jnp.logical_not(x_met))
        def _():
            span = rows_at(k * rows, rows)
            add_in(span, span)

        @pl.when(x_met)
        def _():
            add_in(rows_at(k * rows + place.x * strip, strip), rows_at(k * rows, strip))
            add_in(
                rows_at(k * rows + (1 - place.x) * strip, strip), rows_at(k * rows + strip, strip)
            )

    tick, drain, ticks = reduce_stages(
        place, chunks, (crossed, met), base, out, both, loc.at[12], xbuf, xsum, zbuf, zsum, fbuf, sems, arrived
    )

    def plain(t, carry):
        tick(t)
        return carry

    lax.fori_loop(0, first_ticks, plain, 0)

    def wait(k, carry):
        dq_copy(k).wait()
        dkv_copy(k).wait()
        return carry

    lax.fori_loop(1, count, wait, 0)
    for copy in locals_:
        copy.wait()
    vec_out[...] = vec_ref[...]
    low = low_lanes(HALF)
    for quarter in range(4):
        load_packed(who, quarter, dq_in, mixed.at[quarter], 0)
        for pair in range(2):
            for half in range(2):
                span = slice(half * HALF, half * HALF + HALF)
                even = dkv_in[chunk_of(who, quarter, 2 * pair, half)].astype(F32)
                odd = dkv_in[chunk_of(who, quarter, 2 * pair + 1, half)].astype(F32)
                k_at = 256 + pair * 128
                mixed[quarter, span, k_at : k_at + 128] = jnp.where(low, even, swap_lanes(odd)).astype(BF16)
                mixed[quarter, span, k_at + 256 : k_at + 384] = jnp.where(low, swap_lanes(even), odd).astype(BF16)
    mixed_copies = [
        remote(mixed.at[2 * i + 1], mixed_sib.at[i], ms.at[i], mr.at[i], place.core_partner)
        for i in range(2)
    ]
    for copy in mixed_copies:
        copy.start()
    tick(first_ticks)

    for quarter in range(4):
        absolute = (who[0] * 2 + who[1]) ^ quarter
        lanes = pl.ds(pl.multiple_of(absolute * 256, 256), 256)
        for row, left in ((10, 0), (11, 512)):
            vec_out[row : row + 1, lanes] = jnp.sum(
                mixed[quarter, :, left : left + 256].astype(F32), axis=0, keepdims=True
            )
    gains = jnp.zeros((1, base.shape[1]), F32)
    shifts = jnp.zeros((1, base.shape[1]), F32)
    for part in range(2):
        span = slice(part * HALF, part * HALF + HALF)
        d_normed = jnp.zeros((HALF, base.shape[1]), F32)
        for quarter in range(4):
            for which in range(3):
                lanes = slice(which * col, which * col + col)
                d_normed += dot_nt(mixed[quarter, span, lanes], w_s[quarter, which])
        xhat, rstd = norm_parts(x_s[span, :].astype(F32))
        e = d_normed * gain_ref[0:1, :]
        grad = rstd * (
            e
            - jnp.mean(e, axis=-1, keepdims=True)
            - xhat * jnp.mean(e * xhat, axis=-1, keepdims=True)
        )
        gx_ref[span, :] += grad
        gains += jnp.sum(d_normed * xhat, axis=0, keepdims=True)
        shifts += jnp.sum(d_normed, axis=0, keepdims=True)
        tick(first_ticks + 1 + part)
    vec_out[0:1, :] = gains
    vec_out[4:5, :] = shifts

    for copy in mixed_copies:
        copy.wait()
    late = pl.ds(early, base.shape[0] - early)
    for i, target in ((1, far), (0, base.at[late])):
        for row in range(0, target.shape[0], 256):
            span = slice(row, row + 256)
            target[span, :] = (
                lax.dot_general(
                    mixed[2 * i, :, span], normed[...], (((0,), (0,)), ((), ())), preferred_element_type=F32
                )
                + lax.dot_general(
                    mixed_sib[i, :, span], normed_sib[...], (((0,), (0,)), ((), ())),
                    preferred_element_type=F32,
                )
            ).astype(BF16)
            if i == 1:
                for k in range(settled + row // rows, settled + (row + 256) // rows):
                    tp_copy(k, far, settled).start()

    partners = [place.core_partner, place.tp_partner, place.x_partner] + [
        (place.seq ^ bit, place.tp) for bit in (4, 8)
    ]

    def vector_copy(step):
        return remote(
            slots.at[step], slots.at[VECTOR_STEPS + step], vs.at[step], vr.at[step], partners[step]
        )

    def vector_tick(step):
        if step > 0:
            vector_copy(step - 1).wait()
            vec_out[...] += slots[VECTOR_STEPS + step - 1]
        if step < VECTOR_STEPS:
            slots[step] = vec_out[...]
            vector_copy(step).start()

    def last(t, carry):
        tick(t)
        for step in range(VECTOR_STEPS + 1):
            @pl.when(t == first_ticks + 3 + step)
            def _():
                vector_tick(step)
        return carry

    lax.fori_loop(first_ticks + 3, ticks, last, 0)

    def sent(k, carry):
        tp_copy(k, base, 0).wait_send()
        return carry

    lax.fori_loop(met, chunks, sent, 0)
    drain()


def finish(gain, dq_chunks, mine, theirs, near, far_up, far, over_x, normed, normed_sib, x, d_hidden, weights, vectors):
    early, cols = near.shape
    late = 3 * weights[1].shape[2]
    total = early + late
    chunks = total // CHUNK_ROWS
    count = dq_chunks.shape[0]
    rows = x.shape[0]
    dma = pltpu.SemaphoreType.DMA
    anywhere = pl.BlockSpec(memory_space=pl.ANY)
    scratch = [
        pltpu.VMEM((total, cols), BF16),
        pltpu.VMEM((total, cols), BF16),
        pltpu.VMEM((late, cols), BF16),
        pltpu.VMEM((total, cols), BF16),
        pltpu.VMEM((total // 2, cols), BF16),
        pltpu.VMEM((total // 2, cols), BF16),
        pltpu.VMEM((total // 4, cols), BF16),
        pltpu.VMEM((total // 4, cols), BF16),
        pltpu.VMEM((total // 8, cols), BF16),
        pltpu.VMEM(dq_chunks.shape, BF16),
        pltpu.VMEM(mine.shape, BF16),
        pltpu.VMEM(mine.shape, BF16),
        pltpu.VMEM(mine.shape, BF16),
        pltpu.VMEM((4, rows, late), BF16),
        pltpu.VMEM((2, rows, late), BF16),
        pltpu.VMEM((rows, cols), BF16),
        pltpu.VMEM((rows, cols), BF16),
        pltpu.VMEM((rows, cols), BF16),
        pltpu.VMEM((4,) + weights[1].shape, BF16),
        pltpu.VMEM((2 * VECTOR_STEPS,) + vectors.shape, F32),
    ]
    scratch += [dma((2, chunks) if name[0] == "z" else (chunks,)) for name in SEM_NAMES]
    scratch += [dma((count,))] * 4 + [dma((chunks,))] * 2 + [dma((3,))] * 2
    scratch += [dma((VECTOR_STEPS,))] * 2 + [dma((14 + over_x.shape[0] // CHUNK_ROWS,))]
    return pl.pallas_call(
        functools.partial(finish_kernel, chunks, FIRST_TICKS),
        out_shape=(
            jax.ShapeDtypeStruct((2, total, cols), BF16),
            jax.ShapeDtypeStruct((rows, cols), F32),
            jax.ShapeDtypeStruct(vectors.shape, F32),
        ),
        in_specs=vmem(1) + [anywhere] * 14 + vmem(1),
        out_specs=(anywhere, vmem(1)[0], vmem(1)[0]),
        scratch_shapes=scratch,
        compiler_params=pltpu.CompilerParams(
            collective_id=1, has_side_effects=True, vmem_limit_bytes=VMEM_MIDDLE
        ),
        name="finish",
    )(
        gain, dq_chunks, mine, theirs, near, far_up, far, over_x, normed, normed_sib, x, d_hidden, *weights,
        vectors,
    )


def join_kernel(core_ref, in_ref, out_ref):
    out_ref[...] = in_ref[0].astype(F32)


def join_turned_kernel(core_ref, in_ref, out_ref):
    out_ref[0] = in_ref[0].astype(F32).T


def join(core, both, size, first, count, shape, place, turned=False):
    cols = both.shape[2]
    block = (1, cols, size) if turned else (size, cols)
    return pl.pallas_call(
        join_turned_kernel if turned else join_kernel,
        grid_spec=pltpu.PrefetchScalarGridSpec(
            num_scalar_prefetch=1,
            grid=(2, count),
            in_specs=[pl.BlockSpec((1, size, cols), lambda p, i, c: ((p + c[0]) % 2, first + i, 0))],
            out_specs=pl.BlockSpec(block, lambda p, i, c: place(p, i)),
        ),
        out_shape=jax.ShapeDtypeStruct(shape, F32),
        compiler_params=pltpu.CompilerParams(vmem_limit_bytes=VMEM_LIMIT),
        name="join",
    )(core.reshape(1).astype(jnp.int32), both)


def begin_kernel(
    x_ref, gain_ref, shift_ref, bias_ref, w_ref, wo_ref, wu_ref,
    normed_ref, normed_sib, q_in, kv_own, kv_sib, bias_far, w2, w3, wo2, wo3, wu0,
    w0, w1, q_st, kv_st, *sems,
):
    place = Place()
    count = q_in.shape[0]
    width = x_ref.shape[1]
    me = place.seq * 2 + place.tp
    who = (place.tp, lax.rem(place.seq, 2))
    ks, kr, qs, qr, fs, fr, ws, wr, ls = sems
    greet_all(count, me, place.seq, place.tp)
    core = who[1]
    col, wo_rows = w0.shape[2], wo2.shape[0]
    w_own = w_ref.at[:, :, rows_at(core * col, col)]
    w_far = remote(w_own, w2, ws.at[0], wr.at[0], place.tp_partner)
    w_far.start()
    bias_pair = remote(bias_ref, bias_far, ws.at[5], wr.at[5], place.tp_partner)
    bias_pair.start()
    w_loads = [
        pltpu.make_async_copy(w_own, w0, ls.at[0]),
        pltpu.make_async_copy(w_ref.at[:, :, rows_at((1 - core) * col, col)], w1, ls.at[1]),
    ]
    wu_copy = pltpu.make_async_copy(wu_ref.at[:, rows_at(core * wu0.shape[1], wu0.shape[1])], wu0, ls.at[2])
    wu_copy.start()
    for copy in w_loads:
        copy.start()
    wo_far = remote(wo_ref.at[rows_at(core * wo_rows, wo_rows)], wo2, ws.at[1], wr.at[1], place.tp_partner)
    wo_far.start()
    w_last = remote(w2, w3, ws.at[2], wr.at[2], place.core_partner)
    wo_last = remote(wo2, wo3, ws.at[3], wr.at[3], place.core_partner)

    def norm(part, carry):
        span = rows_at(part * 64, 64)
        normed_ref[span, :] = layer_norm(
            x_ref[span, :].astype(F32), gain_ref[0:1, :], shift_ref[0:1, :]
        ).astype(BF16)
        return carry

    lax.fori_loop(0, x_ref.shape[0] // 64, norm, 0, unroll=2)

    normed_pair = remote(normed_ref, normed_sib, ws.at[4], wr.at[4], place.core_partner)
    normed_pair.start()

    def kv_copy(other):
        return remote(kv_st.at[other], kv_own.at[me], ks.at[other], kr.at[me], (other // 2, lax.rem(other, 2)))

    def q_copy(other):
        return remote(q_st.at[other], q_in.at[me], qs.at[other], qr.at[me], (other // 2, lax.rem(other, 2)))

    def kv_came(other):
        return remote(kv_st.at[other], kv_own.at[other], ks.at[other], kr.at[other], (other // 2, lax.rem(other, 2)))

    def q_came(other):
        return remote(q_st.at[other], q_in.at[other], qs.at[other], qr.at[other], (other // 2, lax.rem(other, 2)))

    def forward(other):
        return remote(kv_own.at[other], kv_sib.at[other], fs.at[other], fr.at[other], place.core_partner)

    low = low_lanes(HALF)

    def project(quarter, w):
        bias = bias_ref if quarter < 2 else bias_far
        side = core if quarter % 2 == 0 else 1 - core

        def bias_at(which):
            return bias[2:3, rows_at(which * 2 * col + side * col, col)]

        def dot(which):
            return dot_nn(normed_ref[...], w[which])

        keys, values = dot(1), dot(2) + bias_at(1)
        for pair in range(2):
            lanes = slice(pair * 128, pair * 128 + 128)
            for half in range(2):
                rows = slice(half * HALF, half * HALF + HALF)
                k, v = keys[rows, lanes], values[rows, lanes]
                kv_st[chunk_of(who, quarter, 2 * pair, half)] = jnp.where(low, k, swap_lanes(v)).astype(BF16)
                kv_st[chunk_of(who, quarter, 2 * pair + 1, half)] = jnp.where(low, swap_lanes(k), v).astype(BF16)
        store_packed(who, quarter, dot(0) + bias_at(0), q_st)

        def send(i, carry):
            turned = lax.rem(i + 2 * (place.seq // 2) + 2, 8)
            other = chunk_of(who, quarter, turned // 2, lax.rem(turned, 2))

            @pl.when(other != me)
            def _():
                kv_copy(other).start()
                q_copy(other).start()

            @pl.when(other == me)
            def _():
                kv_own[me] = kv_st[me]
                q_in[me] = q_st[me]

            return carry

        lax.fori_loop(0, 8, send, 0)

    for copy in w_loads:
        copy.wait()
    project(0, w0)
    project(1, w1)
    w_far.wait()
    bias_pair.wait()
    w_last.start()
    project(2, w2)
    w_last.wait()
    project(3, w3)
    wo_far.wait()
    wo_last.start()
    forward(me).start()

    def receive(i, carry):
        other = lax.rem(place.seq + lax.rem(i, count // 2), count // 2) * 2 + lax.rem(
            place.tp + i // (count // 2), 2
        )
        kv_came(other).wait_recv()
        forward(other).start()
        return carry

    lax.fori_loop(1, count, receive, 0)

    def rest(k, carry):
        other = lax.rem(me + k, count)
        q_came(other).wait_recv()
        kv_copy(other).wait_send()
        q_copy(other).wait_send()
        return carry

    lax.fori_loop(1, count, rest, 0)

    def forwarded(k, carry):
        forward(k).wait()
        return carry

    lax.fori_loop(0, count, forwarded, 0)
    wo_last.wait()
    normed_pair.wait()
    wu_copy.wait()


def begin(x, gains, shifts, bias, w, wo, wu):
    rows, width = x.shape
    count = 32
    dma = pltpu.SemaphoreType.DMA
    anywhere = pl.BlockSpec(memory_space=pl.ANY)
    q_shape, kv_shape = (count, QUART, 2 * HEAD), (count, HALF, 2 * HEAD)
    w_quarter = (3, width, w.shape[2] // 2)
    wo_quarter = (wo.shape[0] // 2, wo.shape[1])
    return pl.pallas_call(
        begin_kernel,
        out_shape=(
            jax.ShapeDtypeStruct((rows, width), BF16),
            jax.ShapeDtypeStruct((rows, width), BF16),
            jax.ShapeDtypeStruct(q_shape, BF16),
            jax.ShapeDtypeStruct(kv_shape, BF16),
            jax.ShapeDtypeStruct(kv_shape, BF16),
            jax.ShapeDtypeStruct(bias.shape, F32),
            jax.ShapeDtypeStruct(w_quarter, BF16),
            jax.ShapeDtypeStruct(w_quarter, BF16),
            jax.ShapeDtypeStruct(wo_quarter, BF16),
            jax.ShapeDtypeStruct(wo_quarter, BF16),
            jax.ShapeDtypeStruct((wu.shape[0], wu.shape[1] // 2), BF16),
        ),
        in_specs=vmem(4) + [anywhere] * 3,
        out_specs=tuple(vmem(1) + [anywhere] + vmem(6) + [anywhere] * 3),
        scratch_shapes=[pltpu.VMEM(w_quarter, BF16)] * 2
        + [pltpu.VMEM(q_shape, BF16), pltpu.VMEM(kv_shape, BF16)]
        + [dma((count,))] * 6
        + [dma((6,))] * 2
        + [dma((3,))],
        compiler_params=pltpu.CompilerParams(
            collective_id=3, has_side_effects=True, vmem_limit_bytes=VMEM_LIMIT
        ),
        name="begin",
    )(x, gains, shifts, bias, w, wo, wu)


def norm_parts(values):
    mean = jnp.mean(values, axis=-1, keepdims=True)
    centred = values - mean
    rstd = lax.rsqrt(jnp.mean(centred * centred, axis=-1, keepdims=True) + EPS)
    return centred * rstd, rstd


GELU_A = 0.7978845608028654
GELU_B = 0.044715


def gelu_parts(u):
    square = u * u
    t = jnp.tanh(GELU_A * u * (1.0 + GELU_B * square))
    rise = 0.5 * (1.0 + t)
    return u * rise, rise + 0.5 * u * (1.0 - t * t) * (GELU_A * (1.0 + 3.0 * GELU_B * square))


def col_sum(values):
    return jnp.sum(values, axis=0, keepdims=True)


def back_rows(xhat, rstd, gain, upstream):
    e = upstream * gain
    return rstd * (
        e - jnp.mean(e, axis=-1, keepdims=True) - xhat * jnp.mean(e * xhat, axis=-1, keepdims=True)
    )


def dot_nn(a, b):
    return jnp.dot(a, b, preferred_element_type=F32)


def dot_nt(a, b):
    return lax.dot_general(a, b, (((1,), (1,)), ((), ())), preferred_element_type=F32)


def dot_tn(a, b):
    return lax.dot_general(a, b, (((0,), (0,)), ((), ())), preferred_element_type=F32)


def middle_kernel(
    gains, shifts, bias_out, bias_down, bias_own, bias_far, att_ref, x_ref, og_ref,
    wo_ref, wo2, wo3, wu_ref, wu2, wd_ref,
    result, da_in, dh, vec, near_ref, far_up_ref, far_ref, over_x_ref,
    att_in, att_s, att_sib, wo_s, wu_s, wd_s, x_s, branch_s, hidden_s, inner_s, inner_sib, act_s, act_sib,
    dg_s, dup_sib, down_s, dd_s, dd_sib, db_s, db_sib, da_st,
    ats, atr, das, dar, ws, wr, cs, cr, loc,
):
    place = Place()
    count = att_in.shape[0]
    me = place.seq * 2 + place.tp
    who = (place.tp, lax.rem(place.seq, 2))
    rows, width = x_s.shape
    hid = wd_s.shape[1]
    wu0, wu1 = (wu_ref.at[:, rows_at(c * hid, hid)] for c in (who[1], 1 - who[1]))
    wo0, wo1 = (wo_ref.at[rows_at(c * wo2.shape[0], wo2.shape[0])] for c in (who[1], 1 - who[1]))
    wd0, wd1 = (wd_ref.at[rows_at(c * hid, hid)] for c in (who[1], 1 - who[1]))
    greet_all(count, me, place.seq, place.tp)

    def start(k, carry):
        chunk_copy(count, me, k, att_ref, att_in, ats, atr).start()
        return carry

    lax.fori_loop(1, count, start, 0)
    wd_far = remote(wd0, wd_s.at[2], ws.at[0], wr.at[0], place.tp_partner)
    wd_far.start()
    wu_last = remote(wu2, wu_s.at[3], ws.at[1], wr.at[1], place.core_partner)
    wu_last.start()
    wd_last = remote(wd_s.at[2], wd_s.at[3], ws.at[2], wr.at[2], place.core_partner)
    loads = [(att_ref.at[me], att_in.at[me]), (x_ref, x_s), (og_ref, dh)]
    loads += [(w, wo_s.at[r]) for r, w in enumerate((wo0, wo1, wo2, wo3))]
    loads += [(w, wu_s.at[r]) for r, w in enumerate((wu0, wu1, wu2))]
    loads += [(w, wd_s.at[r]) for r, w in enumerate((wd0, wd1))]
    loads = [pltpu.make_async_copy(src, dst, loc.at[i]) for i, (src, dst) in enumerate(loads)]
    for copy in loads:
        copy.start()

    def to_core(i, src, dst):
        return remote(src, dst, cs.at[i], cr.at[i], place.core_partner)

    att_pair = [to_core(i, att_s.at[2 * i + 1], att_sib.at[i]) for i in range(2)]
    act_pair = [to_core(2 + i, act_s.at[2 * i + 1], act_sib.at[i]) for i in range(2)]
    dup_pair = [to_core(4 + i, dg_s.at[2 * i + 1], dup_sib.at[i]) for i in range(2)]
    inner_pair = to_core(6, inner_s, inner_sib)
    dd_pair = to_core(7, dd_s, dd_sib)
    db_pair = to_core(8, db_s, db_sib)

    def came(k, carry):
        chunk_copy(count, me, k, att_ref, att_in, ats, atr).wait()
        return carry

    lax.fori_loop(1, count, came, 0)
    for copy in loads:
        copy.wait()
    for quarter in range(4):
        load_packed(who, quarter, att_in, att_s.at[quarter], 0)
    for copy in att_pair:
        copy.start()

    def cols(i):
        return rows_at(i * 256, 256)

    def project(i, carry):
        span = cols(i)
        branch_s[:, span] = (
            dot_nn(att_s[0], wo_s[0, :, span])
            + dot_nn(att_s[1], wo_s[1, :, span])
            + dot_nn(att_s[2], wo_s[2, :, span])
            + dot_nn(att_s[3], wo_s[3, :, span])
            + bias_out[:, span]
        )
        return carry

    lax.fori_loop(0, width // 256, project, 0)

    def into(i, carry):
        span = rows_at(i * 64, 64)
        hidden = x_s[span, :].astype(F32) + layer_norm(branch_s[span, :], gains[1:2, :], shifts[1:2, :])
        hidden_s[span, :] = hidden
        inner_s[span, :] = layer_norm(hidden, gains[2:3, :], shifts[2:3, :]).astype(BF16)
        return carry

    lax.fori_loop(0, rows // 64, into, 0, unroll=2)
    inner_pair.start()
    for quarter in range(4):
        if quarter == 3:
            wu_last.wait()

        bias = bias_own if quarter < 2 else bias_far
        side = who[1] if quarter % 2 == 0 else 1 - who[1]

        def up(i, carry, quarter=quarter, bias=bias, side=side):
            span = cols(i)
            act, slope = gelu_parts(
                dot_nn(inner_s[...], wu_s[quarter, :, span]) + bias[pl.ds(side, 1), span]
            )
            act_s[quarter, :, span] = act.astype(BF16)
            dg_s[quarter, :, span] = slope.astype(BF16)
            return carry

        lax.fori_loop(0, hid // 256, up, 0)
        if quarter % 2 == 1:
            act_pair[quarter // 2].start()

    def down_own(i, carry):
        span = cols(i)
        down_s[:, span] = (
            dot_nn(act_s[0], wd_s[0, :, span]) + dot_nn(act_s[1], wd_s[1, :, span]) + bias_down[:, span]
        )
        return carry

    lax.fori_loop(0, width // 256, down_own, 0)
    wd_far.wait()
    wd_last.start()
    for quarter in (2, 3):
        if quarter == 3:
            wd_last.wait()

        def down_far(i, carry, quarter=quarter):
            span = cols(i)
            down_s[:, span] += dot_nn(act_s[quarter], wd_s[quarter, :, span])
            return carry

        lax.fori_loop(0, width // 256, down_far, 0)

    none = jnp.zeros((1, width), F32)

    def turn(i, carry):
        gain, shift, bias = carry
        span = rows_at(i * 64, 64)
        xhat, rstd = norm_parts(down_s[span, :])
        result[span, :] = (hidden_s[span, :] + xhat * gains[3:4, :] + shifts[3:4, :]).astype(BF16)
        upstream = dh[span, :]
        d_down = back_rows(xhat, rstd, gains[3:4, :], upstream)
        dd_s[span, :] = d_down.astype(BF16)
        return gain + col_sum(upstream * xhat), shift + col_sum(upstream), bias + col_sum(d_down)

    gain, shift, bias = lax.fori_loop(0, rows // 64, turn, (none,) * 3, unroll=2)
    vec[...] = jnp.zeros_like(vec)
    vec[3:4, :] = gain
    vec[7:8, :] = shift
    vec[9:10, :] = bias
    dd_pair.start()
    for quarter in range(4):
        absolute = (who[0] * 2 + who[1]) ^ quarter

        def back_up(i, carry, quarter=quarter, absolute=absolute):
            span = cols(i)
            d_up = dot_nt(dd_s[...], wd_s[quarter, span, :]) * dg_s[quarter, :, span].astype(F32)
            d_up = d_up.astype(BF16)
            dg_s[quarter, :, span] = d_up
            vec[pl.ds(12 + absolute, 1), span] = col_sum(d_up.astype(F32))
            return carry

        lax.fori_loop(0, hid // 256, back_up, 0)
        if quarter % 2 == 1:
            dup_pair[quarter // 2].start()

    def back_inner(i, carry):
        span = cols(i)
        down_s[:, span] = (
            dot_nt(dg_s[0], wu_s[0, span, :])
            + dot_nt(dg_s[1], wu_s[1, span, :])
            + dot_nt(dg_s[2], wu_s[2, span, :])
            + dot_nt(dg_s[3], wu_s[3, span, :])
        )
        return carry

    lax.fori_loop(0, width // 256, back_inner, 0)

    def out_of(i, carry):
        gain3, shift3, gain2, shift2, bias = carry
        span = rows_at(i * 64, 64)
        d_inner = down_s[span, :]
        xhat, rstd = norm_parts(hidden_s[span, :])
        gain3 = gain3 + col_sum(d_inner * xhat)
        shift3 = shift3 + col_sum(d_inner)
        d_hidden = dh[span, :] + back_rows(xhat, rstd, gains[2:3, :], d_inner)
        dh[span, :] = d_hidden
        xhat, rstd = norm_parts(branch_s[span, :])
        d_branch = back_rows(xhat, rstd, gains[1:2, :], d_hidden)
        db_s[span, :] = d_branch.astype(BF16)
        return (
            gain3, shift3, gain2 + col_sum(d_hidden * xhat), shift2 + col_sum(d_hidden),
            bias + col_sum(d_branch),
        )

    sums = lax.fori_loop(0, rows // 64, out_of, (none,) * 5, unroll=2)
    for row, value in zip((2, 6, 1, 5, 8), sums):
        vec[row : row + 1, :] = value
    db_pair.start()

    def da_copy(other):
        return remote(
            da_st.at[other], da_in.at[me], das.at[other], dar.at[me], (other // 2, lax.rem(other, 2))
        )

    def da_came(other):
        return remote(
            da_st.at[other], da_in.at[other], das.at[other], dar.at[other], (other // 2, lax.rem(other, 2))
        )

    for quarter in range(4):
        store_packed(who, quarter, dot_nt(db_s[...], wo_s[quarter]), da_st)

        def send(i, carry, quarter=quarter):
            turned = lax.rem(i + 2 * (place.seq // 2) + 2, 8)
            other = chunk_of(who, quarter, turned // 2, lax.rem(turned, 2))

            @pl.when(other != me)
            def _():
                da_copy(other).start()

            @pl.when(other == me)
            def _():
                da_in[me] = da_st[me]

            return carry

        lax.fori_loop(0, 8, send, 0)

    for copy in dup_pair + [inner_pair]:
        copy.wait()

    def grad_up(i, carry):
        span = cols(i)
        for near, slot in ((0, 0), (2, 1)):
            wu_s[near, :, span] = (
                dot_tn(inner_s[...], dg_s[near, :, span]) + dot_tn(inner_sib[...], dup_sib[slot, :, span])
            ).astype(BF16)
        return carry

    lax.fori_loop(0, hid // 256, grad_up, 0)
    for copy in att_pair + [db_pair]:
        copy.wait()
    for near, slot in ((0, 0), (2, 1)):
        wo_s[near] = (dot_tn(att_s[near], db_s[...]) + dot_tn(att_sib[slot], db_sib[...])).astype(BF16)
    up_rows, out_rows = wu_s.shape[1], wo_s.shape[1]
    stores = [
        (wu_s.at[0], near_ref.at[pl.ds(0, up_rows)]),
        (wo_s.at[0], near_ref.at[pl.ds(up_rows + hid, out_rows)]),
        (wu_s.at[2], far_up_ref),
        (wo_s.at[2], far_ref.at[pl.ds(hid, out_rows)]),
        (wd_s.at[0], near_ref.at[pl.ds(up_rows, hid)]),
        (wd_s.at[2], far_ref.at[pl.ds(0, hid)]),
    ]
    strip = CHUNK_ROWS // 2
    for j in range(hid // CHUNK_ROWS):
        span = rows_at(j * CHUNK_ROWS + (1 - place.x) * strip, strip)
        for i, slot in enumerate((0, 2)):
            stores.append((wd_s.at[slot, span], over_x_ref.at[pl.ds(j * CHUNK_ROWS + i * strip, strip)]))
    stores = [pltpu.make_async_copy(src, dst, loc.at[i]) for i, (src, dst) in enumerate(stores)]
    for copy in stores[:4]:
        copy.start()
    for copy in act_pair + [dd_pair]:
        copy.wait()

    def grad_down(i, carry):
        span = cols(i)
        for near, slot in ((0, 0), (2, 1)):
            wd_s[near, span, :] = (
                dot_tn(act_s[near, :, span], dd_s[...]) + dot_tn(act_sib[slot, :, span], dd_sib[...])
            ).astype(BF16)
        return carry

    lax.fori_loop(0, hid // 256, grad_down, 0)
    for copy in stores[4:]:
        copy.start()

    def da_wait(k, carry):
        other = lax.rem(me + k, count)
        da_came(other).wait_recv()
        da_copy(other).wait_send()
        return carry

    lax.fori_loop(1, count, da_wait, 0)
    for copy in stores:
        copy.wait()


def middle(gains, shifts, bias_out, bias_down, bias, bias_far, att, x, out_grad, wo3, w_up, wu2, w_down):
    rows, width = x.shape
    count = att.shape[0]
    hid = wu2.shape[1]
    out_rows = wo3[1].shape[0]
    dma = pltpu.SemaphoreType.DMA
    anywhere = pl.BlockSpec(memory_space=pl.ANY)

    def held(*shape, dtype=BF16):
        return pltpu.VMEM(shape, dtype)

    scratch = [
        held(*att.shape),
        held(4, rows, out_rows),
        held(2, rows, out_rows),
        held(4, out_rows, width),
        held(4, width, hid),
        held(4, hid, width),
        held(rows, width),
        held(rows, width, dtype=F32),
        held(rows, width, dtype=F32),
        held(rows, width),
        held(rows, width),
        held(4, rows, hid),
        held(2, rows, hid),
        held(4, rows, hid),
        held(2, rows, hid),
        held(rows, width, dtype=F32),
        held(rows, width),
        held(rows, width),
        held(rows, width),
        held(rows, width),
        held(*att.shape),
    ]
    scratch += [dma((count,))] * 4 + [dma((3,))] * 2 + [dma((9,))] * 2 + [dma((6 + 2 * hid // CHUNK_ROWS,))]
    return pl.pallas_call(
        middle_kernel,
        out_shape=(
            jax.ShapeDtypeStruct((rows, width), BF16),
            jax.ShapeDtypeStruct(att.shape, BF16),
            jax.ShapeDtypeStruct((rows, width), F32),
            jax.ShapeDtypeStruct((16, width), F32),
            jax.ShapeDtypeStruct((hid + width + out_rows, width), BF16),
            jax.ShapeDtypeStruct((width, hid), BF16),
            jax.ShapeDtypeStruct((hid + out_rows, width), BF16),
            jax.ShapeDtypeStruct((hid, width), BF16),
        ),
        in_specs=vmem(6) + [anywhere] * 9,
        out_specs=tuple(vmem(4) + [anywhere] * 4),
        scratch_shapes=scratch,
        compiler_params=pltpu.CompilerParams(
            collective_id=4, has_side_effects=True, vmem_limit_bytes=VMEM_MIDDLE
        ),
        name="middle",
    )(
        gains, shifts, bias_out, bias_down, bias, bias_far, att, x, out_grad, *wo3, w_up, wu2, w_down
    )


def fast_local(
    tokens_in, w_qkv, bias_qv, w_out, bias_out, w_up, bias_up, w_down, bias_down,
    norm_gains, norm_shifts, out_grad, lengths, prefixes, placement,
):
    seq_count = lax.axis_size("seq")
    seq, tp = lax.axis_index("seq"), lax.axis_index("tp")
    core = seq % 2
    over_tp = [(0, 1), (1, 0)]

    def to_tp(values):
        return lax.ppermute(values, "tp", over_tp)

    width = w_qkv.shape[0]
    w3 = jnp.transpose(w_qkv, (1, 0, 2))
    bias = jnp.concatenate([bias_up.reshape(2, width), bias_qv.reshape(1, width)]).astype(F32)
    bias = jnp.pad(bias, ((0, 5), (0, 0)))
    tables = block_tables(lengths, prefixes, placement, core)
    normed, normed_sib, q_own, kv_own, kv_sib, bias_far, wq2, wq3, wo2, wo3, wu0 = begin(
        tokens_in, norm_gains, norm_shifts, bias, w3, w_out, w_up
    )
    wu2 = to_tp(wu0)
    att_chunks, out_t, mass, kv_pack, kv_turned = attend(core, tables, q_own, kv_own, kv_sib)
    result, da_own, d_hidden, vectors, near, far_up, far, over_x = middle(
        norm_gains, norm_shifts, bias_out.astype(F32)[None], bias_down.astype(F32)[None], bias, bias_far,
        att_chunks, tokens_in, out_grad, [w_out, wo2, wo3], w_up, wu2, w_down,
    )
    far_up = to_tp(far_up)
    over_x = lax.ppermute(over_x, "seq", [(i, i ^ 2) for i in range(lax.axis_size("seq"))])
    dq_chunks, mine, theirs = attend_back(core, tables, q_own, da_own, out_t, mass, kv_pack, kv_turned)
    both, grad_x, vectors = finish(
        norm_gains, dq_chunks, mine, theirs, near, far_up, far, over_x, normed, normed_sib, tokens_in, d_hidden,
        [w3, wq2, wq3], vectors,
    )
    up, down, out = (n // 256 for n in (width, wu2.shape[1], wo2.shape[0]))
    g_up = join(core, both, 1024, 0, up // 4, w_up.shape, lambda p, i: (i, p))
    g_down = join(core, both, 1024, up // 4, down // 4, w_down.shape, lambda p, i: (p * (down // 4) + i, 0))
    g_out = join(core, both, 256, up + down, out, w_out.shape, lambda p, i: (p * out + i, 0))
    g_qkv = join(
        core, both, 256, up + down + out, 3, (3, width, w_qkv.shape[2]), lambda p, i: (i, 0, p), turned=True
    )
    g_qkv = jnp.transpose(g_qkv, (1, 0, 2))
    own_cols = bias_qv.shape[1]
    grad_bias_qv = lax.dynamic_slice_in_dim(vectors[10:12], tp * own_cols, own_cols, 1)
    grad_bias_up = lax.dynamic_slice_in_dim(
        vectors[12:16].reshape(-1), tp * bias_up.shape[0], bias_up.shape[0]
    )
    return (
        result,
        grad_x,
        g_qkv,
        grad_bias_qv,
        g_out,
        vectors[8],
        g_up,
        grad_bias_up,
        g_down,
        vectors[9],
        vectors[0:4],
        vectors[4:8],
    )


def pack_tables(lengths, prefixes, row_total):
    where_row = jnp.arange(row_total, dtype=jnp.int32)
    doc_ends = running_ends(lengths)
    document = jnp.sum((where_row[:, None] >= doc_ends[None, :]).astype(jnp.int32), axis=1)
    limits = doc_ends - lengths + prefixes
    doc_pick = document[:, None] == jnp.arange(lengths.shape[0], dtype=jnp.int32)[None, :]
    visible = jnp.sum(jnp.where(doc_pick, limits[None, :], 0), axis=1)
    return (document, visible)


def padded_tables(document, visible, margin):
    row_total = document.shape[0]
    border = jnp.full((margin,), -1, jnp.int32)
    doc_pad = jnp.concatenate([border, document, border])
    pos_pad = jnp.arange(-margin, row_total + margin, dtype=jnp.int32)
    blank = jnp.zeros((margin,), jnp.int32)
    seen_pad = jnp.concatenate([blank, visible, blank])
    return (doc_pad, pos_pad, seen_pad)


def allowed_pairs(query_pos, query_doc, key_pos, key_doc, key_seen):
    return (query_doc[:, None] == key_doc[None, :]) & (
        (key_pos[None, :] <= query_pos[:, None]) | (key_pos[None, :] < key_seen[None, :])
    )


def pick_blocks(blocks, order):
    return lax.map(lambda i: lax.dynamic_index_in_dim(blocks, i, 0, False), order)


def to_pack(stored, pack_order, margin, block_size):
    blocks = stored.reshape((pack_order.shape[0], block_size) + stored.shape[1:])
    ordered = pick_blocks(blocks, pack_order).reshape(stored.shape)
    widths = [(margin, margin)] + [(0, 0)] * (stored.ndim - 1)
    return jnp.pad(ordered, widths)


def from_pack(padded, placement, margin, block_size, row_total):
    core = padded[margin : margin + row_total]
    blocks = core.reshape((placement.shape[0], block_size) + core.shape[1:])
    return pick_blocks(blocks, placement).reshape(core.shape)


def masked_scores(query_h, key_h, allowed):
    scores = query_h.shape[-1] ** (-0.5) * jnp.einsum(
        "qe,ke->qk", query_h, key_h, preferred_element_type=jnp.float32
    )
    return jnp.where(allowed, scores, -jnp.inf)


def forward_block(query_block, key_win, value_win, allowed):

    def forward_one_head(head):
        query_h = lax.dynamic_index_in_dim(query_block, head, 1, False)
        key_h = lax.dynamic_index_in_dim(key_win, head, 1, False)
        value_h = lax.dynamic_index_in_dim(value_win, head, 1, False)
        masked = masked_scores(query_h, key_h, allowed)
        row_top = jnp.max(masked, axis=1, keepdims=True)
        expo = jnp.exp(masked - row_top)
        row_sum = jnp.sum(expo, axis=1, keepdims=True)
        probs_b = (expo / row_sum).astype(jnp.bfloat16)
        output = jnp.dot(probs_b, value_h, preferred_element_type=jnp.float32)
        return (output, (row_top + jnp.log(row_sum))[:, 0])

    return lax.map(forward_one_head, jnp.arange(query_block.shape[1], dtype=jnp.int32))


def attention_grads(
    query_block, d_att_block, mass_block, total_block, key_block, value_block, allowed
):
    score_scale = query_block.shape[-1] ** (-0.5)

    def attention_one_head(head):
        query_h = lax.dynamic_index_in_dim(query_block, head, 1, False)
        d_att_h = lax.dynamic_index_in_dim(d_att_block, head, 1, False)
        key_h = lax.dynamic_index_in_dim(key_block, head, 1, False)
        value_h = lax.dynamic_index_in_dim(value_block, head, 1, False)
        mass_h = lax.dynamic_index_in_dim(mass_block, head, 0, False)
        total_h = lax.dynamic_index_in_dim(total_block, head, 0, False)
        masked = masked_scores(query_h, key_h, allowed)
        probs = jnp.exp(masked - mass_h[:, None])
        d_probs = jnp.einsum("qe,ke->qk", d_att_h, value_h, preferred_element_type=jnp.float32)
        d_scores = (probs * (d_probs - total_h[:, None])).astype(jnp.bfloat16)
        results = []
        results.append(
            score_scale
            * jnp.einsum("qk,ke->qe", d_scores, key_h, preferred_element_type=jnp.float32)
        )
        results.append(
            score_scale
            * jnp.einsum("qk,qe->ke", d_scores, query_h, preferred_element_type=jnp.float32)
        )
        results.append(
            jnp.einsum(
                "qk,qe->ke", probs.astype(jnp.bfloat16), d_att_h, preferred_element_type=jnp.float32
            )
        )
        return tuple(results)

    return lax.map(attention_one_head, jnp.arange(query_block.shape[1], dtype=jnp.int32))


def general_local(
    tokens_in,
    w_qkv,
    bias_qv,
    w_out,
    bias_out,
    w_up,
    bias_up,
    w_down,
    bias_down,
    norm_gains,
    norm_shifts,
    out_grad,
    lengths,
    prefixes,
    placement,
):
    seq_count = lax.axis_size("seq")
    block_total = placement.shape[0]
    blocks_here = block_total // seq_count
    total_rows = block_total * BLK
    own_rows = blocks_here * BLK
    model_width = w_qkv.shape[0]
    head_span = w_qkv.shape[2]
    heads_here = head_span // HEAD
    margin = LONGEST + BLK
    window = LONGEST + 2 * BLK
    document, visible = pack_tables(lengths, prefixes, total_rows)
    doc_pad, pos_pad, seen_pad = padded_tables(document, visible, margin)
    own_blocks = lax.dynamic_slice_in_dim(
        placement, lax.axis_index("seq") * blocks_here, blocks_here
    )
    pack_order = inverse_order(placement)
    offsets = jnp.arange(BLK, dtype=jnp.int32)

    def query_window(index):
        first = own_blocks[index] * BLK
        key_first = margin + first - LONGEST
        allowed = allowed_pairs(
            first + offsets,
            lax.dynamic_slice_in_dim(document, first, BLK),
            lax.dynamic_slice_in_dim(pos_pad, key_first, window),
            lax.dynamic_slice_in_dim(doc_pad, key_first, window),
            lax.dynamic_slice_in_dim(seen_pad, key_first, window),
        )
        return (key_first, allowed)

    input_f32 = tokens_in.astype(jnp.float32)
    normed, back_first = jax.vjp(layer_norm, input_f32, norm_gains[0], norm_shifts[0])
    rows_all = lax.all_gather(normed.astype(jnp.bfloat16), "tp", axis=0, tiled=True)
    flat_qkv = w_qkv.reshape(model_width, 3 * head_span)
    mixed = jnp.dot(rows_all, flat_qkv, preferred_element_type=jnp.float32).reshape(
        own_rows, 3, head_span
    )
    query_b = (mixed[:, 0] + bias_qv[0].astype(jnp.float32)).astype(jnp.bfloat16)
    key_b = mixed[:, 1].astype(jnp.bfloat16)
    value_b = (mixed[:, 2] + bias_qv[1].astype(jnp.float32)).astype(jnp.bfloat16)
    keys_all, values_all = (
        lax.all_gather(key_b, "seq", axis=0, tiled=True),
        lax.all_gather(value_b, "seq", axis=0, tiled=True),
    )
    keys_pad = to_pack(keys_all, pack_order, margin, BLK).reshape(-1, heads_here, HEAD)
    values_pad = to_pack(values_all, pack_order, margin, BLK).reshape(-1, heads_here, HEAD)
    head_shape = (own_rows, heads_here, HEAD)
    query3 = query_b.reshape(head_shape)
    attended_list = []
    mass_list = []
    for index in range(blocks_here):
        key_first, allowed = query_window(index)
        outputs, masses = forward_block(
            query3[index * BLK : (index + 1) * BLK],
            lax.dynamic_slice_in_dim(keys_pad, key_first, window),
            lax.dynamic_slice_in_dim(values_pad, key_first, window),
            allowed,
        )
        attended_list.append(jnp.transpose(outputs, (1, 0, 2)))
        mass_list.append(masses)
    attended32 = jnp.concatenate(attended_list, axis=0)
    log_mass = jnp.concatenate(mass_list, axis=1)
    attended_b = attended32.reshape(own_rows, head_span).astype(jnp.bfloat16)
    branch = lax.psum_scatter(
        jnp.dot(attended_b, w_out, preferred_element_type=jnp.float32).astype(jnp.bfloat16),
        "tp",
        scatter_dimension=0,
        tiled=True,
    ).astype(jnp.float32) + bias_out.astype(jnp.float32)
    post_attn, back_post = jax.vjp(layer_norm, branch, norm_gains[1], norm_shifts[1])
    hidden = input_f32 + post_attn
    inner, back_inner = jax.vjp(layer_norm, hidden, norm_gains[2], norm_shifts[2])
    inner_all = lax.all_gather(inner.astype(jnp.bfloat16), "tp", axis=0, tiled=True)
    upward = jnp.dot(inner_all, w_up, preferred_element_type=jnp.float32) + bias_up.astype(
        jnp.float32
    )
    active, back_gate = jax.vjp(smooth_gate, upward)
    active_b = active.astype(jnp.bfloat16)
    down = lax.psum_scatter(
        jnp.dot(active_b, w_down, preferred_element_type=jnp.float32).astype(jnp.bfloat16),
        "tp",
        scatter_dimension=0,
        tiled=True,
    ).astype(jnp.float32) + bias_down.astype(jnp.float32)
    final, back_final = jax.vjp(layer_norm, down, norm_gains[3], norm_shifts[3])
    result = (hidden + final).astype(jnp.bfloat16)
    d_down, gain_last, shift_last = back_final(out_grad)
    grad_bias_down = jnp.sum(d_down, axis=0)
    d_down_all = lax.all_gather(d_down.astype(jnp.bfloat16), "tp", axis=0, tiled=True)
    grad_w_down = jnp.einsum("tf,td->fd", active_b, d_down_all, preferred_element_type=jnp.float32)
    d_active = jnp.einsum("td,fd->tf", d_down_all, w_down, preferred_element_type=jnp.float32)
    (d_up,) = back_gate(d_active)
    d_up_b = d_up.astype(jnp.bfloat16)
    grad_bias_up = jnp.sum(d_up_b.astype(jnp.float32), axis=0)
    grad_w_up = jnp.einsum("td,tf->df", inner_all, d_up_b, preferred_element_type=jnp.float32)
    d_inner = lax.psum_scatter(
        jnp.einsum("tf,df->td", d_up_b, w_up, preferred_element_type=jnp.float32).astype(
            jnp.bfloat16
        ),
        "tp",
        scatter_dimension=0,
        tiled=True,
    ).astype(jnp.float32)
    d_hidden_part, gain_third, shift_third = back_inner(d_inner)
    d_hidden = out_grad + d_hidden_part
    d_branch, gain_second, shift_second = back_post(d_hidden)
    grad_bias_out = jnp.sum(d_branch, axis=0)
    d_branch_all = lax.all_gather(d_branch.astype(jnp.bfloat16), "tp", axis=0, tiled=True)
    grad_w_out = jnp.einsum(
        "te,td->ed", attended_b, d_branch_all, preferred_element_type=jnp.float32
    )
    d_att_b = jnp.einsum(
        "td,ed->te", d_branch_all, w_out, preferred_element_type=jnp.float32
    ).astype(jnp.bfloat16)
    d_att3 = d_att_b.reshape(head_shape)
    d_total = jnp.sum(d_att3.astype(jnp.float32) * attended32, axis=2).T
    d_query_list = []
    key_buffer = jnp.zeros((total_rows + 2 * margin, head_span), jnp.float32)
    value_buffer = jnp.zeros((total_rows + 2 * margin, head_span), jnp.float32)
    for index in range(blocks_here):
        key_first, allowed = query_window(index)
        rows = slice(index * BLK, (index + 1) * BLK)
        d_query_h, d_key_h, d_value_h = attention_grads(
            query3[rows],
            d_att3[rows],
            log_mass[:, rows],
            d_total[:, rows],
            lax.dynamic_slice_in_dim(keys_pad, key_first, window),
            lax.dynamic_slice_in_dim(values_pad, key_first, window),
            allowed,
        )
        d_query_list.append(jnp.transpose(d_query_h, (1, 0, 2)))
        key_piece = jnp.transpose(d_key_h, (1, 0, 2)).reshape(window, head_span)
        value_piece = jnp.transpose(d_value_h, (1, 0, 2)).reshape(window, head_span)
        key_buffer = lax.dynamic_update_slice_in_dim(
            key_buffer,
            lax.dynamic_slice_in_dim(key_buffer, key_first, window) + key_piece,
            key_first,
            0,
        )
        value_buffer = lax.dynamic_update_slice_in_dim(
            value_buffer,
            lax.dynamic_slice_in_dim(value_buffer, key_first, window) + value_piece,
            key_first,
            0,
        )
    key_terms = from_pack(key_buffer, placement, margin, BLK, total_rows)
    value_terms = from_pack(value_buffer, placement, margin, BLK, total_rows)
    d_keys, d_values = (
        lax.psum_scatter(
            key_terms.astype(jnp.bfloat16), "seq", scatter_dimension=0, tiled=True
        ).astype(jnp.float32),
        lax.psum_scatter(
            value_terms.astype(jnp.bfloat16), "seq", scatter_dimension=0, tiled=True
        ).astype(jnp.float32),
    )
    d_query = jnp.concatenate(d_query_list, axis=0)
    d_query_b = d_query.reshape(own_rows, head_span).astype(jnp.bfloat16)
    d_keys_b = d_keys.astype(jnp.bfloat16)
    d_values_b = d_values.astype(jnp.bfloat16)
    grad_bias_qv = jnp.stack(
        [
            jnp.sum(d_query_b.astype(jnp.float32), axis=0),
            jnp.sum(d_values_b.astype(jnp.float32), axis=0),
        ]
    )
    d_mixed = jnp.concatenate([d_query_b, d_keys_b, d_values_b], axis=1)
    grad_w_qkv = jnp.einsum(
        "td,tc->dc", rows_all, d_mixed, preferred_element_type=jnp.float32
    ).reshape(model_width, 3, head_span)
    d_normed = lax.psum_scatter(
        jnp.einsum("tc,dc->td", d_mixed, flat_qkv, preferred_element_type=jnp.float32).astype(
            jnp.bfloat16
        ),
        "tp",
        scatter_dimension=0,
        tiled=True,
    ).astype(jnp.float32)
    d_input_part, gain_first, shift_first = back_first(d_normed)
    grad_x = d_hidden + d_input_part
    summed = (
        lax.psum(grad_w_qkv.astype(jnp.bfloat16), "seq").astype(jnp.float32),
        lax.psum(grad_bias_qv.astype(jnp.bfloat16), "seq").astype(jnp.float32),
        lax.psum(grad_w_out.astype(jnp.bfloat16), "seq").astype(jnp.float32),
        lax.psum(grad_w_up.astype(jnp.bfloat16), "seq").astype(jnp.float32),
        lax.psum(grad_bias_up.astype(jnp.bfloat16), "seq").astype(jnp.float32),
        lax.psum(grad_w_down.astype(jnp.bfloat16), "seq").astype(jnp.float32),
    )
    gain_stack = jnp.stack([gain_first, gain_second, gain_third, gain_last])
    shift_stack = jnp.stack([shift_first, shift_second, shift_third, shift_last])
    vectors = lax.psum((gain_stack, shift_stack, grad_bias_out, grad_bias_down), ("seq", "tp"))
    return (
        result,
        grad_x,
        summed[0],
        summed[1],
        summed[2],
        vectors[2],
        summed[3],
        summed[4],
        summed[5],
        vectors[3],
        vectors[0],
        vectors[1],
    )


def solution(mesh):
    placed = (
        P(("seq", "tp"), None),
        P(None, None, "tp"),
        P(None, "tp"),
        P("tp", None),
        P(),
        P(None, "tp"),
        P("tp"),
        P("tp", None),
        P(),
        P(),
        P(),
        P(("seq", "tp"), None),
        P(),
        P(),
        P(),
    )
    seq_count, tp_count = mesh.shape["seq"], mesh.shape["tp"]

    def local(*args):
        tokens_in, w_qkv, placement = args[0], args[1], args[-1]
        heads = w_qkv.shape[2] * tp_count // HEAD
        paired = seq_count * tp_count == 2 * heads == placement.shape[0]
        sizes = (tokens_in.shape[0], w_qkv.shape[0], heads, seq_count, tp_count)
        fast = paired and sizes == (BLK, 1024, 16, 16, 2)
        return (fast_local if fast else general_local)(*args)

    return jax.shard_map(
        local,
        mesh=mesh,
        in_specs=placed,
        out_specs=(
            P(("seq", "tp"), None),
            P(("seq", "tp"), None),
            P(None, None, "tp"),
            P(None, "tp"),
            P("tp", None),
            P(),
            P(None, "tp"),
            P("tp"),
            P("tp", None),
            P(),
            P(),
            P(),
        ),
        check_vma=False,
    )
```

```python
import functools

import jax
import jax.numpy as jnp
from jax import lax
from jax.experimental import pallas as pl
from jax.experimental.pallas import tpu as pltpu
from jax.sharding import PartitionSpec as P

HEAD = 64
BLK = 512
HALF = BLK // 2
QUART = BLK // 4
LONGEST = 4096
STEP_F = 1024
STEP_B = 512
UNROLL = 8
CHUNK_ROWS = 256
FIRST_TICKS = 6
VMEM_LIMIT = 58 << 20
VMEM_MIDDLE = 62 << 20

EPS = 1e-05
F32 = jnp.float32
BF16 = jnp.bfloat16
MESH = pl.DeviceIdType.MESH


def layer_norm(row_block, gain_row, shift_row):
    row_mean = jnp.mean(row_block, axis=-1, keepdims=True)
    centred = row_block - row_mean
    spread = jnp.mean(centred * centred, axis=-1, keepdims=True)
    return centred * lax.rsqrt(spread + EPS) * gain_row + shift_row


def smooth_gate(values):
    return jax.nn.gelu(values, approximate=True)


def running_ends(lengths):
    count = lengths.shape[0]
    index = jnp.arange(count, dtype=jnp.int32)
    return jnp.sum(jnp.where(index[None, :] <= index[:, None], lengths[None, :], 0), axis=1)


def inverse_order(placement):
    index = jnp.arange(placement.shape[0], dtype=jnp.int32)
    return jnp.sum(jnp.where(placement[None, :] == index[:, None], index[None, :], 0), axis=1)


def block_tables(lengths, prefixes, placement, part):
    ends = running_ends(lengths)
    starts = ends - lengths
    limits = starts + prefixes
    offset = part * HALF + jnp.arange(HALF, dtype=jnp.int32)
    pos = placement[:, None] * BLK + offset[None, :]
    inside = (pos[:, :, None] >= starts) & (pos[:, :, None] < ends)

    def pick(values):
        return jnp.sum(jnp.where(inside, values, 0), axis=2)

    low = pick(starts)
    high = jnp.minimum(pick(ends), jnp.maximum(pos + 1, pick(limits)))
    table = jnp.stack(
        [
            jnp.min(low, axis=1) // HALF,
            (jnp.max(high, axis=1) - 1) // HALF + 1,
            jnp.max(low, axis=1),
            jnp.min(high, axis=1),
            placement,
        ]
    )
    return low[:, None, :], high[:, None, :], table


def unpack_t(packed):
    turned = packed.astype(F32).T
    return jnp.concatenate([turned[:HEAD], turned[HEAD:]], axis=1)


def pack_t(turned):
    return jnp.concatenate([turned[:, :QUART], turned[:, QUART:]], axis=0).T


def pieces_two(tab, b, keys, step, start):
    count = keys // HALF
    first, last = tab[0, b], tab[1, b]
    total = last - first
    short = lax.rem(total, count)
    many = total // count + (short > count // 2).astype(jnp.int32)

    def visit(size):
        def at_piece(i, state):
            at = pl.multiple_of((first + i * count) * HALF, HALF)
            whole = (at >= tab[2, b]) & (at + size <= tab[3, b])
            return lax.cond(
                whole, lambda st: step(at, st, False, size), lambda st: step(at, st, True, size), state
            )

        return at_piece

    state = lax.fori_loop(0, many, visit(keys), start)
    half_step = ((short > 0) & (short <= count // 2)).astype(jnp.int32)
    return lax.fori_loop(many, many + half_step, visit(keys // 2), state)


def pieces(tab, b, keys, step, start):
    count = keys // HALF
    first = tab[0, b]

    def visit(i, state):
        at = pl.multiple_of((first + i * count) * HALF, HALF)
        whole = (at >= tab[2, b]) & (at + keys <= tab[3, b])
        return lax.cond(whole, lambda st: step(at, st, False), lambda st: step(at, st, True), state)

    return lax.fori_loop(0, (tab[1, b] - first + count - 1) // count, visit, start)


def attend_kernel(
    part_ref, tab, low_ref, high_ref, q_ref, own_ref, sib_ref,
    out_ref, ot_ref, lse_ref, kv, kvt, rhs_s,
):
    part = part_ref[0]
    scale = HEAD**-0.5
    blocks = q_ref.shape[0]
    rows = blocks * BLK
    depth = lax.broadcasted_iota(jnp.int32, (STEP_F, HALF), 0)

    def prepare(b, carry):
        for ref, which in ((own_ref, part), (sib_ref, 1 - part)):
            at = pl.multiple_of(tab[4, b] * BLK + which * HALF, HALF)
            piece = ref[b]
            kv[pl.ds(at, HALF), :] = piece
            kvt[:, pl.ds(at, HALF)] = piece.T
        qt = unpack_t(q_ref[b]) * scale
        rhs_s[b] = jnp.concatenate([qt, jnp.zeros_like(qt)], axis=0).astype(BF16)
        return carry

    lax.fori_loop(0, blocks, prepare, 0, unroll=UNROLL)
    kv[rows:, :] = jnp.zeros((kv.shape[0] - rows, 2 * HEAD), BF16)
    kvt[:, rows:] = jnp.zeros((2 * HEAD, kv.shape[0] - rows), BF16)

    def one(b, carry):
        low, high = low_ref[b], high_ref[b]

        def step(at, state, masked, size):
            top, total, acc = state
            sc = jnp.dot(kv[pl.ds(at, size), :], rhs_s[b], preferred_element_type=F32)
            if masked:
                rows_of = depth[:size]
                sc = jnp.where((rows_of >= low - at) & (rows_of < high - at), sc, -1e30)
            new = jnp.maximum(top, jnp.max(sc, axis=0, keepdims=True))
            alpha = jnp.exp(top - new)
            pr = jnp.exp(sc - new)
            total = total * alpha + jnp.sum(pr, axis=0, keepdims=True)
            acc = acc * alpha + jnp.dot(
                kvt[HEAD:, pl.ds(at, size)], pr.astype(BF16), preferred_element_type=F32
            )
            return new, total, acc

        start = (
            jnp.full((1, HALF), -1e30, F32),
            jnp.zeros((1, HALF), F32),
            jnp.zeros((HEAD, HALF), F32),
        )
        top, total, acc = pieces_two(tab, b, STEP_F, step, start)
        ot_ref[b] = acc * (1.0 / total)
        lse_ref[b] = top + jnp.log(total)
        return carry

    lax.fori_loop(0, blocks, one, 0)

    def finish(b, carry):
        out_ref[b] = pack_t(ot_ref[b]).astype(BF16)
        return carry

    lax.fori_loop(0, blocks, finish, 0, unroll=UNROLL)


def attend_back_kernel(
    part_ref, tab, low_ref, high_ref, q_ref, da_ref, ot_ref, lse_ref, kv, kvt,
    dq_ref, mine_ref, theirs_ref, dkv, rhs_s, rows_s, total_s, dqt_s,
):
    part = part_ref[0]
    scale = HEAD**-0.5
    blocks = q_ref.shape[0]
    depth = lax.broadcasted_iota(jnp.int32, (STEP_B, HALF), 0)
    lane = lax.broadcasted_iota(jnp.int32, (HALF, 2 * HEAD), 1)

    def prepare(b, carry):
        dkv[pl.ds(pl.multiple_of(b * BLK, BLK), BLK), :] = jnp.zeros((BLK, 2 * HEAD), F32)
        qt = unpack_t(q_ref[b]) * scale
        dat = unpack_t(da_ref[b])
        blank = jnp.zeros_like(qt)
        rhs_s[b, :, :HALF] = jnp.concatenate([qt, blank], axis=0).astype(BF16)
        rhs_s[b, :, HALF:] = jnp.concatenate([blank, dat], axis=0).astype(BF16)
        both = jnp.concatenate([qt, dat], axis=0).T
        rows_s[b, :HALF, :] = jnp.where(lane < HEAD, both, 0.0).astype(BF16)
        rows_s[b, HALF:, :] = jnp.where(lane < HEAD, 0.0, both).astype(BF16)
        total_s[b] = jnp.sum(dat * ot_ref[b], axis=0, keepdims=True)
        return carry

    lax.fori_loop(0, blocks, prepare, 0, unroll=UNROLL)
    dkv[blocks * BLK :, :] = jnp.zeros((dkv.shape[0] - blocks * BLK, 2 * HEAD), F32)

    def one(b, carry):
        total = total_s[b]
        lse = lse_ref[b]
        low, high = low_ref[b], high_ref[b]

        def step(at, acc, masked):
            keys = kv[pl.ds(at, STEP_B), :]
            sc = jnp.dot(keys, rhs_s[b, :, :HALF], preferred_element_type=F32)
            dp = jnp.dot(keys, rhs_s[b, :, HALF:], preferred_element_type=F32)
            if masked:
                sc = jnp.where((depth >= low - at) & (depth < high - at), sc, -1e30)
            pr = jnp.exp(sc - lse)
            ds = (pr * (dp - total)).astype(BF16)
            dkv[pl.ds(at, STEP_B), :] += jnp.dot(
                ds, rows_s[b, :HALF, :], preferred_element_type=F32
            ) + jnp.dot(pr.astype(BF16), rows_s[b, HALF:, :], preferred_element_type=F32)
            return acc + jnp.dot(kvt[:HEAD, pl.ds(at, STEP_B)], ds, preferred_element_type=F32)

        dqt_s[b] = pieces(tab, b, STEP_B, step, jnp.zeros((HEAD, HALF), F32))
        return carry

    lax.fori_loop(0, blocks, one, 0)

    def finish(b, carry):
        dq_ref[b] = pack_t(dqt_s[b] * scale).astype(BF16)
        base = tab[4, b] * BLK
        mine_ref[b] = dkv[pl.ds(pl.multiple_of(base + part * HALF, HALF), HALF), :].astype(BF16)
        theirs_ref[b] = dkv[pl.ds(pl.multiple_of(base + (1 - part) * HALF, HALF), HALF), :].astype(BF16)
        return carry

    lax.fori_loop(0, blocks, finish, 0, unroll=UNROLL)


def vmem(count):
    return [pl.BlockSpec(memory_space=pltpu.VMEM)] * count


def smem(count):
    return [pl.BlockSpec(memory_space=pltpu.SMEM)] * count


def attend(part, tables, q_chunks, kv_own, kv_sib):
    low, high, table = tables
    blocks = q_chunks.shape[0]
    rows = blocks * BLK + STEP_F
    return pl.pallas_call(
        attend_kernel,
        out_shape=(
            jax.ShapeDtypeStruct((blocks, QUART, 2 * HEAD), BF16),
            jax.ShapeDtypeStruct((blocks, HEAD, HALF), F32),
            jax.ShapeDtypeStruct((blocks, 1, HALF), F32),
            jax.ShapeDtypeStruct((rows, 2 * HEAD), BF16),
            jax.ShapeDtypeStruct((2 * HEAD, rows), BF16),
        ),
        in_specs=smem(2) + vmem(5),
        out_specs=tuple(vmem(5)),
        scratch_shapes=[pltpu.VMEM((blocks, 2 * HEAD, HALF), BF16)],
        compiler_params=pltpu.CompilerParams(vmem_limit_bytes=VMEM_LIMIT),
        cost_estimate=pl.CostEstimate(
            flops=40 * 10**9, bytes_accessed=20 << 20, transcendentals=blocks * 4 * BLK * HALF
        ),
        name="attend",
    )(part.reshape(1), table, low, high, q_chunks, kv_own, kv_sib)


def attend_back(part, tables, q_chunks, da_chunks, out_t, mass, kv, kvt):
    low, high, table = tables
    blocks = q_chunks.shape[0]
    return pl.pallas_call(
        attend_back_kernel,
        out_shape=(
            jax.ShapeDtypeStruct((blocks, QUART, 2 * HEAD), BF16),
            jax.ShapeDtypeStruct((blocks, HALF, 2 * HEAD), BF16),
            jax.ShapeDtypeStruct((blocks, HALF, 2 * HEAD), BF16),
        ),
        in_specs=smem(2) + vmem(8),
        out_specs=tuple(vmem(3)),
        scratch_shapes=[
            pltpu.VMEM((blocks * BLK + STEP_F, 2 * HEAD), F32),
            pltpu.VMEM((blocks, 2 * HEAD, BLK), BF16),
            pltpu.VMEM((blocks, BLK, 2 * HEAD), BF16),
            pltpu.VMEM((blocks, 1, HALF), F32),
            pltpu.VMEM((blocks, HEAD, HALF), F32),
        ],
        compiler_params=pltpu.CompilerParams(vmem_limit_bytes=VMEM_LIMIT),
        cost_estimate=pl.CostEstimate(
            flops=60 * 10**9, bytes_accessed=30 << 20, transcendentals=blocks * 4 * BLK * HALF
        ),
        name="attend_back",
    )(part.reshape(1), table, low, high, q_chunks, da_chunks, out_t, mass, kv, kvt)


def chunk_of(who, quarter, index, half):
    absolute = (who[0] * 2 + who[1]) ^ quarter
    tp, sub = absolute // 2, absolute % 2
    return ((sub * 4 + index) * 2 + half) * 2 + tp


def swap_lanes(values):
    return pltpu.roll(values, HEAD, 1)


def low_lanes(rows):
    return lax.broadcasted_iota(jnp.int32, (rows, 2 * HEAD), 1) < HEAD


def store_packed(who, quarter, values, out_ref):
    low = low_lanes(QUART)
    for pair in range(2):
        for half in range(2):
            top = half * HALF
            lanes = slice(pair * 128, pair * 128 + 128)
            first, second = values[top : top + QUART, lanes], values[top + QUART : top + HALF, lanes]
            even = jnp.where(low, first, swap_lanes(second))
            odd = jnp.where(low, swap_lanes(first), second)
            out_ref[chunk_of(who, quarter, 2 * pair, half)] = even.astype(BF16)
            out_ref[chunk_of(who, quarter, 2 * pair + 1, half)] = odd.astype(BF16)


def load_packed(who, quarter, ref, out_ref, base):
    low = low_lanes(QUART)
    for pair in range(2):
        for half in range(2):
            even = ref[chunk_of(who, quarter, 2 * pair, half)].astype(F32)
            odd = ref[chunk_of(who, quarter, 2 * pair + 1, half)].astype(F32)
            top = half * HALF
            lanes = slice(base + pair * 128, base + pair * 128 + 128)
            out_ref[top : top + QUART, lanes] = jnp.where(low, even, swap_lanes(odd)).astype(BF16)
            out_ref[top + QUART : top + HALF, lanes] = jnp.where(low, swap_lanes(even), odd).astype(BF16)


class Place:
    def __init__(self):
        self.seq, self.tp = lax.axis_index("seq"), lax.axis_index("tp")
        self.x = lax.rem(self.seq // 2, 2)
        self.z = self.seq // 4
        self.core_partner = (self.seq ^ 1, self.tp)
        self.x_partner = (self.seq ^ 2, self.tp)
        self.z_partners = [(self.seq ^ (4 * d), self.tp) for d in (1, 2)]
        self.tp_partner = (self.seq, self.tp ^ 1)


def greet_all(count, me, seq, tp):
    barrier = pltpu.get_barrier_semaphore()

    def one(k, carry):
        other = lax.rem(me + k, count)
        pl.semaphore_signal(
            barrier, inc=1, device_id=(other // 2, lax.rem(other, 2)), device_id_type=MESH
        )
        return carry

    lax.fori_loop(1, count, one, 0)
    pl.semaphore_wait(barrier, count - 1)


def greet(partners):
    barrier = pltpu.get_barrier_semaphore()
    for partner in partners:
        pl.semaphore_signal(barrier, inc=1, device_id=partner, device_id_type=MESH)
    pl.semaphore_wait(barrier, len(partners))


def remote(src, dst, send, recv, device):
    return pltpu.make_async_remote_copy(
        src_ref=src, dst_ref=dst, send_sem=send, recv_sem=recv, device_id=device, device_id_type=MESH
    )


def chunk_copy(count, me, k, src, dst, send, recv):
    other = lax.rem(me + k, count)
    return remote(src.at[other], dst.at[me], send.at[k], recv.at[k], (other // 2, lax.rem(other, 2)))


def rows_at(start, size):
    return pl.ds(pl.multiple_of(start, size), size)


def reduce_stages(place, chunks, halved, base, out, both, kept, xbuf, xsum, zbuf, zsum, fbuf, sems, arrived):
    rows = base.shape[0] // chunks
    half, piece = rows // 2, rows // 8
    x, odd, upper = place.x, lax.rem(place.z, 2), place.z // 2
    pair = half // 2

    def x_copy(k):
        seq, tp = place.x_partner
        over_tp = (k >= halved[0]) & (k < halved[1])
        return remote(
            base.at[rows_at(k * rows + (1 - x) * half, half)], xbuf.at[rows_at(k * half, half)],
            sems["xs"].at[k], sems["xr"].at[k],
            (jnp.where(over_tp, place.seq, seq), jnp.where(over_tp, place.tp_partner[1], tp)),
        )

    def z_copy(k):
        return remote(
            xsum.at[rows_at(k * half + (1 - odd) * pair, pair)], zbuf.at[rows_at(k * pair, pair)],
            sems["zs"].at[0, k], sems["zr"].at[0, k], place.z_partners[0],
        )

    def far_z_copy(k):
        return remote(
            zsum.at[rows_at(k * pair + (1 - upper) * piece, piece)], fbuf.at[rows_at(k * piece, piece)],
            sems["zs"].at[1, k], sems["zr"].at[1, k], place.z_partners[1],
        )

    def own_pair(k):
        return rows_at(k * rows + x * half + odd * pair, pair)

    def own_piece(k):
        return rows_at(k * rows + x * half + odd * pair + upper * piece, piece)

    def far_zg_copy(k):
        return remote(
            out.at[own_piece(k)], out.at[own_piece(k)],
            sems["zgs"].at[1, k], sems["zgr"].at[1, k], place.z_partners[1],
        )

    def zg_copy(k):
        return remote(
            out.at[own_pair(k)], out.at[own_pair(k)],
            sems["zgs"].at[0, k], sems["zgr"].at[0, k], place.z_partners[0],
        )

    def xg_copy(k):
        span = rows_at(k * rows + x * half, half)
        return remote(out.at[span], out.at[span], sems["xgs"].at[k], sems["xgr"].at[k], place.x_partner)

    def core_copy(k):
        span = rows_at(k * rows, rows)
        return remote(out.at[span], both.at[1, span], sems["cs"].at[k], sems["cr"].at[k], place.core_partner)

    def stage_x(k):
        arrived(k)
        x_copy(k).start()

    def stage_z(k):
        x_copy(k).wait_recv()
        mine = base[rows_at(k * rows + x * half, half), :].astype(F32)
        xsum[rows_at(k * half, half), :] = (
            mine + xbuf[rows_at(k * half, half), :].astype(F32)
        ).astype(BF16)
        z_copy(k).start()

    def stage_far_z(k):
        z_copy(k).wait_recv()
        span = rows_at(k * pair, pair)
        zsum[span, :] = (
            xsum[rows_at(k * half + odd * pair, pair), :].astype(F32) + zbuf[span, :].astype(F32)
        ).astype(BF16)
        far_z_copy(k).start()

    def stage_far_zg(k):
        far_z_copy(k).wait_recv()
        out[own_piece(k), :] = (
            zsum[rows_at(k * pair + upper * piece, piece), :].astype(F32)
            + fbuf[rows_at(k * piece, piece), :].astype(F32)
        ).astype(BF16)
        far_zg_copy(k).start()

    def stage_zg(k):
        far_zg_copy(k).wait_recv()
        zg_copy(k).start()

    def stage_xg(k):
        zg_copy(k).wait_recv()
        xg_copy(k).start()

    def stage_core(k):
        xg_copy(k).wait_recv()
        core_copy(k).start()

    stages = [stage_x, stage_z, stage_far_z, stage_far_zg, stage_zg, stage_xg, stage_core]

    def tick(t):
        for s, stage in enumerate(stages):
            @pl.when((t >= s) & (t - s < chunks))
            def _():
                stage(t - s)

    def drain(k, carry):
        for copy in (x_copy, z_copy, far_z_copy, far_zg_copy, zg_copy, xg_copy):
            copy(k).wait_send()
        core_copy(k).wait()
        return carry

    def finale():
        keep = pltpu.make_async_copy(out, both.at[0], kept)
        keep.start()
        lax.fori_loop(0, chunks, drain, 0)
        keep.wait()

    return tick, finale, chunks + len(stages) - 1


SEM_NAMES = ("xs", "xr", "zs", "zr", "zgs", "zgr", "xgs", "xgr", "cs", "cr")
VECTOR_STEPS = 5


def finish_kernel(
    chunks, first_ticks, gain_ref, dq_ref, mine_ref, theirs_ref, near_ref, far_up_ref, far_ref, over_x_ref,
    normed_ref, normed_sib_ref, x_ref, dh_ref, w_ref, w2, w3, vec_ref,
    both, gx_ref, vec_out,
    out, base, far, ybuf, xbuf, xsum, zbuf, zsum, fbuf, dq_in, dkv_in, dkv_st, dkv_sib, mixed, mixed_sib,
    normed, normed_sib, x_s, w_s, slots, *rest,
):
    place = Place()
    count = dq_ref.shape[0]
    me = place.seq * 2 + place.tp
    who = (place.tp, lax.rem(place.seq, 2))
    sems = dict(zip(SEM_NAMES, rest))
    qs, qr, ks, kr, ys, yr, ms, mr, vs, vr, loc = rest[len(SEM_NAMES) :]
    rows = base.shape[0] // chunks
    early = near_ref.shape[0]
    crossed = far_up_ref.shape[0] // rows
    met = crossed + over_x_ref.shape[0] // rows
    strip = rows // 2
    greet_all(count, me, place.seq, place.tp)
    dkv_pair = remote(theirs_ref, dkv_sib, ms.at[2], mr.at[2], place.core_partner)
    dkv_pair.start()
    mine_copy = pltpu.make_async_copy(mine_ref, dkv_st, loc.at[0])
    mine_copy.start()

    def dq_copy(k):
        return chunk_copy(count, me, k, dq_ref, dq_in, qs, qr)

    def dkv_copy(k):
        return chunk_copy(count, me, k, dkv_st, dkv_in, ks, kr)

    def start_q(k, carry):
        dq_copy(k).start()
        return carry

    lax.fori_loop(1, count, start_q, 0)
    near_copy = pltpu.make_async_copy(near_ref, base.at[pl.ds(0, early)], loc.at[1])
    near_copy.start()
    far_copy = pltpu.make_async_copy(far_up_ref, ybuf.at[pl.ds(0, far_up_ref.shape[0])], loc.at[2])
    far_copy.start()
    over_copy = pltpu.make_async_copy(
        over_x_ref, ybuf.at[pl.ds(crossed * rows, over_x_ref.shape[0])], loc.at[13]
    )
    over_copy.start()
    strips = [
        pltpu.make_async_copy(
            far_ref.at[rows_at(j * rows + place.x * strip, strip)],
            base.at[rows_at((crossed + j) * rows + (1 - place.x) * strip, strip)],
            loc.at[14 + j],
        )
        for j in range(met - crossed)
    ]
    locals_ = [(dq_ref.at[me], dq_in.at[me]), (normed_ref, normed), (normed_sib_ref, normed_sib)]
    locals_ += [(x_ref, x_s), (dh_ref, gx_ref)]
    col = w_s.shape[3]
    halves = [w_ref.at[:, :, rows_at(c * col, col)] for c in (who[1], 1 - who[1])]
    locals_ += [(w, w_s.at[r]) for r, w in enumerate(halves + [w2, w3])]
    locals_ = [pltpu.make_async_copy(src, dst, loc.at[3 + i]) for i, (src, dst) in enumerate(locals_)]

    def tp_copy(k, src, first):
        return remote(
            src.at[rows_at((k - first) * rows, rows)], ybuf.at[rows_at(k * rows, rows)],
            ys.at[k], yr.at[k], place.tp_partner,
        )

    def cross(k, carry):
        tp_copy(k, far_ref, crossed).start()
        return carry

    settled = early // rows
    lax.fori_loop(met, settled, cross, 0)
    mine_copy.wait()
    dkv_pair.wait()

    def add(b, carry):
        dkv_st[b] = (dkv_st[b].astype(F32) + dkv_sib[b].astype(F32)).astype(BF16)
        return carry

    lax.fori_loop(0, count, add, 0)

    def start_kv(k, carry):
        dkv_copy(k).start()
        return carry

    lax.fori_loop(1, count, start_kv, 0)
    dkv_in[me] = dkv_st[me]
    near_copy.wait()
    for copy in strips + locals_:
        copy.start()
    for copy in [far_copy, over_copy] + strips:
        copy.wait()

    def add_in(into, other):
        base[into, :] = (base[into, :].astype(F32) + ybuf[other, :].astype(F32)).astype(BF16)

    def arrived(k):
        x_met = (k >= crossed) & (k < met)

        @pl.when(k >= met)
        def _():
            tp_copy(k, base, 0).wait_recv()

        @pl.when(jnp.logical_not(x_met))
        def _():
            span = rows_at(k * rows, rows)
            add_in(span, span)

        @pl.when(x_met)
        def _():
            add_in(rows_at(k * rows + place.x * strip, strip), rows_at(k * rows, strip))
            add_in(
                rows_at(k * rows + (1 - place.x) * strip, strip), rows_at(k * rows + strip, strip)
            )

    tick, drain, ticks = reduce_stages(
        place, chunks, (crossed, met), base, out, both, loc.at[12], xbuf, xsum, zbuf, zsum, fbuf, sems, arrived
    )

    def plain(t, carry):
        tick(t)
        return carry

    lax.fori_loop(0, first_ticks, plain, 0)

    def wait(k, carry):
        dq_copy(k).wait()
        dkv_copy(k).wait()
        return carry

    lax.fori_loop(1, count, wait, 0)
    for copy in locals_:
        copy.wait()
    vec_out[...] = vec_ref[...]
    low = low_lanes(HALF)
    for quarter in range(4):
        load_packed(who, quarter, dq_in, mixed.at[quarter], 0)
        for pair in range(2):
            for half in range(2):
                span = slice(half * HALF, half * HALF + HALF)
                even = dkv_in[chunk_of(who, quarter, 2 * pair, half)].astype(F32)
                odd = dkv_in[chunk_of(who, quarter, 2 * pair + 1, half)].astype(F32)
                k_at = 256 + pair * 128
                mixed[quarter, span, k_at : k_at + 128] = jnp.where(low, even, swap_lanes(odd)).astype(BF16)
                mixed[quarter, span, k_at + 256 : k_at + 384] = jnp.where(low, swap_lanes(even), odd).astype(BF16)
    mixed_copies = [
        remote(mixed.at[2 * i + 1], mixed_sib.at[i], ms.at[i], mr.at[i], place.core_partner)
        for i in range(2)
    ]
    for copy in mixed_copies:
        copy.start()
    tick(first_ticks)

    for quarter in range(4):
        absolute = (who[0] * 2 + who[1]) ^ quarter
        lanes = pl.ds(pl.multiple_of(absolute * 256, 256), 256)
        for row, left in ((10, 0), (11, 512)):
            vec_out[row : row + 1, lanes] = jnp.sum(
                mixed[quarter, :, left : left + 256].astype(F32), axis=0, keepdims=True
            )
    gains = jnp.zeros((1, base.shape[1]), F32)
    shifts = jnp.zeros((1, base.shape[1]), F32)
    for part in range(2):
        span = slice(part * HALF, part * HALF + HALF)
        d_normed = jnp.zeros((HALF, base.shape[1]), F32)
        for quarter in range(4):
            for which in range(3):
                lanes = slice(which * col, which * col + col)
                d_normed += dot_nt(mixed[quarter, span, lanes], w_s[quarter, which])
        xhat, rstd = norm_parts(x_s[span, :].astype(F32))
        e = d_normed * gain_ref[0:1, :]
        grad = rstd * (
            e
            - jnp.mean(e, axis=-1, keepdims=True)
            - xhat * jnp.mean(e * xhat, axis=-1, keepdims=True)
        )
        gx_ref[span, :] += grad
        gains += jnp.sum(d_normed * xhat, axis=0, keepdims=True)
        shifts += jnp.sum(d_normed, axis=0, keepdims=True)
        tick(first_ticks + 1 + part)
    vec_out[0:1, :] = gains
    vec_out[4:5, :] = shifts

    for copy in mixed_copies:
        copy.wait()
    late = pl.ds(early, base.shape[0] - early)
    for i, target in ((1, far), (0, base.at[late])):
        for row in range(0, target.shape[0], 256):
            span = slice(row, row + 256)
            target[span, :] = (
                lax.dot_general(
                    mixed[2 * i, :, span], normed[...], (((0,), (0,)), ((), ())), preferred_element_type=F32
                )
                + lax.dot_general(
                    mixed_sib[i, :, span], normed_sib[...], (((0,), (0,)), ((), ())),
                    preferred_element_type=F32,
                )
            ).astype(BF16)
            if i == 1:
                for k in range(settled + row // rows, settled + (row + 256) // rows):
                    tp_copy(k, far, settled).start()

    partners = [place.core_partner, place.tp_partner, place.x_partner] + [
        (place.seq ^ bit, place.tp) for bit in (4, 8)
    ]

    def vector_copy(step):
        return remote(
            slots.at[step], slots.at[VECTOR_STEPS + step], vs.at[step], vr.at[step], partners[step]
        )

    def vector_tick(step):
        if step > 0:
            vector_copy(step - 1).wait()
            vec_out[...] += slots[VECTOR_STEPS + step - 1]
        if step < VECTOR_STEPS:
            slots[step] = vec_out[...]
            vector_copy(step).start()

    def last(t, carry):
        tick(t)
        for step in range(VECTOR_STEPS + 1):
            @pl.when(t == first_ticks + 3 + step)
            def _():
                vector_tick(step)
        return carry

    lax.fori_loop(first_ticks + 3, ticks, last, 0)

    def sent(k, carry):
        tp_copy(k, base, 0).wait_send()
        return carry

    lax.fori_loop(met, chunks, sent, 0)
    drain()


def finish(gain, dq_chunks, mine, theirs, near, far_up, far, over_x, normed, normed_sib, x, d_hidden, weights, vectors):
    early, cols = near.shape
    late = 3 * weights[1].shape[2]
    total = early + late
    chunks = total // CHUNK_ROWS
    count = dq_chunks.shape[0]
    rows = x.shape[0]
    dma = pltpu.SemaphoreType.DMA
    anywhere = pl.BlockSpec(memory_space=pl.ANY)
    scratch = [
        pltpu.VMEM((total, cols), BF16),
        pltpu.VMEM((total, cols), BF16),
        pltpu.VMEM((late, cols), BF16),
        pltpu.VMEM((total, cols), BF16),
        pltpu.VMEM((total // 2, cols), BF16),
        pltpu.VMEM((total // 2, cols), BF16),
        pltpu.VMEM((total // 4, cols), BF16),
        pltpu.VMEM((total // 4, cols), BF16),
        pltpu.VMEM((total // 8, cols), BF16),
        pltpu.VMEM(dq_chunks.shape, BF16),
        pltpu.VMEM(mine.shape, BF16),
        pltpu.VMEM(mine.shape, BF16),
        pltpu.VMEM(mine.shape, BF16),
        pltpu.VMEM((4, rows, late), BF16),
        pltpu.VMEM((2, rows, late), BF16),
        pltpu.VMEM((rows, cols), BF16),
        pltpu.VMEM((rows, cols), BF16),
        pltpu.VMEM((rows, cols), BF16),
        pltpu.VMEM((4,) + weights[1].shape, BF16),
        pltpu.VMEM((2 * VECTOR_STEPS,) + vectors.shape, F32),
    ]
    scratch += [dma((2, chunks) if name[0] == "z" else (chunks,)) for name in SEM_NAMES]
    scratch += [dma((count,))] * 4 + [dma((chunks,))] * 2 + [dma((3,))] * 2
    scratch += [dma((VECTOR_STEPS,))] * 2 + [dma((14 + over_x.shape[0] // CHUNK_ROWS,))]
    return pl.pallas_call(
        functools.partial(finish_kernel, chunks, FIRST_TICKS),
        out_shape=(
            jax.ShapeDtypeStruct((2, total, cols), BF16),
            jax.ShapeDtypeStruct((rows, cols), F32),
            jax.ShapeDtypeStruct(vectors.shape, F32),
        ),
        in_specs=vmem(1) + [anywhere] * 14 + vmem(1),
        out_specs=(anywhere, vmem(1)[0], vmem(1)[0]),
        scratch_shapes=scratch,
        compiler_params=pltpu.CompilerParams(
            collective_id=1, has_side_effects=True, vmem_limit_bytes=VMEM_MIDDLE
        ),
        name="finish",
    )(
        gain, dq_chunks, mine, theirs, near, far_up, far, over_x, normed, normed_sib, x, d_hidden, *weights,
        vectors,
    )


def join_kernel(core_ref, in_ref, out_ref):
    out_ref[...] = in_ref[0].astype(F32)


def join_turned_kernel(core_ref, in_ref, out_ref):
    out_ref[0] = in_ref[0].astype(F32).T


def join(core, both, size, first, count, shape, place, turned=False):
    cols = both.shape[2]
    block = (1, cols, size) if turned else (size, cols)
    return pl.pallas_call(
        join_turned_kernel if turned else join_kernel,
        grid_spec=pltpu.PrefetchScalarGridSpec(
            num_scalar_prefetch=1,
            grid=(2, count),
            in_specs=[pl.BlockSpec((1, size, cols), lambda p, i, c: ((p + c[0]) % 2, first + i, 0))],
            out_specs=pl.BlockSpec(block, lambda p, i, c: place(p, i)),
        ),
        out_shape=jax.ShapeDtypeStruct(shape, F32),
        compiler_params=pltpu.CompilerParams(vmem_limit_bytes=VMEM_LIMIT),
        name="join",
    )(core.reshape(1).astype(jnp.int32), both)


def begin_kernel(
    x_ref, gain_ref, shift_ref, bias_ref, w_ref, wo_ref, wu_ref,
    normed_ref, normed_sib, q_in, kv_own, kv_sib, bias_far, w2, w3, wo2, wo3, wu0,
    w0, w1, q_st, kv_st, *sems,
):
    place = Place()
    count = q_in.shape[0]
    width = x_ref.shape[1]
    me = place.seq * 2 + place.tp
    who = (place.tp, lax.rem(place.seq, 2))
    ks, kr, qs, qr, fs, fr, ws, wr, ls = sems
    greet_all(count, me, place.seq, place.tp)
    core = who[1]
    col, wo_rows = w0.shape[2], wo2.shape[0]
    w_own = w_ref.at[:, :, rows_at(core * col, col)]
    w_far = remote(w_own, w2, ws.at[0], wr.at[0], place.tp_partner)
    w_far.start()
    bias_pair = remote(bias_ref, bias_far, ws.at[5], wr.at[5], place.tp_partner)
    bias_pair.start()
    w_loads = [
        pltpu.make_async_copy(w_own, w0, ls.at[0]),
        pltpu.make_async_copy(w_ref.at[:, :, rows_at((1 - core) * col, col)], w1, ls.at[1]),
    ]
    wu_copy = pltpu.make_async_copy(wu_ref.at[:, rows_at(core * wu0.shape[1], wu0.shape[1])], wu0, ls.at[2])
    wu_copy.start()
    for copy in w_loads:
        copy.start()
    wo_far = remote(wo_ref.at[rows_at(core * wo_rows, wo_rows)], wo2, ws.at[1], wr.at[1], place.tp_partner)
    wo_far.start()
    w_last = remote(w2, w3, ws.at[2], wr.at[2], place.core_partner)
    wo_last = remote(wo2, wo3, ws.at[3], wr.at[3], place.core_partner)

    def norm(part, carry):
        span = rows_at(part * 64, 64)
        normed_ref[span, :] = layer_norm(
            x_ref[span, :].astype(F32), gain_ref[0:1, :], shift_ref[0:1, :]
        ).astype(BF16)
        return carry

    lax.fori_loop(0, x_ref.shape[0] // 64, norm, 0, unroll=2)

    normed_pair = remote(normed_ref, normed_sib, ws.at[4], wr.at[4], place.core_partner)
    normed_pair.start()

    def kv_copy(other):
        return remote(kv_st.at[other], kv_own.at[me], ks.at[other], kr.at[me], (other // 2, lax.rem(other, 2)))

    def q_copy(other):
        return remote(q_st.at[other], q_in.at[me], qs.at[other], qr.at[me], (other // 2, lax.rem(other, 2)))

    def kv_came(other):
        return remote(kv_st.at[other], kv_own.at[other], ks.at[other], kr.at[other], (other // 2, lax.rem(other, 2)))

    def q_came(other):
        return remote(q_st.at[other], q_in.at[other], qs.at[other], qr.at[other], (other // 2, lax.rem(other, 2)))

    def forward(other):
        return remote(kv_own.at[other], kv_sib.at[other], fs.at[other], fr.at[other], place.core_partner)

    low = low_lanes(HALF)

    def project(quarter, w):
        bias = bias_ref if quarter < 2 else bias_far
        side = core if quarter % 2 == 0 else 1 - core

        def bias_at(which):
            return bias[2:3, rows_at(which * 2 * col + side * col, col)]

        def dot(which):
            return dot_nn(normed_ref[...], w[which])

        keys, values = dot(1), dot(2) + bias_at(1)
        for pair in range(2):
            lanes = slice(pair * 128, pair * 128 + 128)
            for half in range(2):
                rows = slice(half * HALF, half * HALF + HALF)
                k, v = keys[rows, lanes], values[rows, lanes]
                kv_st[chunk_of(who, quarter, 2 * pair, half)] = jnp.where(low, k, swap_lanes(v)).astype(BF16)
                kv_st[chunk_of(who, quarter, 2 * pair + 1, half)] = jnp.where(low, swap_lanes(k), v).astype(BF16)
        store_packed(who, quarter, dot(0) + bias_at(0), q_st)

        def send(i, carry):
            turned = lax.rem(i + 2 * (place.seq // 2) + 2, 8)
            other = chunk_of(who, quarter, turned // 2, lax.rem(turned, 2))

            @pl.when(other != me)
            def _():
                kv_copy(other).start()
                q_copy(other).start()

            @pl.when(other == me)
            def _():
                kv_own[me] = kv_st[me]
                q_in[me] = q_st[me]

            return carry

        lax.fori_loop(0, 8, send, 0)

    for copy in w_loads:
        copy.wait()
    project(0, w0)
    project(1, w1)
    w_far.wait()
    bias_pair.wait()
    w_last.start()
    project(2, w2)
    w_last.wait()
    project(3, w3)
    wo_far.wait()
    wo_last.start()
    forward(me).start()

    def receive(i, carry):
        other = lax.rem(place.seq + lax.rem(i, count // 2), count // 2) * 2 + lax.rem(
            place.tp + i // (count // 2), 2
        )
        kv_came(other).wait_recv()
        forward(other).start()
        return carry

    lax.fori_loop(1, count, receive, 0)

    def rest(k, carry):
        other = lax.rem(me + k, count)
        q_came(other).wait_recv()
        kv_copy(other).wait_send()
        q_copy(other).wait_send()
        return carry

    lax.fori_loop(1, count, rest, 0)

    def forwarded(k, carry):
        forward(k).wait()
        return carry

    lax.fori_loop(0, count, forwarded, 0)
    wo_last.wait()
    normed_pair.wait()
    wu_copy.wait()


def begin(x, gains, shifts, bias, w, wo, wu):
    rows, width = x.shape
    count = 32
    dma = pltpu.SemaphoreType.DMA
    anywhere = pl.BlockSpec(memory_space=pl.ANY)
    q_shape, kv_shape = (count, QUART, 2 * HEAD), (count, HALF, 2 * HEAD)
    w_quarter = (3, width, w.shape[2] // 2)
    wo_quarter = (wo.shape[0] // 2, wo.shape[1])
    return pl.pallas_call(
        begin_kernel,
        out_shape=(
            jax.ShapeDtypeStruct((rows, width), BF16),
            jax.ShapeDtypeStruct((rows, width), BF16),
            jax.ShapeDtypeStruct(q_shape, BF16),
            jax.ShapeDtypeStruct(kv_shape, BF16),
            jax.ShapeDtypeStruct(kv_shape, BF16),
            jax.ShapeDtypeStruct(bias.shape, F32),
            jax.ShapeDtypeStruct(w_quarter, BF16),
            jax.ShapeDtypeStruct(w_quarter, BF16),
            jax.ShapeDtypeStruct(wo_quarter, BF16),
            jax.ShapeDtypeStruct(wo_quarter, BF16),
            jax.ShapeDtypeStruct((wu.shape[0], wu.shape[1] // 2), BF16),
        ),
        in_specs=vmem(4) + [anywhere] * 3,
        out_specs=tuple(vmem(1) + [anywhere] + vmem(6) + [anywhere] * 3),
        scratch_shapes=[pltpu.VMEM(w_quarter, BF16)] * 2
        + [pltpu.VMEM(q_shape, BF16), pltpu.VMEM(kv_shape, BF16)]
        + [dma((count,))] * 6
        + [dma((6,))] * 2
        + [dma((3,))],
        compiler_params=pltpu.CompilerParams(
            collective_id=3, has_side_effects=True, vmem_limit_bytes=VMEM_LIMIT
        ),
        name="begin",
    )(x, gains, shifts, bias, w, wo, wu)


def norm_parts(values):
    mean = jnp.mean(values, axis=-1, keepdims=True)
    centred = values - mean
    rstd = lax.rsqrt(jnp.mean(centred * centred, axis=-1, keepdims=True) + EPS)
    return centred * rstd, rstd


GELU_A = 0.7978845608028654
GELU_B = 0.044715


def gelu_parts(u):
    square = u * u
    t = jnp.tanh(GELU_A * u * (1.0 + GELU_B * square))
    rise = 0.5 * (1.0 + t)
    return u * rise, rise + 0.5 * u * (1.0 - t * t) * (GELU_A * (1.0 + 3.0 * GELU_B * square))


def col_sum(values):
    return jnp.sum(values, axis=0, keepdims=True)


def back_rows(xhat, rstd, gain, upstream):
    e = upstream * gain
    return rstd * (
        e - jnp.mean(e, axis=-1, keepdims=True) - xhat * jnp.mean(e * xhat, axis=-1, keepdims=True)
    )


def dot_nn(a, b):
    return jnp.dot(a, b, preferred_element_type=F32)


def dot_nt(a, b):
    return lax.dot_general(a, b, (((1,), (1,)), ((), ())), preferred_element_type=F32)


def dot_tn(a, b):
    return lax.dot_general(a, b, (((0,), (0,)), ((), ())), preferred_element_type=F32)


def middle_kernel(
    gains, shifts, bias_out, bias_down, bias_own, bias_far, att_ref, x_ref, og_ref,
    wo_ref, wo2, wo3, wu_ref, wu2, wd_ref,
    result, da_in, dh, vec, near_ref, far_up_ref, far_ref, over_x_ref,
    att_in, att_s, att_sib, wo_s, wu_s, wd_s, x_s, branch_s, hidden_s, inner_s, inner_sib, act_s, act_sib,
    dg_s, dup_sib, down_s, dd_s, dd_sib, db_s, db_sib, da_st,
    ats, atr, das, dar, ws, wr, cs, cr, loc,
):
    place = Place()
    count = att_in.shape[0]
    me = place.seq * 2 + place.tp
    who = (place.tp, lax.rem(place.seq, 2))
    rows, width = x_s.shape
    hid = wd_s.shape[1]
    wu0, wu1 = (wu_ref.at[:, rows_at(c * hid, hid)] for c in (who[1], 1 - who[1]))
    wo0, wo1 = (wo_ref.at[rows_at(c * wo2.shape[0], wo2.shape[0])] for c in (who[1], 1 - who[1]))
    wd0, wd1 = (wd_ref.at[rows_at(c * hid, hid)] for c in (who[1], 1 - who[1]))
    greet_all(count, me, place.seq, place.tp)

    def start(k, carry):
        chunk_copy(count, me, k, att_ref, att_in, ats, atr).start()
        return carry

    lax.fori_loop(1, count, start, 0)
    wd_far = remote(wd0, wd_s.at[2], ws.at[0], wr.at[0], place.tp_partner)
    wd_far.start()
    wu_last = remote(wu2, wu_s.at[3], ws.at[1], wr.at[1], place.core_partner)
    wu_last.start()
    wd_last = remote(wd_s.at[2], wd_s.at[3], ws.at[2], wr.at[2], place.core_partner)
    loads = [(att_ref.at[me], att_in.at[me]), (x_ref, x_s), (og_ref, dh)]
    loads += [(w, wo_s.at[r]) for r, w in enumerate((wo0, wo1, wo2, wo3))]
    loads += [(w, wu_s.at[r]) for r, w in enumerate((wu0, wu1, wu2))]
    loads += [(w, wd_s.at[r]) for r, w in enumerate((wd0, wd1))]
    loads = [pltpu.make_async_copy(src, dst, loc.at[i]) for i, (src, dst) in enumerate(loads)]
    for copy in loads:
        copy.start()

    def to_core(i, src, dst):
        return remote(src, dst, cs.at[i], cr.at[i], place.core_partner)

    att_pair = [to_core(i, att_s.at[2 * i + 1], att_sib.at[i]) for i in range(2)]
    act_pair = [to_core(2 + i, act_s.at[2 * i + 1], act_sib.at[i]) for i in range(2)]
    dup_pair = [to_core(4 + i, dg_s.at[2 * i + 1], dup_sib.at[i]) for i in range(2)]
    inner_pair = to_core(6, inner_s, inner_sib)
    dd_pair = to_core(7, dd_s, dd_sib)
    db_pair = to_core(8, db_s, db_sib)

    def came(k, carry):
        chunk_copy(count, me, k, att_ref, att_in, ats, atr).wait()
        return carry

    lax.fori_loop(1, count, came, 0)
    for copy in loads:
        copy.wait()
    for quarter in range(4):
        load_packed(who, quarter, att_in, att_s.at[quarter], 0)
    for copy in att_pair:
        copy.start()

    def cols(i):
        return rows_at(i * 256, 256)

    def project(i, carry):
        span = cols(i)
        branch_s[:, span] = (
            dot_nn(att_s[0], wo_s[0, :, span])
            + dot_nn(att_s[1], wo_s[1, :, span])
            + dot_nn(att_s[2], wo_s[2, :, span])
            + dot_nn(att_s[3], wo_s[3, :, span])
            + bias_out[:, span]
        )
        return carry

    lax.fori_loop(0, width // 256, project, 0)

    def into(i, carry):
        span = rows_at(i * 64, 64)
        hidden = x_s[span, :].astype(F32) + layer_norm(branch_s[span, :], gains[1:2, :], shifts[1:2, :])
        hidden_s[span, :] = hidden
        inner_s[span, :] = layer_norm(hidden, gains[2:3, :], shifts[2:3, :]).astype(BF16)
        return carry

    lax.fori_loop(0, rows // 64, into, 0, unroll=2)
    inner_pair.start()
    for quarter in range(4):
        if quarter == 3:
            wu_last.wait()

        bias = bias_own if quarter < 2 else bias_far
        side = who[1] if quarter % 2 == 0 else 1 - who[1]

        def up(i, carry, quarter=quarter, bias=bias, side=side):
            span = cols(i)
            act, slope = gelu_parts(
                dot_nn(inner_s[...], wu_s[quarter, :, span]) + bias[pl.ds(side, 1), span]
            )
            act_s[quarter, :, span] = act.astype(BF16)
            dg_s[quarter, :, span] = slope.astype(BF16)
            return carry

        lax.fori_loop(0, hid // 256, up, 0)
        if quarter % 2 == 1:
            act_pair[quarter // 2].start()

    def down_own(i, carry):
        span = cols(i)
        down_s[:, span] = (
            dot_nn(act_s[0], wd_s[0, :, span]) + dot_nn(act_s[1], wd_s[1, :, span]) + bias_down[:, span]
        )
        return carry

    lax.fori_loop(0, width // 256, down_own, 0)
    wd_far.wait()
    wd_last.start()
    for quarter in (2, 3):
        if quarter == 3:
            wd_last.wait()

        def down_far(i, carry, quarter=quarter):
            span = cols(i)
            down_s[:, span] += dot_nn(act_s[quarter], wd_s[quarter, :, span])
            return carry

        lax.fori_loop(0, width // 256, down_far, 0)

    none = jnp.zeros((1, width), F32)

    def turn(i, carry):
        gain, shift, bias = carry
        span = rows_at(i * 64, 64)
        xhat, rstd = norm_parts(down_s[span, :])
        result[span, :] = (hidden_s[span, :] + xhat * gains[3:4, :] + shifts[3:4, :]).astype(BF16)
        upstream = dh[span, :]
        d_down = back_rows(xhat, rstd, gains[3:4, :], upstream)
        dd_s[span, :] = d_down.astype(BF16)
        return gain + col_sum(upstream * xhat), shift + col_sum(upstream), bias + col_sum(d_down)

    gain, shift, bias = lax.fori_loop(0, rows // 64, turn, (none,) * 3, unroll=2)
    vec[...] = jnp.zeros_like(vec)
    vec[3:4, :] = gain
    vec[7:8, :] = shift
    vec[9:10, :] = bias
    dd_pair.start()
    for quarter in range(4):
        absolute = (who[0] * 2 + who[1]) ^ quarter

        def back_up(i, carry, quarter=quarter, absolute=absolute):
            span = cols(i)
            d_up = dot_nt(dd_s[...], wd_s[quarter, span, :]) * dg_s[quarter, :, span].astype(F32)
            d_up = d_up.astype(BF16)
            dg_s[quarter, :, span] = d_up
            vec[pl.ds(12 + absolute, 1), span] = col_sum(d_up.astype(F32))
            return carry

        lax.fori_loop(0, hid // 256, back_up, 0)
        if quarter % 2 == 1:
            dup_pair[quarter // 2].start()

    def back_inner(i, carry):
        span = cols(i)
        down_s[:, span] = (
            dot_nt(dg_s[0], wu_s[0, span, :])
            + dot_nt(dg_s[1], wu_s[1, span, :])
            + dot_nt(dg_s[2], wu_s[2, span, :])
            + dot_nt(dg_s[3], wu_s[3, span, :])
        )
        return carry

    lax.fori_loop(0, width // 256, back_inner, 0)

    def out_of(i, carry):
        gain3, shift3, gain2, shift2, bias = carry
        span = rows_at(i * 64, 64)
        d_inner = down_s[span, :]
        xhat, rstd = norm_parts(hidden_s[span, :])
        gain3 = gain3 + col_sum(d_inner * xhat)
        shift3 = shift3 + col_sum(d_inner)
        d_hidden = dh[span, :] + back_rows(xhat, rstd, gains[2:3, :], d_inner)
        dh[span, :] = d_hidden
        xhat, rstd = norm_parts(branch_s[span, :])
        d_branch = back_rows(xhat, rstd, gains[1:2, :], d_hidden)
        db_s[span, :] = d_branch.astype(BF16)
        return (
            gain3, shift3, gain2 + col_sum(d_hidden * xhat), shift2 + col_sum(d_hidden),
            bias + col_sum(d_branch),
        )

    sums = lax.fori_loop(0, rows // 64, out_of, (none,) * 5, unroll=2)
    for row, value in zip((2, 6, 1, 5, 8), sums):
        vec[row : row + 1, :] = value
    db_pair.start()

    def da_copy(other):
        return remote(
            da_st.at[other], da_in.at[me], das.at[other], dar.at[me], (other // 2, lax.rem(other, 2))
        )

    def da_came(other):
        return remote(
            da_st.at[other], da_in.at[other], das.at[other], dar.at[other], (other // 2, lax.rem(other, 2))
        )

    for quarter in range(4):
        store_packed(who, quarter, dot_nt(db_s[...], wo_s[quarter]), da_st)

        def send(i, carry, quarter=quarter):
            turned = lax.rem(i + 2 * (place.seq // 2) + 2, 8)
            other = chunk_of(who, quarter, turned // 2, lax.rem(turned, 2))

            @pl.when(other != me)
            def _():
                da_copy(other).start()

            @pl.when(other == me)
            def _():
                da_in[me] = da_st[me]

            return carry

        lax.fori_loop(0, 8, send, 0)

    for copy in dup_pair + [inner_pair]:
        copy.wait()

    def grad_up(i, carry):
        span = cols(i)
        for near, slot in ((0, 0), (2, 1)):
            wu_s[near, :, span] = (
                dot_tn(inner_s[...], dg_s[near, :, span]) + dot_tn(inner_sib[...], dup_sib[slot, :, span])
            ).astype(BF16)
        return carry

    lax.fori_loop(0, hid // 256, grad_up, 0)
    for copy in att_pair + [db_pair]:
        copy.wait()
    for near, slot in ((0, 0), (2, 1)):
        wo_s[near] = (dot_tn(att_s[near], db_s[...]) + dot_tn(att_sib[slot], db_sib[...])).astype(BF16)
    up_rows, out_rows = wu_s.shape[1], wo_s.shape[1]
    stores = [
        (wu_s.at[0], near_ref.at[pl.ds(0, up_rows)]),
        (wo_s.at[0], near_ref.at[pl.ds(up_rows + hid, out_rows)]),
        (wu_s.at[2], far_up_ref),
        (wo_s.at[2], far_ref.at[pl.ds(hid, out_rows)]),
        (wd_s.at[0], near_ref.at[pl.ds(up_rows, hid)]),
        (wd_s.at[2], far_ref.at[pl.ds(0, hid)]),
    ]
    strip = CHUNK_ROWS // 2
    for j in range(hid // CHUNK_ROWS):
        span = rows_at(j * CHUNK_ROWS + (1 - place.x) * strip, strip)
        for i, slot in enumerate((0, 2)):
            stores.append((wd_s.at[slot, span], over_x_ref.at[pl.ds(j * CHUNK_ROWS + i * strip, strip)]))
    stores = [pltpu.make_async_copy(src, dst, loc.at[i]) for i, (src, dst) in enumerate(stores)]
    for copy in stores[:4]:
        copy.start()
    for copy in act_pair + [dd_pair]:
        copy.wait()

    def grad_down(i, carry):
        span = cols(i)
        for near, slot in ((0, 0), (2, 1)):
            wd_s[near, span, :] = (
                dot_tn(act_s[near, :, span], dd_s[...]) + dot_tn(act_sib[slot, :, span], dd_sib[...])
            ).astype(BF16)
        return carry

    lax.fori_loop(0, hid // 256, grad_down, 0)
    for copy in stores[4:]:
        copy.start()

    def da_wait(k, carry):
        other = lax.rem(me + k, count)
        da_came(other).wait_recv()
        da_copy(other).wait_send()
        return carry

    lax.fori_loop(1, count, da_wait, 0)
    for copy in stores:
        copy.wait()


def middle(gains, shifts, bias_out, bias_down, bias, bias_far, att, x, out_grad, wo3, w_up, wu2, w_down):
    rows, width = x.shape
    count = att.shape[0]
    hid = wu2.shape[1]
    out_rows = wo3[1].shape[0]
    dma = pltpu.SemaphoreType.DMA
    anywhere = pl.BlockSpec(memory_space=pl.ANY)

    def held(*shape, dtype=BF16):
        return pltpu.VMEM(shape, dtype)

    scratch = [
        held(*att.shape),
        held(4, rows, out_rows),
        held(2, rows, out_rows),
        held(4, out_rows, width),
        held(4, width, hid),
        held(4, hid, width),
        held(rows, width),
        held(rows, width, dtype=F32),
        held(rows, width, dtype=F32),
        held(rows, width),
        held(rows, width),
        held(4, rows, hid),
        held(2, rows, hid),
        held(4, rows, hid),
        held(2, rows, hid),
        held(rows, width, dtype=F32),
        held(rows, width),
        held(rows, width),
        held(rows, width),
        held(rows, width),
        held(*att.shape),
    ]
    scratch += [dma((count,))] * 4 + [dma((3,))] * 2 + [dma((9,))] * 2 + [dma((6 + 2 * hid // CHUNK_ROWS,))]
    return pl.pallas_call(
        middle_kernel,
        out_shape=(
            jax.ShapeDtypeStruct((rows, width), BF16),
            jax.ShapeDtypeStruct(att.shape, BF16),
            jax.ShapeDtypeStruct((rows, width), F32),
            jax.ShapeDtypeStruct((16, width), F32),
            jax.ShapeDtypeStruct((hid + width + out_rows, width), BF16),
            jax.ShapeDtypeStruct((width, hid), BF16),
            jax.ShapeDtypeStruct((hid + out_rows, width), BF16),
            jax.ShapeDtypeStruct((hid, width), BF16),
        ),
        in_specs=vmem(6) + [anywhere] * 9,
        out_specs=tuple(vmem(4) + [anywhere] * 4),
        scratch_shapes=scratch,
        compiler_params=pltpu.CompilerParams(
            collective_id=4, has_side_effects=True, vmem_limit_bytes=VMEM_MIDDLE
        ),
        name="middle",
    )(
        gains, shifts, bias_out, bias_down, bias, bias_far, att, x, out_grad, *wo3, w_up, wu2, w_down
    )


def fast_local(
    tokens_in, w_qkv, bias_qv, w_out, bias_out, w_up, bias_up, w_down, bias_down,
    norm_gains, norm_shifts, out_grad, lengths, prefixes, placement,
):
    seq_count = lax.axis_size("seq")
    seq, tp = lax.axis_index("seq"), lax.axis_index("tp")
    core = seq % 2
    over_tp = [(0, 1), (1, 0)]

    def to_tp(values):
        return lax.ppermute(values, "tp", over_tp)

    width = w_qkv.shape[0]
    w3 = jnp.transpose(w_qkv, (1, 0, 2))
    bias = jnp.concatenate([bias_up.reshape(2, width), bias_qv.reshape(1, width)]).astype(F32)
    bias = jnp.pad(bias, ((0, 5), (0, 0)))
    tables = block_tables(lengths, prefixes, placement, core)
    normed, normed_sib, q_own, kv_own, kv_sib, bias_far, wq2, wq3, wo2, wo3, wu0 = begin(
        tokens_in, norm_gains, norm_shifts, bias, w3, w_out, w_up
    )
    wu2 = to_tp(wu0)
    att_chunks, out_t, mass, kv_pack, kv_turned = attend(core, tables, q_own, kv_own, kv_sib)
    result, da_own, d_hidden, vectors, near, far_up, far, over_x = middle(
        norm_gains, norm_shifts, bias_out.astype(F32)[None], bias_down.astype(F32)[None], bias, bias_far,
        att_chunks, tokens_in, out_grad, [w_out, wo2, wo3], w_up, wu2, w_down,
    )
    far_up = to_tp(far_up)
    over_x = lax.ppermute(over_x, "seq", [(i, i ^ 2) for i in range(lax.axis_size("seq"))])
    dq_chunks, mine, theirs = attend_back(core, tables, q_own, da_own, out_t, mass, kv_pack, kv_turned)
    both, grad_x, vectors = finish(
        norm_gains, dq_chunks, mine, theirs, near, far_up, far, over_x, normed, normed_sib, tokens_in, d_hidden,
        [w3, wq2, wq3], vectors,
    )
    up, down, out = (n // 256 for n in (width, wu2.shape[1], wo2.shape[0]))
    g_up = join(core, both, 1024, 0, up // 4, w_up.shape, lambda p, i: (i, p))
    g_down = join(core, both, 1024, up // 4, down // 4, w_down.shape, lambda p, i: (p * (down // 4) + i, 0))
    g_out = join(core, both, 256, up + down, out, w_out.shape, lambda p, i: (p * out + i, 0))
    g_qkv = join(
        core, both, 256, up + down + out, 3, (3, width, w_qkv.shape[2]), lambda p, i: (i, 0, p), turned=True
    )
    g_qkv = jnp.transpose(g_qkv, (1, 0, 2))
    own_cols = bias_qv.shape[1]
    grad_bias_qv = lax.dynamic_slice_in_dim(vectors[10:12], tp * own_cols, own_cols, 1)
    grad_bias_up = lax.dynamic_slice_in_dim(
        vectors[12:16].reshape(-1), tp * bias_up.shape[0], bias_up.shape[0]
    )
    return (
        result,
        grad_x,
        g_qkv,
        grad_bias_qv,
        g_out,
        vectors[8],
        g_up,
        grad_bias_up,
        g_down,
        vectors[9],
        vectors[0:4],
        vectors[4:8],
    )


def pack_tables(lengths, prefixes, row_total):
    where_row = jnp.arange(row_total, dtype=jnp.int32)
    doc_ends = running_ends(lengths)
    document = jnp.sum((where_row[:, None] >= doc_ends[None, :]).astype(jnp.int32), axis=1)
    limits = doc_ends - lengths + prefixes
    doc_pick = document[:, None] == jnp.arange(lengths.shape[0], dtype=jnp.int32)[None, :]
    visible = jnp.sum(jnp.where(doc_pick, limits[None, :], 0), axis=1)
    return (document, visible)


def padded_tables(document, visible, margin):
    row_total = document.shape[0]
    border = jnp.full((margin,), -1, jnp.int32)
    doc_pad = jnp.concatenate([border, document, border])
    pos_pad = jnp.arange(-margin, row_total + margin, dtype=jnp.int32)
    blank = jnp.zeros((margin,), jnp.int32)
    seen_pad = jnp.concatenate([blank, visible, blank])
    return (doc_pad, pos_pad, seen_pad)


def allowed_pairs(query_pos, query_doc, key_pos, key_doc, key_seen):
    return (query_doc[:, None] == key_doc[None, :]) & (
        (key_pos[None, :] <= query_pos[:, None]) | (key_pos[None, :] < key_seen[None, :])
    )


def pick_blocks(blocks, order):
    return lax.map(lambda i: lax.dynamic_index_in_dim(blocks, i, 0, False), order)


def to_pack(stored, pack_order, margin, block_size):
    blocks = stored.reshape((pack_order.shape[0], block_size) + stored.shape[1:])
    ordered = pick_blocks(blocks, pack_order).reshape(stored.shape)
    widths = [(margin, margin)] + [(0, 0)] * (stored.ndim - 1)
    return jnp.pad(ordered, widths)


def from_pack(padded, placement, margin, block_size, row_total):
    core = padded[margin : margin + row_total]
    blocks = core.reshape((placement.shape[0], block_size) + core.shape[1:])
    return pick_blocks(blocks, placement).reshape(core.shape)


def masked_scores(query_h, key_h, allowed):
    scores = query_h.shape[-1] ** (-0.5) * jnp.einsum(
        "qe,ke->qk", query_h, key_h, preferred_element_type=jnp.float32
    )
    return jnp.where(allowed, scores, -jnp.inf)


def forward_block(query_block, key_win, value_win, allowed):

    def forward_one_head(head):
        query_h = lax.dynamic_index_in_dim(query_block, head, 1, False)
        key_h = lax.dynamic_index_in_dim(key_win, head, 1, False)
        value_h = lax.dynamic_index_in_dim(value_win, head, 1, False)
        masked = masked_scores(query_h, key_h, allowed)
        row_top = jnp.max(masked, axis=1, keepdims=True)
        expo = jnp.exp(masked - row_top)
        row_sum = jnp.sum(expo, axis=1, keepdims=True)
        probs_b = (expo / row_sum).astype(jnp.bfloat16)
        output = jnp.dot(probs_b, value_h, preferred_element_type=jnp.float32)
        return (output, (row_top + jnp.log(row_sum))[:, 0])

    return lax.map(forward_one_head, jnp.arange(query_block.shape[1], dtype=jnp.int32))


def attention_grads(
    query_block, d_att_block, mass_block, total_block, key_block, value_block, allowed
):
    score_scale = query_block.shape[-1] ** (-0.5)

    def attention_one_head(head):
        query_h = lax.dynamic_index_in_dim(query_block, head, 1, False)
        d_att_h = lax.dynamic_index_in_dim(d_att_block, head, 1, False)
        key_h = lax.dynamic_index_in_dim(key_block, head, 1, False)
        value_h = lax.dynamic_index_in_dim(value_block, head, 1, False)
        mass_h = lax.dynamic_index_in_dim(mass_block, head, 0, False)
        total_h = lax.dynamic_index_in_dim(total_block, head, 0, False)
        masked = masked_scores(query_h, key_h, allowed)
        probs = jnp.exp(masked - mass_h[:, None])
        d_probs = jnp.einsum("qe,ke->qk", d_att_h, value_h, preferred_element_type=jnp.float32)
        d_scores = (probs * (d_probs - total_h[:, None])).astype(jnp.bfloat16)
        results = []
        results.append(
            score_scale
            * jnp.einsum("qk,ke->qe", d_scores, key_h, preferred_element_type=jnp.float32)
        )
        results.append(
            score_scale
            * jnp.einsum("qk,qe->ke", d_scores, query_h, preferred_element_type=jnp.float32)
        )
        results.append(
            jnp.einsum(
                "qk,qe->ke", probs.astype(jnp.bfloat16), d_att_h, preferred_element_type=jnp.float32
            )
        )
        return tuple(results)

    return lax.map(attention_one_head, jnp.arange(query_block.shape[1], dtype=jnp.int32))


def general_local(
    tokens_in,
    w_qkv,
    bias_qv,
    w_out,
    bias_out,
    w_up,
    bias_up,
    w_down,
    bias_down,
    norm_gains,
    norm_shifts,
    out_grad,
    lengths,
    prefixes,
    placement,
):
    seq_count = lax.axis_size("seq")
    block_total = placement.shape[0]
    blocks_here = block_total // seq_count
    total_rows = block_total * BLK
    own_rows = blocks_here * BLK
    model_width = w_qkv.shape[0]
    head_span = w_qkv.shape[2]
    heads_here = head_span // HEAD
    margin = LONGEST + BLK
    window = LONGEST + 2 * BLK
    document, visible = pack_tables(lengths, prefixes, total_rows)
    doc_pad, pos_pad, seen_pad = padded_tables(document, visible, margin)
    own_blocks = lax.dynamic_slice_in_dim(
        placement, lax.axis_index("seq") * blocks_here, blocks_here
    )
    pack_order = inverse_order(placement)
    offsets = jnp.arange(BLK, dtype=jnp.int32)

    def query_window(index):
        first = own_blocks[index] * BLK
        key_first = margin + first - LONGEST
        allowed = allowed_pairs(
            first + offsets,
            lax.dynamic_slice_in_dim(document, first, BLK),
            lax.dynamic_slice_in_dim(pos_pad, key_first, window),
            lax.dynamic_slice_in_dim(doc_pad, key_first, window),
            lax.dynamic_slice_in_dim(seen_pad, key_first, window),
        )
        return (key_first, allowed)

    input_f32 = tokens_in.astype(jnp.float32)
    normed, back_first = jax.vjp(layer_norm, input_f32, norm_gains[0], norm_shifts[0])
    rows_all = lax.all_gather(normed.astype(jnp.bfloat16), "tp", axis=0, tiled=True)
    flat_qkv = w_qkv.reshape(model_width, 3 * head_span)
    mixed = jnp.dot(rows_all, flat_qkv, preferred_element_type=jnp.float32).reshape(
        own_rows, 3, head_span
    )
    query_b = (mixed[:, 0] + bias_qv[0].astype(jnp.float32)).astype(jnp.bfloat16)
    key_b = mixed[:, 1].astype(jnp.bfloat16)
    value_b = (mixed[:, 2] + bias_qv[1].astype(jnp.float32)).astype(jnp.bfloat16)
    keys_all, values_all = (
        lax.all_gather(key_b, "seq", axis=0, tiled=True),
        lax.all_gather(value_b, "seq", axis=0, tiled=True),
    )
    keys_pad = to_pack(keys_all, pack_order, margin, BLK).reshape(-1, heads_here, HEAD)
    values_pad = to_pack(values_all, pack_order, margin, BLK).reshape(-1, heads_here, HEAD)
    head_shape = (own_rows, heads_here, HEAD)
    query3 = query_b.reshape(head_shape)
    attended_list = []
    mass_list = []
    for index in range(blocks_here):
        key_first, allowed = query_window(index)
        outputs, masses = forward_block(
            query3[index * BLK : (index + 1) * BLK],
            lax.dynamic_slice_in_dim(keys_pad, key_first, window),
            lax.dynamic_slice_in_dim(values_pad, key_first, window),
            allowed,
        )
        attended_list.append(jnp.transpose(outputs, (1, 0, 2)))
        mass_list.append(masses)
    attended32 = jnp.concatenate(attended_list, axis=0)
    log_mass = jnp.concatenate(mass_list, axis=1)
    attended_b = attended32.reshape(own_rows, head_span).astype(jnp.bfloat16)
    branch = lax.psum_scatter(
        jnp.dot(attended_b, w_out, preferred_element_type=jnp.float32).astype(jnp.bfloat16),
        "tp",
        scatter_dimension=0,
        tiled=True,
    ).astype(jnp.float32) + bias_out.astype(jnp.float32)
    post_attn, back_post = jax.vjp(layer_norm, branch, norm_gains[1], norm_shifts[1])
    hidden = input_f32 + post_attn
    inner, back_inner = jax.vjp(layer_norm, hidden, norm_gains[2], norm_shifts[2])
    inner_all = lax.all_gather(inner.astype(jnp.bfloat16), "tp", axis=0, tiled=True)
    upward = jnp.dot(inner_all, w_up, preferred_element_type=jnp.float32) + bias_up.astype(
        jnp.float32
    )
    active, back_gate = jax.vjp(smooth_gate, upward)
    active_b = active.astype(jnp.bfloat16)
    down = lax.psum_scatter(
        jnp.dot(active_b, w_down, preferred_element_type=jnp.float32).astype(jnp.bfloat16),
        "tp",
        scatter_dimension=0,
        tiled=True,
    ).astype(jnp.float32) + bias_down.astype(jnp.float32)
    final, back_final = jax.vjp(layer_norm, down, norm_gains[3], norm_shifts[3])
    result = (hidden + final).astype(jnp.bfloat16)
    d_down, gain_last, shift_last = back_final(out_grad)
    grad_bias_down = jnp.sum(d_down, axis=0)
    d_down_all = lax.all_gather(d_down.astype(jnp.bfloat16), "tp", axis=0, tiled=True)
    grad_w_down = jnp.einsum("tf,td->fd", active_b, d_down_all, preferred_element_type=jnp.float32)
    d_active = jnp.einsum("td,fd->tf", d_down_all, w_down, preferred_element_type=jnp.float32)
    (d_up,) = back_gate(d_active)
    d_up_b = d_up.astype(jnp.bfloat16)
    grad_bias_up = jnp.sum(d_up_b.astype(jnp.float32), axis=0)
    grad_w_up = jnp.einsum("td,tf->df", inner_all, d_up_b, preferred_element_type=jnp.float32)
    d_inner = lax.psum_scatter(
        jnp.einsum("tf,df->td", d_up_b, w_up, preferred_element_type=jnp.float32).astype(
            jnp.bfloat16
        ),
        "tp",
        scatter_dimension=0,
        tiled=True,
    ).astype(jnp.float32)
    d_hidden_part, gain_third, shift_third = back_inner(d_inner)
    d_hidden = out_grad + d_hidden_part
    d_branch, gain_second, shift_second = back_post(d_hidden)
    grad_bias_out = jnp.sum(d_branch, axis=0)
    d_branch_all = lax.all_gather(d_branch.astype(jnp.bfloat16), "tp", axis=0, tiled=True)
    grad_w_out = jnp.einsum(
        "te,td->ed", attended_b, d_branch_all, preferred_element_type=jnp.float32
    )
    d_att_b = jnp.einsum(
        "td,ed->te", d_branch_all, w_out, preferred_element_type=jnp.float32
    ).astype(jnp.bfloat16)
    d_att3 = d_att_b.reshape(head_shape)
    d_total = jnp.sum(d_att3.astype(jnp.float32) * attended32, axis=2).T
    d_query_list = []
    key_buffer = jnp.zeros((total_rows + 2 * margin, head_span), jnp.float32)
    value_buffer = jnp.zeros((total_rows + 2 * margin, head_span), jnp.float32)
    for index in range(blocks_here):
        key_first, allowed = query_window(index)
        rows = slice(index * BLK, (index + 1) * BLK)
        d_query_h, d_key_h, d_value_h = attention_grads(
            query3[rows],
            d_att3[rows],
            log_mass[:, rows],
            d_total[:, rows],
            lax.dynamic_slice_in_dim(keys_pad, key_first, window),
            lax.dynamic_slice_in_dim(values_pad, key_first, window),
            allowed,
        )
        d_query_list.append(jnp.transpose(d_query_h, (1, 0, 2)))
        key_piece = jnp.transpose(d_key_h, (1, 0, 2)).reshape(window, head_span)
        value_piece = jnp.transpose(d_value_h, (1, 0, 2)).reshape(window, head_span)
        key_buffer = lax.dynamic_update_slice_in_dim(
            key_buffer,
            lax.dynamic_slice_in_dim(key_buffer, key_first, window) + key_piece,
            key_first,
            0,
        )
        value_buffer = lax.dynamic_update_slice_in_dim(
            value_buffer,
            lax.dynamic_slice_in_dim(value_buffer, key_first, window) + value_piece,
            key_first,
            0,
        )
    key_terms = from_pack(key_buffer, placement, margin, BLK, total_rows)
    value_terms = from_pack(value_buffer, placement, margin, BLK, total_rows)
    d_keys, d_values = (
        lax.psum_scatter(
            key_terms.astype(jnp.bfloat16), "seq", scatter_dimension=0, tiled=True
        ).astype(jnp.float32),
        lax.psum_scatter(
            value_terms.astype(jnp.bfloat16), "seq", scatter_dimension=0, tiled=True
        ).astype(jnp.float32),
    )
    d_query = jnp.concatenate(d_query_list, axis=0)
    d_query_b = d_query.reshape(own_rows, head_span).astype(jnp.bfloat16)
    d_keys_b = d_keys.astype(jnp.bfloat16)
    d_values_b = d_values.astype(jnp.bfloat16)
    grad_bias_qv = jnp.stack(
        [
            jnp.sum(d_query_b.astype(jnp.float32), axis=0),
            jnp.sum(d_values_b.astype(jnp.float32), axis=0),
        ]
    )
    d_mixed = jnp.concatenate([d_query_b, d_keys_b, d_values_b], axis=1)
    grad_w_qkv = jnp.einsum(
        "td,tc->dc", rows_all, d_mixed, preferred_element_type=jnp.float32
    ).reshape(model_width, 3, head_span)
    d_normed = lax.psum_scatter(
        jnp.einsum("tc,dc->td", d_mixed, flat_qkv, preferred_element_type=jnp.float32).astype(
            jnp.bfloat16
        ),
        "tp",
        scatter_dimension=0,
        tiled=True,
    ).astype(jnp.float32)
    d_input_part, gain_first, shift_first = back_first(d_normed)
    grad_x = d_hidden + d_input_part
    summed = (
        lax.psum(grad_w_qkv.astype(jnp.bfloat16), "seq").astype(jnp.float32),
        lax.psum(grad_bias_qv.astype(jnp.bfloat16), "seq").astype(jnp.float32),
        lax.psum(grad_w_out.astype(jnp.bfloat16), "seq").astype(jnp.float32),
        lax.psum(grad_w_up.astype(jnp.bfloat16), "seq").astype(jnp.float32),
        lax.psum(grad_bias_up.astype(jnp.bfloat16), "seq").astype(jnp.float32),
        lax.psum(grad_w_down.astype(jnp.bfloat16), "seq").astype(jnp.float32),
    )
    gain_stack = jnp.stack([gain_first, gain_second, gain_third, gain_last])
    shift_stack = jnp.stack([shift_first, shift_second, shift_third, shift_last])
    vectors = lax.psum((gain_stack, shift_stack, grad_bias_out, grad_bias_down), ("seq", "tp"))
    return (
        result,
        grad_x,
        summed[0],
        summed[1],
        summed[2],
        vectors[2],
        summed[3],
        summed[4],
        summed[5],
        vectors[3],
        vectors[0],
        vectors[1],
    )


def solution(mesh):
    placed = (
        P(("seq", "tp"), None),
        P(None, None, "tp"),
        P(None, "tp"),
        P("tp", None),
        P(),
        P(None, "tp"),
        P("tp"),
        P("tp", None),
        P(),
        P(),
        P(),
        P(("seq", "tp"), None),
        P(),
        P(),
        P(),
    )
    seq_count, tp_count = mesh.shape["seq"], mesh.shape["tp"]

    def local(*args):
        tokens_in, w_qkv, placement = args[0], args[1], args[-1]
        heads = w_qkv.shape[2] * tp_count // HEAD
        paired = seq_count * tp_count == 2 * heads == placement.shape[0]
        sizes = (tokens_in.shape[0], w_qkv.shape[0], heads, seq_count, tp_count)
        fast = paired and sizes == (BLK, 1024, 16, 16, 2)
        return (fast_local if fast else general_local)(*args)

    return jax.shard_map(
        local,
        mesh=mesh,
        in_specs=placed,
        out_specs=(
            P(("seq", "tp"), None),
            P(("seq", "tp"), None),
            P(None, None, "tp"),
            P(None, "tp"),
            P("tp", None),
            P(),
            P(None, "tp"),
            P("tp"),
            P("tp", None),
            P(),
            P(),
            P(),
        ),
        check_vma=False,
    )
```
